32 devices in a mesh: dp: 8 (over z, y), tensor: 4 (over x, core).
Axes of the slice: x: 2, y: 2, z: 4, core: 2. Of those that a mesh axis runs over, the one named last changes fastest.
Arguments:
- prompt_hidden_input: bfloat16 [10240, 5120], P('dp', 'tensor'), may hold values from -100 to 100
- input_norm_gain: float32 [5120], P('tensor'), may hold values from 0.5 to 1.5
- frozen_key_value: bfloat16 [5120, 2048], P(None, 'tensor'), may hold values from -0.078125 to 0.078125
- down_factor_matrix: float32 [5120, 2, 64], P('tensor'), may hold values from -6 to 6
- down_moment_first: float32 [5120, 2, 64], P('tensor'), may hold values from -6 to 6
- down_moment_second: float32 [5120, 2, 64], P('tensor'), may hold values from 0.5 to 4
- up_factor_matrix: float32 [64, 2048], P(None, 'tensor'), may hold values from -6 to 6
- up_moment_first: float32 [64, 2048], P(None, 'tensor'), may hold values from -6 to 6
- up_moment_second: float32 [64, 2048], P(None, 'tensor'), may hold values from 0.5 to 4
- down_gradient: float32 [8, 5120, 2, 64], P('dp', 'tensor'), may hold values from -20 to 20
- up_gradient: float32 [8, 64, 2048], P('dp', None, 'tensor'), may hold values from -20 to 20
Outputs:
- a_next: float32 [3, 5120, 2, 64], P(None, ('tensor', 'dp'))
- b_next: float32 [3, 64, 2048], P(None, 'dp', 'tensor')
- keys_values: bfloat16 [10240, 2048], P('dp', 'tensor')
The draws below stay inside these ranges and needn't reach their ends.
All inputs are finite; a program needn't handle non-finite values.
Results may differ from the reference program's by a relative error of at most 0.0052.
The reference program's roundings to bfloat16 on the way count: a program that leaves them out, or rounds other values in their place, can miss the bound.
Values may be sent and summed in bfloat16 or wider, within the bound.
No kernel may reach another device: no remote copies, remote signals or barrier semaphores. Data moves between devices by JAX's collectives and lax.ppermute only.
A program may use at most 128 MiB of HBM per device.

```python
import math
import jax
import jax.numpy as jnp
from jax import lax

MODEL_WIDTH = 5120
KEY_VALUE_WIDTH = 1024
LOW_RANK = 64
STEP = 100
TOKENS = 10240
N_DP = 8


def replica_rise(count):
    position = jnp.arange(count, dtype=jnp.float32) / max(count - 1, 1)
    return 3.0 ** position


def rough_grad(key, array_shape):
    key_main = jax.random.fold_in(key, 1)
    key_factor = jax.random.fold_in(key, 3)
    factor = jnp.exp(jax.random.uniform(key_factor, array_shape, jnp.float32, 0.0, 0.7))
    values = jax.random.normal(key_main, array_shape, jnp.float32)
    rise = replica_rise(array_shape[0]).reshape((array_shape[0],) + (1,) * (len(array_shape) - 1))
    return jnp.clip(values * factor * rise, -20.0, 20.0)


def draw_down_gradient(key, part):
    key = jax.random.fold_in(key, 11)
    return rough_grad(key, (N_DP, MODEL_WIDTH, 2, LOW_RANK))


def draw_up_gradient(key, part):
    key = jax.random.fold_in(key, 13)
    return rough_grad(key, (N_DP, LOW_RANK, 2 * KEY_VALUE_WIDTH))


def draw_prompt_hidden_input(key, part):
    key = jax.random.fold_in(key, 17)
    key_scale = jax.random.fold_in(key, 1)
    key_values = jax.random.fold_in(key, 2)
    row_scale = jnp.exp(jax.random.uniform(key_scale, (TOKENS, 1), jnp.float32, 0.0, 2.3))
    values = jax.random.normal(key_values, (TOKENS, MODEL_WIDTH), jnp.float32)
    return jnp.clip(values * row_scale, -100.0, 100.0).astype(jnp.bfloat16)


def block_scale(stream_key, shape, cuts, smallest, largest):
    level = 1.0
    for axis_at, blocks in cuts:
        heights = jax.random.uniform(jax.random.fold_in(jax.random.fold_in(stream_key, 6), axis_at), (blocks,), jnp.float32, smallest / len(cuts), largest / len(cuts))
        level = level * jnp.repeat(jnp.exp(heights), shape[axis_at] // blocks).reshape((-1,) + (1,) * (len(shape) - 1 - axis_at))
    return level


def bell_draw(rng, extent, deviation, limit, pieces=(), kind=jnp.bfloat16):
    loudness = block_scale(rng, extent, pieces, -0.22, 0.18) if pieces else 1.0
    drawn = jax.random.normal(rng, extent, jnp.float32) * deviation * loudness
    return jnp.minimum(jnp.maximum(drawn, -limit), limit).astype(kind)


def setup_inputs(seed: int = 0) -> dict:
    key_of = jax.random.split(jax.random.key(seed), 12)
    prompt_hidden_input = draw_prompt_hidden_input(jax.random.fold_in(key_of[11], 71), 0)
    input_norm_gain = jnp.clip(1.0 + 0.1 * jax.random.normal(key_of[1], (MODEL_WIDTH,), jnp.float32), 0.5, 1.5)
    frozen_key_value = bell_draw(key_of[2], (MODEL_WIDTH, 2 * KEY_VALUE_WIDTH), MODEL_WIDTH ** -0.5, 0.078125, ((1, 4),))
    down_factor_matrix = bell_draw(key_of[3], (MODEL_WIDTH, 2, LOW_RANK), 1.0, 6.0, ((0, 4),), jnp.float32)
    down_moment_first = bell_draw(key_of[4], (MODEL_WIDTH, 2, LOW_RANK), 1.0, 6.0, ((0, 4),), jnp.float32)
    down_moment_second = jnp.clip(jnp.exp(math.log(4.0) - 2.0794415 * jax.random.uniform(key_of[5], (MODEL_WIDTH, 2, LOW_RANK), jnp.float32) ** block_scale(key_of[5], (MODEL_WIDTH, 2, LOW_RANK), ((0, 4),), -0.2, 0.2)), 0.5, 4.0)
    up_factor_matrix = bell_draw(key_of[6], (LOW_RANK, 2 * KEY_VALUE_WIDTH), 1.0, 6.0, ((1, 4),), jnp.float32)
    up_moment_first = bell_draw(key_of[7], (LOW_RANK, 2 * KEY_VALUE_WIDTH), 1.0, 6.0, ((1, 4),), jnp.float32)
    up_moment_second = jnp.clip(jnp.exp(math.log(4.0) - 2.0794415 * jax.random.uniform(key_of[8], (LOW_RANK, 2 * KEY_VALUE_WIDTH), jnp.float32) ** block_scale(key_of[8], (LOW_RANK, 2 * KEY_VALUE_WIDTH), ((1, 4),), -0.2, 0.2)), 0.5, 4.0)
    down_gradient = draw_down_gradient(jax.random.fold_in(key_of[11], 71), 0)
    up_gradient = draw_up_gradient(jax.random.fold_in(key_of[11], 71), 0)
    return dict(prompt_hidden_input=prompt_hidden_input, input_norm_gain=input_norm_gain, frozen_key_value=frozen_key_value, down_factor_matrix=down_factor_matrix, down_moment_first=down_moment_first, down_moment_second=down_moment_second, up_factor_matrix=up_factor_matrix, up_moment_first=up_moment_first, up_moment_second=up_moment_second, down_gradient=down_gradient, up_gradient=up_gradient)


def adaptive_moment_update(param, first, second, grad_mean):
    first_new = 0.9 * first + 0.1 * grad_mean
    second_new = 0.999 * second + 0.001 * grad_mean * grad_mean
    step_size = first_new / (1.0 - 0.9 ** STEP) / (jnp.sqrt(second_new / (1.0 - 0.999 ** STEP)) + 1e-08)
    return (param - 0.1 * step_size, first_new, second_new)

def reference(prompt_hidden_input, input_norm_gain, frozen_key_value, down_factor_matrix, down_moment_first, down_moment_second, up_factor_matrix, up_moment_first, up_moment_second, down_gradient, up_gradient):
    down_gradient_average = lax.optimization_barrier(jnp.sum(down_gradient, axis=0)) / N_DP
    up_gradient_average = lax.optimization_barrier(jnp.sum(up_gradient, axis=0)) / N_DP
    down_parameter, down_first_moment, down_second_moment = adaptive_moment_update(down_factor_matrix, down_moment_first, down_moment_second, down_gradient_average)
    up_parameter, up_first_moment, up_second_moment = adaptive_moment_update(up_factor_matrix, up_moment_first, up_moment_second, up_gradient_average)
    a_next = jnp.stack([down_parameter, down_first_moment, down_second_moment])
    b_next = jnp.stack([up_parameter, up_first_moment, up_second_moment])
    factor_a = down_parameter.astype(jnp.bfloat16).astype(jnp.float32)
    factor_b = up_parameter.astype(jnp.bfloat16).astype(jnp.float32).reshape(LOW_RANK, 2, KEY_VALUE_WIDTH)
    adapter_scale = 0.5 / math.sqrt(MODEL_WIDTH * LOW_RANK)
    weight_change = jnp.einsum('djr,rjc->djc', factor_a, factor_b).reshape(MODEL_WIDTH, 2 * KEY_VALUE_WIDTH)
    merged_weight = (frozen_key_value.astype(jnp.float32) + adapter_scale * weight_change).astype(jnp.bfloat16)
    widened = prompt_hidden_input.astype(jnp.float32)
    scaled = (widened * input_norm_gain[None, :]).astype(jnp.bfloat16)
    inv_rms = lax.rsqrt(lax.optimization_barrier(jnp.mean(widened * widened, axis=1)) + 1e-06)
    product = jnp.dot(scaled, merged_weight, preferred_element_type=jnp.float32)
    keys_values = (product * inv_rms[:, None]).astype(jnp.bfloat16)
    return (a_next, b_next, keys_values)
```

```python
import functools
import math

import jax
import jax.numpy as jnp
from jax import lax
from jax.experimental import pallas as pl
from jax.experimental.pallas import tpu as pltpu
from jax.sharding import PartitionSpec as P

KEY_VALUE_WIDTH = 1024
STEP = 100
CORES = 2
CHUNKS = 4


def adaptive_moment_update(param, first, second, grad_mean):
    first_new = 0.9 * first + 0.1 * grad_mean
    second_new = 0.999 * second + 0.001 * grad_mean * grad_mean
    step_size = first_new / (1.0 - 0.9**STEP) / (jnp.sqrt(second_new / (1.0 - 0.999**STEP)) + 1e-08)
    return (param - 0.1 * step_size, first_new, second_new)


def pack_kernel(down_ref, up_ref, out_ref):
    shares, rows, lanes = out_ref.shape
    down = down_ref[...].T
    up = up_ref[...]
    down_rows = down.shape[0] // shares
    up_rows = up.shape[0] // shares
    for i in range(shares):
        pieces = [down[i * down_rows : (i + 1) * down_rows]]
        for k in range(up.shape[1] // lanes):
            pieces.append(up[i * up_rows : (i + 1) * up_rows, k * lanes : (k + 1) * lanes])
        out_ref[i] = jnp.concatenate(pieces, axis=0).astype(jnp.bfloat16)


def adam_kernel(
    replicas, grad_ref, dp_ref, dm_ref, dv_ref, up_ref, um_ref, uv_ref, a_ref, b_ref, fa_ref, fb_ref
):
    total = jnp.sum(grad_ref[...].astype(jnp.float32), axis=0) / replicas
    down_rows = dp_ref.shape[1]
    up_rows, columns = up_ref.shape
    lanes = total.shape[1]
    down = total[:down_rows].T
    up = jnp.concatenate(
        [
            total[down_rows + k * up_rows : down_rows + (k + 1) * up_rows]
            for k in range(columns // lanes)
        ],
        axis=1,
    )
    p, m, v = adaptive_moment_update(dp_ref[...], dm_ref[...], dv_ref[...], down)
    a_ref[0], a_ref[1], a_ref[2] = p, m, v
    fa_ref[...] = p.T.astype(jnp.bfloat16)
    p, m, v = adaptive_moment_update(up_ref[...], um_ref[...], uv_ref[...], up)
    b_ref[0], b_ref[1], b_ref[2] = p, m, v
    fb_ref[...] = p.astype(jnp.bfloat16)


def vmem(count):
    return [pl.BlockSpec(memory_space=pltpu.VMEM)] * count


def body(
    prompt_hidden_input,
    input_norm_gain,
    frozen_key_value,
    down_factor_matrix,
    down_moment_first,
    down_moment_second,
    up_factor_matrix,
    up_moment_first,
    up_moment_second,
    down_gradient,
    up_gradient,
):
    n_dp = lax.axis_size("dp")
    n_tensor = lax.axis_size("tensor")
    chips = n_tensor // CORES
    replica = lax.axis_index("dp")
    place = lax.axis_index("tensor")
    chip, core = place // CORES, place % CORES
    tokens, features = prompt_hidden_input.shape
    width, columns = frozen_key_value.shape
    rank = up_factor_matrix.shape[0]
    factors = down_factor_matrix.shape[1] * rank
    chip_features = CORES * features

    def to_sibling(value):
        return lax.ppermute(value, "tensor", [(t, t ^ 1) for t in range(n_tensor)])

    def to_chip(value, step):
        pairs = [
            (CORES * q + k, CORES * ((q + step) % chips) + k)
            for q in range(chips)
            for k in range(CORES)
        ]
        return lax.ppermute(value, "tensor", pairs)

    share = chip_features // n_dp
    pieces = []
    for step in range(1, chips):
        row = (chip + step) % chips * chip_features + replica * share
        pieces.append(to_chip(lax.dynamic_slice_in_dim(frozen_key_value, row, share, 0), step))
    gathered = [lax.all_gather(piece, "dp", axis=0, tiled=True) for piece in pieces]

    sibling_input = to_sibling(prompt_hidden_input)
    sibling_gain = to_sibling(input_norm_gain)

    down_rows = features // n_dp
    up_rows = rank // n_dp
    packed_rows = down_rows + up_rows * columns // 128

    def by_rank(value):
        return jnp.transpose(value, (1, 2, 0)).reshape(factors, features)

    packed = pl.pallas_call(
        pack_kernel,
        out_shape=jax.ShapeDtypeStruct((n_dp, packed_rows, 128), jnp.bfloat16),
        in_specs=vmem(2),
        out_specs=vmem(1)[0],
    )(by_rank(down_gradient[0]), up_gradient[0])
    exchanged = lax.all_to_all(packed, "dp", 0, 0, tiled=True)

    def own_down(value):
        return lax.dynamic_slice_in_dim(by_rank(value), replica * down_rows, down_rows, 1)

    def own_up(value):
        return lax.dynamic_slice_in_dim(value, replica * up_rows, up_rows, 0)

    a_next, b_next, share_a, share_b = pl.pallas_call(
        functools.partial(adam_kernel, n_dp),
        out_shape=(
            jax.ShapeDtypeStruct((3, factors, down_rows), jnp.float32),
            jax.ShapeDtypeStruct((3, up_rows, columns), jnp.float32),
            jax.ShapeDtypeStruct((down_rows, factors), jnp.bfloat16),
            jax.ShapeDtypeStruct((up_rows, columns), jnp.bfloat16),
        ),
        in_specs=vmem(7),
        out_specs=tuple(vmem(4)),
    )(
        exchanged,
        own_down(down_factor_matrix),
        own_down(down_moment_first),
        own_down(down_moment_second),
        own_up(up_factor_matrix),
        own_up(up_moment_first),
        own_up(up_moment_second),
    )
    a_next = jnp.transpose(
        a_next.reshape(3, factors // rank, rank, down_rows), (0, 3, 1, 2)
    )

    def over_replicas(value):
        copies = jnp.broadcast_to(value[None], (n_dp,) + value.shape)
        return lax.all_to_all(copies, "dp", 0, 0, tiled=True).reshape(
            (n_dp * value.shape[0],) + value.shape[1:]
        )

    factor_a = over_replicas(share_a)
    factor_b = over_replicas(share_b)
    sibling_a = to_sibling(factor_a)

    adapter_scale = 0.5 / math.sqrt(width * rank)

    def merged(weights, first_row, factor_b, owner):
        part = owner * columns // KEY_VALUE_WIDTH
        halves = []
        for factor, half in ((factor_a, core), (sibling_a, 1 - core)):
            chosen = lax.dynamic_slice_in_dim(factor, part * rank, rank, 1)
            change = jnp.dot(chosen, factor_b, preferred_element_type=jnp.float32)
            block = lax.dynamic_slice_in_dim(weights, first_row + half * features, features, 0)
            halves.append(
                (block.astype(jnp.float32) + adapter_scale * change).astype(jnp.bfloat16)
            )
        return jnp.concatenate(halves, axis=0)

    own_wide = prompt_hidden_input.astype(jnp.float32)
    sibling_wide = sibling_input.astype(jnp.float32)
    squares = jnp.sum(own_wide * own_wide, axis=1) + jnp.sum(sibling_wide * sibling_wide, axis=1)
    squares = squares + sum(to_chip(squares, step) for step in range(1, chips))
    inv_rms = lax.rsqrt(squares / width + 1e-06)
    scaled = jnp.concatenate(
        [
            (own_wide * input_norm_gain[None, :]).astype(jnp.bfloat16),
            (sibling_wide * sibling_gain[None, :]).astype(jnp.bfloat16),
        ],
        axis=1,
    )

    received = []
    for step in range(1, chips):
        owner = CORES * ((chip - step) % chips) + core
        weights = merged(gathered[step - 1], 0, to_chip(factor_b, step), owner)
        parts = []
        for rows in jnp.split(scaled, CHUNKS, axis=0):
            product = jnp.dot(rows, weights, preferred_element_type=jnp.float32)
            parts.append(to_chip(product.astype(jnp.bfloat16), chips - step))
        received.append(jnp.concatenate(parts, axis=0).astype(jnp.float32))
    own_weights = merged(frozen_key_value, chip * chip_features, factor_b, place)
    totals = jnp.dot(scaled, own_weights, preferred_element_type=jnp.float32)
    totals = totals + sum(received)
    keys_values = (totals * inv_rms[:, None]).astype(jnp.bfloat16)
    return (a_next, b_next, keys_values)


def solution(mesh):
    placed = (
        P("dp", "tensor"),
        P("tensor"),
        P(None, "tensor"),
        P("tensor", None, None),
        P("tensor", None, None),
        P("tensor", None, None),
        P(None, "tensor"),
        P(None, "tensor"),
        P(None, "tensor"),
        P("dp", "tensor", None, None),
        P("dp", None, "tensor"),
    )
    return jax.shard_map(
        body,
        mesh=mesh,
        in_specs=placed,
        out_specs=(
            P(None, ("tensor", "dp"), None, None),
            P(None, "dp", "tensor"),
            P("dp", "tensor"),
        ),
        check_vma=False,
    )
```

```python
import functools
import math

import jax
import jax.numpy as jnp
from jax import lax
from jax.experimental import pallas as pl
from jax.experimental.pallas import tpu as pltpu
from jax.sharding import PartitionSpec as P

KEY_VALUE_WIDTH = 1024
STEP = 100
CORES = 2
COLUMN_HALVES = 2
TOKEN_HALVES = 2


def adaptive_moment_update(param, first, second, grad_mean):
    first_new = 0.9 * first + 0.1 * grad_mean
    second_new = 0.999 * second + 0.001 * grad_mean * grad_mean
    step_size = first_new / (1.0 - 0.9**STEP) / (jnp.sqrt(second_new / (1.0 - 0.999**STEP)) + 1e-08)
    return (param - 0.1 * step_size, first_new, second_new)


def pack_kernel(down_ref, up_ref, out_ref):
    shares, rows, lanes = out_ref.shape
    down = down_ref[...].T
    up = up_ref[...]
    down_rows = down.shape[0] // shares
    up_rows = up.shape[0] // shares
    for i in range(shares):
        pieces = [down[i * down_rows : (i + 1) * down_rows]]
        for k in range(up.shape[1] // lanes):
            pieces.append(up[i * up_rows : (i + 1) * up_rows, k * lanes : (k + 1) * lanes])
        out_ref[i] = jnp.concatenate(pieces, axis=0).astype(jnp.bfloat16)


def adam_kernel(
    replicas, grad_ref, dp_ref, dm_ref, dv_ref, up_ref, um_ref, uv_ref, a_ref, b_ref, factor_ref
):
    total = jnp.sum(grad_ref[...].astype(jnp.float32), axis=0) / replicas
    down_rows = dp_ref.shape[1]
    up_rows, columns = up_ref.shape
    lanes = total.shape[1]
    strips = columns // lanes
    down = total[:down_rows].T
    up = jnp.concatenate(
        [total[down_rows + k * up_rows : down_rows + (k + 1) * up_rows] for k in range(strips)],
        axis=1,
    )
    p, m, v = adaptive_moment_update(dp_ref[...], dm_ref[...], dv_ref[...], down)
    a_ref[0], a_ref[1], a_ref[2] = p, m, v
    pieces = [p.T]
    p, m, v = adaptive_moment_update(up_ref[...], um_ref[...], uv_ref[...], up)
    b_ref[0], b_ref[1], b_ref[2] = p, m, v
    pieces += [p[:, k * lanes : (k + 1) * lanes] for k in range(strips)]
    rounded = jnp.concatenate(pieces, axis=0).astype(jnp.bfloat16)
    for i in range(replicas):
        factor_ref[i] = rounded


def finish_kernel(*refs):
    own_ref, received_ref, inv_ref, out_ref = refs[0], refs[1], refs[2], refs[-1]
    total = own_ref[...] + received_ref[...].astype(jnp.float32)
    out_ref[...] = (total * inv_ref[:, :1]).astype(out_ref.dtype)


def finish(own, received, inv_rms, at, before):
    rows, columns = received.shape
    block = pl.BlockSpec((rows, columns), lambda i: at)
    in_specs = [
        block,
        pl.BlockSpec((rows, columns), lambda i: (0, 0)),
        pl.BlockSpec((rows, 128), lambda i: (at[0], 0)),
    ]
    operands = [own, received, inv_rms]
    aliases = {}
    if before is not None:
        in_specs.append(pl.BlockSpec(memory_space=pl.ANY))
        operands.append(before)
        aliases = {3: 0}
    return pl.pallas_call(
        finish_kernel,
        grid=(1,),
        out_shape=jax.ShapeDtypeStruct(own.shape, jnp.bfloat16),
        in_specs=in_specs,
        out_specs=block,
        input_output_aliases=aliases,
    )(*operands)


def vmem(count):
    return [pl.BlockSpec(memory_space=pltpu.VMEM)] * count


def body(
    prompt_hidden_input,
    input_norm_gain,
    frozen_key_value,
    down_factor_matrix,
    down_moment_first,
    down_moment_second,
    up_factor_matrix,
    up_moment_first,
    up_moment_second,
    down_gradient,
    up_gradient,
):
    n_dp = lax.axis_size("dp")
    n_tensor = lax.axis_size("tensor")
    chips = n_tensor // CORES
    replica = lax.axis_index("dp")
    place = lax.axis_index("tensor")
    chip, core = place // CORES, place % CORES
    tokens, features = prompt_hidden_input.shape
    width, columns = frozen_key_value.shape
    rank = up_factor_matrix.shape[0]
    factors = down_factor_matrix.shape[1] * rank
    chip_features = CORES * features

    def to_sibling(value):
        return lax.ppermute(value, "tensor", [(t, t ^ 1) for t in range(n_tensor)])

    def to_chip(value, step):
        pairs = [
            (CORES * q + k, CORES * ((q + step) % chips) + k)
            for q in range(chips)
            for k in range(CORES)
        ]
        return lax.ppermute(value, "tensor", pairs)

    halves = min(COLUMN_HALVES, columns // 128)
    wide = columns // halves
    odd = replica % 2

    def swap(value):
        return lax.ppermute(value, "dp", [(k, k ^ 1) for k in range(n_dp)])

    def outside_weights(half, after):
        arrived = []
        for step in range(1, chips):
            row = (chip + step) % chips * chip_features + (core ^ odd) * features
            block = lax.dynamic_slice(
                frozen_key_value, (row, half * wide), (features, wide)
            )
            if after is not None:
                block, _ = lax.optimization_barrier((block, after))
            arrived.append(to_chip(block, step))
        return arrived

    first_half = outside_weights(0, None)

    down_rows = features // n_dp
    up_rows = rank // n_dp
    strips = columns // 128
    packed_rows = down_rows + up_rows * strips

    def by_rank(value):
        return jnp.transpose(value, (1, 2, 0)).reshape(factors, features)

    packed = pl.pallas_call(
        pack_kernel,
        out_shape=jax.ShapeDtypeStruct((n_dp, packed_rows, 128), jnp.bfloat16),
        in_specs=vmem(2),
        out_specs=vmem(1)[0],
    )(by_rank(down_gradient[0]), up_gradient[0])
    exchanged = lax.all_to_all(packed, "dp", 0, 0, tiled=True)

    def own_down(value):
        return lax.dynamic_slice_in_dim(by_rank(value), replica * down_rows, down_rows, 1)

    def own_up(value):
        return lax.dynamic_slice_in_dim(value, replica * up_rows, up_rows, 0)

    a_next, b_next, copies = pl.pallas_call(
        functools.partial(adam_kernel, n_dp),
        out_shape=(
            jax.ShapeDtypeStruct((3, factors, down_rows), jnp.float32),
            jax.ShapeDtypeStruct((3, up_rows, columns), jnp.float32),
            jax.ShapeDtypeStruct((n_dp, packed_rows, 128), jnp.bfloat16),
        ),
        in_specs=vmem(7),
        out_specs=tuple(vmem(3)),
    )(
        exchanged,
        own_down(down_factor_matrix),
        own_down(down_moment_first),
        own_down(down_moment_second),
        own_up(up_factor_matrix),
        own_up(up_moment_first),
        own_up(up_moment_second),
    )
    a_next = jnp.transpose(
        a_next.reshape(3, factors // rank, rank, down_rows), (0, 3, 1, 2)
    )
    own_factors = lax.all_to_all(copies, "dp", 0, 0, tiled=True)

    widened = prompt_hidden_input.astype(jnp.float32)
    squares = jnp.sum(widened * widened, axis=1)
    own_scaled = (widened * input_norm_gain[None, :]).astype(jnp.bfloat16)
    sibling_scaled = to_sibling(own_scaled)
    squares = squares + to_sibling(squares)
    squares = squares + sum(to_chip(squares, step) for step in range(1, chips))
    inv_rms = lax.rsqrt(squares / width + 1e-06)
    inv_rms = jnp.broadcast_to(inv_rms[:, None], (tokens, 128))

    outside = [first_half]
    for half in range(1, halves):
        outside.append(outside_weights(half, (outside[-1], copies)))
    outside = [[(mine, swap(mine)) for mine in arrived] for arrived in outside]

    sibling_factors = to_sibling(own_factors)
    adapter_scale = 0.5 / math.sqrt(width * rank)

    def factor_a(packed):
        return packed[:, :down_rows].reshape(features, factors)

    def factor_b(packed, owner):
        value = packed.reshape(n_dp, strips, up_rows, 128)
        value = jnp.transpose(value, (0, 2, 1, 3)).reshape(rank, columns)
        part = owner * columns // KEY_VALUE_WIDTH
        return jnp.concatenate(
            [jnp.where(part == j, value, jnp.zeros_like(value)) for j in range(factors // rank)],
            axis=0,
        )

    own_a, sibling_a = factor_a(own_factors), factor_a(sibling_factors)
    packed_b = own_factors[:, down_rows:]

    def merged(block, a, b):
        change = jnp.dot(a, b, preferred_element_type=jnp.float32)
        return (block.astype(jnp.float32) + adapter_scale * change).astype(jnp.bfloat16)

    def apply(rows, own_weights, sibling_weights):
        return jnp.dot(
            own_scaled[rows], own_weights, preferred_element_type=jnp.float32
        ) + jnp.dot(sibling_scaled[rows], sibling_weights, preferred_element_type=jnp.float32)

    token_slices = [
        slice(k * tokens // TOKEN_HALVES, (k + 1) * tokens // TOKEN_HALVES)
        for k in range(TOKEN_HALVES)
    ]
    other_b = [
        factor_b(to_chip(packed_b, step), CORES * ((chip - step) % chips) + core)
        for step in range(1, chips)
    ]
    received = {}
    for half in range(halves):
        for step in range(1, chips):
            mine, other = outside[half][step - 1]
            b = other_b[step - 1][:, half * wide : (half + 1) * wide]
            own_weights = merged(jnp.where(odd == 0, mine, other), own_a, b)
            sibling_weights = merged(jnp.where(odd == 0, other, mine), sibling_a, b)
            for k, rows in enumerate(token_slices):
                product = apply(rows, own_weights, sibling_weights).astype(jnp.bfloat16)
                received.setdefault((k, half), []).append(to_chip(product, chips - step))

    own_b = factor_b(packed_b, place)
    row = chip * chip_features
    own_weights = merged(
        lax.dynamic_slice_in_dim(frozen_key_value, row + core * features, features, 0),
        own_a,
        own_b,
    )
    sibling_weights = merged(
        lax.dynamic_slice_in_dim(frozen_key_value, row + (1 - core) * features, features, 0),
        sibling_a,
        own_b,
    )
    totals = apply(slice(None), own_weights, sibling_weights)
    keys_values = None
    for at, arrived in received.items():
        for value in arrived[1:]:
            arrived = [arrived[0].astype(jnp.float32) + value.astype(jnp.float32)]
        keys_values = finish(totals, arrived[0], inv_rms, at, keys_values)
    return (a_next, b_next, keys_values)


def solution(mesh):
    placed = (
        P("dp", "tensor"),
        P("tensor"),
        P(None, "tensor"),
        P("tensor", None, None),
        P("tensor", None, None),
        P("tensor", None, None),
        P(None, "tensor"),
        P(None, "tensor"),
        P(None, "tensor"),
        P("dp", "tensor", None, None),
        P("dp", None, "tensor"),
    )
    return jax.shard_map(
        body,
        mesh=mesh,
        in_specs=placed,
        out_specs=(
            P(None, ("tensor", "dp"), None, None),
            P(None, "dp", "tensor"),
            P("dp", "tensor"),
        ),
        check_vma=False,
    )
```

```python
import functools
import math

import jax
import jax.numpy as jnp
from jax import lax
from jax.experimental import pallas as pl
from jax.experimental.pallas import tpu as pltpu
from jax.sharding import PartitionSpec as P

KEY_VALUE_WIDTH = 1024
STEP = 100
CORES = 2
LANES = 128
VMEM_BYTES = 40 * 2**20


def adaptive_moment_update(param, first, second, grad_mean):
    first_new = 0.9 * first + 0.1 * grad_mean
    second_new = 0.999 * second + 0.001 * grad_mean * grad_mean
    step_size = first_new / (1.0 - 0.9**STEP) / (jnp.sqrt(second_new / (1.0 - 0.999**STEP)) + 1e-08)
    return (param - 0.1 * step_size, first_new, second_new)


def in_vmem(count):
    return [pl.BlockSpec(memory_space=pltpu.VMEM)] * count


def anywhere(count):
    return [pl.BlockSpec(memory_space=pl.ANY)] * count


SCALARS = pl.BlockSpec(memory_space=pltpu.SMEM)


def params(**more):
    return pltpu.CompilerParams(vmem_limit_bytes=VMEM_BYTES, **more)


def pack_kernel(down_ref, up_ref, out_ref):
    shares = out_ref.shape[0]
    down = down_ref[...].T
    up = up_ref[...]
    down_rows = down.shape[0] // shares
    up_rows = up.shape[0] // shares
    for i in range(shares):
        pieces = [down[i * down_rows : (i + 1) * down_rows]]
        for k in range(up.shape[1] // LANES):
            pieces.append(up[i * up_rows : (i + 1) * up_rows, k * LANES : (k + 1) * LANES])
        out_ref[i] = jnp.concatenate(pieces, axis=0).astype(jnp.bfloat16)


def update(grad_ref, down, up, a_ref, b_ref, factor_ref):
    replicas = grad_ref.shape[0]
    total = jnp.sum(grad_ref[...].astype(jnp.float32), axis=0) / replicas
    down_rows = a_ref.shape[2]
    up_rows, columns = b_ref.shape[1:]
    strips = columns // LANES
    down_mean = total[:down_rows].T
    up_mean = jnp.concatenate(
        [total[down_rows + k * up_rows : down_rows + (k + 1) * up_rows] for k in range(strips)],
        axis=1,
    )
    p, m, v = adaptive_moment_update(*down(), down_mean)
    a_ref[0], a_ref[1], a_ref[2] = p, m, v
    pieces = [p.T]
    p, m, v = adaptive_moment_update(*up(), up_mean)
    b_ref[0], b_ref[1], b_ref[2] = p, m, v
    pieces += [p[:, k * LANES : (k + 1) * LANES] for k in range(strips)]
    rounded = jnp.concatenate(pieces, axis=0).astype(jnp.bfloat16)
    for i in range(replicas):
        factor_ref[i] = rounded


def adam_sliced_kernel(grad_ref, dp, dm, dv, up, um, uv, a_ref, b_ref, factor_ref):
    update(
        grad_ref,
        lambda: [ref[...] for ref in (dp, dm, dv)],
        lambda: [ref[...] for ref in (up, um, uv)],
        a_ref,
        b_ref,
        factor_ref,
    )


def adam_kernel(
    replica_ref, grad_ref, dp, dm, dv, up, um, uv, a_ref, b_ref, factor_ref, down_buf, up_buf, sem
):
    down_rows, window = a_ref.shape[2], down_buf.shape[2]
    up_rows = b_ref.shape[1]
    first = replica_ref[0] * down_rows
    lane = jnp.minimum(first // LANES * LANES, dp.shape[1] - window)
    copies = []
    for i, ref in enumerate((dp, dm, dv)):
        source = ref.at[:, pl.ds(pl.multiple_of(lane, LANES), window)]
        copies.append(pltpu.make_async_copy(source, down_buf.at[i], sem.at[i]))
    for i, ref in enumerate((up, um, uv)):
        row = pl.multiple_of(replica_ref[0] * up_rows, up_rows)
        copies.append(
            pltpu.make_async_copy(ref.at[pl.ds(row, up_rows)], up_buf.at[i], sem.at[3 + i])
        )
    for copy in copies:
        copy.start()
    for copy in copies:
        copy.wait()
    shift = window - (first - lane)
    update(
        grad_ref,
        lambda: [pltpu.roll(down_buf[i], shift, 1)[:, :down_rows] for i in range(3)],
        lambda: [up_buf[i] for i in range(3)],
        a_ref,
        b_ref,
        factor_ref,
    )


def factor_a(packed_ref, down_rows):
    pieces = [packed_ref[i].astype(jnp.float32)[:down_rows] for i in range(packed_ref.shape[0])]
    return jnp.concatenate(pieces, axis=0).astype(jnp.bfloat16)


def factor_b(packed, part, parts, strip, up_rows):
    pieces = [
        packed[i].astype(jnp.float32)[strip * up_rows : (strip + 1) * up_rows]
        for i in range(packed.shape[0])
    ]
    value = jnp.concatenate(pieces, axis=0)
    rows = [jnp.where(part == j, value, jnp.zeros_like(value)) for j in range(parts)]
    return jnp.concatenate(rows, axis=0).astype(jnp.bfloat16)


def merge(scale, block, a, b):
    change = jnp.dot(a, b, preferred_element_type=jnp.float32)
    return (block.astype(jnp.float32) + scale * change).astype(jnp.bfloat16)


def tile_of(size):
    return 256 if size % 256 == 0 else size


def apply(own_x, sibling_x, own_w, sibling_w, store):
    tile = tile_of(own_x.shape[0])

    @pl.loop(0, own_x.shape[0] // tile)
    def _(i):
        rows = pl.ds(pl.multiple_of(i * tile, tile), tile)
        store(
            rows,
            jnp.dot(own_x[rows, :], own_w[...], preferred_element_type=jnp.float32)
            + jnp.dot(sibling_x[rows, :], sibling_w[...], preferred_element_type=jnp.float32),
        )


def outside_kernel(
    static, numbers, mine, other, own_f, sibling_f, b_ref, own_x, sibling_x, out, own_w, sibling_w
):
    scale, parts, strip, up_rows = static
    odd, part = numbers[0], numbers[1]
    down_rows = own_f.shape[1] - b_ref.shape[1]
    b = factor_b(b_ref[...], part, parts, strip, up_rows)
    for factors, first, second, target in (
        (own_f, mine, other, own_w),
        (sibling_f, other, mine, sibling_w),
    ):
        block = jnp.where(odd == 0, first[...], second[...])
        target[...] = merge(scale, block, factor_a(factors, down_rows), b)

    def store(rows, value):
        out[rows, :] = value.astype(jnp.bfloat16)

    apply(own_x, sibling_x, own_w, sibling_w, store)


def own_kernel(
    static, numbers, own_block, sibling_block, own_f, sibling_f, own_x, sibling_x, *refs
):
    scale, parts, up_rows = static
    outs, (own_w, sibling_w) = refs[:-2], refs[-2:]
    part = numbers[2]
    strips = len(outs)
    down_rows = own_f.shape[1] - strips * up_rows
    packed = own_f[:, down_rows:]
    b = jnp.concatenate(
        [factor_b(packed, part, parts, strip, up_rows) for strip in range(strips)], axis=1
    )
    for factors, block, target in (
        (own_f, own_block, own_w),
        (sibling_f, sibling_block, sibling_w),
    ):
        target[...] = merge(scale, block[...], factor_a(factors, down_rows), b)

    def store(rows, value):
        for k, out in enumerate(outs):
            out[rows, :] = value[:, k * LANES : (k + 1) * LANES]

    apply(own_x, sibling_x, own_w, sibling_w, store)


def finish_kernel(sources, own, inv, *refs):
    total = own[...]
    for value in refs[:sources]:
        total = total + value[...].astype(jnp.float32)
    refs[-1][...] = (total * inv[...]).astype(refs[-1].dtype)


def finish(own, inv_rms, received, strip, columns, before):
    rows = own.shape[0]
    operands = [own, inv_rms] + received
    in_specs = in_vmem(len(operands))
    aliases = {}
    if before is not None:
        aliases = {len(operands): 0}
        in_specs += anywhere(1)
        operands.append(before)
    return pl.pallas_call(
        functools.partial(finish_kernel, len(received)),
        grid=(1,),
        out_shape=jax.ShapeDtypeStruct((rows, columns), jnp.bfloat16),
        in_specs=in_specs,
        out_specs=pl.BlockSpec((rows, LANES), lambda i: (0, strip)),
        input_output_aliases=aliases,
        compiler_params=params(),
    )(*operands)


def body(
    prompt_hidden_input,
    input_norm_gain,
    frozen_key_value,
    down_factor_matrix,
    down_moment_first,
    down_moment_second,
    up_factor_matrix,
    up_moment_first,
    up_moment_second,
    down_gradient,
    up_gradient,
):
    n_dp = lax.axis_size("dp")
    n_tensor = lax.axis_size("tensor")
    chips = n_tensor // CORES
    replica = lax.axis_index("dp")
    place = lax.axis_index("tensor")
    chip, core = place // CORES, place % CORES
    odd = replica % 2
    tokens, features = prompt_hidden_input.shape
    width, columns = frozen_key_value.shape
    rank = up_factor_matrix.shape[0]
    parts = down_factor_matrix.shape[1]
    factors = parts * rank
    strips = columns // LANES
    down_rows = features // n_dp
    up_rows = rank // n_dp
    packed_rows = down_rows + up_rows * strips
    steps = range(1, chips)
    f32, bf16 = jnp.float32, jnp.bfloat16

    def to_sibling(value):
        return lax.ppermute(value, "tensor", [(t, t ^ 1) for t in range(n_tensor)])

    def to_chip(value, step):
        pairs = [
            (CORES * q + k, CORES * ((q + step) % chips) + k)
            for q in range(chips)
            for k in range(CORES)
        ]
        return lax.ppermute(value, "tensor", pairs)

    def swap(value):
        return lax.ppermute(value, "dp", [(k, k ^ 1) for k in range(n_dp)])

    def owner(step):
        return CORES * ((chip - step) % chips) + core

    def by_rank(value):
        return jnp.transpose(value, (1, 2, 0)).reshape(factors, features)

    packed = pl.pallas_call(
        pack_kernel,
        out_shape=jax.ShapeDtypeStruct((n_dp, packed_rows, LANES), bf16),
        in_specs=in_vmem(2),
        out_specs=in_vmem(1)[0],
        compiler_params=params(),
    )(by_rank(down_gradient[0]), up_gradient[0])
    exchanged = lax.all_to_all(packed, "dp", 0, 0, tiled=True)

    mine = []
    for step in steps:
        row = ((chip + step) % chips * CORES + (core ^ odd)) * features
        mine.append(
            to_chip(lax.dynamic_slice_in_dim(frozen_key_value, row, features, 0), step)
        )

    widened = prompt_hidden_input.astype(f32)
    squares = jnp.sum(widened * widened, axis=1)
    own_x = (widened * input_norm_gain[None, :]).astype(bf16)
    sibling_x = to_sibling(own_x)
    squares = squares + to_sibling(squares)

    down_state = [by_rank(v) for v in (down_factor_matrix, down_moment_first, down_moment_second)]
    up_state = [up_factor_matrix, up_moment_first, up_moment_second]
    out_shape = (
        jax.ShapeDtypeStruct((3, factors, down_rows), f32),
        jax.ShapeDtypeStruct((3, up_rows, columns), f32),
        jax.ShapeDtypeStruct((n_dp, packed_rows, LANES), bf16),
    )
    window = pl.cdiv(down_rows + LANES, LANES) * LANES
    if features % LANES == 0 and window <= features and up_rows % 8 == 0:
        a_next, b_next, copies = pl.pallas_call(
            adam_kernel,
            out_shape=out_shape,
            in_specs=[SCALARS] + in_vmem(1) + anywhere(6),
            out_specs=tuple(in_vmem(3)),
            scratch_shapes=[
                pltpu.VMEM((3, factors, window), f32),
                pltpu.VMEM((3, up_rows, columns), f32),
                pltpu.SemaphoreType.DMA((6,)),
            ],
            compiler_params=params(),
        )(replica[None].astype(jnp.int32), exchanged, *down_state, *up_state)
    else:
        down_state = [
            lax.dynamic_slice_in_dim(v, replica * down_rows, down_rows, 1) for v in down_state
        ]
        up_state = [lax.dynamic_slice_in_dim(v, replica * up_rows, up_rows, 0) for v in up_state]
        a_next, b_next, copies = pl.pallas_call(
            adam_sliced_kernel,
            out_shape=out_shape,
            in_specs=in_vmem(7),
            out_specs=tuple(in_vmem(3)),
            compiler_params=params(),
        )(exchanged, *down_state, *up_state)
    a_next = jnp.transpose(a_next.reshape(3, parts, rank, down_rows), (0, 3, 1, 2))

    own_f = lax.all_to_all(copies, "dp", 0, 0, tiled=True)
    sibling_f = to_sibling(own_f)
    packed_b = own_f[:, down_rows:]
    other_b = [to_chip(packed_b, step) for step in steps]

    held, other = [], []
    for strip in range(strips):
        for value in mine:
            value, _ = lax.optimization_barrier((value, copies))
            held.append(value[:, strip * LANES : (strip + 1) * LANES])
            other.append(swap(held[-1]))

    squares, _ = lax.optimization_barrier((squares, other_b))
    squares = squares + sum(to_chip(squares, step) for step in steps)
    inv_rms = jnp.broadcast_to(lax.rsqrt(squares / width + 1e-06)[:, None], (tokens, LANES))

    scale = 0.5 / math.sqrt(width * rank)
    weight_scratch = lambda n: [pltpu.VMEM((features, n), bf16)] * 2

    def part_of(who):
        return who * columns // KEY_VALUE_WIDTH

    received = [[] for _ in range(strips)]
    product = None
    for strip in range(strips):
        for step in steps:
            at = strip * len(steps) + step - 1
            numbers = jnp.stack([odd, part_of(owner(step))]).astype(jnp.int32)
            if product is not None:
                numbers, _ = lax.optimization_barrier((numbers, product))
            product = pl.pallas_call(
                functools.partial(outside_kernel, (scale, parts, strip, up_rows)),
                out_shape=jax.ShapeDtypeStruct((tokens, LANES), bf16),
                in_specs=[SCALARS] + in_vmem(7),
                out_specs=in_vmem(1)[0],
                scratch_shapes=weight_scratch(LANES),
                compiler_params=params(),
                cost_estimate=pl.CostEstimate(
                    flops=2 * tokens * CORES * features * LANES,
                    bytes_accessed=4 * tokens * features,
                    transcendentals=0,
                ),
            )(numbers, held[at], other[at], own_f, sibling_f, other_b[step - 1], own_x, sibling_x)
            received[strip].append(to_chip(product, chips - step))

    numbers = jnp.stack([place, place ^ 1, part_of(place)]).astype(jnp.int32)
    numbers, _ = lax.optimization_barrier((numbers, product))
    totals = pl.pallas_call(
        functools.partial(own_kernel, (scale, parts, up_rows)),
        out_shape=(jax.ShapeDtypeStruct((tokens, LANES), f32),) * strips,
        grid_spec=pltpu.PrefetchScalarGridSpec(
            num_scalar_prefetch=1,
            grid=(1,),
            in_specs=[
                pl.BlockSpec((features, columns), lambda i, numbers: (numbers[0], 0)),
                pl.BlockSpec((features, columns), lambda i, numbers: (numbers[1], 0)),
            ]
            + in_vmem(4),
            out_specs=tuple(in_vmem(strips)),
            scratch_shapes=weight_scratch(columns),
        ),
        compiler_params=params(),
        cost_estimate=pl.CostEstimate(
            flops=2 * tokens * CORES * features * columns,
            bytes_accessed=4 * tokens * features,
            transcendentals=0,
        ),
    )(numbers, frozen_key_value, frozen_key_value, own_f, sibling_f, own_x, sibling_x)

    keys_values = None
    for strip in range(strips):
        keys_values = finish(
            totals[strip], inv_rms, received[strip], strip, columns, keys_values
        )
    return (a_next, b_next, keys_values)


def solution(mesh):
    placed = (
        P("dp", "tensor"),
        P("tensor"),
        P(None, "tensor"),
        P("tensor", None, None),
        P("tensor", None, None),
        P("tensor", None, None),
        P(None, "tensor"),
        P(None, "tensor"),
        P(None, "tensor"),
        P("dp", "tensor", None, None),
        P("dp", None, "tensor"),
    )
    return jax.shard_map(
        body,
        mesh=mesh,
        in_specs=placed,
        out_specs=(
            P(None, ("tensor", "dp"), None, None),
            P(None, "dp", "tensor"),
            P("dp", "tensor"),
        ),
        check_vma=False,
    )
```

```python
import functools
import math

import jax
import jax.numpy as jnp
from jax import lax
from jax.experimental import pallas as pl
from jax.experimental.pallas import tpu as pltpu
from jax.sharding import PartitionSpec as P

KEY_VALUE_WIDTH = 1024
STEP = 100
CORES = 2
LANES = 128
COLUMN_HALVES = 2
TOKEN_HALVES = 2
VMEM_BYTES = 40 * 2**20


def adaptive_moment_update(param, first, second, grad_mean):
    first_new = 0.9 * first + 0.1 * grad_mean
    second_new = 0.999 * second + 0.001 * grad_mean * grad_mean
    step_size = first_new / (1.0 - 0.9**STEP) / (jnp.sqrt(second_new / (1.0 - 0.999**STEP)) + 1e-08)
    return (param - 0.1 * step_size, first_new, second_new)


def in_vmem(count):
    return [pl.BlockSpec(memory_space=pltpu.VMEM)] * count


def anywhere(count):
    return [pl.BlockSpec(memory_space=pl.ANY)] * count


SCALARS = pl.BlockSpec(memory_space=pltpu.SMEM)


def params(**more):
    return pltpu.CompilerParams(vmem_limit_bytes=VMEM_BYTES, **more)


def pack_kernel(down_ref, up_ref, out_ref):
    shares = out_ref.shape[0]
    down = down_ref[...].T
    up = up_ref[...]
    down_rows = down.shape[0] // shares
    up_rows = up.shape[0] // shares
    for i in range(shares):
        pieces = [down[i * down_rows : (i + 1) * down_rows]]
        for k in range(up.shape[1] // LANES):
            pieces.append(up[i * up_rows : (i + 1) * up_rows, k * LANES : (k + 1) * LANES])
        out_ref[i] = jnp.concatenate(pieces, axis=0).astype(jnp.bfloat16)


def take_kernel(rows_ref, weights_ref, *refs):
    outs, sem = refs[:-1], refs[-1]
    features, wide = outs[0].shape
    groups = weights_ref.shape[1] // wide
    copies = []
    for i, out in enumerate(outs):
        row = pl.multiple_of(rows_ref[i // groups] * features, features)
        source = weights_ref.at[pl.ds(row, features), pl.ds(i % groups * wide, wide)]
        copies.append(pltpu.make_async_copy(source, out, sem.at[i]))
    for copy in copies:
        copy.start()
    for copy in copies:
        copy.wait()


def update(grad_ref, down, up, a_ref, b_ref, factor_ref):
    replicas = grad_ref.shape[0]
    total = jnp.sum(grad_ref[...].astype(jnp.float32), axis=0) / replicas
    down_rows = a_ref.shape[2]
    up_rows, columns = b_ref.shape[1:]
    strips = columns // LANES
    down_mean = total[:down_rows].T
    up_mean = jnp.concatenate(
        [total[down_rows + k * up_rows : down_rows + (k + 1) * up_rows] for k in range(strips)],
        axis=1,
    )
    p, m, v = adaptive_moment_update(*down(), down_mean)
    a_ref[0], a_ref[1], a_ref[2] = p, m, v
    pieces = [p.T]
    p, m, v = adaptive_moment_update(*up(), up_mean)
    b_ref[0], b_ref[1], b_ref[2] = p, m, v
    pieces += [p[:, k * LANES : (k + 1) * LANES] for k in range(strips)]
    rounded = jnp.concatenate(pieces, axis=0).astype(jnp.bfloat16)
    for i in range(replicas):
        factor_ref[i] = rounded


def adam_sliced_kernel(grad_ref, dp, dm, dv, up, um, uv, a_ref, b_ref, factor_ref):
    update(
        grad_ref,
        lambda: [ref[...] for ref in (dp, dm, dv)],
        lambda: [ref[...] for ref in (up, um, uv)],
        a_ref,
        b_ref,
        factor_ref,
    )


def adam_kernel(
    replica_ref, grad_ref, dp, dm, dv, up, um, uv, a_ref, b_ref, factor_ref, down_buf, up_buf, sem
):
    down_rows, window = a_ref.shape[2], down_buf.shape[2]
    up_rows = b_ref.shape[1]
    first = replica_ref[0] * down_rows
    lane = jnp.minimum(first // LANES * LANES, dp.shape[1] - window)
    copies = []
    for i, ref in enumerate((dp, dm, dv)):
        source = ref.at[:, pl.ds(pl.multiple_of(lane, LANES), window)]
        copies.append(pltpu.make_async_copy(source, down_buf.at[i], sem.at[i]))
    for i, ref in enumerate((up, um, uv)):
        row = pl.multiple_of(replica_ref[0] * up_rows, up_rows)
        copies.append(
            pltpu.make_async_copy(ref.at[pl.ds(row, up_rows)], up_buf.at[i], sem.at[3 + i])
        )
    for copy in copies:
        copy.start()
    for copy in copies:
        copy.wait()
    shift = window - (first - lane)
    update(
        grad_ref,
        lambda: [pltpu.roll(down_buf[i], shift, 1)[:, :down_rows] for i in range(3)],
        lambda: [up_buf[i] for i in range(3)],
        a_ref,
        b_ref,
        factor_ref,
    )


def factor_a(packed_ref, down_rows):
    pieces = [packed_ref[i].astype(jnp.float32)[:down_rows] for i in range(packed_ref.shape[0])]
    return jnp.concatenate(pieces, axis=0).astype(jnp.bfloat16)


def factor_b(packed, part, parts, strip, up_rows):
    pieces = [
        packed[i].astype(jnp.float32)[strip * up_rows : (strip + 1) * up_rows]
        for i in range(packed.shape[0])
    ]
    value = jnp.concatenate(pieces, axis=0)
    rows = [jnp.where(part == j, value, jnp.zeros_like(value)) for j in range(parts)]
    return jnp.concatenate(rows, axis=0).astype(jnp.bfloat16)


def merge(scale, block, a, b):
    change = jnp.dot(a, b, preferred_element_type=jnp.float32)
    return (block.astype(jnp.float32) + scale * change).astype(jnp.bfloat16)


def tile_of(size):
    return 256 if size % 256 == 0 else size


def up_factor(static, packed, part):
    _, parts, up_rows, strips = static
    return jnp.concatenate(
        [factor_b(packed, part, parts, strip, up_rows) for strip in strips], axis=1
    )


def outside_kernel(static, numbers, mine, other, own_f, sibling_f, b_ref, out):
    odd, part = numbers[0], numbers[1]
    features = mine.shape[0]
    down_rows = own_f.shape[1] - b_ref.shape[1]
    b = up_factor(static, b_ref[...], part)
    for at, factors, first, second in (
        (0, own_f, mine, other),
        (features, sibling_f, other, mine),
    ):
        block = jnp.where(odd == 0, first[...], second[...])
        out[at : at + features] = merge(static[0], block, factor_a(factors, down_rows), b)


def own_kernel(static, numbers, own_block, sibling_block, own_f, sibling_f, x, *refs):
    outs, weights = refs[:-1], refs[-1]
    features = own_block.shape[0]
    wide = outs[0].shape[1]
    down_rows = own_f.shape[1] - len(static[3]) * static[2]
    b = up_factor(static, own_f[:, down_rows:], numbers[2])
    for at, factors, block in ((0, own_f, own_block), (features, sibling_f, sibling_block)):
        weights[at : at + features] = merge(static[0], block[...], factor_a(factors, down_rows), b)
    tile = tile_of(x.shape[0])

    @pl.loop(0, x.shape[0] // tile)
    def _(i):
        rows = pl.ds(pl.multiple_of(i * tile, tile), tile)
        value = jnp.dot(x[rows, :], weights[...], preferred_element_type=jnp.float32)
        for k, out in enumerate(outs):
            out[rows, :] = value[:, k * wide : (k + 1) * wide]


def finish_kernel(sources, first, own, inv, *refs):
    rows = pl.ds(first, refs[-1].shape[0])
    total = own[rows, :]
    for value in refs[:sources]:
        total = total + value[...].astype(jnp.float32)
    refs[-1][...] = (total * inv[rows, :1]).astype(refs[-1].dtype)


def finish(own, inv_rms, received, at, shape, before):
    block = received[0].shape
    operands = [own, inv_rms] + received
    in_specs = in_vmem(len(operands))
    aliases = {}
    if before is not None:
        aliases = {len(operands): 0}
        in_specs += anywhere(1)
        operands.append(before)
    return pl.pallas_call(
        functools.partial(finish_kernel, len(received), at[0] * block[0]),
        grid=(1,),
        out_shape=jax.ShapeDtypeStruct(shape, jnp.bfloat16),
        in_specs=in_specs,
        out_specs=pl.BlockSpec(block, lambda i: at),
        input_output_aliases=aliases,
        compiler_params=params(),
    )(*operands)


def body(
    prompt_hidden_input,
    input_norm_gain,
    frozen_key_value,
    down_factor_matrix,
    down_moment_first,
    down_moment_second,
    up_factor_matrix,
    up_moment_first,
    up_moment_second,
    down_gradient,
    up_gradient,
):
    n_dp = lax.axis_size("dp")
    n_tensor = lax.axis_size("tensor")
    chips = n_tensor // CORES
    replica = lax.axis_index("dp")
    place = lax.axis_index("tensor")
    chip, core = place // CORES, place % CORES
    odd = replica % 2
    tokens, features = prompt_hidden_input.shape
    width, columns = frozen_key_value.shape
    rank = up_factor_matrix.shape[0]
    parts = down_factor_matrix.shape[1]
    factors = parts * rank
    strips = columns // LANES
    down_rows = features // n_dp
    up_rows = rank // n_dp
    packed_rows = down_rows + up_rows * strips
    steps = range(1, chips)
    f32, bf16 = jnp.float32, jnp.bfloat16

    def to_sibling(value):
        return lax.ppermute(value, "tensor", [(t, t ^ 1) for t in range(n_tensor)])

    def to_chip(value, step):
        pairs = [
            (CORES * q + k, CORES * ((q + step) % chips) + k)
            for q in range(chips)
            for k in range(CORES)
        ]
        return lax.ppermute(value, "tensor", pairs)

    def swap(value):
        return lax.ppermute(value, "dp", [(k, k ^ 1) for k in range(n_dp)])

    def owner(step):
        return CORES * ((chip - step) % chips) + core

    halves = min(COLUMN_HALVES, strips)
    wide = columns // halves
    blocks = jnp.stack(
        [(chip + step) % chips * CORES + (core ^ odd) for step in steps]
    ).astype(jnp.int32)
    count = len(steps) * halves
    pieces = pl.pallas_call(
        take_kernel,
        out_shape=(jax.ShapeDtypeStruct((features, wide), bf16),) * count,
        in_specs=[SCALARS] + anywhere(1),
        out_specs=tuple(anywhere(count)),
        scratch_shapes=[pltpu.SemaphoreType.DMA((count,))],
        compiler_params=params(),
    )(blocks, frozen_key_value)

    def by_rank(value):
        return jnp.transpose(value, (1, 2, 0)).reshape(factors, features)

    up_sent, _ = lax.optimization_barrier((up_gradient[0], pieces))
    packed = pl.pallas_call(
        pack_kernel,
        out_shape=jax.ShapeDtypeStruct((n_dp, packed_rows, LANES), bf16),
        in_specs=in_vmem(2),
        out_specs=in_vmem(1)[0],
        compiler_params=params(),
    )(by_rank(down_gradient[0]), up_sent)
    exchanged = lax.all_to_all(packed, "dp", 0, 0, tiled=True)

    mine = []
    for half in range(halves):
        for step in steps:
            piece = pieces[(step - 1) * halves + half]
            if half > 0:
                piece, _ = lax.optimization_barrier((piece, packed))
            mine.append(to_chip(piece, step))

    hidden, _ = lax.optimization_barrier((prompt_hidden_input, packed))
    widened = hidden.astype(f32)
    squares = jnp.sum(widened * widened, axis=1)
    own_x = (widened * input_norm_gain[None, :]).astype(bf16)
    x = lax.optimization_barrier(jnp.concatenate([own_x, to_sibling(own_x)], axis=1))
    squares = squares + to_sibling(squares)

    down_state = [by_rank(v) for v in (down_factor_matrix, down_moment_first, down_moment_second)]
    up_state = [up_factor_matrix, up_moment_first, up_moment_second]
    out_shape = (
        jax.ShapeDtypeStruct((3, factors, down_rows), f32),
        jax.ShapeDtypeStruct((3, up_rows, columns), f32),
        jax.ShapeDtypeStruct((n_dp, packed_rows, LANES), bf16),
    )
    window = pl.cdiv(down_rows + LANES, LANES) * LANES
    if features % LANES == 0 and window <= features and up_rows % 8 == 0:
        a_next, b_next, copies = pl.pallas_call(
            adam_kernel,
            out_shape=out_shape,
            in_specs=[SCALARS] + in_vmem(1) + anywhere(6),
            out_specs=tuple(in_vmem(3)),
            scratch_shapes=[
                pltpu.VMEM((3, factors, window), f32),
                pltpu.VMEM((3, up_rows, columns), f32),
                pltpu.SemaphoreType.DMA((6,)),
            ],
            compiler_params=params(),
        )(replica[None].astype(jnp.int32), exchanged, *down_state, *up_state)
    else:
        down_state = [
            lax.dynamic_slice_in_dim(v, replica * down_rows, down_rows, 1) for v in down_state
        ]
        up_state = [lax.dynamic_slice_in_dim(v, replica * up_rows, up_rows, 0) for v in up_state]
        a_next, b_next, copies = pl.pallas_call(
            adam_sliced_kernel,
            out_shape=out_shape,
            in_specs=in_vmem(7),
            out_specs=tuple(in_vmem(3)),
            compiler_params=params(),
        )(exchanged, *down_state, *up_state)
    a_next = jnp.transpose(a_next.reshape(3, parts, rank, down_rows), (0, 3, 1, 2))

    own_f = lax.all_to_all(copies, "dp", 0, 0, tiled=True)
    sibling_f = to_sibling(own_f)
    packed_b, _ = lax.optimization_barrier((own_f[:, down_rows:], x))
    other_b = [to_chip(packed_b, step) for step in steps]

    held = [lax.optimization_barrier((value, copies))[0] for value in mine]
    other = [swap(value) for value in held]

    squares, _ = lax.optimization_barrier((squares, other_b))
    squares = squares + sum(to_chip(squares, step) for step in steps)
    inv_rms = jnp.broadcast_to(lax.rsqrt(squares / width + 1e-06)[:, None], (tokens, LANES))

    scale = 0.5 / math.sqrt(width * rank)

    def part_of(who):
        return who * columns // KEY_VALUE_WIDTH

    token_slices = [
        slice(k * tokens // TOKEN_HALVES, (k + 1) * tokens // TOKEN_HALVES)
        for k in range(TOKEN_HALVES)
    ]
    received = {}
    product = None
    for half in range(halves):
        group = range(half * strips // halves, (half + 1) * strips // halves)
        for step in steps:
            at = half * len(steps) + step - 1
            numbers = jnp.stack([odd, part_of(owner(step))]).astype(jnp.int32)
            if product is not None:
                numbers, _ = lax.optimization_barrier((numbers, product))
            weights = pl.pallas_call(
                functools.partial(outside_kernel, (scale, parts, up_rows, group)),
                out_shape=jax.ShapeDtypeStruct((CORES * features, wide), bf16),
                in_specs=[SCALARS] + in_vmem(5),
                out_specs=in_vmem(1)[0],
                compiler_params=params(),
            )(numbers, held[at], other[at], own_f, sibling_f, other_b[step - 1])
            for k, rows in enumerate(token_slices):
                if k > 0:
                    weights, _ = lax.optimization_barrier((weights, product))
                product = jnp.dot(x[rows], weights, preferred_element_type=f32).astype(bf16)
                received.setdefault((k, half), []).append(to_chip(product, chips - step))

    numbers = jnp.stack([place, place ^ 1, part_of(place)]).astype(jnp.int32)
    numbers, _ = lax.optimization_barrier((numbers, (product, received[0, 0])))
    totals = pl.pallas_call(
        functools.partial(own_kernel, (scale, parts, up_rows, range(strips))),
        out_shape=(jax.ShapeDtypeStruct((tokens, wide), f32),) * halves,
        grid_spec=pltpu.PrefetchScalarGridSpec(
            num_scalar_prefetch=1,
            grid=(1,),
            in_specs=[
                pl.BlockSpec((features, columns), lambda i, numbers: (numbers[0], 0)),
                pl.BlockSpec((features, columns), lambda i, numbers: (numbers[1], 0)),
            ]
            + in_vmem(3),
            out_specs=tuple(in_vmem(halves)),
            scratch_shapes=[pltpu.VMEM((CORES * features, columns), bf16)],
        ),
        compiler_params=params(),
        cost_estimate=pl.CostEstimate(
            flops=2 * tokens * CORES * features * columns,
            bytes_accessed=4 * tokens * features,
            transcendentals=0,
        ),
    )(numbers, frozen_key_value, frozen_key_value, own_f, sibling_f, x)

    keys_values = None
    for at, pieces in received.items():
        keys_values = finish(
            totals[at[1]], inv_rms, pieces, at, (tokens, columns), keys_values
        )
    return (a_next, b_next, keys_values)


def solution(mesh):
    placed = (
        P("dp", "tensor"),
        P("tensor"),
        P(None, "tensor"),
        P("tensor", None, None),
        P("tensor", None, None),
        P("tensor", None, None),
        P(None, "tensor"),
        P(None, "tensor"),
        P(None, "tensor"),
        P("dp", "tensor", None, None),
        P("dp", None, "tensor"),
    )
    return jax.shard_map(
        body,
        mesh=mesh,
        in_specs=placed,
        out_specs=(
            P(None, ("tensor", "dp"), None, None),
            P(None, "dp", "tensor"),
            P("dp", "tensor"),
        ),
        check_vma=False,
    )
```

```python
import functools
import math

import jax
import jax.numpy as jnp
from jax import lax
from jax.experimental import pallas as pl
from jax.experimental.pallas import tpu as pltpu
from jax.sharding import PartitionSpec as P

KEY_VALUE_WIDTH = 1024
STEP = 100
CORES = 2
LANES = 128
COLUMN_HALVES = 2
TOKEN_HALVES = 2
VMEM_BYTES = 40 * 2**20


def adaptive_moment_update(param, first, second, grad_mean):
    first_new = 0.9 * first + 0.1 * grad_mean
    second_new = 0.999 * second + 0.001 * grad_mean * grad_mean
    step_size = first_new / (1.0 - 0.9**STEP) / (jnp.sqrt(second_new / (1.0 - 0.999**STEP)) + 1e-08)
    return (param - 0.1 * step_size, first_new, second_new)


def in_vmem(count):
    return [pl.BlockSpec(memory_space=pltpu.VMEM)] * count


def anywhere(count):
    return [pl.BlockSpec(memory_space=pl.ANY)] * count


SCALARS = pl.BlockSpec(memory_space=pltpu.SMEM)


def params(**more):
    return pltpu.CompilerParams(vmem_limit_bytes=VMEM_BYTES, **more)


def share_of(down, up, down_at, up_at, down_rows, up_rows):
    pieces = [down[down_at : down_at + down_rows]] if isinstance(down_at, int) else [
        down[pl.ds(down_at, down_rows)]
    ]
    rows = up[up_at : up_at + up_rows] if isinstance(up_at, int) else up[pl.ds(up_at, up_rows)]
    for k in range(rows.shape[1] // LANES):
        pieces.append(rows[:, k * LANES : (k + 1) * LANES])
    return jnp.concatenate(pieces, axis=0).astype(jnp.bfloat16)


def pack_kernel(down_ref, up_ref, out_ref):
    shares = out_ref.shape[0]
    down, up = down_ref[...].T, up_ref[...]
    down_rows, up_rows = down.shape[0] // shares, up.shape[0] // shares
    for i in range(shares):
        out_ref[i] = share_of(down, up, i * down_rows, i * up_rows, down_rows, up_rows)


def pack_direct_kernel(replica, down_ref, up_ref, *refs):
    outs, down = refs[:-1], refs[-1]
    down[...] = down_ref[...].T
    down_rows, up_rows = down.shape[0] // len(outs), up_ref.shape[0] // len(outs)
    for k, out in enumerate(outs):
        i = replica[0] ^ k
        down_at = pl.multiple_of(i * down_rows, down_rows)
        up_at = pl.multiple_of(i * up_rows, up_rows)
        out[...] = share_of(down, up_ref, down_at, up_at, down_rows, up_rows)


def take_kernel(rows_ref, weights_ref, *refs):
    outs, sem = refs[:-1], refs[-1]
    features = outs[0].shape[0]
    strips = weights_ref.shape[1] // LANES
    copies = []
    for i, out in enumerate(outs):
        row = pl.multiple_of(rows_ref[i] * features, features)
        source = weights_ref.at[pl.ds(row, features), pl.ds(i % strips * LANES, LANES)]
        copies.append(pltpu.make_async_copy(source, out, sem.at[i]))
    for copy in copies:
        copy.start()
    for copy in copies:
        copy.wait()


def join_kernel(own_ref, sibling_ref, out_ref):
    rows, features = own_ref.shape
    tile = tile_of(rows)

    @pl.loop(0, rows // tile)
    def _(i):
        at = pl.ds(pl.multiple_of(i * tile, tile), tile)
        out_ref[at, :features] = own_ref[at, :]
        out_ref[at, features:] = sibling_ref[at, :]


def update(total, down, up, a_ref, b_ref):
    down_rows = a_ref.shape[2]
    up_rows, columns = b_ref.shape[1:]
    strips = columns // LANES
    down_mean = total[:down_rows].T
    up_mean = jnp.concatenate(
        [total[down_rows + k * up_rows : down_rows + (k + 1) * up_rows] for k in range(strips)],
        axis=1,
    )
    p, m, v = adaptive_moment_update(*down(), down_mean)
    a_ref[0], a_ref[1], a_ref[2] = p, m, v
    pieces = [p.T]
    p, m, v = adaptive_moment_update(*up(), up_mean)
    b_ref[0], b_ref[1], b_ref[2] = p, m, v
    pieces += [p[:, k * LANES : (k + 1) * LANES] for k in range(strips)]
    return jnp.concatenate(pieces, axis=0).astype(jnp.bfloat16)


def adam_kernel(grad_ref, dp, dm, dv, up, um, uv, a_ref, b_ref, factor_ref):
    replicas = grad_ref.shape[0]
    rounded = update(
        jnp.sum(grad_ref[...].astype(jnp.float32), axis=0) / replicas,
        lambda: [ref[...] for ref in (dp, dm, dv)],
        lambda: [ref[...] for ref in (up, um, uv)],
        a_ref,
        b_ref,
    )
    for i in range(replicas):
        factor_ref[i] = rounded


def adam_direct_kernel(replicas, replica, *refs):
    grads, refs = refs[:replicas], refs[replicas:]
    down_state, up_state, refs = refs[:3], refs[3:6], refs[6:]
    a_ref, b_ref, factor_ref, down_buf, up_buf, sem = refs
    down_rows, window = a_ref.shape[2], down_buf.shape[2]
    up_rows = b_ref.shape[1]
    first = replica[0] * down_rows
    lane = jnp.minimum(first // LANES * LANES, down_state[0].shape[1] - window)
    row = pl.multiple_of(replica[0] * up_rows, up_rows)
    copies = []
    for i, ref in enumerate(down_state):
        source = ref.at[:, pl.ds(pl.multiple_of(lane, LANES), window)]
        copies.append(pltpu.make_async_copy(source, down_buf.at[i], sem.at[i]))
    for i, ref in enumerate(up_state):
        source = ref.at[pl.ds(row, up_rows)]
        copies.append(pltpu.make_async_copy(source, up_buf.at[i], sem.at[3 + i]))
    for copy in copies:
        copy.start()
    total = grads[0][...].astype(jnp.float32)
    for grad in grads[1:]:
        total = total + grad[...].astype(jnp.float32)
    for copy in copies:
        copy.wait()
    shift = window - (first - lane)
    factor_ref[...] = update(
        total / replicas,
        lambda: [pltpu.roll(down_buf[i], shift, 1)[:, :down_rows] for i in range(3)],
        lambda: [up_buf[i] for i in range(3)],
        a_ref,
        b_ref,
    )


def assemble_kernel(replica, *refs):
    shares, (factor_ref, b_ref) = refs[:-2], refs[-2:]
    down_rows = factor_ref.shape[1] - b_ref.shape[1]
    for k, share in enumerate(shares):
        i = replica[0] ^ k
        factor_ref[i] = share[...]
        b_ref[i] = share[down_rows:]


def factor_a(packed_ref, down_rows):
    pieces = [packed_ref[i].astype(jnp.float32)[:down_rows] for i in range(packed_ref.shape[0])]
    return jnp.concatenate(pieces, axis=0).astype(jnp.bfloat16)


def factor_b(packed, part, parts, strip, up_rows):
    pieces = [
        packed[i].astype(jnp.float32)[strip * up_rows : (strip + 1) * up_rows]
        for i in range(packed.shape[0])
    ]
    value = jnp.concatenate(pieces, axis=0)
    rows = [jnp.where(part == j, value, jnp.zeros_like(value)) for j in range(parts)]
    return jnp.concatenate(rows, axis=0).astype(jnp.bfloat16)


def merge(scale, block, a, b):
    change = jnp.dot(a, b, preferred_element_type=jnp.float32)
    return (block.astype(jnp.float32) + scale * change).astype(jnp.bfloat16)


def tile_of(size):
    return 256 if size % 256 == 0 else size


def up_factor(static, packed, part):
    _, parts, up_rows, strips = static
    return jnp.concatenate(
        [factor_b(packed, part, parts, strip, up_rows) for strip in strips], axis=1
    )


def outside_kernel(static, numbers, own_f, sibling_f, b_ref, *refs):
    out = refs[-1]
    strips = static[3]
    features = refs[0].shape[0]
    down_rows = own_f.shape[1] - b_ref.shape[1]
    b = up_factor(static, b_ref[...], numbers[0])
    own_a, sibling_a = factor_a(own_f, down_rows), factor_a(sibling_f, down_rows)
    for k in range(len(strips)):
        mine, other = refs[2 * k : 2 * k + 2]
        odd = numbers[1 + k]
        lanes = slice(k * LANES, (k + 1) * LANES)
        block = jnp.where(odd == 0, mine[...], other[...])
        out[:features, lanes] = merge(static[0], block, own_a, b[:, lanes])
        block = jnp.where(odd == 0, other[...], mine[...])
        out[features:, lanes] = merge(static[0], block, sibling_a, b[:, lanes])


def own_kernel(static, numbers, own_block, sibling_block, own_f, sibling_f, x, *refs):
    outs, weights = refs[:-1], refs[-1]
    features = own_block.shape[0]
    wide = outs[0].shape[1]
    down_rows = own_f.shape[1] - len(static[3]) * static[2]
    b = up_factor(static, own_f[:, down_rows:], numbers[2])
    for at, factors, block in ((0, own_f, own_block), (features, sibling_f, sibling_block)):
        weights[at : at + features] = merge(static[0], block[...], factor_a(factors, down_rows), b)
    tile = tile_of(x.shape[0])

    @pl.loop(0, x.shape[0] // tile)
    def _(i):
        rows = pl.ds(pl.multiple_of(i * tile, tile), tile)
        value = jnp.dot(x[rows, :], weights[...], preferred_element_type=jnp.float32)
        for k, out in enumerate(outs):
            out[rows, :] = value[:, k * wide : (k + 1) * wide]


def finish_kernel(sources, first, own, inv, *refs):
    rows = pl.ds(first, refs[-1].shape[0])
    total = own[rows, :]
    for value in refs[:sources]:
        total = total + value[...].astype(jnp.float32)
    refs[-1][...] = (total * inv[rows, :1]).astype(refs[-1].dtype)


def finish(own, inv_rms, received, at, shape, before):
    block = received[0].shape
    operands = [own, inv_rms] + received
    in_specs = in_vmem(len(operands))
    aliases = {}
    if before is not None:
        aliases = {len(operands): 0}
        in_specs += anywhere(1)
        operands.append(before)
    return pl.pallas_call(
        functools.partial(finish_kernel, len(received), at[0] * block[0]),
        grid=(1,),
        out_shape=jax.ShapeDtypeStruct(shape, jnp.bfloat16),
        in_specs=in_specs,
        out_specs=pl.BlockSpec(block, lambda i: at),
        input_output_aliases=aliases,
        compiler_params=params(),
    )(*operands)


def body(
    prompt_hidden_input,
    input_norm_gain,
    frozen_key_value,
    down_factor_matrix,
    down_moment_first,
    down_moment_second,
    up_factor_matrix,
    up_moment_first,
    up_moment_second,
    down_gradient,
    up_gradient,
):
    n_dp = lax.axis_size("dp")
    n_tensor = lax.axis_size("tensor")
    chips = n_tensor // CORES
    replica = lax.axis_index("dp")
    place = lax.axis_index("tensor")
    chip, core = place // CORES, place % CORES
    tokens, features = prompt_hidden_input.shape
    width, columns = frozen_key_value.shape
    rank = up_factor_matrix.shape[0]
    parts = down_factor_matrix.shape[1]
    factors = parts * rank
    strips = columns // LANES
    down_rows = features // n_dp
    up_rows = rank // n_dp
    packed_rows = down_rows + up_rows * strips
    steps = range(1, chips)
    f32, bf16 = jnp.float32, jnp.bfloat16

    def to_sibling(value):
        return lax.ppermute(value, "tensor", [(t, t ^ 1) for t in range(n_tensor)])

    def to_chip(value, step):
        pairs = [
            (CORES * q + k, CORES * ((q + step) % chips) + k)
            for q in range(chips)
            for k in range(CORES)
        ]
        return lax.ppermute(value, "tensor", pairs)

    def owner(step):
        return CORES * ((chip - step) % chips) + core

    turns = [1, 2] if n_dp % 4 == 0 else [1, 1]
    turn = [turns[strip % 2] for strip in range(strips)]
    odds = [replica // k % 2 for k in turn]
    blocks = jnp.stack(
        [(chip + step) % chips * CORES + (core ^ odd) for step in steps for odd in odds]
    ).astype(jnp.int32)
    count = len(steps) * strips
    pieces = pl.pallas_call(
        take_kernel,
        out_shape=(jax.ShapeDtypeStruct((features, LANES), bf16),) * count,
        in_specs=[SCALARS, pl.BlockSpec(memory_space=pltpu.HBM)],
        out_specs=tuple(anywhere(count)),
        scratch_shapes=[pltpu.SemaphoreType.DMA((count,))],
        compiler_params=params(),
    )(blocks, frozen_key_value)
    mine = [
        [to_chip(pieces[(step - 1) * strips + strip], step) for step in steps]
        for strip in range(strips)
    ]
    halves = min(COLUMN_HALVES, strips)
    wide = columns // halves
    groups = [range(k * strips // halves, (k + 1) * strips // halves) for k in range(halves)]

    up_sent, _ = lax.optimization_barrier((up_gradient[0], pieces))
    widened = prompt_hidden_input.astype(f32)
    squares = jnp.sum(widened * widened, axis=1)
    own_x = (widened * input_norm_gain[None, :]).astype(bf16)
    x = pl.pallas_call(
        join_kernel,
        out_shape=jax.ShapeDtypeStruct((tokens, CORES * features), bf16),
        in_specs=in_vmem(2),
        out_specs=in_vmem(1)[0],
        compiler_params=params(),
    )(own_x, to_sibling(own_x))
    squares = squares + to_sibling(squares)

    def by_rank(value):
        return jnp.transpose(value, (1, 2, 0)).reshape(factors, features)

    down_sent = by_rank(down_gradient[0])
    down_state = [by_rank(v) for v in (down_factor_matrix, down_moment_first, down_moment_second)]
    up_state = [up_factor_matrix, up_moment_first, up_moment_second]
    share = jax.ShapeDtypeStruct((packed_rows, LANES), bf16)
    shares = jax.ShapeDtypeStruct((n_dp, packed_rows, LANES), bf16)
    updated = (
        jax.ShapeDtypeStruct((3, factors, down_rows), f32),
        jax.ShapeDtypeStruct((3, up_rows, columns), f32),
    )
    window = pl.cdiv(down_rows + LANES, LANES) * LANES
    aligned = features % LANES == 0 and window <= features
    aligned = aligned and up_rows % 8 == 0 and down_rows % 16 == 0
    if aligned and n_dp in (2, 4, 8):
        number = replica[None].astype(jnp.int32)

        def to_partner(value, k):
            return lax.ppermute(value, "dp", [(i, i ^ k) for i in range(n_dp)])

        packed = pl.pallas_call(
            pack_direct_kernel,
            out_shape=(share,) * n_dp,
            in_specs=[SCALARS] + in_vmem(2),
            out_specs=tuple(in_vmem(n_dp)),
            scratch_shapes=[pltpu.VMEM((features, factors), f32)],
            compiler_params=params(),
        )(number, down_sent, up_sent)
        grads = [packed[0]] + [to_partner(packed[k], k) for k in range(1, n_dp)]
        grads, first = lax.optimization_barrier((grads, [mine[i] for i in groups[0]]))
        a_next, b_next, rounded = pl.pallas_call(
            functools.partial(adam_direct_kernel, n_dp),
            out_shape=updated + (share,),
            in_specs=[SCALARS] + in_vmem(n_dp) + anywhere(6),
            out_specs=tuple(in_vmem(3)),
            scratch_shapes=[
                pltpu.VMEM((3, factors, window), f32),
                pltpu.VMEM((3, up_rows, columns), f32),
                pltpu.SemaphoreType.DMA((6,)),
            ],
            compiler_params=params(),
        )(number, *grads, *down_state, *up_state)
        sent = rounded
        gathered = [rounded] + [to_partner(rounded, k) for k in range(1, n_dp)]
        gathered, _ = lax.optimization_barrier((gathered, (x, mine)))
        own_f, packed_b = pl.pallas_call(
            assemble_kernel,
            out_shape=(shares, jax.ShapeDtypeStruct((n_dp, packed_rows - down_rows, LANES), bf16)),
            in_specs=[SCALARS] + in_vmem(n_dp),
            out_specs=tuple(in_vmem(2)),
            compiler_params=params(),
        )(number, *gathered)
    else:
        packed = pl.pallas_call(
            pack_kernel,
            out_shape=shares,
            in_specs=in_vmem(2),
            out_specs=in_vmem(1)[0],
            compiler_params=params(),
        )(down_sent, up_sent)
        exchanged = lax.all_to_all(packed, "dp", 0, 0, tiled=True)
        down_state = [
            lax.dynamic_slice_in_dim(v, replica * down_rows, down_rows, 1) for v in down_state
        ]
        up_state = [lax.dynamic_slice_in_dim(v, replica * up_rows, up_rows, 0) for v in up_state]
        a_next, b_next, sent = pl.pallas_call(
            adam_kernel,
            out_shape=updated + (shares,),
            in_specs=in_vmem(7),
            out_specs=tuple(in_vmem(3)),
            compiler_params=params(),
        )(exchanged, *down_state, *up_state)
        own_f = lax.all_to_all(sent, "dp", 0, 0, tiled=True)
        packed_b = own_f[:, down_rows:]
    a_next = jnp.transpose(a_next.reshape(3, parts, rank, down_rows), (0, 3, 1, 2))

    sibling_f = to_sibling(own_f)
    other_b = [to_chip(packed_b, step) for step in steps]

    def swap(value, k):
        value, _ = lax.optimization_barrier((value, sent))
        return value, lax.ppermute(value, "dp", [(i, i ^ k) for i in range(n_dp)])

    outside = [[swap(value, turn[strip]) for value in mine[strip]] for strip in range(strips)]

    squares, _ = lax.optimization_barrier((squares, packed_b))
    squares = squares + sum(to_chip(squares, step) for step in steps)
    inv_rms = jnp.broadcast_to(lax.rsqrt(squares / width + 1e-06)[:, None], (tokens, LANES))

    scale = 0.5 / math.sqrt(width * rank)

    def part_of(who):
        return who * columns // KEY_VALUE_WIDTH

    token_slices = [
        slice(k * tokens // TOKEN_HALVES, (k + 1) * tokens // TOKEN_HALVES)
        for k in range(TOKEN_HALVES)
    ]
    received = {}
    product = None
    for half in range(halves):
        group = groups[half]
        for step in steps:
            numbers = [part_of(owner(step))] + [odds[strip] for strip in group]
            numbers = jnp.stack(numbers).astype(jnp.int32)
            after = squares if product is None else product
            numbers, _ = lax.optimization_barrier((numbers, after))
            blocks = [value for strip in group for value in outside[strip][step - 1]]
            weights = pl.pallas_call(
                functools.partial(outside_kernel, (scale, parts, up_rows, group)),
                out_shape=jax.ShapeDtypeStruct((CORES * features, wide), bf16),
                in_specs=[SCALARS] + in_vmem(3 + len(blocks)),
                out_specs=in_vmem(1)[0],
                compiler_params=params(),
            )(numbers, own_f, sibling_f, other_b[step - 1], *blocks)
            for k, rows in enumerate(token_slices):
                if k > 0:
                    weights, _ = lax.optimization_barrier((weights, product))
                product = jnp.dot(x[rows], weights, preferred_element_type=f32).astype(bf16)
                received.setdefault((k, half), []).append(to_chip(product, chips - step))

    numbers = jnp.stack([place, place ^ 1, part_of(place)]).astype(jnp.int32)
    numbers, _ = lax.optimization_barrier((numbers, (product, received[0, 0])))
    totals = pl.pallas_call(
        functools.partial(own_kernel, (scale, parts, up_rows, range(strips))),
        out_shape=(jax.ShapeDtypeStruct((tokens, wide), f32),) * halves,
        grid_spec=pltpu.PrefetchScalarGridSpec(
            num_scalar_prefetch=1,
            grid=(1,),
            in_specs=[
                pl.BlockSpec((features, columns), lambda i, numbers: (numbers[0], 0)),
                pl.BlockSpec((features, columns), lambda i, numbers: (numbers[1], 0)),
            ]
            + in_vmem(3),
            out_specs=tuple(in_vmem(halves)),
            scratch_shapes=[pltpu.VMEM((CORES * features, columns), bf16)],
        ),
        compiler_params=params(),
        cost_estimate=pl.CostEstimate(
            flops=2 * tokens * CORES * features * columns,
            bytes_accessed=4 * tokens * features,
            transcendentals=0,
        ),
    )(numbers, frozen_key_value, frozen_key_value, own_f, sibling_f, x)

    keys_values = None
    for at, pieces in received.items():
        keys_values = finish(
            totals[at[1]], inv_rms, pieces, at, (tokens, columns), keys_values
        )
    return (a_next, b_next, keys_values)


def solution(mesh):
    placed = (
        P("dp", "tensor"),
        P("tensor"),
        P(None, "tensor"),
        P("tensor", None, None),
        P("tensor", None, None),
        P("tensor", None, None),
        P(None, "tensor"),
        P(None, "tensor"),
        P(None, "tensor"),
        P("dp", "tensor", None, None),
        P("dp", None, "tensor"),
    )
    return jax.shard_map(
        body,
        mesh=mesh,
        in_specs=placed,
        out_specs=(
            P(None, ("tensor", "dp"), None, None),
            P(None, "dp", "tensor"),
            P("dp", "tensor"),
        ),
        check_vma=False,
    )
```

```python
import functools
import math

import jax
import jax.numpy as jnp
from jax import lax
from jax.experimental import pallas as pl
from jax.experimental.pallas import tpu as pltpu
from jax.sharding import PartitionSpec as P

KEY_VALUE_WIDTH = 1024
STEP = 100
CORES = 2
LANES = 128
COLUMN_HALVES = 2
TOKEN_HALVES = 2
VMEM_BYTES = 32 * 2**20
TAKE_VMEM_BYTES = 60 * 2**20


def adaptive_moment_update(param, first, second, grad_mean):
    first_new = 0.9 * first + 0.1 * grad_mean
    second_new = 0.999 * second + 0.001 * grad_mean * grad_mean
    step_size = first_new / (1.0 - 0.9**STEP) / (jnp.sqrt(second_new / (1.0 - 0.999**STEP)) + 1e-08)
    return (param - 0.1 * step_size, first_new, second_new)


def in_vmem(count):
    return [pl.BlockSpec(memory_space=pltpu.VMEM)] * count


def anywhere(count):
    return [pl.BlockSpec(memory_space=pl.ANY)] * count


SCALARS = pl.BlockSpec(memory_space=pltpu.SMEM)


def params(**more):
    return pltpu.CompilerParams(vmem_limit_bytes=VMEM_BYTES, **more)


def pack_kernel(down_ref, up_ref, out_ref):
    shares = out_ref.shape[0]
    down, up = down_ref[...].T, up_ref[...]
    down_rows, up_rows = down.shape[0] // shares, up.shape[0] // shares
    for i in range(shares):
        pieces = [down[i * down_rows : (i + 1) * down_rows]]
        for k in range(up.shape[1] // LANES):
            pieces.append(up[i * up_rows : (i + 1) * up_rows, k * LANES : (k + 1) * LANES])
        out_ref[i] = jnp.concatenate(pieces, axis=0).astype(jnp.bfloat16)


def take_kernel(rows_ref, weights_ref, *refs):
    outs, sem = refs[:-1], refs[-1]
    strips, features, _ = outs[0].shape
    copies = []
    for i in range(len(outs) * strips):
        row = pl.multiple_of(rows_ref[i] * features, features)
        source = weights_ref.at[pl.ds(row, features), pl.ds(i % strips * LANES, LANES)]
        copies.append(
            pltpu.make_async_copy(source, outs[i // strips].at[i % strips], sem.at[i])
        )
    for copy in copies:
        copy.start()
    for copy in copies:
        copy.wait()


def split_kernel(in_ref, *outs):
    for k, out in enumerate(outs):
        out[...] = in_ref[k]


def prepare_kernel(own_ref, sibling_ref, own_gain, sibling_gain, x_ref, squares_ref):
    rows, features = own_ref.shape
    tile = 64 if rows % 64 == 0 else rows

    @pl.loop(0, rows // tile)
    def _(i):
        at = pl.ds(pl.multiple_of(i * tile, tile), tile)
        total = jnp.zeros((tile, 1), jnp.float32)
        for k, (ref, gain) in enumerate(((own_ref, own_gain), (sibling_ref, sibling_gain))):
            wide = ref[at, :].astype(jnp.float32)
            total += jnp.sum(wide * wide, axis=1, keepdims=True)
            x_ref[at, k * features : (k + 1) * features] = (wide * gain[...]).astype(x_ref.dtype)
        squares_ref[at, :] = jnp.broadcast_to(total, (tile, LANES))


def tail_kernel(in_ref, out_ref):
    out_ref[...] = in_ref[:, in_ref.shape[1] - out_ref.shape[1] :]


def update(total, down, up, a_ref, b_ref):
    down_rows = a_ref.shape[2]
    up_rows, columns = b_ref.shape[1:]
    strips = columns // LANES
    down_mean = total[:down_rows].T
    up_mean = jnp.concatenate(
        [total[down_rows + k * up_rows : down_rows + (k + 1) * up_rows] for k in range(strips)],
        axis=1,
    )
    p, m, v = adaptive_moment_update(*down(), down_mean)
    a_ref[0], a_ref[1], a_ref[2] = p, m, v
    pieces = [p.T]
    p, m, v = adaptive_moment_update(*up(), up_mean)
    b_ref[0], b_ref[1], b_ref[2] = p, m, v
    pieces += [p[:, k * LANES : (k + 1) * LANES] for k in range(strips)]
    return jnp.concatenate(pieces, axis=0).astype(jnp.bfloat16)


def adam_kernel(grad_ref, dp, dm, dv, up, um, uv, a_ref, b_ref, factor_ref):
    replicas = grad_ref.shape[0]
    rounded = update(
        jnp.sum(grad_ref[...].astype(jnp.float32), axis=0) / replicas,
        lambda: [ref[...] for ref in (dp, dm, dv)],
        lambda: [ref[...] for ref in (up, um, uv)],
        a_ref,
        b_ref,
    )
    for i in range(replicas):
        factor_ref[i] = rounded


def adam_copy_kernel(replica, grad_ref, *refs):
    down_state, up_state, refs = refs[:3], refs[3:6], refs[6:]
    a_ref, b_ref, factor_ref, down_buf, up_buf, sem = refs
    replicas = grad_ref.shape[0]
    down_rows, window = a_ref.shape[2], down_buf.shape[2]
    up_rows = b_ref.shape[1]
    first = replica[0] * down_rows
    lane = jnp.minimum(first // LANES * LANES, down_state[0].shape[1] - window)
    row = pl.multiple_of(replica[0] * up_rows, up_rows)
    copies = []
    for i, ref in enumerate(down_state):
        source = ref.at[:, pl.ds(pl.multiple_of(lane, LANES), window)]
        copies.append(pltpu.make_async_copy(source, down_buf.at[i], sem.at[i]))
    for i, ref in enumerate(up_state):
        source = ref.at[pl.ds(row, up_rows)]
        copies.append(pltpu.make_async_copy(source, up_buf.at[i], sem.at[3 + i]))
    for copy in copies:
        copy.start()
    total = jnp.sum(grad_ref[...].astype(jnp.float32), axis=0) / replicas
    for copy in copies:
        copy.wait()
    shift = window - (first - lane)
    rounded = update(
        total,
        lambda: [pltpu.roll(down_buf[i], shift, 1)[:, :down_rows] for i in range(3)],
        lambda: [up_buf[i] for i in range(3)],
        a_ref,
        b_ref,
    )
    for i in range(replicas):
        factor_ref[i] = rounded


def factor_a(packed_ref, down_rows):
    pieces = [packed_ref[i].astype(jnp.float32)[:down_rows] for i in range(packed_ref.shape[0])]
    return jnp.concatenate(pieces, axis=0).astype(jnp.bfloat16)


def factor_b(packed, part, parts, strip, up_rows):
    pieces = [
        packed[i].astype(jnp.float32)[strip * up_rows : (strip + 1) * up_rows]
        for i in range(packed.shape[0])
    ]
    value = jnp.concatenate(pieces, axis=0)
    rows = [jnp.where(part == j, value, jnp.zeros_like(value)) for j in range(parts)]
    return jnp.concatenate(rows, axis=0).astype(jnp.bfloat16)


def merge(scale, block, a, b):
    change = jnp.dot(a, b, preferred_element_type=jnp.float32)
    return (block.astype(jnp.float32) + scale * change).astype(jnp.bfloat16)


def tile_of(size):
    return 256 if size % 256 == 0 else size


def up_factor(static, packed, part):
    _, parts, up_rows, strips = static
    return jnp.concatenate(
        [factor_b(packed, part, parts, strip, up_rows) for strip in strips], axis=1
    )


def outside_kernel(static, numbers, own_f, sibling_f, b_ref, *refs):
    out = refs[-1]
    strips = static[3]
    features = refs[0].shape[0]
    down_rows = own_f.shape[1] - b_ref.shape[1]
    b = up_factor(static, b_ref[...], numbers[0])
    own_a, sibling_a = factor_a(own_f, down_rows), factor_a(sibling_f, down_rows)
    for k in range(len(strips)):
        mine, other = refs[2 * k : 2 * k + 2]
        odd = numbers[1 + k]
        lanes = slice(k * LANES, (k + 1) * LANES)
        block = jnp.where(odd == 0, mine[...], other[...])
        out[:features, lanes] = merge(static[0], block, own_a, b[:, lanes])
        block = jnp.where(odd == 0, other[...], mine[...])
        out[features:, lanes] = merge(static[0], block, sibling_a, b[:, lanes])


def own_kernel(static, numbers, own_block, sibling_block, own_f, sibling_f, x, *refs):
    outs, weights = refs[:-1], refs[-1]
    features = own_block.shape[0]
    wide = outs[0].shape[1]
    down_rows = own_f.shape[1] - len(static[3]) * static[2]
    b = up_factor(static, own_f[:, down_rows:], numbers[2])
    for at, factors, block in ((0, own_f, own_block), (features, sibling_f, sibling_block)):
        weights[at : at + features] = merge(static[0], block[...], factor_a(factors, down_rows), b)
    tile = tile_of(x.shape[0])

    @pl.loop(0, x.shape[0] // tile)
    def _(i):
        rows = pl.ds(pl.multiple_of(i * tile, tile), tile)
        value = jnp.dot(x[rows, :], weights[...], preferred_element_type=jnp.float32)
        for k, out in enumerate(outs):
            out[rows, :] = value[:, k * wide : (k + 1) * wide]


def finish_kernel(sources, first, own, inv, *refs):
    rows = pl.ds(first, refs[-1].shape[0])
    total = own[rows, :]
    for value in refs[:sources]:
        total = total + value[...].astype(jnp.float32)
    refs[-1][...] = (total * inv[rows, :1]).astype(refs[-1].dtype)


def finish(own, inv_rms, received, at, shape, before):
    block = received[0].shape
    operands = [own, inv_rms] + received
    in_specs = in_vmem(len(operands))
    aliases = {}
    if before is not None:
        aliases = {len(operands): 0}
        in_specs += anywhere(1)
        operands.append(before)
    return pl.pallas_call(
        functools.partial(finish_kernel, len(received), at[0] * block[0]),
        grid=(1,),
        out_shape=jax.ShapeDtypeStruct(shape, jnp.bfloat16),
        in_specs=in_specs,
        out_specs=pl.BlockSpec(block, lambda i: at),
        input_output_aliases=aliases,
        compiler_params=params(),
    )(*operands)


def body(
    prompt_hidden_input,
    input_norm_gain,
    frozen_key_value,
    down_factor_matrix,
    down_moment_first,
    down_moment_second,
    up_factor_matrix,
    up_moment_first,
    up_moment_second,
    down_gradient,
    up_gradient,
):
    n_dp = lax.axis_size("dp")
    n_tensor = lax.axis_size("tensor")
    chips = n_tensor // CORES
    replica = lax.axis_index("dp")
    place = lax.axis_index("tensor")
    chip, core = place // CORES, place % CORES
    tokens, features = prompt_hidden_input.shape
    width, columns = frozen_key_value.shape
    rank = up_factor_matrix.shape[0]
    parts = down_factor_matrix.shape[1]
    factors = parts * rank
    strips = columns // LANES
    down_rows = features // n_dp
    up_rows = rank // n_dp
    packed_rows = down_rows + up_rows * strips
    steps = range(1, chips)
    f32, bf16 = jnp.float32, jnp.bfloat16

    def to_sibling(value):
        return lax.ppermute(value, "tensor", [(t, t ^ 1) for t in range(n_tensor)])

    def to_chip(value, step):
        pairs = [
            (CORES * q + k, CORES * ((q + step) % chips) + k)
            for q in range(chips)
            for k in range(CORES)
        ]
        return lax.ppermute(value, "tensor", pairs)

    def owner(step):
        return CORES * ((chip - step) % chips) + core

    turns = [1, 2] if n_dp % 4 == 0 else [1, 1]
    turn = [turns[strip % 2] for strip in range(strips)]
    odds = [replica // k % 2 for k in turn]
    blocks = jnp.stack(
        [(chip + step) % chips * CORES + (core ^ odd) for step in steps for odd in odds]
    ).astype(jnp.int32)
    taken = pl.pallas_call(
        take_kernel,
        out_shape=(jax.ShapeDtypeStruct((strips, features, LANES), bf16),) * len(steps),
        in_specs=[SCALARS] + anywhere(1),
        out_specs=tuple(anywhere(len(steps))),
        scratch_shapes=[pltpu.SemaphoreType.DMA((len(steps) * strips,))],
        compiler_params=pltpu.CompilerParams(vmem_limit_bytes=TAKE_VMEM_BYTES),
    )(blocks, frozen_key_value)
    mine = [to_chip(value, step) for value, step in zip(taken, steps)]
    halves = min(COLUMN_HALVES, strips)
    wide = columns // halves
    groups = [range(k * strips // halves, (k + 1) * strips // halves) for k in range(halves)]

    hidden, up_sent, _ = lax.optimization_barrier(
        (prompt_hidden_input, up_gradient[0], taken)
    )
    gain = input_norm_gain[None, :]
    x, squares = pl.pallas_call(
        prepare_kernel,
        out_shape=(
            jax.ShapeDtypeStruct((tokens, CORES * features), bf16),
            jax.ShapeDtypeStruct((tokens, LANES), f32),
        ),
        in_specs=in_vmem(4),
        out_specs=tuple(in_vmem(2)),
        compiler_params=params(),
    )(hidden, to_sibling(hidden), gain, to_sibling(gain))
    squares = squares[:, 0]

    def by_rank(value):
        return jnp.transpose(value, (1, 2, 0)).reshape(factors, features)

    down_sent = by_rank(down_gradient[0])
    down_state = [by_rank(v) for v in (down_factor_matrix, down_moment_first, down_moment_second)]
    up_state = [up_factor_matrix, up_moment_first, up_moment_second]
    shares = jax.ShapeDtypeStruct((n_dp, packed_rows, LANES), bf16)
    updated = (
        jax.ShapeDtypeStruct((3, factors, down_rows), f32),
        jax.ShapeDtypeStruct((3, up_rows, columns), f32),
    )
    window = pl.cdiv(down_rows + LANES, LANES) * LANES
    aligned = features % LANES == 0 and window <= features
    aligned = aligned and up_rows % 8 == 0 and down_rows % 16 == 0
    packed = pl.pallas_call(
        pack_kernel,
        out_shape=shares,
        in_specs=in_vmem(2),
        out_specs=in_vmem(1)[0],
        compiler_params=params(),
    )(down_sent, up_sent)
    exchanged = lax.all_to_all(packed, "dp", 0, 0, tiled=True)
    if aligned:
        a_next, b_next, sent = pl.pallas_call(
            adam_copy_kernel,
            out_shape=updated + (shares,),
            in_specs=[SCALARS] + in_vmem(1) + anywhere(6),
            out_specs=tuple(in_vmem(3)),
            scratch_shapes=[
                pltpu.VMEM((3, factors, window), f32),
                pltpu.VMEM((3, up_rows, columns), f32),
                pltpu.SemaphoreType.DMA((6,)),
            ],
            compiler_params=params(),
        )(replica[None].astype(jnp.int32), exchanged, *down_state, *up_state)
    else:
        down_state = [
            lax.dynamic_slice_in_dim(v, replica * down_rows, down_rows, 1) for v in down_state
        ]
        up_state = [lax.dynamic_slice_in_dim(v, replica * up_rows, up_rows, 0) for v in up_state]
        a_next, b_next, sent = pl.pallas_call(
            adam_kernel,
            out_shape=updated + (shares,),
            in_specs=in_vmem(7),
            out_specs=tuple(in_vmem(3)),
            compiler_params=params(),
        )(exchanged, *down_state, *up_state)
    own_f = lax.all_to_all(sent, "dp", 0, 0, tiled=True)
    a_next = jnp.transpose(a_next.reshape(3, parts, rank, down_rows), (0, 3, 1, 2))

    own_f, x, squares = lax.optimization_barrier((own_f, x, squares))
    sibling_f = to_sibling(own_f)
    packed_b = pl.pallas_call(
        tail_kernel,
        out_shape=jax.ShapeDtypeStruct((n_dp, packed_rows - down_rows, LANES), bf16),
        in_specs=in_vmem(1),
        out_specs=in_vmem(1)[0],
        compiler_params=params(),
    )(own_f)
    other_b = [to_chip(packed_b, step) for step in steps]

    outside = [[] for _ in range(strips)]
    for value in mine:
        value, _ = lax.optimization_barrier((value, sent))
        split = pl.pallas_call(
            split_kernel,
            out_shape=(jax.ShapeDtypeStruct((features, LANES), bf16),) * strips,
            in_specs=in_vmem(1),
            out_specs=tuple(in_vmem(strips)),
            compiler_params=params(),
        )(value)
        for strip in range(strips):
            pairs = [(i, i ^ turn[strip]) for i in range(n_dp)]
            outside[strip].append((split[strip], lax.ppermute(split[strip], "dp", pairs)))

    squares = squares + sum(to_chip(squares, step) for step in steps)
    inv_rms = jnp.broadcast_to(lax.rsqrt(squares / width + 1e-06)[:, None], (tokens, LANES))

    scale = 0.5 / math.sqrt(width * rank)

    def part_of(who):
        return who * columns // KEY_VALUE_WIDTH

    token_slices = [
        slice(k * tokens // TOKEN_HALVES, (k + 1) * tokens // TOKEN_HALVES)
        for k in range(TOKEN_HALVES)
    ]
    received = {}
    product = None
    for half in range(halves):
        group = groups[half]
        for step in steps:
            numbers = [part_of(owner(step))] + [odds[strip] for strip in group]
            numbers = jnp.stack(numbers).astype(jnp.int32)
            if product is not None:
                numbers, _ = lax.optimization_barrier((numbers, product))
            blocks = [value for strip in group for value in outside[strip][step - 1]]
            weights = pl.pallas_call(
                functools.partial(outside_kernel, (scale, parts, up_rows, group)),
                out_shape=jax.ShapeDtypeStruct((CORES * features, wide), bf16),
                in_specs=[SCALARS] + in_vmem(3 + len(blocks)),
                out_specs=in_vmem(1)[0],
                compiler_params=params(),
            )(numbers, own_f, sibling_f, other_b[step - 1], *blocks)
            for k, rows in enumerate(token_slices):
                if k > 0:
                    weights, _ = lax.optimization_barrier((weights, (product, squares)))
                product = jnp.dot(x[rows], weights, preferred_element_type=f32).astype(bf16)
                received.setdefault((k, half), []).append(to_chip(product, chips - step))

    numbers = jnp.stack([place, place ^ 1, part_of(place)]).astype(jnp.int32)
    numbers, _ = lax.optimization_barrier((numbers, (product, received[0, 0])))
    totals = pl.pallas_call(
        functools.partial(own_kernel, (scale, parts, up_rows, range(strips))),
        out_shape=(jax.ShapeDtypeStruct((tokens, wide), f32),) * halves,
        grid_spec=pltpu.PrefetchScalarGridSpec(
            num_scalar_prefetch=1,
            grid=(1,),
            in_specs=[
                pl.BlockSpec((features, columns), lambda i, numbers: (numbers[0], 0)),
                pl.BlockSpec((features, columns), lambda i, numbers: (numbers[1], 0)),
            ]
            + in_vmem(3),
            out_specs=tuple(in_vmem(halves)),
            scratch_shapes=[pltpu.VMEM((CORES * features, columns), bf16)],
        ),
        compiler_params=params(),
        cost_estimate=pl.CostEstimate(
            flops=2 * tokens * CORES * features * columns,
            bytes_accessed=4 * tokens * features,
            transcendentals=0,
        ),
    )(numbers, frozen_key_value, frozen_key_value, own_f, sibling_f, x)

    keys_values = None
    for at, pieces in received.items():
        keys_values = finish(
            totals[at[1]], inv_rms, pieces, at, (tokens, columns), keys_values
        )
    return (a_next, b_next, keys_values)


def solution(mesh):
    placed = (
        P("dp", "tensor"),
        P("tensor"),
        P(None, "tensor"),
        P("tensor", None, None),
        P("tensor", None, None),
        P("tensor", None, None),
        P(None, "tensor"),
        P(None, "tensor"),
        P(None, "tensor"),
        P("dp", "tensor", None, None),
        P("dp", None, "tensor"),
    )
    return jax.shard_map(
        body,
        mesh=mesh,
        in_specs=placed,
        out_specs=(
            P(None, ("tensor", "dp"), None, None),
            P(None, "dp", "tensor"),
            P("dp", "tensor"),
        ),
        check_vma=False,
    )
```

```python
import functools
import math

import jax
import jax.numpy as jnp
from jax import lax
from jax.experimental import pallas as pl
from jax.experimental.pallas import tpu as pltpu
from jax.sharding import PartitionSpec as P

KEY_VALUE_WIDTH = 1024
STEP = 100
CORES = 2
LANES = 128
COLUMN_HALVES = 2
TOKEN_HALVES = 2
VMEM_BYTES = 16 * 2**20
TAKE_VMEM_BYTES = 58 * 2**20


def adaptive_moment_update(param, first, second, grad_mean):
    first_new = 0.9 * first + 0.1 * grad_mean
    second_new = 0.999 * second + 0.001 * grad_mean * grad_mean
    step_size = first_new / (1.0 - 0.9**STEP) / (jnp.sqrt(second_new / (1.0 - 0.999**STEP)) + 1e-08)
    return (param - 0.1 * step_size, first_new, second_new)


def in_vmem(count):
    return [pl.BlockSpec(memory_space=pltpu.VMEM)] * count


def anywhere(count):
    return [pl.BlockSpec(memory_space=pl.ANY)] * count


SCALARS = pl.BlockSpec(memory_space=pltpu.SMEM)


def params(**more):
    return pltpu.CompilerParams(vmem_limit_bytes=VMEM_BYTES, **more)


def pack_kernel(down_ref, up_ref, out_ref):
    shares = out_ref.shape[0]
    down, up = down_ref[...].T, up_ref[...]
    down_rows, up_rows = down.shape[0] // shares, up.shape[0] // shares
    for i in range(shares):
        pieces = [down[i * down_rows : (i + 1) * down_rows]]
        for k in range(up.shape[1] // LANES):
            pieces.append(up[i * up_rows : (i + 1) * up_rows, k * LANES : (k + 1) * LANES])
        out_ref[i] = jnp.concatenate(pieces, axis=0).astype(jnp.bfloat16)


def take_kernel(chips, turn, weights_ref, *refs):
    outs, sem = refs[:-1], refs[-1]
    features = outs[0].shape[1]
    place, replica = lax.axis_index("tensor"), lax.axis_index("dp")
    chip, core = place // CORES, place % CORES
    copies = []
    for i, out in enumerate(outs):
        step, first = 1 + i % (chips - 1), i // (chips - 1) * out.shape[0]
        for k in range(out.shape[0]):
            half = (core + replica // turn[first + k]) % 2
            row = ((chip + step) % chips * CORES + half) * features
            source = weights_ref.at[
                pl.ds(pl.multiple_of(row, features), features),
                pl.ds((first + k) * LANES, LANES),
            ]
            copies.append(pltpu.make_async_copy(source, out.at[k], sem.at[len(copies)]))
    for copy in copies:
        copy.start()
    for copy in copies:
        copy.wait()


def split_kernel(in_ref, *outs):
    for k, out in enumerate(outs):
        out[...] = in_ref[k]


def prepare_kernel(own_ref, sibling_ref, own_gain, sibling_gain, x_ref, squares_ref):
    rows, features = own_ref.shape
    tile = 64 if rows % 64 == 0 else rows

    @pl.loop(0, rows // tile)
    def _(i):
        at = pl.ds(pl.multiple_of(i * tile, tile), tile)
        total = jnp.zeros((tile, 1), jnp.float32)
        for k, (ref, gain) in enumerate(((own_ref, own_gain), (sibling_ref, sibling_gain))):
            wide = ref[at, :].astype(jnp.float32)
            total += jnp.sum(wide * wide, axis=1, keepdims=True)
            x_ref[at, k * features : (k + 1) * features] = (wide * gain[...]).astype(x_ref.dtype)
        squares_ref[at, :] = jnp.broadcast_to(total, (tile, LANES))


def tail_kernel(in_ref, out_ref):
    out_ref[...] = in_ref[:, in_ref.shape[1] - out_ref.shape[1] :]


def update(total, down, up, a_ref, b_ref):
    down_rows = a_ref.shape[2]
    up_rows, columns = b_ref.shape[1:]
    strips = columns // LANES
    down_mean = total[:down_rows].T
    up_mean = jnp.concatenate(
        [total[down_rows + k * up_rows : down_rows + (k + 1) * up_rows] for k in range(strips)],
        axis=1,
    )
    p, m, v = adaptive_moment_update(*down(), down_mean)
    a_ref[0], a_ref[1], a_ref[2] = p, m, v
    pieces = [p.T]
    p, m, v = adaptive_moment_update(*up(), up_mean)
    b_ref[0], b_ref[1], b_ref[2] = p, m, v
    pieces += [p[:, k * LANES : (k + 1) * LANES] for k in range(strips)]
    return jnp.concatenate(pieces, axis=0).astype(jnp.bfloat16)


def adam_kernel(grad_ref, dp, dm, dv, up, um, uv, a_ref, b_ref, factor_ref):
    replicas = grad_ref.shape[0]
    rounded = update(
        jnp.sum(grad_ref[...].astype(jnp.float32), axis=0) / replicas,
        lambda: [ref[...] for ref in (dp, dm, dv)],
        lambda: [ref[...] for ref in (up, um, uv)],
        a_ref,
        b_ref,
    )
    for i in range(replicas):
        factor_ref[i] = rounded


def adam_copy_kernel(replica, grad_ref, *refs):
    down_state, up_state, refs = refs[:3], refs[3:6], refs[6:]
    a_ref, b_ref, factor_ref, down_buf, up_buf, sem = refs
    replicas = grad_ref.shape[0]
    down_rows, window = a_ref.shape[2], down_buf.shape[2]
    up_rows = b_ref.shape[1]
    first = replica[0] * down_rows
    lane = jnp.minimum(first // LANES * LANES, down_state[0].shape[1] - window)
    row = pl.multiple_of(replica[0] * up_rows, up_rows)
    copies = []
    for i, ref in enumerate(down_state):
        source = ref.at[:, pl.ds(pl.multiple_of(lane, LANES), window)]
        copies.append(pltpu.make_async_copy(source, down_buf.at[i], sem.at[i]))
    for i, ref in enumerate(up_state):
        source = ref.at[pl.ds(row, up_rows)]
        copies.append(pltpu.make_async_copy(source, up_buf.at[i], sem.at[3 + i]))
    for copy in copies:
        copy.start()
    total = jnp.sum(grad_ref[...].astype(jnp.float32), axis=0) / replicas
    for copy in copies:
        copy.wait()
    shift = window - (first - lane)
    rounded = update(
        total,
        lambda: [pltpu.roll(down_buf[i], shift, 1)[:, :down_rows] for i in range(3)],
        lambda: [up_buf[i] for i in range(3)],
        a_ref,
        b_ref,
    )
    for i in range(replicas):
        factor_ref[i] = rounded


def factor_a(packed_ref, down_rows):
    pieces = [packed_ref[i].astype(jnp.float32)[:down_rows] for i in range(packed_ref.shape[0])]
    return jnp.concatenate(pieces, axis=0).astype(jnp.bfloat16)


def factor_b(packed, part, parts, strip, up_rows):
    pieces = [
        packed[i].astype(jnp.float32)[strip * up_rows : (strip + 1) * up_rows]
        for i in range(packed.shape[0])
    ]
    value = jnp.concatenate(pieces, axis=0)
    rows = [jnp.where(part == j, value, jnp.zeros_like(value)) for j in range(parts)]
    return jnp.concatenate(rows, axis=0).astype(jnp.bfloat16)


def merge(scale, block, a, b):
    change = jnp.dot(a, b, preferred_element_type=jnp.float32)
    return (block.astype(jnp.float32) + scale * change).astype(jnp.bfloat16)


def tile_of(size):
    return 256 if size % 256 == 0 else size


def up_factor(static, packed, part):
    _, parts, up_rows, strips = static
    return jnp.concatenate(
        [factor_b(packed, part, parts, strip, up_rows) for strip in strips], axis=1
    )


def outside_kernel(static, numbers, own_f, sibling_f, b_ref, *refs):
    out = refs[-1]
    strips = static[3]
    features = refs[0].shape[0]
    down_rows = own_f.shape[1] - b_ref.shape[1]
    b = up_factor(static, b_ref[...], numbers[0])
    own_a, sibling_a = factor_a(own_f, down_rows), factor_a(sibling_f, down_rows)
    for k in range(len(strips)):
        mine, other = refs[2 * k : 2 * k + 2]
        odd = numbers[1 + k]
        lanes = slice(k * LANES, (k + 1) * LANES)
        block = jnp.where(odd == 0, mine[...], other[...])
        out[:features, lanes] = merge(static[0], block, own_a, b[:, lanes])
        block = jnp.where(odd == 0, other[...], mine[...])
        out[features:, lanes] = merge(static[0], block, sibling_a, b[:, lanes])


def own_kernel(static, numbers, own_block, sibling_block, own_f, sibling_f, x, *refs):
    outs, weights = refs[:-1], refs[-1]
    features = own_block.shape[0]
    wide = outs[0].shape[1]
    down_rows = own_f.shape[1] - len(static[3]) * static[2]
    b = up_factor(static, own_f[:, down_rows:], numbers[2])
    for at, factors, block in ((0, own_f, own_block), (features, sibling_f, sibling_block)):
        weights[at : at + features] = merge(static[0], block[...], factor_a(factors, down_rows), b)
    tile = tile_of(x.shape[0])

    @pl.loop(0, x.shape[0] // tile)
    def _(i):
        rows = pl.ds(pl.multiple_of(i * tile, tile), tile)
        value = jnp.dot(x[rows, :], weights[...], preferred_element_type=jnp.float32)
        for k, out in enumerate(outs):
            out[rows, :] = value[:, k * wide : (k + 1) * wide]


def finish_kernel(sources, first, own, inv, *refs):
    rows = pl.ds(first, refs[-1].shape[0])
    total = own[rows, :]
    for value in refs[:sources]:
        total = total + value[...].astype(jnp.float32)
    refs[-1][...] = (total * inv[rows, :1]).astype(refs[-1].dtype)


def finish(own, inv_rms, received, at, shape, before):
    block = received[0].shape
    operands = [own, inv_rms] + received
    in_specs = in_vmem(len(operands))
    aliases = {}
    if before is not None:
        aliases = {len(operands): 0}
        in_specs += anywhere(1)
        operands.append(before)
    return pl.pallas_call(
        functools.partial(finish_kernel, len(received), at[0] * block[0]),
        grid=(1,),
        out_shape=jax.ShapeDtypeStruct(shape, jnp.bfloat16),
        in_specs=in_specs,
        out_specs=pl.BlockSpec(block, lambda i: at),
        input_output_aliases=aliases,
        compiler_params=params(),
    )(*operands)


def body(
    prompt_hidden_input,
    input_norm_gain,
    frozen_key_value,
    down_factor_matrix,
    down_moment_first,
    down_moment_second,
    up_factor_matrix,
    up_moment_first,
    up_moment_second,
    down_gradient,
    up_gradient,
):
    n_dp = lax.axis_size("dp")
    n_tensor = lax.axis_size("tensor")
    chips = n_tensor // CORES
    replica = lax.axis_index("dp")
    place = lax.axis_index("tensor")
    chip, core = place // CORES, place % CORES
    tokens, features = prompt_hidden_input.shape
    width, columns = frozen_key_value.shape
    rank = up_factor_matrix.shape[0]
    parts = down_factor_matrix.shape[1]
    factors = parts * rank
    strips = columns // LANES
    down_rows = features // n_dp
    up_rows = rank // n_dp
    packed_rows = down_rows + up_rows * strips
    steps = range(1, chips)
    f32, bf16 = jnp.float32, jnp.bfloat16

    def to_sibling(value):
        return lax.ppermute(value, "tensor", [(t, t ^ 1) for t in range(n_tensor)])

    def to_chip(value, step):
        pairs = [
            (CORES * q + k, CORES * ((q + step) % chips) + k)
            for q in range(chips)
            for k in range(CORES)
        ]
        return lax.ppermute(value, "tensor", pairs)

    def owner(step):
        return CORES * ((chip - step) % chips) + core

    turns = [1, 2] if n_dp % 4 == 0 else [1, 1]
    turn = [turns[strip % 2] for strip in range(strips)]
    odds = [replica // k % 2 for k in turn]
    halves = min(COLUMN_HALVES, strips)
    wide = columns // halves
    groups = [range(k * strips // halves, (k + 1) * strips // halves) for k in range(halves)]
    taken = pl.pallas_call(
        functools.partial(take_kernel, chips, turn),
        out_shape=tuple(
            jax.ShapeDtypeStruct((len(group), features, LANES), bf16)
            for group in groups
            for _ in steps
        ),
        in_specs=anywhere(1),
        out_specs=tuple(in_vmem(halves * len(steps))),
        scratch_shapes=[pltpu.SemaphoreType.DMA((len(steps) * strips,))],
        compiler_params=pltpu.CompilerParams(vmem_limit_bytes=TAKE_VMEM_BYTES),
    )(frozen_key_value)
    mine = []
    for half in range(halves):
        sent_half = taken[half * len(steps) : (half + 1) * len(steps)]
        if half > 0:
            sent_half, _ = lax.optimization_barrier((sent_half, mine[-1]))
        mine.append([to_chip(value, step) for value, step in zip(sent_half, steps)])

    hidden, up_sent, _ = lax.optimization_barrier(
        (prompt_hidden_input, up_gradient[0], taken)
    )
    gain = input_norm_gain[None, :]
    x, squares = pl.pallas_call(
        prepare_kernel,
        out_shape=(
            jax.ShapeDtypeStruct((tokens, CORES * features), bf16),
            jax.ShapeDtypeStruct((tokens, LANES), f32),
        ),
        in_specs=in_vmem(4),
        out_specs=tuple(in_vmem(2)),
        compiler_params=params(),
    )(hidden, to_sibling(hidden), gain, to_sibling(gain))
    squares = squares[:, 0]

    def by_rank(value):
        return jnp.transpose(value, (1, 2, 0)).reshape(factors, features)

    down_sent = by_rank(down_gradient[0])
    down_state = [by_rank(v) for v in (down_factor_matrix, down_moment_first, down_moment_second)]
    up_state = [up_factor_matrix, up_moment_first, up_moment_second]
    shares = jax.ShapeDtypeStruct((n_dp, packed_rows, LANES), bf16)
    updated = (
        jax.ShapeDtypeStruct((3, factors, down_rows), f32),
        jax.ShapeDtypeStruct((3, up_rows, columns), f32),
    )
    window = pl.cdiv(down_rows + LANES, LANES) * LANES
    aligned = features % LANES == 0 and window <= features
    aligned = aligned and up_rows % 8 == 0 and down_rows % 16 == 0
    packed = pl.pallas_call(
        pack_kernel,
        out_shape=shares,
        in_specs=in_vmem(2),
        out_specs=in_vmem(1)[0],
        compiler_params=params(),
    )(down_sent, up_sent)
    exchanged = lax.all_to_all(packed, "dp", 0, 0, tiled=True)
    if aligned:
        a_next, b_next, sent = pl.pallas_call(
            adam_copy_kernel,
            out_shape=updated + (shares,),
            in_specs=[SCALARS] + in_vmem(1) + anywhere(6),
            out_specs=tuple(in_vmem(3)),
            scratch_shapes=[
                pltpu.VMEM((3, factors, window), f32),
                pltpu.VMEM((3, up_rows, columns), f32),
                pltpu.SemaphoreType.DMA((6,)),
            ],
            compiler_params=params(),
        )(replica[None].astype(jnp.int32), exchanged, *down_state, *up_state)
    else:
        down_state = [
            lax.dynamic_slice_in_dim(v, replica * down_rows, down_rows, 1) for v in down_state
        ]
        up_state = [lax.dynamic_slice_in_dim(v, replica * up_rows, up_rows, 0) for v in up_state]
        a_next, b_next, sent = pl.pallas_call(
            adam_kernel,
            out_shape=updated + (shares,),
            in_specs=in_vmem(7),
            out_specs=tuple(in_vmem(3)),
            compiler_params=params(),
        )(exchanged, *down_state, *up_state)
    own_f = lax.all_to_all(sent, "dp", 0, 0, tiled=True)
    a_next = jnp.transpose(a_next.reshape(3, parts, rank, down_rows), (0, 3, 1, 2))

    own_f, x, squares = lax.optimization_barrier((own_f, x, squares))
    sibling_f = to_sibling(own_f)
    packed_b = pl.pallas_call(
        tail_kernel,
        out_shape=jax.ShapeDtypeStruct((n_dp, packed_rows - down_rows, LANES), bf16),
        in_specs=in_vmem(1),
        out_specs=in_vmem(1)[0],
        compiler_params=params(),
    )(own_f)
    other_b = [to_chip(packed_b, step) for step in steps]

    outside = [[] for _ in range(strips)]
    for half, group in enumerate(groups):
        for value in mine[half]:
            value, _ = lax.optimization_barrier((value, sent if half == 0 else other_b))
            split = pl.pallas_call(
                split_kernel,
                out_shape=(jax.ShapeDtypeStruct((features, LANES), bf16),) * len(group),
                in_specs=in_vmem(1),
                out_specs=tuple(in_vmem(len(group))),
                compiler_params=params(),
            )(value)
            for piece, strip in zip(split, group):
                pairs = [(i, i ^ turn[strip]) for i in range(n_dp)]
                outside[strip].append((piece, lax.ppermute(piece, "dp", pairs)))

    squares, _ = lax.optimization_barrier((squares, other_b))
    squares = squares + sum(to_chip(squares, step) for step in steps)
    inv_rms = jnp.broadcast_to(lax.rsqrt(squares / width + 1e-06)[:, None], (tokens, LANES))

    scale = 0.5 / math.sqrt(width * rank)

    def part_of(who):
        return who * columns // KEY_VALUE_WIDTH

    token_slices = [
        slice(k * tokens // TOKEN_HALVES, (k + 1) * tokens // TOKEN_HALVES)
        for k in range(TOKEN_HALVES)
    ]
    received = {}
    product = None
    for half in range(halves):
        group = groups[half]
        for step in steps:
            numbers = [part_of(owner(step))] + [odds[strip] for strip in group]
            numbers = jnp.stack(numbers).astype(jnp.int32)
            if product is not None:
                numbers, _ = lax.optimization_barrier((numbers, product))
            blocks = [value for strip in group for value in outside[strip][step - 1]]
            weights = pl.pallas_call(
                functools.partial(outside_kernel, (scale, parts, up_rows, group)),
                out_shape=jax.ShapeDtypeStruct((CORES * features, wide), bf16),
                in_specs=[SCALARS] + in_vmem(3 + len(blocks)),
                out_specs=in_vmem(1)[0],
                compiler_params=params(),
            )(numbers, own_f, sibling_f, other_b[step - 1], *blocks)
            for k, rows in enumerate(token_slices):
                if k > 0:
                    weights, _ = lax.optimization_barrier((weights, product))
                product = jnp.dot(x[rows], weights, preferred_element_type=f32).astype(bf16)
                received.setdefault((k, half), []).append(to_chip(product, chips - step))

    numbers = jnp.stack([place, place ^ 1, part_of(place)]).astype(jnp.int32)
    numbers, _ = lax.optimization_barrier((numbers, (product, received[0, 0])))
    totals = pl.pallas_call(
        functools.partial(own_kernel, (scale, parts, up_rows, range(strips))),
        out_shape=(jax.ShapeDtypeStruct((tokens, wide), f32),) * halves,
        grid_spec=pltpu.PrefetchScalarGridSpec(
            num_scalar_prefetch=1,
            grid=(1,),
            in_specs=[
                pl.BlockSpec((features, columns), lambda i, numbers: (numbers[0], 0)),
                pl.BlockSpec((features, columns), lambda i, numbers: (numbers[1], 0)),
            ]
            + in_vmem(3),
            out_specs=tuple(in_vmem(halves)),
            scratch_shapes=[pltpu.VMEM((CORES * features, columns), bf16)],
        ),
        compiler_params=params(),
        cost_estimate=pl.CostEstimate(
            flops=2 * tokens * CORES * features * columns,
            bytes_accessed=4 * tokens * features,
            transcendentals=0,
        ),
    )(numbers, frozen_key_value, frozen_key_value, own_f, sibling_f, x)

    keys_values = None
    for at, pieces in received.items():
        keys_values = finish(
            totals[at[1]], inv_rms, pieces, at, (tokens, columns), keys_values
        )
    return (a_next, b_next, keys_values)


def solution(mesh):
    placed = (
        P("dp", "tensor"),
        P("tensor"),
        P(None, "tensor"),
        P("tensor", None, None),
        P("tensor", None, None),
        P("tensor", None, None),
        P(None, "tensor"),
        P(None, "tensor"),
        P(None, "tensor"),
        P("dp", "tensor", None, None),
        P("dp", None, "tensor"),
    )
    return jax.shard_map(
        body,
        mesh=mesh,
        in_specs=placed,
        out_specs=(
            P(None, ("tensor", "dp"), None, None),
            P(None, "dp", "tensor"),
            P("dp", "tensor"),
        ),
        check_vma=False,
    )
```

```python
import functools
import math

import jax
import jax.numpy as jnp
from jax import lax
from jax.experimental import pallas as pl
from jax.experimental.pallas import tpu as pltpu
from jax.sharding import PartitionSpec as P

KEY_VALUE_WIDTH = 1024
STEP = 100
CORES = 2
LANES = 128
COLUMN_HALVES = 2
TOKEN_HALVES = 2
VMEM_BYTES = 16 * 2**20
TAKE_VMEM_BYTES = 58 * 2**20


def adaptive_moment_update(param, first, second, grad_mean):
    first_new = 0.9 * first + 0.1 * grad_mean
    second_new = 0.999 * second + 0.001 * grad_mean * grad_mean
    step_size = first_new / (1.0 - 0.9**STEP) / (jnp.sqrt(second_new / (1.0 - 0.999**STEP)) + 1e-08)
    return (param - 0.1 * step_size, first_new, second_new)


def in_vmem(count):
    return [pl.BlockSpec(memory_space=pltpu.VMEM)] * count


def anywhere(count):
    return [pl.BlockSpec(memory_space=pl.ANY)] * count


SCALARS = pl.BlockSpec(memory_space=pltpu.SMEM)


def params(**more):
    return pltpu.CompilerParams(vmem_limit_bytes=VMEM_BYTES, **more)


def pack_kernel(down_ref, up_ref, out_ref, mark_ref):
    mark_ref[...] = jnp.zeros_like(mark_ref)
    shares = out_ref.shape[0]
    down, up = down_ref[...].T, up_ref[...]
    down_rows, up_rows = down.shape[0] // shares, up.shape[0] // shares
    for i in range(shares):
        pieces = [down[i * down_rows : (i + 1) * down_rows]]
        for k in range(up.shape[1] // LANES):
            pieces.append(up[i * up_rows : (i + 1) * up_rows, k * LANES : (k + 1) * LANES])
        out_ref[i] = jnp.concatenate(pieces, axis=0).astype(jnp.bfloat16)


def take_kernel(chips, turn, weights_ref, _, *refs):
    outs, sem = refs[:-1], refs[-1]
    features = outs[0].shape[1]
    place, replica = lax.axis_index("tensor"), lax.axis_index("dp")
    chip, core = place // CORES, place % CORES
    copies = []
    for i, out in enumerate(outs):
        step, first = 1 + i % (chips - 1), i // (chips - 1) * out.shape[0]
        for k in range(out.shape[0]):
            half = (core + replica // turn[first + k]) % 2
            row = ((chip + step) % chips * CORES + half) * features
            source = weights_ref.at[
                pl.ds(pl.multiple_of(row, features), features),
                pl.ds((first + k) * LANES, LANES),
            ]
            copies.append(pltpu.make_async_copy(source, out.at[k], sem.at[len(copies)]))
    for copy in copies:
        copy.start()
    for copy in copies:
        copy.wait()


def split_kernel(in_ref, *outs):
    for k, out in enumerate(outs):
        out[...] = in_ref[k]


def prepare_kernel(own_ref, sibling_ref, own_gain, sibling_gain, squares_ref, *x_refs):
    features = own_ref.shape[1]
    rows = x_refs[0].shape[0]
    tile = 16 if rows % 16 == 0 else rows
    for k, x_ref in enumerate(x_refs):

        @pl.loop(0, rows // tile, unroll=2)
        def _(i):
            to = pl.ds(pl.multiple_of(i * tile, tile), tile)
            at = pl.ds(pl.multiple_of(k * rows + i * tile, tile), tile)
            own = own_ref[at, :].astype(jnp.float32)
            x_ref[to, :features] = (own * own_gain[...]).astype(x_ref.dtype)
            total = own * own
            sibling = sibling_ref[at, :].astype(jnp.float32)
            x_ref[to, features:] = (sibling * sibling_gain[...]).astype(x_ref.dtype)
            total += sibling * sibling
            total = jnp.sum(total, axis=1, keepdims=True)
            squares_ref[at, :] = jnp.broadcast_to(total, (tile, LANES))


def tail_kernel(in_ref, out_ref):
    out_ref[...] = in_ref[:, in_ref.shape[1] - out_ref.shape[1] :]


def update(total, down, up, a_ref, b_ref):
    down_rows = a_ref.shape[2]
    up_rows, columns = b_ref.shape[1:]
    strips = columns // LANES
    down_mean = total[:down_rows].T
    up_mean = jnp.concatenate(
        [total[down_rows + k * up_rows : down_rows + (k + 1) * up_rows] for k in range(strips)],
        axis=1,
    )
    p, m, v = adaptive_moment_update(*down(), down_mean)
    a_ref[0], a_ref[1], a_ref[2] = p, m, v
    pieces = [p.T]
    p, m, v = adaptive_moment_update(*up(), up_mean)
    b_ref[0], b_ref[1], b_ref[2] = p, m, v
    pieces += [p[:, k * LANES : (k + 1) * LANES] for k in range(strips)]
    return jnp.concatenate(pieces, axis=0).astype(jnp.bfloat16)


def adam_kernel(grad_ref, dp, dm, dv, up, um, uv, a_ref, b_ref, factor_ref):
    replicas = grad_ref.shape[0]
    rounded = update(
        jnp.sum(grad_ref[...].astype(jnp.float32), axis=0) / replicas,
        lambda: [ref[...] for ref in (dp, dm, dv)],
        lambda: [ref[...] for ref in (up, um, uv)],
        a_ref,
        b_ref,
    )
    for i in range(replicas):
        factor_ref[i] = rounded


def adam_copy_kernel(replica, grad_ref, *refs):
    down_state, up_state, refs = refs[:3], refs[3:6], refs[6:]
    a_ref, b_ref, factor_ref, down_buf, up_buf, sem = refs
    replicas = grad_ref.shape[0]
    down_rows, window = a_ref.shape[2], down_buf.shape[2]
    up_rows = b_ref.shape[1]
    first = replica[0] * down_rows
    lane = jnp.minimum(first // LANES * LANES, down_state[0].shape[1] - window)
    row = pl.multiple_of(replica[0] * up_rows, up_rows)
    copies = []
    for i, ref in enumerate(down_state):
        source = ref.at[:, pl.ds(pl.multiple_of(lane, LANES), window)]
        copies.append(pltpu.make_async_copy(source, down_buf.at[i], sem.at[i]))
    for i, ref in enumerate(up_state):
        source = ref.at[pl.ds(row, up_rows)]
        copies.append(pltpu.make_async_copy(source, up_buf.at[i], sem.at[3 + i]))
    for copy in copies:
        copy.start()
    total = jnp.sum(grad_ref[...].astype(jnp.float32), axis=0) / replicas
    for copy in copies:
        copy.wait()
    shift = window - (first - lane)
    rounded = update(
        total,
        lambda: [pltpu.roll(down_buf[i], shift, 1)[:, :down_rows] for i in range(3)],
        lambda: [up_buf[i] for i in range(3)],
        a_ref,
        b_ref,
    )
    for i in range(replicas):
        factor_ref[i] = rounded


def factor_a(packed_ref, down_rows):
    pieces = [packed_ref[i].astype(jnp.float32)[:down_rows] for i in range(packed_ref.shape[0])]
    return jnp.concatenate(pieces, axis=0).astype(jnp.bfloat16)


def factor_b(packed, part, parts, strip, up_rows):
    pieces = [
        packed[i].astype(jnp.float32)[strip * up_rows : (strip + 1) * up_rows]
        for i in range(packed.shape[0])
    ]
    value = jnp.concatenate(pieces, axis=0)
    rows = [jnp.where(part == j, value, jnp.zeros_like(value)) for j in range(parts)]
    return jnp.concatenate(rows, axis=0).astype(jnp.bfloat16)


def merge(scale, block, a, b):
    change = jnp.dot(a, b, preferred_element_type=jnp.float32)
    return (block.astype(jnp.float32) + scale * change).astype(jnp.bfloat16)


def tile_of(size):
    return 256 if size % 256 == 0 else size


def up_factor(static, packed, part):
    _, parts, up_rows, strips = static
    return jnp.concatenate(
        [factor_b(packed, part, parts, strip, up_rows) for strip in strips], axis=1
    )


def outside_kernel(static, numbers, own_f, sibling_f, b_ref, *refs):
    out = refs[-1]
    strips = static[3]
    features = refs[0].shape[0]
    down_rows = own_f.shape[1] - b_ref.shape[1]
    b = up_factor(static, b_ref[...], numbers[0])
    own_a, sibling_a = factor_a(own_f, down_rows), factor_a(sibling_f, down_rows)
    for k in range(len(strips)):
        mine, other = refs[2 * k : 2 * k + 2]
        odd = numbers[1 + k]
        lanes = slice(k * LANES, (k + 1) * LANES)
        block = jnp.where(odd == 0, mine[...], other[...])
        out[:features, lanes] = merge(static[0], block, own_a, b[:, lanes])
        block = jnp.where(odd == 0, other[...], mine[...])
        out[features:, lanes] = merge(static[0], block, sibling_a, b[:, lanes])


def own_kernel(static, numbers, own_block, sibling_block, own_f, sibling_f, *refs):
    xs, outs, weights = refs[: static[4]], refs[static[4] : -1], refs[-1]
    features = own_block.shape[0]
    wide = outs[0].shape[1]
    down_rows = own_f.shape[1] - len(static[3]) * static[2]
    b = up_factor(static[:4], own_f[:, down_rows:], numbers[2])
    for at, factors, block in ((0, own_f, own_block), (features, sibling_f, sibling_block)):
        weights[at : at + features] = merge(static[0], block[...], factor_a(factors, down_rows), b)
    for h, x in enumerate(xs):
        rows = x.shape[0]
        tile = 128 if rows % 128 == 0 else rows

        @pl.loop(0, rows // tile)
        def _(i):
            at = pl.ds(pl.multiple_of(i * tile, tile), tile)
            to = pl.ds(pl.multiple_of(h * rows + i * tile, tile), tile)
            value = jnp.dot(x[at, :], weights[...], preferred_element_type=jnp.float32)
            for k, out in enumerate(outs):
                out[to, :] = value[:, k * wide : (k + 1) * wide]


def finish_kernel(sources, first, own, inv, *refs):
    rows = pl.ds(first, refs[-1].shape[0])
    total = own[rows, :]
    for value in refs[:sources]:
        total = total + value[...].astype(jnp.float32)
    refs[-1][...] = (total * inv[rows, :1]).astype(refs[-1].dtype)


def finish(own, inv_rms, received, at, shape, before):
    block = received[0].shape
    operands = [own, inv_rms] + received
    in_specs = in_vmem(len(operands))
    aliases = {}
    if before is not None:
        aliases = {len(operands): 0}
        in_specs += anywhere(1)
        operands.append(before)
    return pl.pallas_call(
        functools.partial(finish_kernel, len(received), at[0] * block[0]),
        grid=(1,),
        out_shape=jax.ShapeDtypeStruct(shape, jnp.bfloat16),
        in_specs=in_specs,
        out_specs=pl.BlockSpec(block, lambda i: at),
        input_output_aliases=aliases,
        compiler_params=params(),
    )(*operands)


def body(
    prompt_hidden_input,
    input_norm_gain,
    frozen_key_value,
    down_factor_matrix,
    down_moment_first,
    down_moment_second,
    up_factor_matrix,
    up_moment_first,
    up_moment_second,
    down_gradient,
    up_gradient,
):
    n_dp = lax.axis_size("dp")
    n_tensor = lax.axis_size("tensor")
    chips = n_tensor // CORES
    replica = lax.axis_index("dp")
    place = lax.axis_index("tensor")
    chip, core = place // CORES, place % CORES
    tokens, features = prompt_hidden_input.shape
    width, columns = frozen_key_value.shape
    rank = up_factor_matrix.shape[0]
    parts = down_factor_matrix.shape[1]
    factors = parts * rank
    strips = columns // LANES
    down_rows = features // n_dp
    up_rows = rank // n_dp
    packed_rows = down_rows + up_rows * strips
    steps = range(1, chips)
    f32, bf16 = jnp.float32, jnp.bfloat16

    def to_sibling(value):
        return lax.ppermute(value, "tensor", [(t, t ^ 1) for t in range(n_tensor)])

    def to_chip(value, step):
        pairs = [
            (CORES * q + k, CORES * ((q + step) % chips) + k)
            for q in range(chips)
            for k in range(CORES)
        ]
        return lax.ppermute(value, "tensor", pairs)

    def owner(step):
        return CORES * ((chip - step) % chips) + core

    def by_rank(value):
        return jnp.transpose(value, (1, 2, 0)).reshape(factors, features)

    down_sent = by_rank(down_gradient[0])
    down_state = [by_rank(v) for v in (down_factor_matrix, down_moment_first, down_moment_second)]
    up_state = [up_factor_matrix, up_moment_first, up_moment_second]
    shares = jax.ShapeDtypeStruct((n_dp, packed_rows, LANES), bf16)
    updated = (
        jax.ShapeDtypeStruct((3, factors, down_rows), f32),
        jax.ShapeDtypeStruct((3, up_rows, columns), f32),
    )
    window = pl.cdiv(down_rows + LANES, LANES) * LANES
    aligned = features % LANES == 0 and window <= features
    aligned = aligned and up_rows % 8 == 0 and down_rows % 16 == 0
    packed, mark = pl.pallas_call(
        pack_kernel,
        out_shape=(shares, jax.ShapeDtypeStruct((8, LANES), f32)),
        in_specs=in_vmem(2),
        out_specs=tuple(in_vmem(2)),
        compiler_params=params(),
    )(down_sent, up_gradient[0])

    turns = [1, 2] if n_dp % 4 == 0 else [1, 1]
    turn = [turns[strip % 2] for strip in range(strips)]
    odds = [replica // k % 2 for k in turn]
    halves = min(COLUMN_HALVES, strips)
    wide = columns // halves
    groups = [range(k * strips // halves, (k + 1) * strips // halves) for k in range(halves)]
    taken = pl.pallas_call(
        functools.partial(take_kernel, chips, turn),
        out_shape=tuple(
            jax.ShapeDtypeStruct((len(group), features, LANES), bf16)
            for group in groups
            for _ in steps
        ),
        in_specs=anywhere(1) + in_vmem(1),
        out_specs=tuple(in_vmem(halves * len(steps))),
        scratch_shapes=[pltpu.SemaphoreType.DMA((len(steps) * strips,))],
        compiler_params=pltpu.CompilerParams(vmem_limit_bytes=TAKE_VMEM_BYTES),
    )(frozen_key_value, mark)
    mine = [
        [to_chip(taken[half * len(steps) + step - 1], step) for step in steps]
        for half in range(halves)
    ]

    gain = input_norm_gain[None, :]
    squares, *x = pl.pallas_call(
        prepare_kernel,
        out_shape=(jax.ShapeDtypeStruct((tokens, LANES), f32),)
        + (jax.ShapeDtypeStruct((tokens // TOKEN_HALVES, CORES * features), bf16),) * TOKEN_HALVES,
        in_specs=in_vmem(4),
        out_specs=tuple(in_vmem(1 + TOKEN_HALVES)),
        compiler_params=params(),
    )(prompt_hidden_input, to_sibling(prompt_hidden_input), gain, to_sibling(gain))
    squares = squares[:, 0]

    exchanged = lax.all_to_all(packed, "dp", 0, 0, tiled=True)
    if aligned:
        a_next, b_next, sent = pl.pallas_call(
            adam_copy_kernel,
            out_shape=updated + (shares,),
            in_specs=[SCALARS] + in_vmem(1) + anywhere(6),
            out_specs=tuple(in_vmem(3)),
            scratch_shapes=[
                pltpu.VMEM((3, factors, window), f32),
                pltpu.VMEM((3, up_rows, columns), f32),
                pltpu.SemaphoreType.DMA((6,)),
            ],
            compiler_params=params(),
        )(replica[None].astype(jnp.int32), exchanged, *down_state, *up_state)
    else:
        down_state = [
            lax.dynamic_slice_in_dim(v, replica * down_rows, down_rows, 1) for v in down_state
        ]
        up_state = [lax.dynamic_slice_in_dim(v, replica * up_rows, up_rows, 0) for v in up_state]
        a_next, b_next, sent = pl.pallas_call(
            adam_kernel,
            out_shape=updated + (shares,),
            in_specs=in_vmem(7),
            out_specs=tuple(in_vmem(3)),
            compiler_params=params(),
        )(exchanged, *down_state, *up_state)
    own_f = lax.all_to_all(sent, "dp", 0, 0, tiled=True)
    a_next = jnp.transpose(a_next.reshape(3, parts, rank, down_rows), (0, 3, 1, 2))

    outside = [[] for _ in range(strips)]

    def swap_half(half, after):
        for value in mine[half]:
            value, _ = lax.optimization_barrier((value, after))
            split = pl.pallas_call(
                split_kernel,
                out_shape=(jax.ShapeDtypeStruct((features, LANES), bf16),) * len(groups[half]),
                in_specs=in_vmem(1),
                out_specs=tuple(in_vmem(len(groups[half]))),
                compiler_params=params(),
            )(value)
            for piece, strip in zip(split, groups[half]):
                pairs = [(i, i ^ turn[strip]) for i in range(n_dp)]
                outside[strip].append((piece, lax.ppermute(piece, "dp", pairs)))

    swap_half(0, sent)
    own_f, squares, _ = lax.optimization_barrier((own_f, squares, outside))
    sibling_f = to_sibling(own_f)
    packed_b = pl.pallas_call(
        tail_kernel,
        out_shape=jax.ShapeDtypeStruct((n_dp, packed_rows - down_rows, LANES), bf16),
        in_specs=in_vmem(1),
        out_specs=in_vmem(1)[0],
        compiler_params=params(),
    )(own_f)
    other_b = [to_chip(packed_b, step) for step in steps]

    for half in range(1, halves):
        swap_half(half, other_b)

    squares, _ = lax.optimization_barrier((squares, other_b))
    squares = squares + sum(to_chip(squares, step) for step in steps)
    inv_rms = jnp.broadcast_to(lax.rsqrt(squares / width + 1e-06)[:, None], (tokens, LANES))

    scale = 0.5 / math.sqrt(width * rank)

    def part_of(who):
        return who * columns // KEY_VALUE_WIDTH

    received = {}
    products = None
    for half in range(halves):
        group = groups[half]
        for step in steps:
            numbers = [part_of(owner(step))] + [odds[strip] for strip in group]
            numbers = jnp.stack(numbers).astype(jnp.int32)
            if products is not None:
                numbers, _ = lax.optimization_barrier((numbers, products))
            blocks = [value for strip in group for value in outside[strip][step - 1]]
            weights = pl.pallas_call(
                functools.partial(outside_kernel, (scale, parts, up_rows, group)),
                out_shape=jax.ShapeDtypeStruct((CORES * features, wide), bf16),
                in_specs=[SCALARS] + in_vmem(3 + len(blocks)),
                out_specs=in_vmem(1)[0],
                compiler_params=params(),
            )(numbers, own_f, sibling_f, other_b[step - 1], *blocks)
            products = [
                jnp.dot(rows, weights, preferred_element_type=f32).astype(bf16) for rows in x
            ]
            for k, product in enumerate(products):
                received.setdefault((k, half), []).append(to_chip(product, chips - step))

    numbers = jnp.stack([place, place ^ 1, part_of(place)]).astype(jnp.int32)
    numbers, _ = lax.optimization_barrier((numbers, (products, received[0, 0])))
    totals = pl.pallas_call(
        functools.partial(own_kernel, (scale, parts, up_rows, range(strips), TOKEN_HALVES)),
        out_shape=(jax.ShapeDtypeStruct((tokens, wide), f32),) * halves,
        grid_spec=pltpu.PrefetchScalarGridSpec(
            num_scalar_prefetch=1,
            grid=(1,),
            in_specs=[
                pl.BlockSpec((features, columns), lambda i, numbers: (numbers[0], 0)),
                pl.BlockSpec((features, columns), lambda i, numbers: (numbers[1], 0)),
            ]
            + in_vmem(2 + TOKEN_HALVES),
            out_specs=tuple(in_vmem(halves)),
            scratch_shapes=[pltpu.VMEM((CORES * features, columns), bf16)],
        ),
        compiler_params=params(),
        cost_estimate=pl.CostEstimate(
            flops=2 * tokens * CORES * features * columns,
            bytes_accessed=4 * tokens * features,
            transcendentals=0,
        ),
    )(numbers, frozen_key_value, frozen_key_value, own_f, sibling_f, *x)

    keys_values = None
    for at, pieces in received.items():
        keys_values = finish(
            totals[at[1]], inv_rms, pieces, at, (tokens, columns), keys_values
        )
    return (a_next, b_next, keys_values)


def solution(mesh):
    placed = (
        P("dp", "tensor"),
        P("tensor"),
        P(None, "tensor"),
        P("tensor", None, None),
        P("tensor", None, None),
        P("tensor", None, None),
        P(None, "tensor"),
        P(None, "tensor"),
        P(None, "tensor"),
        P("dp", "tensor", None, None),
        P("dp", None, "tensor"),
    )
    return jax.shard_map(
        body,
        mesh=mesh,
        in_specs=placed,
        out_specs=(
            P(None, ("tensor", "dp"), None, None),
            P(None, "dp", "tensor"),
            P("dp", "tensor"),
        ),
        check_vma=False,
    )
```

```python
import functools
import math

import jax
import jax.numpy as jnp
from jax import lax
from jax.experimental import pallas as pl
from jax.experimental.pallas import tpu as pltpu
from jax.sharding import PartitionSpec as P

KEY_VALUE_WIDTH = 1024
STEP = 100
CORES = 2
LANES = 128
COLUMN_HALVES = 2
TOKEN_HALVES = 2
VMEM_BYTES = 16 * 2**20


def adaptive_moment_update(param, first, second, grad_mean):
    first_new = 0.9 * first + 0.1 * grad_mean
    second_new = 0.999 * second + 0.001 * grad_mean * grad_mean
    step_size = first_new / (1.0 - 0.9**STEP) / (jnp.sqrt(second_new / (1.0 - 0.999**STEP)) + 1e-08)
    return (param - 0.1 * step_size, first_new, second_new)


def in_vmem(count):
    return [pl.BlockSpec(memory_space=pltpu.VMEM)] * count


def anywhere(count):
    return [pl.BlockSpec(memory_space=pl.ANY)] * count


SCALARS = pl.BlockSpec(memory_space=pltpu.SMEM)


def params(**more):
    return pltpu.CompilerParams(vmem_limit_bytes=VMEM_BYTES, **more)


def pack_kernel(down_ref, up_ref, out_ref, mark_ref):
    mark_ref[...] = jnp.zeros_like(mark_ref)
    shares = out_ref.shape[0]
    down, up = down_ref[...].T, up_ref[...]
    down_rows, up_rows = down.shape[0] // shares, up.shape[0] // shares
    for i in range(shares):
        pieces = [down[i * down_rows : (i + 1) * down_rows]]
        for k in range(up.shape[1] // LANES):
            pieces.append(up[i * up_rows : (i + 1) * up_rows, k * LANES : (k + 1) * LANES])
        out_ref[i] = jnp.concatenate(pieces, axis=0).astype(jnp.bfloat16)


def take_kernel(chips, turn, weights_ref, _, *refs):
    outs, sem = refs[:-1], refs[-1]
    features = outs[0].shape[1]
    place, replica = lax.axis_index("tensor"), lax.axis_index("dp")
    chip, core = place // CORES, place % CORES
    copies = []
    for i, out in enumerate(outs):
        step, first = 1 + i % (chips - 1), i // (chips - 1) * out.shape[0]
        for k in range(out.shape[0]):
            half = (core + replica // turn[first + k]) % 2
            row = ((chip + step) % chips * CORES + half) * features
            source = weights_ref.at[
                pl.ds(pl.multiple_of(row, features), features),
                pl.ds((first + k) * LANES, LANES),
            ]
            copies.append(pltpu.make_async_copy(source, out.at[k], sem.at[len(copies)]))
    for copy in copies:
        copy.start()
    for copy in copies:
        copy.wait()


def split_kernel(in_ref, *outs):
    for k, out in enumerate(outs):
        out[...] = in_ref[k]


def prepare_kernel(own_ref, sibling_ref, own_gain, sibling_gain, squares_ref, *x_refs):
    features = own_ref.shape[1]
    rows = x_refs[0].shape[0]
    tile = 16 if rows % 16 == 0 else rows
    for k, x_ref in enumerate(x_refs):

        @pl.loop(0, rows // tile, unroll=2)
        def _(i):
            to = pl.ds(pl.multiple_of(i * tile, tile), tile)
            at = pl.ds(pl.multiple_of(k * rows + i * tile, tile), tile)
            own = own_ref[at, :].astype(jnp.float32)
            x_ref[to, :features] = (own * own_gain[...]).astype(x_ref.dtype)
            total = own * own
            sibling = sibling_ref[at, :].astype(jnp.float32)
            x_ref[to, features:] = (sibling * sibling_gain[...]).astype(x_ref.dtype)
            total += sibling * sibling
            total = jnp.sum(total, axis=1, keepdims=True)
            squares_ref[at, :] = jnp.broadcast_to(total, (tile, LANES))


def tail_kernel(in_ref, out_ref):
    out_ref[...] = in_ref[:, in_ref.shape[1] - out_ref.shape[1] :]


def update(total, down, up, a_ref, b_ref):
    down_rows = a_ref.shape[2]
    up_rows, columns = b_ref.shape[1:]
    strips = columns // LANES
    down_mean = total[:down_rows].T
    up_mean = jnp.concatenate(
        [total[down_rows + k * up_rows : down_rows + (k + 1) * up_rows] for k in range(strips)],
        axis=1,
    )
    p, m, v = adaptive_moment_update(*down(), down_mean)
    a_ref[0], a_ref[1], a_ref[2] = p, m, v
    pieces = [p.T]
    p, m, v = adaptive_moment_update(*up(), up_mean)
    b_ref[0], b_ref[1], b_ref[2] = p, m, v
    pieces += [p[:, k * LANES : (k + 1) * LANES] for k in range(strips)]
    return jnp.concatenate(pieces, axis=0).astype(jnp.bfloat16)


def adam_kernel(grad_ref, dp, dm, dv, up, um, uv, a_ref, b_ref, factor_ref):
    replicas = grad_ref.shape[0]
    rounded = update(
        jnp.sum(grad_ref[...].astype(jnp.float32), axis=0) / replicas,
        lambda: [ref[...] for ref in (dp, dm, dv)],
        lambda: [ref[...] for ref in (up, um, uv)],
        a_ref,
        b_ref,
    )
    for i in range(replicas):
        factor_ref[i] = rounded


def adam_copy_kernel(replica, grad_ref, *refs):
    down_state, up_state, refs = refs[:3], refs[3:6], refs[6:]
    a_ref, b_ref, factor_ref, down_buf, up_buf, sem = refs
    replicas = grad_ref.shape[0]
    down_rows, window = a_ref.shape[2], down_buf.shape[2]
    up_rows = b_ref.shape[1]
    first = replica[0] * down_rows
    lane = jnp.minimum(first // LANES * LANES, down_state[0].shape[1] - window)
    row = pl.multiple_of(replica[0] * up_rows, up_rows)
    copies = []
    for i, ref in enumerate(down_state):
        source = ref.at[:, pl.ds(pl.multiple_of(lane, LANES), window)]
        copies.append(pltpu.make_async_copy(source, down_buf.at[i], sem.at[i]))
    for i, ref in enumerate(up_state):
        source = ref.at[pl.ds(row, up_rows)]
        copies.append(pltpu.make_async_copy(source, up_buf.at[i], sem.at[3 + i]))
    for copy in copies:
        copy.start()
    total = jnp.sum(grad_ref[...].astype(jnp.float32), axis=0) / replicas
    for copy in copies:
        copy.wait()
    shift = window - (first - lane)
    rounded = update(
        total,
        lambda: [pltpu.roll(down_buf[i], shift, 1)[:, :down_rows] for i in range(3)],
        lambda: [up_buf[i] for i in range(3)],
        a_ref,
        b_ref,
    )
    for i in range(replicas):
        factor_ref[i] = rounded


def factor_a(packed_ref, down_rows):
    pieces = [packed_ref[i].astype(jnp.float32)[:down_rows] for i in range(packed_ref.shape[0])]
    return jnp.concatenate(pieces, axis=0).astype(jnp.bfloat16)


def factor_b(packed, part, parts, strip, up_rows):
    pieces = [
        packed[i].astype(jnp.float32)[strip * up_rows : (strip + 1) * up_rows]
        for i in range(packed.shape[0])
    ]
    value = jnp.concatenate(pieces, axis=0)
    rows = [jnp.where(part == j, value, jnp.zeros_like(value)) for j in range(parts)]
    return jnp.concatenate(rows, axis=0).astype(jnp.bfloat16)


def merge(scale, block, a, b):
    change = jnp.dot(a, b, preferred_element_type=jnp.float32)
    return (block.astype(jnp.float32) + scale * change).astype(jnp.bfloat16)


def tile_of(size):
    return 256 if size % 256 == 0 else size


def up_factor(static, packed, part):
    _, parts, up_rows, strips = static
    return jnp.concatenate(
        [factor_b(packed, part, parts, strip, up_rows) for strip in strips], axis=1
    )


def outside_kernel(static, numbers, own_f, sibling_f, b_ref, *refs):
    out = refs[-1]
    strips = static[3]
    features = refs[0].shape[0]
    down_rows = own_f.shape[1] - b_ref.shape[1]
    b = up_factor(static, b_ref[...], numbers[0])
    own_a, sibling_a = factor_a(own_f, down_rows), factor_a(sibling_f, down_rows)
    for k in range(len(strips)):
        mine, other = refs[2 * k : 2 * k + 2]
        odd = numbers[1 + k]
        lanes = slice(k * LANES, (k + 1) * LANES)
        block = jnp.where(odd == 0, mine[...], other[...])
        out[:features, lanes] = merge(static[0], block, own_a, b[:, lanes])
        block = jnp.where(odd == 0, other[...], mine[...])
        out[features:, lanes] = merge(static[0], block, sibling_a, b[:, lanes])


def own_kernel(static, numbers, own_block, sibling_block, own_f, sibling_f, *refs):
    xs, outs, weights = refs[: static[4]], refs[static[4] : -1], refs[-1]
    features = own_block.shape[0]
    wide = outs[0].shape[1]
    down_rows = own_f.shape[1] - len(static[3]) * static[2]
    b = up_factor(static[:4], own_f[:, down_rows:], numbers[2])
    for at, factors, block in ((0, own_f, own_block), (features, sibling_f, sibling_block)):
        weights[at : at + features] = merge(static[0], block[...], factor_a(factors, down_rows), b)
    for h, x in enumerate(xs):
        rows = x.shape[0]
        tile = 128 if rows % 128 == 0 else rows

        @pl.loop(0, rows // tile)
        def _(i):
            at = pl.ds(pl.multiple_of(i * tile, tile), tile)
            to = pl.ds(pl.multiple_of(h * rows + i * tile, tile), tile)
            value = jnp.dot(x[at, :], weights[...], preferred_element_type=jnp.float32)
            for k, out in enumerate(outs):
                out[to, :] = value[:, k * wide : (k + 1) * wide]


def finish_kernel(sources, first, own, inv, *refs):
    rows = pl.ds(first, refs[-1].shape[0])
    total = own[rows, :]
    for value in refs[:sources]:
        total = total + value[...].astype(jnp.float32)
    refs[-1][...] = (total * inv[rows, :1]).astype(refs[-1].dtype)


def finish(own, inv_rms, received, at, shape, before):
    block = received[0].shape
    operands = [own, inv_rms] + received
    in_specs = in_vmem(len(operands))
    aliases = {}
    if before is not None:
        aliases = {len(operands): 0}
        in_specs += anywhere(1)
        operands.append(before)
    return pl.pallas_call(
        functools.partial(finish_kernel, len(received), at[0] * block[0]),
        grid=(1,),
        out_shape=jax.ShapeDtypeStruct(shape, jnp.bfloat16),
        in_specs=in_specs,
        out_specs=pl.BlockSpec(block, lambda i: at),
        input_output_aliases=aliases,
        compiler_params=params(),
    )(*operands)


def body(
    prompt_hidden_input,
    input_norm_gain,
    frozen_key_value,
    down_factor_matrix,
    down_moment_first,
    down_moment_second,
    up_factor_matrix,
    up_moment_first,
    up_moment_second,
    down_gradient,
    up_gradient,
):
    n_dp = lax.axis_size("dp")
    n_tensor = lax.axis_size("tensor")
    chips = n_tensor // CORES
    replica = lax.axis_index("dp")
    place = lax.axis_index("tensor")
    chip, core = place // CORES, place % CORES
    tokens, features = prompt_hidden_input.shape
    width, columns = frozen_key_value.shape
    rank = up_factor_matrix.shape[0]
    parts = down_factor_matrix.shape[1]
    factors = parts * rank
    strips = columns // LANES
    down_rows = features // n_dp
    up_rows = rank // n_dp
    packed_rows = down_rows + up_rows * strips
    steps = range(1, chips)
    f32, bf16 = jnp.float32, jnp.bfloat16

    def to_sibling(value):
        return lax.ppermute(value, "tensor", [(t, t ^ 1) for t in range(n_tensor)])

    def to_chip(value, step):
        pairs = [
            (CORES * q + k, CORES * ((q + step) % chips) + k)
            for q in range(chips)
            for k in range(CORES)
        ]
        return lax.ppermute(value, "tensor", pairs)

    def owner(step):
        return CORES * ((chip - step) % chips) + core

    def by_rank(value):
        return jnp.transpose(value, (1, 2, 0)).reshape(factors, features)

    down_sent = by_rank(down_gradient[0])
    down_state = [by_rank(v) for v in (down_factor_matrix, down_moment_first, down_moment_second)]
    up_state = [up_factor_matrix, up_moment_first, up_moment_second]
    shares = jax.ShapeDtypeStruct((n_dp, packed_rows, LANES), bf16)
    updated = (
        jax.ShapeDtypeStruct((3, factors, down_rows), f32),
        jax.ShapeDtypeStruct((3, up_rows, columns), f32),
    )
    window = pl.cdiv(down_rows + LANES, LANES) * LANES
    aligned = features % LANES == 0 and window <= features
    aligned = aligned and up_rows % 8 == 0 and down_rows % 16 == 0
    packed, mark = pl.pallas_call(
        pack_kernel,
        out_shape=(shares, jax.ShapeDtypeStruct((8, LANES), f32)),
        in_specs=in_vmem(2),
        out_specs=tuple(in_vmem(2)),
        compiler_params=params(),
    )(down_sent, up_gradient[0])

    turns = [1, 2] if n_dp % 4 == 0 else [1, 1]
    turn = [turns[strip % 2] for strip in range(strips)]
    odds = [replica // k % 2 for k in turn]
    halves = min(COLUMN_HALVES, strips)
    wide = columns // halves
    groups = [range(k * strips // halves, (k + 1) * strips // halves) for k in range(halves)]
    taken = pl.pallas_call(
        functools.partial(take_kernel, chips, turn),
        out_shape=tuple(
            jax.ShapeDtypeStruct((len(group), features, LANES), bf16)
            for group in groups
            for _ in steps
        ),
        in_specs=anywhere(1) + in_vmem(1),
        out_specs=tuple(in_vmem(halves * len(steps))),
        scratch_shapes=[pltpu.SemaphoreType.DMA((len(steps) * strips,))],
        compiler_params=params(),
    )(frozen_key_value, mark)
    mine = []

    def send_half(half, after):
        blocks = taken[half * len(steps) : (half + 1) * len(steps)]
        if after is not None:
            blocks, _ = lax.optimization_barrier((blocks, after))
        mine.append([to_chip(value, step) for value, step in zip(blocks, steps)])

    send_half(0, None)

    gain = input_norm_gain[None, :]
    squares, *x = pl.pallas_call(
        prepare_kernel,
        out_shape=(jax.ShapeDtypeStruct((tokens, LANES), f32),)
        + (jax.ShapeDtypeStruct((tokens // TOKEN_HALVES, CORES * features), bf16),) * TOKEN_HALVES,
        in_specs=in_vmem(4),
        out_specs=tuple(in_vmem(1 + TOKEN_HALVES)),
        compiler_params=params(),
    )(prompt_hidden_input, to_sibling(prompt_hidden_input), gain, to_sibling(gain))
    squares = squares[:, 0]

    exchanged = lax.all_to_all(packed, "dp", 0, 0, tiled=True)
    exchanged, squares = lax.optimization_barrier((exchanged, squares))
    if aligned:
        a_next, b_next, sent = pl.pallas_call(
            adam_copy_kernel,
            out_shape=updated + (shares,),
            in_specs=[SCALARS] + in_vmem(1) + anywhere(6),
            out_specs=tuple(in_vmem(3)),
            scratch_shapes=[
                pltpu.VMEM((3, factors, window), f32),
                pltpu.VMEM((3, up_rows, columns), f32),
                pltpu.SemaphoreType.DMA((6,)),
            ],
            compiler_params=params(),
        )(replica[None].astype(jnp.int32), exchanged, *down_state, *up_state)
    else:
        down_state = [
            lax.dynamic_slice_in_dim(v, replica * down_rows, down_rows, 1) for v in down_state
        ]
        up_state = [lax.dynamic_slice_in_dim(v, replica * up_rows, up_rows, 0) for v in up_state]
        a_next, b_next, sent = pl.pallas_call(
            adam_kernel,
            out_shape=updated + (shares,),
            in_specs=in_vmem(7),
            out_specs=tuple(in_vmem(3)),
            compiler_params=params(),
        )(exchanged, *down_state, *up_state)
    own_f = lax.all_to_all(sent, "dp", 0, 0, tiled=True)
    for half in range(1, halves):
        send_half(half, (mine[-1], sent))
    a_next = jnp.transpose(a_next.reshape(3, parts, rank, down_rows), (0, 3, 1, 2))

    outside = [[] for _ in range(strips)]

    def swap_half(half, after):
        for value in mine[half]:
            value, _ = lax.optimization_barrier((value, after))
            split = pl.pallas_call(
                split_kernel,
                out_shape=(jax.ShapeDtypeStruct((features, LANES), bf16),) * len(groups[half]),
                in_specs=in_vmem(1),
                out_specs=tuple(in_vmem(len(groups[half]))),
                compiler_params=params(),
            )(value)
            for piece, strip in zip(split, groups[half]):
                pairs = [(i, i ^ turn[strip]) for i in range(n_dp)]
                outside[strip].append((piece, lax.ppermute(piece, "dp", pairs)))

    swap_half(0, sent)
    own_f, _ = lax.optimization_barrier((own_f, outside))
    sibling_f = to_sibling(own_f)
    packed_b = pl.pallas_call(
        tail_kernel,
        out_shape=jax.ShapeDtypeStruct((n_dp, packed_rows - down_rows, LANES), bf16),
        in_specs=in_vmem(1),
        out_specs=in_vmem(1)[0],
        compiler_params=params(),
    )(own_f)
    other_b = [to_chip(packed_b, step) for step in steps]

    for half in range(1, halves):
        swap_half(half, other_b)

    squares, _ = lax.optimization_barrier((squares, other_b))
    squares = squares + sum(to_chip(squares, step) for step in steps)
    inv_rms = jnp.broadcast_to(lax.rsqrt(squares / width + 1e-06)[:, None], (tokens, LANES))

    scale = 0.5 / math.sqrt(width * rank)

    def part_of(who):
        return who * columns // KEY_VALUE_WIDTH

    received = {}
    products = None
    for half in range(halves):
        group = groups[half]
        for step in steps:
            numbers = [part_of(owner(step))] + [odds[strip] for strip in group]
            numbers = jnp.stack(numbers).astype(jnp.int32)
            if products is not None:
                numbers, _ = lax.optimization_barrier((numbers, products))
            blocks = [value for strip in group for value in outside[strip][step - 1]]
            weights = pl.pallas_call(
                functools.partial(outside_kernel, (scale, parts, up_rows, group)),
                out_shape=jax.ShapeDtypeStruct((CORES * features, wide), bf16),
                in_specs=[SCALARS] + in_vmem(3 + len(blocks)),
                out_specs=in_vmem(1)[0],
                compiler_params=params(),
            )(numbers, own_f, sibling_f, other_b[step - 1], *blocks)
            products = [
                jnp.dot(rows, weights, preferred_element_type=f32).astype(bf16) for rows in x
            ]
            for k, product in enumerate(products):
                received.setdefault((k, half), []).append(to_chip(product, chips - step))

    numbers = jnp.stack([place, place ^ 1, part_of(place)]).astype(jnp.int32)
    numbers, _ = lax.optimization_barrier((numbers, (products, received[0, 0])))
    totals = pl.pallas_call(
        functools.partial(own_kernel, (scale, parts, up_rows, range(strips), TOKEN_HALVES)),
        out_shape=(jax.ShapeDtypeStruct((tokens, wide), f32),) * halves,
        grid_spec=pltpu.PrefetchScalarGridSpec(
            num_scalar_prefetch=1,
            grid=(1,),
            in_specs=[
                pl.BlockSpec((features, columns), lambda i, numbers: (numbers[0], 0)),
                pl.BlockSpec((features, columns), lambda i, numbers: (numbers[1], 0)),
            ]
            + in_vmem(2 + TOKEN_HALVES),
            out_specs=tuple(in_vmem(halves)),
            scratch_shapes=[pltpu.VMEM((CORES * features, columns), bf16)],
        ),
        compiler_params=params(),
        cost_estimate=pl.CostEstimate(
            flops=2 * tokens * CORES * features * columns,
            bytes_accessed=4 * tokens * features,
            transcendentals=0,
        ),
    )(numbers, frozen_key_value, frozen_key_value, own_f, sibling_f, *x)

    keys_values = None
    for at, pieces in received.items():
        keys_values = finish(
            totals[at[1]], inv_rms, pieces, at, (tokens, columns), keys_values
        )
    return (a_next, b_next, keys_values)


def solution(mesh):
    placed = (
        P("dp", "tensor"),
        P("tensor"),
        P(None, "tensor"),
        P("tensor", None, None),
        P("tensor", None, None),
        P("tensor", None, None),
        P(None, "tensor"),
        P(None, "tensor"),
        P(None, "tensor"),
        P("dp", "tensor", None, None),
        P("dp", None, "tensor"),
    )
    return jax.shard_map(
        body,
        mesh=mesh,
        in_specs=placed,
        out_specs=(
            P(None, ("tensor", "dp"), None, None),
            P(None, "dp", "tensor"),
            P("dp", "tensor"),
        ),
        check_vma=False,
    )
```

```python
import functools
import math

import jax
import jax.numpy as jnp
from jax import lax
from jax.experimental import pallas as pl
from jax.experimental.pallas import tpu as pltpu
from jax.sharding import PartitionSpec as P

KEY_VALUE_WIDTH = 1024
STEP = 100
CORES = 2
LANES = 128
COLUMN_HALVES = 2
TOKEN_HALVES = 2
VMEM_BYTES = 16 * 2**20
BEGIN_VMEM_BYTES = 58 * 2**20


def adaptive_moment_update(param, first, second, grad_mean):
    first_new = 0.9 * first + 0.1 * grad_mean
    second_new = 0.999 * second + 0.001 * grad_mean * grad_mean
    step_size = first_new / (1.0 - 0.9**STEP) / (jnp.sqrt(second_new / (1.0 - 0.999**STEP)) + 1e-08)
    return (param - 0.1 * step_size, first_new, second_new)


def in_vmem(count):
    return [pl.BlockSpec(memory_space=pltpu.VMEM)] * count


def anywhere(count):
    return [pl.BlockSpec(memory_space=pl.ANY)] * count


SCALARS = pl.BlockSpec(memory_space=pltpu.SMEM)


def params(**more):
    return pltpu.CompilerParams(vmem_limit_bytes=VMEM_BYTES, **more)


def pack(down, up, out_ref):
    shares = out_ref.shape[0]
    down = down.T
    down_rows, up_rows = down.shape[0] // shares, up.shape[0] // shares
    for i in range(shares):
        pieces = [down[i * down_rows : (i + 1) * down_rows]]
        for k in range(up.shape[1] // LANES):
            pieces.append(up[i * up_rows : (i + 1) * up_rows, k * LANES : (k + 1) * LANES])
        out_ref[i] = jnp.concatenate(pieces, axis=0).astype(jnp.bfloat16)


def first_lane(share, window, size):
    return jnp.minimum(share // LANES * LANES, size - window)


def begin_kernel(chips, turn, aligned, *refs):
    down_ref, up_ref, weights_ref = refs[:3]
    state, refs = refs[3 : 3 + 6 * aligned], refs[3 + 6 * aligned :]
    packed, refs = refs[0], refs[1:]
    windows, refs = refs[: 2 * aligned], refs[2 * aligned :]
    outs, (down, up, sem) = refs[:-3], refs[-3:]
    features = outs[0].shape[1]
    place, replica = lax.axis_index("tensor"), lax.axis_index("dp")
    chip, core = place // CORES, place % CORES
    copies = []

    def add(source, target):
        copies.append(pltpu.make_async_copy(source, target, sem.at[len(copies)]))
        copies[-1].start()

    add(down_ref, down)
    add(up_ref, up)
    for i, out in enumerate(outs):
        step, first = 1 + i % (chips - 1), i // (chips - 1) * out.shape[0]
        for k in range(out.shape[0]):
            half = (core + replica // turn[first + k]) % 2
            row = ((chip + step) % chips * CORES + half) * features
            add(
                weights_ref.at[
                    pl.ds(pl.multiple_of(row, features), features),
                    pl.ds((first + k) * LANES, LANES),
                ],
                out.at[k],
            )
    if aligned:
        down_win, up_win = windows
        window, up_rows = down_win.shape[2], up_win.shape[1]
        share = replica * (features // packed.shape[0])
        lane = pl.multiple_of(first_lane(share, window, features), LANES)
        row = pl.multiple_of(replica * up_rows, up_rows)
        for i in range(3):
            add(state[i].at[:, pl.ds(lane, window)], down_win.at[i])
            add(state[3 + i].at[pl.ds(row, up_rows)], up_win.at[i])
    copies[0].wait()
    copies[1].wait()
    pack(down[...], up[...], packed)
    for copy in copies[2:]:
        copy.wait()


def split_kernel(in_ref, *outs):
    for k, out in enumerate(outs):
        out[...] = in_ref[k]


def prepare_kernel(first, own_ref, sibling_ref, own_gain, sibling_gain, *refs):
    x_ref, sums_ref, squares = refs[-3:]
    features = own_ref.shape[1]
    rows = x_ref.shape[0]
    tile = 16 if rows % 16 == 0 else rows

    @pl.loop(0, rows // tile, unroll=2)
    def _(i):
        to = pl.ds(pl.multiple_of(i * tile, tile), tile)
        at = pl.ds(pl.multiple_of(first + i * tile, tile), tile)
        own = own_ref[at, :].astype(jnp.float32)
        x_ref[to, :features] = (own * own_gain[...]).astype(x_ref.dtype)
        total = own * own
        sibling = sibling_ref[at, :].astype(jnp.float32)
        x_ref[to, features:] = (sibling * sibling_gain[...]).astype(x_ref.dtype)
        total += sibling * sibling
        total = jnp.sum(total, axis=1, keepdims=True)
        squares[to, :] = jnp.broadcast_to(total, (tile, LANES))

    for ref in refs[:-3]:
        sums_ref[: ref.shape[0]] = ref[...]
    for i in range(rows // LANES):
        at = first // LANES + i
        sums_ref[at : at + 1] = squares[i * LANES : (i + 1) * LANES, :].T[:1]


def inverse_kernel(width, *refs):
    out = refs[-1]
    total = refs[0][...]
    for ref in refs[1:-1]:
        total = total + ref[...]
    inverse = lax.rsqrt(total / width + 1e-06)
    for i in range(inverse.shape[0]):
        out[i * LANES : (i + 1) * LANES, :] = jnp.broadcast_to(
            inverse[i : i + 1], (LANES, LANES)
        ).T


def tail_kernel(in_ref, out_ref):
    out_ref[...] = in_ref[:, in_ref.shape[1] - out_ref.shape[1] :]


def update(total, down, up, a_ref, b_ref):
    down_rows = a_ref.shape[2]
    up_rows, columns = b_ref.shape[1:]
    strips = columns // LANES
    down_mean = total[:down_rows].T
    up_mean = jnp.concatenate(
        [total[down_rows + k * up_rows : down_rows + (k + 1) * up_rows] for k in range(strips)],
        axis=1,
    )
    p, m, v = adaptive_moment_update(*down(), down_mean)
    a_ref[0], a_ref[1], a_ref[2] = p, m, v
    pieces = [p.T]
    p, m, v = adaptive_moment_update(*up(), up_mean)
    b_ref[0], b_ref[1], b_ref[2] = p, m, v
    pieces += [p[:, k * LANES : (k + 1) * LANES] for k in range(strips)]
    return jnp.concatenate(pieces, axis=0).astype(jnp.bfloat16)


def adam_kernel(grad_ref, down_win, up_win, a_ref, b_ref, factor_ref):
    replicas = grad_ref.shape[0]
    down_rows, window = a_ref.shape[2], down_win.shape[2]
    total = jnp.sum(grad_ref[...].astype(jnp.float32), axis=0) / replicas

    def down():
        if window == down_rows:
            return [down_win[i] for i in range(3)]
        share = lax.axis_index("dp") * down_rows
        shift = window - (share - first_lane(share, window, down_rows * replicas))
        return [pltpu.roll(down_win[i], shift, 1)[:, :down_rows] for i in range(3)]

    rounded = update(total, down, lambda: [up_win[i] for i in range(3)], a_ref, b_ref)
    for i in range(replicas):
        factor_ref[i] = rounded


def factor_a(packed_ref, down_rows):
    pieces = [packed_ref[i].astype(jnp.float32)[:down_rows] for i in range(packed_ref.shape[0])]
    return jnp.concatenate(pieces, axis=0).astype(jnp.bfloat16)


def factor_b(packed, part, parts, strip, up_rows):
    pieces = [
        packed[i].astype(jnp.float32)[strip * up_rows : (strip + 1) * up_rows]
        for i in range(packed.shape[0])
    ]
    value = jnp.concatenate(pieces, axis=0)
    rows = [jnp.where(part == j, value, jnp.zeros_like(value)) for j in range(parts)]
    return jnp.concatenate(rows, axis=0).astype(jnp.bfloat16)


def merge(scale, block, a, b):
    change = jnp.dot(a, b, preferred_element_type=jnp.float32)
    return (block.astype(jnp.float32) + scale * change).astype(jnp.bfloat16)


def multiply(x, weights, store):
    rows = x.shape[0]
    tile = rows // 2 if rows % 32 == 0 else rows

    @pl.loop(0, rows // tile)
    def _(i):
        at = pl.ds(pl.multiple_of(i * tile, tile), tile)
        store(i * tile, tile, jnp.dot(x[at, :], weights[...], preferred_element_type=jnp.float32))


def up_factor(static, packed, owner):
    _, parts, up_rows, strips, columns = static
    part = owner * columns // KEY_VALUE_WIDTH
    return jnp.concatenate(
        [factor_b(packed, part, parts, strip, up_rows) for strip in strips], axis=1
    )


def outside_kernel(static, chips, step, turn, own_f, sibling_f, b_ref, x, *refs):
    weights, product = refs[-2:]
    strips = static[3]
    features = refs[0].shape[0]
    down_rows = own_f.shape[1] - b_ref.shape[1]
    place, replica = lax.axis_index("tensor"), lax.axis_index("dp")
    owner = (place // CORES - step + chips) % chips * CORES + place % CORES
    b = up_factor(static, b_ref[...], owner)
    own_a, sibling_a = factor_a(own_f, down_rows), factor_a(sibling_f, down_rows)
    for k, strip in enumerate(strips):
        mine, other = refs[2 * k : 2 * k + 2]
        even = replica // turn[strip] % 2 == 0
        lanes = slice(k * LANES, (k + 1) * LANES)
        block = jnp.where(even, mine[...], other[...])
        weights[:features, lanes] = merge(static[0], block, own_a, b[:, lanes])
        block = jnp.where(even, other[...], mine[...])
        weights[features:, lanes] = merge(static[0], block, sibling_a, b[:, lanes])
    more_kernel(x, weights, product)


def more_kernel(x, weights, product):
    def store(first, size, value):
        product[pl.ds(first, size), :] = value.astype(product.dtype)

    multiply(x, weights, store)


def own_kernel(static, own_f, sibling_f, own_block, sibling_block, *refs):
    xs, weights = refs[: static[5]], refs[-1]
    outs = refs[len(refs) - 1 - static[6] : -1]
    features = own_block.shape[0]
    wide = outs[0].shape[1]
    down_rows = own_f.shape[1] - len(static[3]) * static[2]
    b = up_factor(static[:5], own_f[:, down_rows:], lax.axis_index("tensor"))
    for at, factors, block in ((0, own_f, own_block), (features, sibling_f, sibling_block)):
        weights[at : at + features] = merge(static[0], block[...], factor_a(factors, down_rows), b)
    for h, x in enumerate(xs):

        def store(first, size, value):
            to = pl.ds(pl.multiple_of(h * x.shape[0] + first, 16), size)
            for k, out in enumerate(outs):
                out[to, :] = value[:, k * wide : (k + 1) * wide]

        multiply(x, weights, store)


def finish_kernel(sources, first, own, inv, *refs):
    rows = pl.ds(first, refs[-1].shape[0])
    total = own[rows, :]
    for value in refs[:sources]:
        total = total + value[...].astype(jnp.float32)
    refs[-1][...] = (total * inv[rows, :1]).astype(refs[-1].dtype)


def finish(own, inv_rms, received, at, shape, before):
    block = received[0].shape
    operands = [own, inv_rms] + received
    in_specs = in_vmem(len(operands))
    aliases = {}
    if before is not None:
        aliases = {len(operands): 0}
        in_specs += anywhere(1)
        operands.append(before)
    return pl.pallas_call(
        functools.partial(finish_kernel, len(received), at[0] * block[0]),
        grid=(1,),
        out_shape=jax.ShapeDtypeStruct(shape, jnp.bfloat16),
        in_specs=in_specs,
        out_specs=pl.BlockSpec(block, lambda i: at),
        input_output_aliases=aliases,
        compiler_params=params(),
    )(*operands)


def body(
    prompt_hidden_input,
    input_norm_gain,
    frozen_key_value,
    down_factor_matrix,
    down_moment_first,
    down_moment_second,
    up_factor_matrix,
    up_moment_first,
    up_moment_second,
    down_gradient,
    up_gradient,
):
    n_dp = lax.axis_size("dp")
    n_tensor = lax.axis_size("tensor")
    chips = n_tensor // CORES
    replica = lax.axis_index("dp")
    tokens, features = prompt_hidden_input.shape
    width, columns = frozen_key_value.shape
    rank = up_factor_matrix.shape[0]
    parts = down_factor_matrix.shape[1]
    factors = parts * rank
    strips = columns // LANES
    down_rows = features // n_dp
    up_rows = rank // n_dp
    packed_rows = down_rows + up_rows * strips
    steps = range(1, chips)
    f32, bf16 = jnp.float32, jnp.bfloat16

    def to_sibling(value):
        return lax.ppermute(value, "tensor", [(t, t ^ 1) for t in range(n_tensor)])

    def to_chip(value, step):
        pairs = [
            (CORES * q + k, CORES * ((q + step) % chips) + k)
            for q in range(chips)
            for k in range(CORES)
        ]
        return lax.ppermute(value, "tensor", pairs)

    def by_rank(value):
        return jnp.transpose(value, (1, 2, 0)).reshape(factors, features)

    down_sent = by_rank(down_gradient[0])
    down_state = [by_rank(v) for v in (down_factor_matrix, down_moment_first, down_moment_second)]
    up_state = [up_factor_matrix, up_moment_first, up_moment_second]
    shares = jax.ShapeDtypeStruct((n_dp, packed_rows, LANES), bf16)
    window = pl.cdiv(down_rows + LANES, LANES) * LANES
    aligned = features % LANES == 0 and window <= features
    aligned = aligned and up_rows % 8 == 0 and down_rows % 16 == 0
    window = window if aligned else down_rows
    windows = (
        jax.ShapeDtypeStruct((3, factors, window), f32),
        jax.ShapeDtypeStruct((3, up_rows, columns), f32),
    )

    turns = [1, 2] if n_dp % 4 == 0 else [1, 1]
    turn = [turns[strip % 2] for strip in range(strips)]
    halves = min(COLUMN_HALVES, strips)
    wide = columns // halves
    groups = [range(k * strips // halves, (k + 1) * strips // halves) for k in range(halves)]
    out_shape = (shares,) + windows * aligned
    out_shape += tuple(
        jax.ShapeDtypeStruct((len(group), features, LANES), bf16)
        for group in groups
        for _ in steps
    )
    state = (down_state + up_state) * aligned
    packed, *rest = pl.pallas_call(
        functools.partial(begin_kernel, chips, turn, aligned),
        out_shape=out_shape,
        in_specs=anywhere(3 + len(state)),
        out_specs=tuple(in_vmem(len(out_shape))),
        scratch_shapes=[
            pltpu.VMEM((factors, features), f32),
            pltpu.VMEM((rank, columns), f32),
            pltpu.SemaphoreType.DMA((2 + len(steps) * strips + len(state),)),
        ],
        compiler_params=pltpu.CompilerParams(vmem_limit_bytes=BEGIN_VMEM_BYTES),
    )(down_sent, up_gradient[0], frozen_key_value, *state)
    exchanged = lax.all_to_all(packed, "dp", 0, 0, tiled=True)
    if aligned:
        down_win, up_win, *taken = rest
    else:
        taken = rest
        down_win = jnp.stack(
            [lax.dynamic_slice_in_dim(v, replica * down_rows, down_rows, 1) for v in down_state]
        )
        up_win = jnp.stack(
            [lax.dynamic_slice_in_dim(v, replica * up_rows, up_rows, 0) for v in up_state]
        )
    mine = []

    def send_half(half, after):
        blocks = taken[half * len(steps) : (half + 1) * len(steps)]
        if after is not None:
            blocks, _ = lax.optimization_barrier((blocks, after))
        mine.append([to_chip(value, step) for value, step in zip(blocks, steps)])

    send_half(0, None)

    gain = input_norm_gain[None, :]
    operands = [prompt_hidden_input, to_sibling(prompt_hidden_input), gain, to_sibling(gain)]
    x, squares = [], None
    some = tokens // TOKEN_HALVES
    for h in range(TOKEN_HALVES):
        before = [] if squares is None else [squares]
        value, squares = pl.pallas_call(
            functools.partial(prepare_kernel, h * some),
            out_shape=(
                jax.ShapeDtypeStruct((some, CORES * features), bf16),
                jax.ShapeDtypeStruct(((h + 1) * some // LANES, LANES), f32),
            ),
            in_specs=in_vmem(4 + len(before)),
            out_specs=tuple(in_vmem(2)),
            scratch_shapes=[pltpu.VMEM((some, LANES), f32)],
            compiler_params=params(),
        )(*operands, *before)
        x.append(value)
        if h == 0:
            exchanged, squares = lax.optimization_barrier((exchanged, squares))

    a_next, b_next, sent = pl.pallas_call(
        adam_kernel,
        out_shape=(
            jax.ShapeDtypeStruct((3, factors, down_rows), f32),
            jax.ShapeDtypeStruct((3, up_rows, columns), f32),
            shares,
        ),
        in_specs=in_vmem(3),
        out_specs=tuple(in_vmem(3)),
        compiler_params=params(),
    )(exchanged, down_win, up_win)
    own_f = lax.all_to_all(sent, "dp", 0, 0, tiled=True)
    for half in range(1, halves):
        send_half(half, (mine[-1], sent))
    a_next = jnp.transpose(a_next.reshape(3, parts, rank, down_rows), (0, 3, 1, 2))

    outside = [[] for _ in range(strips)]

    def swap_half(half, after):
        for value in mine[half]:
            value, _ = lax.optimization_barrier((value, after))
            split = pl.pallas_call(
                split_kernel,
                out_shape=(jax.ShapeDtypeStruct((features, LANES), bf16),) * len(groups[half]),
                in_specs=in_vmem(1),
                out_specs=tuple(in_vmem(len(groups[half]))),
                compiler_params=params(),
            )(value)
            for piece, strip in zip(split, groups[half]):
                pairs = [(i, i ^ turn[strip]) for i in range(n_dp)]
                outside[strip].append((piece, lax.ppermute(piece, "dp", pairs)))

    swap_half(0, sent)
    own_f, squares, _ = lax.optimization_barrier((own_f, squares, outside))
    sibling_f = to_sibling(own_f)
    packed_b = pl.pallas_call(
        tail_kernel,
        out_shape=jax.ShapeDtypeStruct((n_dp, packed_rows - down_rows, LANES), bf16),
        in_specs=in_vmem(1),
        out_specs=in_vmem(1)[0],
        compiler_params=params(),
    )(own_f)
    other_b = [to_chip(packed_b, step) for step in steps]

    for half in range(1, halves):
        swap_half(half, other_b)

    squares, _ = lax.optimization_barrier((squares, other_b))
    inv_rms = pl.pallas_call(
        functools.partial(inverse_kernel, width),
        out_shape=jax.ShapeDtypeStruct((tokens, LANES), f32),
        in_specs=in_vmem(chips),
        out_specs=in_vmem(1)[0],
        compiler_params=params(),
    )(squares, *[to_chip(squares, step) for step in steps])

    scale = 0.5 / math.sqrt(width * rank)

    received = {}
    after = [inv_rms]
    weights_shape = jax.ShapeDtypeStruct((CORES * features, wide), bf16)
    product_shape = jax.ShapeDtypeStruct((some, wide), bf16)
    for half, group in enumerate(groups):
        static = (scale, parts, up_rows, group, columns)
        for step in steps:
            blocks = [value for strip in group for value in outside[strip][step - 1]]
            weights, product = pl.pallas_call(
                functools.partial(outside_kernel, static, chips, step, turn),
                out_shape=(weights_shape, product_shape),
                in_specs=in_vmem(4 + len(blocks) + len(after)),
                out_specs=tuple(in_vmem(2)),
                compiler_params=params(),
            )(own_f, sibling_f, other_b[step - 1], x[0], *blocks, *after)
            after = [product]
            received.setdefault((0, half), []).append(to_chip(product, chips - step))
            for k in range(1, TOKEN_HALVES):
                product = pl.pallas_call(
                    more_kernel,
                    out_shape=product_shape,
                    in_specs=in_vmem(2),
                    out_specs=in_vmem(1)[0],
                    compiler_params=params(),
                )(x[k], weights)
                after.append(product)
                received.setdefault((k, half), []).append(to_chip(product, chips - step))

    after.append(received[0, 0][0])
    static = (scale, parts, up_rows, range(strips), columns, TOKEN_HALVES, halves)
    totals = pl.pallas_call(
        functools.partial(own_kernel, static),
        out_shape=(jax.ShapeDtypeStruct((tokens, wide), f32),) * halves,
        grid=(1,),
        in_specs=in_vmem(2)
        + [
            pl.BlockSpec((features, columns), lambda i: (lax.axis_index("tensor"), 0)),
            pl.BlockSpec((features, columns), lambda i: (lax.axis_index("tensor") ^ 1, 0)),
        ]
        + in_vmem(TOKEN_HALVES + len(after)),
        out_specs=tuple(in_vmem(halves)),
        scratch_shapes=[pltpu.VMEM((CORES * features, columns), bf16)],
        compiler_params=params(),
        cost_estimate=pl.CostEstimate(
            flops=2 * tokens * CORES * features * columns,
            bytes_accessed=4 * tokens * features,
            transcendentals=0,
        ),
    )(own_f, sibling_f, frozen_key_value, frozen_key_value, *x, *after)

    keys_values = None
    for at, pieces in received.items():
        keys_values = finish(
            totals[at[1]], inv_rms, pieces, at, (tokens, columns), keys_values
        )
    return (a_next, b_next, keys_values)


def solution(mesh):
    placed = (
        P("dp", "tensor"),
        P("tensor"),
        P(None, "tensor"),
        P("tensor", None, None),
        P("tensor", None, None),
        P("tensor", None, None),
        P(None, "tensor"),
        P(None, "tensor"),
        P(None, "tensor"),
        P("dp", "tensor", None, None),
        P("dp", None, "tensor"),
    )
    return jax.shard_map(
        body,
        mesh=mesh,
        in_specs=placed,
        out_specs=(
            P(None, ("tensor", "dp"), None, None),
            P(None, "dp", "tensor"),
            P("dp", "tensor"),
        ),
        check_vma=False,
    )
```

```python
import functools
import math

import jax
import jax.numpy as jnp
from jax import lax
from jax.experimental import pallas as pl
from jax.experimental.pallas import tpu as pltpu
from jax.sharding import PartitionSpec as P

KEY_VALUE_WIDTH = 1024
STEP = 100
CORES = 2
LANES = 128
COLUMN_HALVES = 2
TOKEN_HALVES = 2
VMEM_BYTES = 16 * 2**20
LARGE_VMEM_BYTES = 58 * 2**20


def adaptive_moment_update(param, first, second, grad_mean):
    first_new = 0.9 * first + 0.1 * grad_mean
    second_new = 0.999 * second + 0.001 * grad_mean * grad_mean
    step_size = first_new / (1.0 - 0.9**STEP) / (jnp.sqrt(second_new / (1.0 - 0.999**STEP)) + 1e-08)
    return (param - 0.1 * step_size, first_new, second_new)


def in_vmem(count):
    return [pl.BlockSpec(memory_space=pltpu.VMEM)] * count


def anywhere(count):
    return [pl.BlockSpec(memory_space=pl.ANY)] * count


SCALARS = pl.BlockSpec(memory_space=pltpu.SMEM)


def params(**more):
    return pltpu.CompilerParams(vmem_limit_bytes=VMEM_BYTES, **more)


def pack(down, up, out_ref):
    shares = out_ref.shape[0]
    down = down.T
    down_rows, up_rows = down.shape[0] // shares, up.shape[0] // shares
    for i in range(shares):
        pieces = [down[i * down_rows : (i + 1) * down_rows]]
        for k in range(up.shape[1] // LANES):
            pieces.append(up[i * up_rows : (i + 1) * up_rows, k * LANES : (k + 1) * LANES])
        out_ref[i] = jnp.concatenate(pieces, axis=0).astype(jnp.bfloat16)


def first_lane(share, window, size):
    return jnp.minimum(share // LANES * LANES, size - window)


def begin_kernel(chips, turn, aligned, *refs):
    down_ref, up_ref, weights_ref = refs[:3]
    state, refs = refs[3 : 3 + 6 * aligned], refs[3 + 6 * aligned :]
    packed, refs = refs[0], refs[1:]
    windows, refs = refs[: 2 * aligned], refs[2 * aligned :]
    outs, (down, up, sem) = refs[:-3], refs[-3:]
    features = outs[0].shape[1]
    place, replica = lax.axis_index("tensor"), lax.axis_index("dp")
    chip, core = place // CORES, place % CORES
    copies = []

    def add(source, target):
        copies.append(pltpu.make_async_copy(source, target, sem.at[len(copies)]))
        copies[-1].start()

    add(down_ref, down)
    add(up_ref, up)
    for i, out in enumerate(outs):
        step, first = 1 + i % (chips - 1), i // (chips - 1) * out.shape[0]
        for k in range(out.shape[0]):
            half = (core + replica // turn[first + k]) % 2
            row = ((chip + step) % chips * CORES + half) * features
            add(
                weights_ref.at[
                    pl.ds(pl.multiple_of(row, features), features),
                    pl.ds((first + k) * LANES, LANES),
                ],
                out.at[k],
            )
    if aligned:
        down_win, up_win = windows
        window, up_rows = down_win.shape[2], up_win.shape[1]
        share = replica * (features // packed.shape[0])
        lane = pl.multiple_of(first_lane(share, window, features), LANES)
        row = pl.multiple_of(replica * up_rows, up_rows)
        for i in range(3):
            add(state[i].at[:, pl.ds(lane, window)], down_win.at[i])
            add(state[3 + i].at[pl.ds(row, up_rows)], up_win.at[i])
    copies[0].wait()
    copies[1].wait()
    pack(down[...], up[...], packed)
    for copy in copies[2:]:
        copy.wait()


def split_kernel(in_ref, *outs):
    for k, out in enumerate(outs):
        out[...] = in_ref[k]


def prepare_kernel(own_ref, sibling_ref, own_gain, sibling_gain, *refs):
    xs, (sums_ref, squares) = refs[:-2], refs[-2:]
    block, features = own_ref.shape
    step, steps = pl.program_id(0), pl.num_programs(0)
    tile = 16 if block % 16 == 0 else block
    for k, x_ref in enumerate(xs):

        @pl.when(step // (steps // len(xs)) == k)
        def _():
            @pl.loop(0, block // tile, unroll=2)
            def _(i):
                at = pl.ds(pl.multiple_of(i * tile, tile), tile)
                own = own_ref[at, :].astype(jnp.float32)
                x_ref[at, :features] = (own * own_gain[...]).astype(x_ref.dtype)
                total = own * own
                sibling = sibling_ref[at, :].astype(jnp.float32)
                x_ref[at, features:] = (sibling * sibling_gain[...]).astype(x_ref.dtype)
                total += sibling * sibling
                total = jnp.sum(total, axis=1, keepdims=True)
                to = pl.ds(pl.multiple_of(step * block + i * tile, tile), tile)
                squares[to, :] = jnp.broadcast_to(total, (tile, LANES))

    @pl.when(step == steps - 1)
    def _():
        for i in range(sums_ref.shape[0]):
            sums_ref[i : i + 1] = squares[i * LANES : (i + 1) * LANES, :].T[:1]


def message_kernel(factor_ref, sums_ref, out_ref, sem):
    shares, up_rows = factor_ref.shape[0], out_ref.shape[1]
    copy = pltpu.make_async_copy(
        factor_ref.at[:, pl.ds(factor_ref.shape[1] - up_rows, up_rows)],
        out_ref.at[pl.ds(0, shares)],
        sem,
    )
    copy.start()
    left = sums_ref[...]
    terms = []
    for _ in range(3):
        terms.append(left.astype(jnp.bfloat16).astype(jnp.float32))
        left = left - terms[-1]
    rest = (out_ref.shape[0] - shares) * up_rows - 3 * left.shape[0]
    if rest > 0:
        terms.append(jnp.zeros((rest, LANES), jnp.float32))
    rows = jnp.concatenate(terms, axis=0)
    for i in range(out_ref.shape[0] - shares):
        out_ref[shares + i] = rows[i * up_rows : (i + 1) * up_rows].astype(jnp.bfloat16)
    copy.wait()


def inverse_kernel(width, shares, sums_ref, *refs):
    messages, out = refs[:-1], refs[-1]
    total = sums_ref[...]
    count = total.shape[0]
    for ref in messages:
        rows = [ref[i].astype(jnp.float32) for i in range(shares, ref.shape[0])]
        rows = jnp.concatenate(rows, axis=0)
        total += rows[:count] + rows[count : 2 * count] + rows[2 * count : 3 * count]
    inverse = lax.rsqrt(total / width + 1e-06)
    for i in range(count):
        out[i * LANES : (i + 1) * LANES, :] = jnp.broadcast_to(
            inverse[i : i + 1], (LANES, LANES)
        ).T


def update(total, down, up, a_ref, b_ref):
    down_rows = a_ref.shape[2]
    up_rows, columns = b_ref.shape[1:]
    strips = columns // LANES
    down_mean = total[:down_rows].T
    up_mean = jnp.concatenate(
        [total[down_rows + k * up_rows : down_rows + (k + 1) * up_rows] for k in range(strips)],
        axis=1,
    )
    p, m, v = adaptive_moment_update(*down(), down_mean)
    a_ref[0], a_ref[1], a_ref[2] = p, m, v
    pieces = [p.T]
    p, m, v = adaptive_moment_update(*up(), up_mean)
    b_ref[0], b_ref[1], b_ref[2] = p, m, v
    pieces += [p[:, k * LANES : (k + 1) * LANES] for k in range(strips)]
    return jnp.concatenate(pieces, axis=0).astype(jnp.bfloat16)


def adam_kernel(grad_in, down_in, up_in, a_ref, b_ref, factor_ref, grad_ref, down_win, up_win, sem):
    copies = [
        pltpu.make_async_copy(source, target, sem.at[i])
        for i, (source, target) in enumerate(
            ((grad_in, grad_ref), (down_in, down_win), (up_in, up_win))
        )
    ]
    for copy in copies:
        copy.start()
    for copy in copies:
        copy.wait()
    replicas = grad_ref.shape[0]
    down_rows, window = a_ref.shape[2], down_win.shape[2]
    total = jnp.sum(grad_ref[...].astype(jnp.float32), axis=0) / replicas

    def down():
        if window == down_rows:
            return [down_win[i] for i in range(3)]
        share = lax.axis_index("dp") * down_rows
        shift = window - (share - first_lane(share, window, down_rows * replicas))
        return [pltpu.roll(down_win[i], shift, 1)[:, :down_rows] for i in range(3)]

    rounded = update(total, down, lambda: [up_win[i] for i in range(3)], a_ref, b_ref)
    for i in range(replicas):
        factor_ref[i] = rounded


def factor_a(packed_ref, down_rows):
    pieces = [packed_ref[i].astype(jnp.float32)[:down_rows] for i in range(packed_ref.shape[0])]
    return jnp.concatenate(pieces, axis=0).astype(jnp.bfloat16)


def factor_b(packed, part, parts, strip, up_rows):
    pieces = [
        packed[i].astype(jnp.float32)[strip * up_rows : (strip + 1) * up_rows]
        for i in range(packed.shape[0])
    ]
    value = jnp.concatenate(pieces, axis=0)
    rows = [jnp.where(part == j, value, jnp.zeros_like(value)) for j in range(parts)]
    return jnp.concatenate(rows, axis=0).astype(jnp.bfloat16)


def merge(scale, block, a, b):
    change = jnp.dot(a, b, preferred_element_type=jnp.float32)
    return (block.astype(jnp.float32) + scale * change).astype(jnp.bfloat16)


def multiply(x, weights, store):
    rows = x.shape[0]
    tile = rows // 2 if rows % 32 == 0 else rows

    @pl.loop(0, rows // tile)
    def _(i):
        at = pl.ds(pl.multiple_of(i * tile, tile), tile)
        store(i * tile, tile, jnp.dot(x[at, :], weights[...], preferred_element_type=jnp.float32))


def up_factor(static, packed, owner):
    _, parts, up_rows, strips, columns = static
    part = owner * columns // KEY_VALUE_WIDTH
    return jnp.concatenate(
        [factor_b(packed, part, parts, strip, up_rows) for strip in strips], axis=1
    )


def outside_kernel(static, chips, step, turn, own_f, sibling_f, b_ref, x_in, *refs):
    weights, product, x, sem = refs[-4:]
    copy = pltpu.make_async_copy(x_in, x, sem)
    copy.start()
    strips = static[3]
    features = refs[0].shape[0]
    down_rows = own_f.shape[1] - b_ref.shape[1]
    place, replica = lax.axis_index("tensor"), lax.axis_index("dp")
    owner = (place // CORES - step + chips) % chips * CORES + place % CORES
    b = up_factor(static, b_ref[: own_f.shape[0]], owner)
    own_a, sibling_a = factor_a(own_f, down_rows), factor_a(sibling_f, down_rows)
    for k, strip in enumerate(strips):
        mine, other = refs[2 * k : 2 * k + 2]
        even = replica // turn[strip] % 2 == 0
        lanes = slice(k * LANES, (k + 1) * LANES)
        block = jnp.where(even, mine[...], other[...])
        weights[:features, lanes] = merge(static[0], block, own_a, b[:, lanes])
        block = jnp.where(even, other[...], mine[...])
        weights[features:, lanes] = merge(static[0], block, sibling_a, b[:, lanes])
    copy.wait()
    more_kernel(x, weights, product)


def more_kernel(x, weights, product):
    def store(first, size, value):
        product[pl.ds(first, size), :] = value.astype(product.dtype)

    multiply(x, weights, store)


def own_kernel(static, own_f, sibling_f, own_block, sibling_block, *refs):
    xs, weights = refs[: static[5]], refs[-1]
    outs = refs[len(refs) - 1 - static[6] : -1]
    features = own_block.shape[0]
    wide = outs[0].shape[1]
    down_rows = own_f.shape[1] - len(static[3]) * static[2]
    b = up_factor(static[:5], own_f[:, down_rows:], lax.axis_index("tensor"))
    for at, factors, block in ((0, own_f, own_block), (features, sibling_f, sibling_block)):
        weights[at : at + features] = merge(static[0], block[...], factor_a(factors, down_rows), b)
    for h, x in enumerate(xs):

        def store(first, size, value):
            to = pl.ds(pl.multiple_of(h * x.shape[0] + first, 16), size)
            for k, out in enumerate(outs):
                out[to, :] = value[:, k * wide : (k + 1) * wide]

        multiply(x, weights, store)


def finish_kernel(sources, first, own, inv, *refs):
    rows = pl.ds(first, refs[-1].shape[0])
    total = own[rows, :]
    for value in refs[:sources]:
        total = total + value[...].astype(jnp.float32)
    refs[-1][...] = (total * inv[rows, :1]).astype(refs[-1].dtype)


def finish(own, inv_rms, received, at, shape, before):
    block = received[0].shape
    operands = [own, inv_rms] + received
    in_specs = in_vmem(len(operands))
    aliases = {}
    if before is not None:
        aliases = {len(operands): 0}
        in_specs += anywhere(1)
        operands.append(before)
    return pl.pallas_call(
        functools.partial(finish_kernel, len(received), at[0] * block[0]),
        grid=(1,),
        out_shape=jax.ShapeDtypeStruct(shape, jnp.bfloat16),
        in_specs=in_specs,
        out_specs=pl.BlockSpec(block, lambda i: at),
        input_output_aliases=aliases,
        compiler_params=params(),
    )(*operands)


def body(
    prompt_hidden_input,
    input_norm_gain,
    frozen_key_value,
    down_factor_matrix,
    down_moment_first,
    down_moment_second,
    up_factor_matrix,
    up_moment_first,
    up_moment_second,
    down_gradient,
    up_gradient,
):
    n_dp = lax.axis_size("dp")
    n_tensor = lax.axis_size("tensor")
    chips = n_tensor // CORES
    replica = lax.axis_index("dp")
    tokens, features = prompt_hidden_input.shape
    width, columns = frozen_key_value.shape
    rank = up_factor_matrix.shape[0]
    parts = down_factor_matrix.shape[1]
    factors = parts * rank
    strips = columns // LANES
    down_rows = features // n_dp
    up_rows = rank // n_dp
    packed_rows = down_rows + up_rows * strips
    steps = range(1, chips)
    f32, bf16 = jnp.float32, jnp.bfloat16

    def to_sibling(value):
        return lax.ppermute(value, "tensor", [(t, t ^ 1) for t in range(n_tensor)])

    def to_chip(value, step):
        pairs = [
            (CORES * q + k, CORES * ((q + step) % chips) + k)
            for q in range(chips)
            for k in range(CORES)
        ]
        return lax.ppermute(value, "tensor", pairs)

    def by_rank(value):
        return jnp.transpose(value, (1, 2, 0)).reshape(factors, features)

    down_sent = by_rank(down_gradient[0])
    down_state = [by_rank(v) for v in (down_factor_matrix, down_moment_first, down_moment_second)]
    up_state = [up_factor_matrix, up_moment_first, up_moment_second]
    shares = jax.ShapeDtypeStruct((n_dp, packed_rows, LANES), bf16)
    window = pl.cdiv(down_rows + LANES, LANES) * LANES
    aligned = features % LANES == 0 and window <= features
    aligned = aligned and up_rows % 8 == 0 and down_rows % 16 == 0
    window = window if aligned else down_rows
    windows = (
        jax.ShapeDtypeStruct((3, factors, window), f32),
        jax.ShapeDtypeStruct((3, up_rows, columns), f32),
    )

    turns = [1, 2] if n_dp % 4 == 0 else [1, 1]
    turn = [turns[strip % 2] for strip in range(strips)]
    halves = min(COLUMN_HALVES, strips)
    wide = columns // halves
    groups = [range(k * strips // halves, (k + 1) * strips // halves) for k in range(halves)]
    out_shape = (shares,) + windows * aligned
    out_shape += tuple(
        jax.ShapeDtypeStruct((len(group), features, LANES), bf16)
        for group in groups
        for _ in steps
    )
    state = (down_state + up_state) * aligned
    packed, *rest = pl.pallas_call(
        functools.partial(begin_kernel, chips, turn, aligned),
        out_shape=out_shape,
        in_specs=anywhere(3 + len(state)),
        out_specs=tuple(in_vmem(len(out_shape))),
        scratch_shapes=[
            pltpu.VMEM((factors, features), f32),
            pltpu.VMEM((rank, columns), f32),
            pltpu.SemaphoreType.DMA((2 + len(steps) * strips + len(state),)),
        ],
        compiler_params=pltpu.CompilerParams(vmem_limit_bytes=LARGE_VMEM_BYTES),
    )(down_sent, up_gradient[0], frozen_key_value, *state)
    exchanged = lax.all_to_all(packed, "dp", 0, 0, tiled=True)
    if aligned:
        down_win, up_win, *taken = rest
    else:
        taken = rest
        down_win = jnp.stack(
            [lax.dynamic_slice_in_dim(v, replica * down_rows, down_rows, 1) for v in down_state]
        )
        up_win = jnp.stack(
            [lax.dynamic_slice_in_dim(v, replica * up_rows, up_rows, 0) for v in up_state]
        )
    mine = []

    def send_half(half, after):
        blocks = taken[half * len(steps) : (half + 1) * len(steps)]
        if after is not None:
            blocks, _ = lax.optimization_barrier((blocks, after))
        mine.append([to_chip(value, step) for value, step in zip(blocks, steps)])

    send_half(0, None)

    gain = input_norm_gain[None, :]
    some = tokens // TOKEN_HALVES
    rows = LANES if some % LANES == 0 else some
    groups_of = some // rows
    token_block = pl.BlockSpec((rows, features), lambda i: (i, 0))
    gain_block = pl.BlockSpec((1, features), lambda i: (0, 0))
    *x, squares = pl.pallas_call(
        prepare_kernel,
        grid=(TOKEN_HALVES * groups_of,),
        out_shape=(jax.ShapeDtypeStruct((some, CORES * features), bf16),) * TOKEN_HALVES
        + (jax.ShapeDtypeStruct((tokens // LANES, LANES), f32),),
        in_specs=[token_block, token_block, gain_block, gain_block],
        out_specs=tuple(
            pl.BlockSpec(
                (rows, CORES * features),
                lambda i, k=k: (jnp.clip(i - k * groups_of, 0, groups_of - 1), 0),
            )
            for k in range(TOKEN_HALVES)
        )
        + (pl.BlockSpec((tokens // LANES, LANES), lambda i: (0, 0)),),
        scratch_shapes=[pltpu.VMEM((tokens, LANES), f32)],
        compiler_params=pltpu.CompilerParams(vmem_limit_bytes=LARGE_VMEM_BYTES),
    )(prompt_hidden_input, to_sibling(prompt_hidden_input), gain, to_sibling(gain))
    exchanged, squares = lax.optimization_barrier((exchanged, squares))
    a_next, b_next, sent = pl.pallas_call(
        adam_kernel,
        out_shape=(
            jax.ShapeDtypeStruct((3, factors, down_rows), f32),
            jax.ShapeDtypeStruct((3, up_rows, columns), f32),
            shares,
        ),
        in_specs=anywhere(3),
        out_specs=tuple(in_vmem(3)),
        scratch_shapes=[
            pltpu.VMEM((n_dp, packed_rows, LANES), bf16),
            pltpu.VMEM((3, factors, window), f32),
            pltpu.VMEM((3, up_rows, columns), f32),
            pltpu.SemaphoreType.DMA((3,)),
        ],
        compiler_params=pltpu.CompilerParams(vmem_limit_bytes=LARGE_VMEM_BYTES),
    )(exchanged, down_win, up_win)
    own_f = lax.all_to_all(sent, "dp", 0, 0, tiled=True)
    for half in range(1, halves):
        send_half(half, (mine[-1], sent))
    a_next = jnp.transpose(a_next.reshape(3, parts, rank, down_rows), (0, 3, 1, 2))

    outside = [[] for _ in range(strips)]

    def swap_half(half, after):
        for value in mine[half]:
            value, _ = lax.optimization_barrier((value, after))
            split = pl.pallas_call(
                split_kernel,
                out_shape=(jax.ShapeDtypeStruct((features, LANES), bf16),) * len(groups[half]),
                in_specs=in_vmem(1),
                out_specs=tuple(in_vmem(len(groups[half]))),
                compiler_params=params(),
            )(value)
            for piece, strip in zip(split, groups[half]):
                pairs = [(i, i ^ turn[strip]) for i in range(n_dp)]
                outside[strip].append((piece, lax.ppermute(piece, "dp", pairs)))

    swap_half(0, sent)
    own_f, _ = lax.optimization_barrier((own_f, outside))
    sibling_f = to_sibling(own_f)
    up_packed = packed_rows - down_rows
    more = pl.cdiv(3 * (tokens // LANES), up_packed)
    message = pl.pallas_call(
        message_kernel,
        out_shape=jax.ShapeDtypeStruct((n_dp + more, up_packed, LANES), bf16),
        in_specs=anywhere(1) + in_vmem(1),
        out_specs=in_vmem(1)[0],
        scratch_shapes=[pltpu.SemaphoreType.DMA],
        compiler_params=params(),
    )(own_f, squares)
    messages = [to_chip(message, step) for step in steps]
    inv_rms = pl.pallas_call(
        functools.partial(inverse_kernel, width, n_dp),
        out_shape=jax.ShapeDtypeStruct((tokens, LANES), f32),
        in_specs=in_vmem(chips),
        out_specs=in_vmem(1)[0],
        compiler_params=params(),
    )(squares, *messages)

    scale = 0.5 / math.sqrt(width * rank)

    received = {}
    after = []
    weights_shape = jax.ShapeDtypeStruct((CORES * features, wide), bf16)
    product_shape = jax.ShapeDtypeStruct((some, wide), bf16)
    for half, group in enumerate(groups):
        static = (scale, parts, up_rows, group, columns)
        if half > 0:
            swap_half(half, after)
        for step in steps:
            blocks = [value for strip in group for value in outside[strip][step - 1]]
            weights, product = pl.pallas_call(
                functools.partial(outside_kernel, static, chips, step, turn),
                out_shape=(weights_shape, product_shape),
                in_specs=in_vmem(3) + anywhere(1) + in_vmem(len(blocks) + len(after)),
                out_specs=tuple(in_vmem(2)),
                scratch_shapes=[
                    pltpu.VMEM((some, CORES * features), bf16),
                    pltpu.SemaphoreType.DMA,
                ],
                compiler_params=params(),
            )(own_f, sibling_f, messages[step - 1], x[0], *blocks, *after)
            after = [product]
            received.setdefault((0, half), []).append(to_chip(product, chips - step))
            for k in range(1, TOKEN_HALVES):
                product = pl.pallas_call(
                    more_kernel,
                    out_shape=product_shape,
                    in_specs=in_vmem(2),
                    out_specs=in_vmem(1)[0],
                    compiler_params=params(),
                )(x[k], weights)
                after.append(product)
                received.setdefault((k, half), []).append(to_chip(product, chips - step))

    after.append(received[0, 0][0])
    static = (scale, parts, up_rows, range(strips), columns, TOKEN_HALVES, halves)
    totals = pl.pallas_call(
        functools.partial(own_kernel, static),
        out_shape=(jax.ShapeDtypeStruct((tokens, wide), f32),) * halves,
        grid=(1,),
        in_specs=in_vmem(2)
        + [
            pl.BlockSpec((features, columns), lambda i: (lax.axis_index("tensor"), 0)),
            pl.BlockSpec((features, columns), lambda i: (lax.axis_index("tensor") ^ 1, 0)),
        ]
        + in_vmem(TOKEN_HALVES + len(after)),
        out_specs=tuple(in_vmem(halves)),
        scratch_shapes=[pltpu.VMEM((CORES * features, columns), bf16)],
        compiler_params=params(),
        cost_estimate=pl.CostEstimate(
            flops=2 * tokens * CORES * features * columns,
            bytes_accessed=4 * tokens * features,
            transcendentals=0,
        ),
    )(own_f, sibling_f, frozen_key_value, frozen_key_value, *x, *after)

    keys_values = None
    for at, pieces in received.items():
        keys_values = finish(
            totals[at[1]], inv_rms, pieces, at, (tokens, columns), keys_values
        )
    return (a_next, b_next, keys_values)


def solution(mesh):
    placed = (
        P("dp", "tensor"),
        P("tensor"),
        P(None, "tensor"),
        P("tensor", None, None),
        P("tensor", None, None),
        P("tensor", None, None),
        P(None, "tensor"),
        P(None, "tensor"),
        P(None, "tensor"),
        P("dp", "tensor", None, None),
        P("dp", None, "tensor"),
    )
    return jax.shard_map(
        body,
        mesh=mesh,
        in_specs=placed,
        out_specs=(
            P(None, ("tensor", "dp"), None, None),
            P(None, "dp", "tensor"),
            P("dp", "tensor"),
        ),
        check_vma=False,
    )
```

```python
import functools
import math

import jax
import jax.numpy as jnp
from jax import lax
from jax.experimental import pallas as pl
from jax.experimental.pallas import tpu as pltpu
from jax.sharding import PartitionSpec as P

KEY_VALUE_WIDTH = 1024
STEP = 100
CORES = 2
LANES = 128
COLUMN_HALVES = 2
TOKEN_HALVES = 2
FACTOR_PIECES = 2
VMEM_BYTES = 16 * 2**20
LARGE_VMEM_BYTES = 58 * 2**20
PREPARE_VMEM_BYTES = 40 * 2**20


def adaptive_moment_update(param, first, second, grad_mean):
    first_new = 0.9 * first + 0.1 * grad_mean
    second_new = 0.999 * second + 0.001 * grad_mean * grad_mean
    step_size = first_new / (1.0 - 0.9**STEP) / (jnp.sqrt(second_new / (1.0 - 0.999**STEP)) + 1e-08)
    return (param - 0.1 * step_size, first_new, second_new)


def in_vmem(count):
    return [pl.BlockSpec(memory_space=pltpu.VMEM)] * count


def anywhere(count):
    return [pl.BlockSpec(memory_space=pl.ANY)] * count


SCALARS = pl.BlockSpec(memory_space=pltpu.SMEM)


def params(**more):
    return pltpu.CompilerParams(vmem_limit_bytes=VMEM_BYTES, **more)


def pack(down, up, out_ref):
    shares = out_ref.shape[0]
    down = down.T
    down_rows, up_rows = down.shape[0] // shares, up.shape[0] // shares
    for i in range(shares):
        pieces = [down[i * down_rows : (i + 1) * down_rows]]
        for k in range(up.shape[1] // LANES):
            pieces.append(up[i * up_rows : (i + 1) * up_rows, k * LANES : (k + 1) * LANES])
        out_ref[i] = jnp.concatenate(pieces, axis=0).astype(jnp.bfloat16)


def first_lane(share, window, size):
    return jnp.minimum(share // LANES * LANES, size - window)


def begin_kernel(chips, turn, aligned, *refs):
    down_ref, up_ref, weights_ref = refs[:3]
    state, refs = refs[3 : 3 + 6 * aligned], refs[3 + 6 * aligned :]
    packed, refs = refs[0], refs[1:]
    windows, refs = refs[: 2 * aligned], refs[2 * aligned :]
    outs, (down, up, sem) = refs[:-3], refs[-3:]
    features = outs[0].shape[1]
    place, replica = lax.axis_index("tensor"), lax.axis_index("dp")
    chip, core = place // CORES, place % CORES
    copies = []

    def add(source, target):
        copies.append(pltpu.make_async_copy(source, target, sem.at[len(copies)]))
        copies[-1].start()

    add(down_ref, down)
    add(up_ref, up)
    for i, out in enumerate(outs):
        step, first = 1 + i % (chips - 1), i // (chips - 1) * out.shape[0]
        for k in range(out.shape[0]):
            half = (core + replica // turn[first + k]) % 2
            row = ((chip + step) % chips * CORES + half) * features
            add(
                weights_ref.at[
                    pl.ds(pl.multiple_of(row, features), features),
                    pl.ds((first + k) * LANES, LANES),
                ],
                out.at[k],
            )
    if aligned:
        down_win, up_win = windows
        window, up_rows = down_win.shape[2], up_win.shape[1]
        share = replica * (features // packed.shape[0])
        lane = pl.multiple_of(first_lane(share, window, features), LANES)
        row = pl.multiple_of(replica * up_rows, up_rows)
        for i in range(3):
            add(state[i].at[:, pl.ds(lane, window)], down_win.at[i])
            add(state[3 + i].at[pl.ds(row, up_rows)], up_win.at[i])
    copies[0].wait()
    copies[1].wait()
    pack(down[...], up[...], packed)
    for copy in copies[2:]:
        copy.wait()


def split_kernel(in_ref, *outs):
    for k, out in enumerate(outs):
        out[...] = in_ref[k]


def prepare(own_ref, sibling_ref, own_gain, sibling_gain, x_ref, sums_ref, squares):
    block, features = own_ref.shape
    step = pl.program_id(0)
    tile = 16 if block % 16 == 0 else block

    @pl.loop(0, block // tile, unroll=2)
    def _(i):
        at = pl.ds(pl.multiple_of(i * tile, tile), tile)
        to = pl.ds(pl.multiple_of(step * block + i * tile, tile), tile)
        own = own_ref[at, :].astype(jnp.float32)
        x_ref[to, :features] = (own * own_gain[...]).astype(x_ref.dtype)
        total = own * own
        sibling = sibling_ref[at, :].astype(jnp.float32)
        x_ref[to, features:] = (sibling * sibling_gain[...]).astype(x_ref.dtype)
        total += sibling * sibling
        total = jnp.sum(total, axis=1, keepdims=True)
        squares[to, :] = jnp.broadcast_to(total, (tile, LANES))

    @pl.when(step == pl.num_programs(0) - 1)
    def _():
        for i in range(sums_ref.shape[0]):
            sums_ref[i : i + 1] = squares[i * LANES : (i + 1) * LANES, :].T[:1]

    return pl.ds(pl.multiple_of(step * block, block), block)


def prepare_kernel(*refs):
    prepare(*refs)


def prepare_multiply_kernel(own_ref, sibling_ref, own_gain, sibling_gain, weights, *refs):
    x_ref, sums_ref, product, squares = refs
    rows = prepare(own_ref, sibling_ref, own_gain, sibling_gain, x_ref, sums_ref, squares)
    value = jnp.dot(x_ref[rows, :], weights[...], preferred_element_type=jnp.float32)
    product[rows, :] = value.astype(product.dtype)


def message_kernel(factor_ref, sums_ref, out_ref, *refs):
    pieces, sem = refs[:-1], refs[-1]
    shares, up_rows = factor_ref.shape[0], out_ref.shape[1]
    copies = [
        pltpu.make_async_copy(
            factor_ref.at[:, pl.ds(factor_ref.shape[1] - up_rows, up_rows)],
            out_ref.at[pl.ds(0, shares)],
            sem.at[0],
        )
    ]
    for k, piece in enumerate(pieces):
        size = piece.shape[0]
        copies.append(
            pltpu.make_async_copy(factor_ref.at[pl.ds(k * size, size)], piece, sem.at[1 + k])
        )
    for copy in copies:
        copy.start()
    left = sums_ref[...]
    terms = []
    for _ in range(3):
        terms.append(left.astype(jnp.bfloat16).astype(jnp.float32))
        left = left - terms[-1]
    rest = (out_ref.shape[0] - shares) * up_rows - 3 * left.shape[0]
    if rest > 0:
        terms.append(jnp.zeros((rest, LANES), jnp.float32))
    rows = jnp.concatenate(terms, axis=0)
    for i in range(out_ref.shape[0] - shares):
        out_ref[shares + i] = rows[i * up_rows : (i + 1) * up_rows].astype(jnp.bfloat16)
    for copy in copies:
        copy.wait()


def inverse_kernel(width, shares, sums_ref, *refs):
    messages, out = refs[:-1], refs[-1]
    total = sums_ref[...]
    count = total.shape[0]
    for ref in messages:
        if shares == 0:
            total += ref[...]
            continue
        rows = [ref[i].astype(jnp.float32) for i in range(shares, ref.shape[0])]
        rows = jnp.concatenate(rows, axis=0)
        total += rows[:count] + rows[count : 2 * count] + rows[2 * count : 3 * count]
    inverse = lax.rsqrt(total / width + 1e-06)
    for i in range(count):
        out[i * LANES : (i + 1) * LANES, :] = jnp.broadcast_to(
            inverse[i : i + 1], (LANES, LANES)
        ).T


def update(total, down, up, a_ref, b_ref):
    down_rows = a_ref.shape[2]
    up_rows, columns = b_ref.shape[1:]
    strips = columns // LANES
    down_mean = total[:down_rows].T
    up_mean = jnp.concatenate(
        [total[down_rows + k * up_rows : down_rows + (k + 1) * up_rows] for k in range(strips)],
        axis=1,
    )
    p, m, v = adaptive_moment_update(*down(), down_mean)
    a_ref[0], a_ref[1], a_ref[2] = p, m, v
    pieces = [p.T]
    p, m, v = adaptive_moment_update(*up(), up_mean)
    b_ref[0], b_ref[1], b_ref[2] = p, m, v
    pieces += [p[:, k * LANES : (k + 1) * LANES] for k in range(strips)]
    return jnp.concatenate(pieces, axis=0).astype(jnp.bfloat16)


def adam_kernel(grad_in, down_in, up_in, a_ref, b_ref, factor_ref, grad_ref, down_win, up_win, sem):
    copies = [
        pltpu.make_async_copy(source, target, sem.at[i])
        for i, (source, target) in enumerate(
            ((grad_in, grad_ref), (down_in, down_win), (up_in, up_win))
        )
    ]
    for copy in copies:
        copy.start()
    for copy in copies:
        copy.wait()
    replicas = grad_ref.shape[0]
    down_rows, window = a_ref.shape[2], down_win.shape[2]
    total = jnp.sum(grad_ref[...].astype(jnp.float32), axis=0) / replicas

    def down():
        if window == down_rows:
            return [down_win[i] for i in range(3)]
        share = lax.axis_index("dp") * down_rows
        shift = window - (share - first_lane(share, window, down_rows * replicas))
        return [pltpu.roll(down_win[i], shift, 1)[:, :down_rows] for i in range(3)]

    rounded = update(total, down, lambda: [up_win[i] for i in range(3)], a_ref, b_ref)
    for i in range(replicas):
        factor_ref[i] = rounded


def factor_a(refs, down_rows):
    pieces = []
    for ref in refs:
        pieces += [ref[i].astype(jnp.float32)[:down_rows] for i in range(ref.shape[0])]
    return jnp.concatenate(pieces, axis=0).astype(jnp.bfloat16)


def factor_b(packed, part, parts, strip, up_rows):
    pieces = [
        packed[i].astype(jnp.float32)[strip * up_rows : (strip + 1) * up_rows]
        for i in range(packed.shape[0])
    ]
    value = jnp.concatenate(pieces, axis=0)
    rows = [jnp.where(part == j, value, jnp.zeros_like(value)) for j in range(parts)]
    return jnp.concatenate(rows, axis=0).astype(jnp.bfloat16)


def merge(scale, block, a, b):
    change = jnp.dot(a, b, preferred_element_type=jnp.float32)
    return (block.astype(jnp.float32) + scale * change).astype(jnp.bfloat16)


def multiply(x, weights, store):
    rows = x.shape[0]
    tile = rows // 2 if rows % 32 == 0 else rows

    @pl.loop(0, rows // tile)
    def _(i):
        at = pl.ds(pl.multiple_of(i * tile, tile), tile)
        store(i * tile, tile, jnp.dot(x[at, :], weights[...], preferred_element_type=jnp.float32))


def up_factor(static, packed, owner):
    _, parts, up_rows, strips, columns = static
    part = owner * columns // KEY_VALUE_WIDTH
    return jnp.concatenate(
        [factor_b(packed, part, parts, strip, up_rows) for strip in strips], axis=1
    )


def outside_kernel(static, chips, step, turn, own_f, b_ref, x, *refs):
    sibling_f, blocks = refs[:FACTOR_PIECES], refs[FACTOR_PIECES:]
    weights, product = refs[-2:]
    strips = static[3]
    features = blocks[0].shape[0]
    down_rows = own_f.shape[1] - b_ref.shape[1]
    place, replica = lax.axis_index("tensor"), lax.axis_index("dp")
    owner = (place // CORES - step + chips) % chips * CORES + place % CORES
    b = up_factor(static, b_ref[: own_f.shape[0]], owner)
    own_a, sibling_a = factor_a([own_f], down_rows), factor_a(sibling_f, down_rows)
    for k, strip in enumerate(strips):
        mine, other = blocks[2 * k : 2 * k + 2]
        even = replica // turn[strip] % 2 == 0
        lanes = slice(k * LANES, (k + 1) * LANES)
        block = jnp.where(even, mine[...], other[...])
        weights[:features, lanes] = merge(static[0], block, own_a, b[:, lanes])
        block = jnp.where(even, other[...], mine[...])
        weights[features:, lanes] = merge(static[0], block, sibling_a, b[:, lanes])
    more_kernel(x, weights, product)


def more_kernel(x, weights, product):
    def store(first, size, value):
        product[pl.ds(first, size), :] = value.astype(product.dtype)

    multiply(x, weights, store)


def own_kernel(static, own_block, sibling_block, own_f, *refs):
    sibling_f, refs = refs[:FACTOR_PIECES], refs[FACTOR_PIECES:]
    xs, weights = refs[: static[5]], refs[-1]
    outs = refs[len(refs) - 1 - static[6] : -1]
    features = own_block.shape[0]
    wide = outs[0].shape[1]
    down_rows = own_f.shape[1] - len(static[3]) * static[2]
    b = up_factor(static[:5], own_f[:, down_rows:], lax.axis_index("tensor"))
    for at, factors, block in ((0, [own_f], own_block), (features, sibling_f, sibling_block)):
        weights[at : at + features] = merge(static[0], block[...], factor_a(factors, down_rows), b)
    for h, x in enumerate(xs):

        def store(first, size, value):
            to = pl.ds(pl.multiple_of(h * x.shape[0] + first, 16), size)
            for k, out in enumerate(outs):
                out[to, :] = value[:, k * wide : (k + 1) * wide]

        multiply(x, weights, store)


def finish_kernel(sources, first, own, inv, *refs):
    total = own[pl.ds(first, refs[-1].shape[0]), :]
    for value in refs[:sources]:
        total = total + value[...].astype(jnp.float32)
    refs[-1][...] = (total * inv[:, :1]).astype(refs[-1].dtype)


def finish(own, inv_rms, received, at, shape, before):
    block = received[0].shape
    operands = [own, inv_rms] + received
    in_specs = in_vmem(len(operands))
    aliases = {}
    if before is not None:
        aliases = {len(operands): 0}
        in_specs += anywhere(1)
        operands.append(before)
    return pl.pallas_call(
        functools.partial(finish_kernel, len(received), at[0] * block[0]),
        grid=(1,),
        out_shape=jax.ShapeDtypeStruct(shape, jnp.bfloat16),
        in_specs=in_specs,
        out_specs=pl.BlockSpec(block, lambda i: at),
        input_output_aliases=aliases,
        compiler_params=params(),
    )(*operands)


def body(
    prompt_hidden_input,
    input_norm_gain,
    frozen_key_value,
    down_factor_matrix,
    down_moment_first,
    down_moment_second,
    up_factor_matrix,
    up_moment_first,
    up_moment_second,
    down_gradient,
    up_gradient,
):
    n_dp = lax.axis_size("dp")
    n_tensor = lax.axis_size("tensor")
    chips = n_tensor // CORES
    replica = lax.axis_index("dp")
    tokens, features = prompt_hidden_input.shape
    width, columns = frozen_key_value.shape
    rank = up_factor_matrix.shape[0]
    parts = down_factor_matrix.shape[1]
    factors = parts * rank
    strips = columns // LANES
    down_rows = features // n_dp
    up_rows = rank // n_dp
    packed_rows = down_rows + up_rows * strips
    steps = range(1, chips)
    f32, bf16 = jnp.float32, jnp.bfloat16

    def to_sibling(value):
        return lax.ppermute(value, "tensor", [(t, t ^ 1) for t in range(n_tensor)])

    def to_chip(value, step):
        pairs = [
            (CORES * q + k, CORES * ((q + step) % chips) + k)
            for q in range(chips)
            for k in range(CORES)
        ]
        return lax.ppermute(value, "tensor", pairs)

    def by_rank(value):
        return jnp.transpose(value, (1, 2, 0)).reshape(factors, features)

    down_sent = by_rank(down_gradient[0])
    down_state = [by_rank(v) for v in (down_factor_matrix, down_moment_first, down_moment_second)]
    up_state = [up_factor_matrix, up_moment_first, up_moment_second]
    shares = jax.ShapeDtypeStruct((n_dp, packed_rows, LANES), bf16)
    window = pl.cdiv(down_rows + LANES, LANES) * LANES
    aligned = features % LANES == 0 and window <= features
    aligned = aligned and up_rows % 8 == 0 and down_rows % 16 == 0
    window = window if aligned else down_rows
    windows = (
        jax.ShapeDtypeStruct((3, factors, window), f32),
        jax.ShapeDtypeStruct((3, up_rows, columns), f32),
    )

    turns = [1, 2] if n_dp % 4 == 0 else [1, 1]
    turn = [turns[strip % 2] for strip in range(strips)]
    halves = min(COLUMN_HALVES, strips)
    wide = columns // halves
    groups = [range(k * strips // halves, (k + 1) * strips // halves) for k in range(halves)]
    out_shape = (shares,) + windows * aligned
    out_shape += tuple(
        jax.ShapeDtypeStruct((len(group), features, LANES), bf16)
        for group in groups
        for _ in steps
    )
    state = (down_state + up_state) * aligned
    packed, *rest = pl.pallas_call(
        functools.partial(begin_kernel, chips, turn, aligned),
        out_shape=out_shape,
        in_specs=anywhere(3 + len(state)),
        out_specs=tuple(in_vmem(len(out_shape))),
        scratch_shapes=[
            pltpu.VMEM((factors, features), f32),
            pltpu.VMEM((rank, columns), f32),
            pltpu.SemaphoreType.DMA((2 + len(steps) * strips + len(state),)),
        ],
        compiler_params=pltpu.CompilerParams(vmem_limit_bytes=LARGE_VMEM_BYTES),
    )(down_sent, up_gradient[0], frozen_key_value, *state)
    exchanged = lax.all_to_all(packed, "dp", 0, 0, tiled=True)
    if aligned:
        down_win, up_win, *taken = rest
    else:
        taken = rest
        down_win = jnp.stack(
            [lax.dynamic_slice_in_dim(v, replica * down_rows, down_rows, 1) for v in down_state]
        )
        up_win = jnp.stack(
            [lax.dynamic_slice_in_dim(v, replica * up_rows, up_rows, 0) for v in up_state]
        )
    mine = []

    def send_half(half, after):
        blocks = taken[half * len(steps) : (half + 1) * len(steps)]
        if after is not None:
            blocks, _ = lax.optimization_barrier((blocks, after))
        mine.append([to_chip(value, step) for value, step in zip(blocks, steps)])

    send_half(0, None)

    gain = input_norm_gain[None, :]
    some = tokens // TOKEN_HALVES
    rows = LANES if some % LANES == 0 else some
    operands = [prompt_hidden_input, to_sibling(prompt_hidden_input), gain, to_sibling(gain)]

    def prepared(half, kernel, more, limit):
        token_block = pl.BlockSpec((rows, features), lambda i: (half * (some // rows) + i, 0))
        gain_block = pl.BlockSpec((1, features), lambda i: (0, 0))
        out_shape = (
            jax.ShapeDtypeStruct((some, CORES * features), bf16),
            jax.ShapeDtypeStruct((some // LANES, LANES), f32),
        )
        out_shape += (jax.ShapeDtypeStruct((some, wide), bf16),) * len(more)
        return pl.pallas_call(
            kernel,
            grid=(some // rows,),
            out_shape=out_shape,
            in_specs=[token_block, token_block, gain_block, gain_block] + in_vmem(len(more)),
            out_specs=tuple(in_vmem(len(out_shape))),
            scratch_shapes=[pltpu.VMEM((some, LANES), f32)],
            compiler_params=pltpu.CompilerParams(vmem_limit_bytes=limit),
        )(*operands, *more)

    x0, squares = prepared(0, prepare_kernel, [], PREPARE_VMEM_BYTES)
    exchanged, squares = lax.optimization_barrier((exchanged, squares))
    a_next, b_next, sent = pl.pallas_call(
        adam_kernel,
        out_shape=(
            jax.ShapeDtypeStruct((3, factors, down_rows), f32),
            jax.ShapeDtypeStruct((3, up_rows, columns), f32),
            shares,
        ),
        in_specs=anywhere(3),
        out_specs=tuple(in_vmem(3)),
        scratch_shapes=[
            pltpu.VMEM((n_dp, packed_rows, LANES), bf16),
            pltpu.VMEM((3, factors, window), f32),
            pltpu.VMEM((3, up_rows, columns), f32),
            pltpu.SemaphoreType.DMA((3,)),
        ],
        compiler_params=pltpu.CompilerParams(vmem_limit_bytes=LARGE_VMEM_BYTES),
    )(exchanged, down_win, up_win)
    own_f = lax.all_to_all(sent, "dp", 0, 0, tiled=True)
    for half in range(1, halves):
        send_half(half, (mine[-1], sent))
    a_next = jnp.transpose(a_next.reshape(3, parts, rank, down_rows), (0, 3, 1, 2))

    outside = [[] for _ in range(strips)]

    def swap_half(half, after):
        for value in mine[half]:
            value, _ = lax.optimization_barrier((value, after))
            split = pl.pallas_call(
                split_kernel,
                out_shape=(jax.ShapeDtypeStruct((features, LANES), bf16),) * len(groups[half]),
                in_specs=in_vmem(1),
                out_specs=tuple(in_vmem(len(groups[half]))),
                compiler_params=params(),
            )(value)
            for piece, strip in zip(split, groups[half]):
                pairs = [(i, i ^ turn[strip]) for i in range(n_dp)]
                outside[strip].append((piece, lax.ppermute(piece, "dp", pairs)))

    swap_half(0, sent)
    up_packed = packed_rows - down_rows
    more = pl.cdiv(3 * (tokens // TOKEN_HALVES // LANES), up_packed)
    piece = jax.ShapeDtypeStruct((n_dp // FACTOR_PIECES, packed_rows, LANES), bf16)
    message, *pieces = pl.pallas_call(
        message_kernel,
        out_shape=(jax.ShapeDtypeStruct((n_dp + more, up_packed, LANES), bf16),)
        + (piece,) * FACTOR_PIECES,
        in_specs=anywhere(1) + in_vmem(1),
        out_specs=tuple(in_vmem(1 + FACTOR_PIECES)),
        scratch_shapes=[pltpu.SemaphoreType.DMA((1 + FACTOR_PIECES,))],
        compiler_params=params(),
    )(own_f, squares)
    messages = [to_chip(message, step) for step in steps]
    sibling_f = [to_sibling(piece) for piece in pieces]

    def inverse(shares, *sums):
        return pl.pallas_call(
            functools.partial(inverse_kernel, width, shares),
            out_shape=jax.ShapeDtypeStruct((some, LANES), f32),
            in_specs=in_vmem(chips),
            out_specs=in_vmem(1)[0],
            compiler_params=params(),
        )(*sums)

    inv_rms = [inverse(n_dp, squares, *messages)]

    scale = 0.5 / math.sqrt(width * rank)

    received = {}
    after = []
    x1 = None
    weights_shape = jax.ShapeDtypeStruct((CORES * features, wide), bf16)
    product_shape = jax.ShapeDtypeStruct((some, wide), bf16)
    for half, group in enumerate(groups):
        static = (scale, parts, up_rows, group, columns)
        if half > 0:
            swap_half(half, products[0])
        for step in steps:
            blocks = [value for strip in group for value in outside[strip][step - 1]]
            weights, product = pl.pallas_call(
                functools.partial(outside_kernel, static, chips, step, turn),
                out_shape=(weights_shape, product_shape),
                in_specs=in_vmem(3 + FACTOR_PIECES + len(blocks)) + anywhere(len(after)),
                out_specs=tuple(in_vmem(2)),
                compiler_params=params(),
            )(own_f, messages[step - 1], x0, *sibling_f, *blocks, *after)
            received.setdefault((0, half), []).append(to_chip(product, chips - step))
            if x1 is None:
                x1, sums, second = prepared(1, prepare_multiply_kernel, [weights], VMEM_BYTES)
            else:
                second = pl.pallas_call(
                    more_kernel,
                    out_shape=product_shape,
                    in_specs=in_vmem(2),
                    out_specs=in_vmem(1)[0],
                    compiler_params=params(),
                )(x1, weights)
            products = [product, second]
            after = [second]
            received.setdefault((1, half), []).append(to_chip(second, chips - step))
        if half == 0:
            after = [received[0, 0][0]]
            sent_sums, _ = lax.optimization_barrier((sums, products))
            inv_rms.append(inverse(0, sums, *[to_chip(sent_sums, step) for step in steps]))

    after.append(received[1, 0][0])
    static = (scale, parts, up_rows, range(strips), columns, TOKEN_HALVES, halves)
    totals = pl.pallas_call(
        functools.partial(own_kernel, static),
        out_shape=(jax.ShapeDtypeStruct((tokens, wide), f32),) * halves,
        grid=(1,),
        in_specs=[
            pl.BlockSpec((features, columns), lambda i: (lax.axis_index("tensor"), 0)),
            pl.BlockSpec((features, columns), lambda i: (lax.axis_index("tensor") ^ 1, 0)),
        ]
        + in_vmem(1 + FACTOR_PIECES + TOKEN_HALVES)
        + anywhere(len(after)),
        out_specs=tuple(in_vmem(halves)),
        scratch_shapes=[pltpu.VMEM((CORES * features, columns), bf16)],
        compiler_params=params(),
        cost_estimate=pl.CostEstimate(
            flops=2 * tokens * CORES * features * columns,
            bytes_accessed=4 * tokens * features,
            transcendentals=0,
        ),
    )(frozen_key_value, frozen_key_value, own_f, *sibling_f, x0, x1, *after)

    keys_values = None
    for at, pieces in received.items():
        keys_values = finish(
            totals[at[1]], inv_rms[at[0]], pieces, at, (tokens, columns), keys_values
        )
    return (a_next, b_next, keys_values)


def solution(mesh):
    placed = (
        P("dp", "tensor"),
        P("tensor"),
        P(None, "tensor"),
        P("tensor", None, None),
        P("tensor", None, None),
        P("tensor", None, None),
        P(None, "tensor"),
        P(None, "tensor"),
        P(None, "tensor"),
        P("dp", "tensor", None, None),
        P("dp", None, "tensor"),
    )
    return jax.shard_map(
        body,
        mesh=mesh,
        in_specs=placed,
        out_specs=(
            P(None, ("tensor", "dp"), None, None),
            P(None, "dp", "tensor"),
            P("dp", "tensor"),
        ),
        check_vma=False,
    )
```

```python
import functools
import math

import jax
import jax.numpy as jnp
from jax import lax
from jax.experimental import pallas as pl
from jax.experimental.pallas import tpu as pltpu
from jax.sharding import PartitionSpec as P

KEY_VALUE_WIDTH = 1024
STEP = 100
CORES = 2
LANES = 128
COLUMN_HALVES = 2
TOKEN_HALVES = 2
FACTOR_PIECES = 2
VMEM_BYTES = 16 * 2**20
LARGE_VMEM_BYTES = 58 * 2**20
PREPARE_VMEM_BYTES = 40 * 2**20


def adaptive_moment_update(param, first, second, grad_mean):
    first_new = 0.9 * first + 0.1 * grad_mean
    second_new = 0.999 * second + 0.001 * grad_mean * grad_mean
    step_size = first_new / (1.0 - 0.9**STEP) / (jnp.sqrt(second_new / (1.0 - 0.999**STEP)) + 1e-08)
    return (param - 0.1 * step_size, first_new, second_new)


def in_vmem(count):
    return [pl.BlockSpec(memory_space=pltpu.VMEM)] * count


def anywhere(count):
    return [pl.BlockSpec(memory_space=pl.ANY)] * count


SCALARS = pl.BlockSpec(memory_space=pltpu.SMEM)


def params(**more):
    return pltpu.CompilerParams(vmem_limit_bytes=VMEM_BYTES, **more)


def pack(down, up, out_ref):
    shares = out_ref.shape[0]
    down = down.T
    down_rows, up_rows = down.shape[0] // shares, up.shape[0] // shares
    for i in range(shares):
        pieces = [down[i * down_rows : (i + 1) * down_rows]]
        for k in range(up.shape[1] // LANES):
            pieces.append(up[i * up_rows : (i + 1) * up_rows, k * LANES : (k + 1) * LANES])
        out_ref[i] = jnp.concatenate(pieces, axis=0).astype(jnp.bfloat16)


def first_lane(share, window, size):
    return jnp.minimum(share // LANES * LANES, size - window)


def begin_kernel(chips, turn, aligned, *refs):
    down_ref, up_ref, weights_ref = refs[:3]
    state, refs = refs[3 : 3 + 6 * aligned], refs[3 + 6 * aligned :]
    packed, refs = refs[0], refs[1:]
    windows, refs = refs[: 2 * aligned], refs[2 * aligned :]
    outs, (down, up, sem) = refs[:-3], refs[-3:]
    features = outs[0].shape[1]
    place, replica = lax.axis_index("tensor"), lax.axis_index("dp")
    chip, core = place // CORES, place % CORES
    copies = []

    def add(source, target):
        copies.append(pltpu.make_async_copy(source, target, sem.at[len(copies)]))
        copies[-1].start()

    add(down_ref, down)
    add(up_ref, up)
    for i, out in enumerate(outs):
        step, first = 1 + i % (chips - 1), i // (chips - 1) * out.shape[0]
        for k in range(out.shape[0]):
            half = (core + replica // turn[first + k]) % 2
            row = ((chip + step) % chips * CORES + half) * features
            add(
                weights_ref.at[
                    pl.ds(pl.multiple_of(row, features), features),
                    pl.ds((first + k) * LANES, LANES),
                ],
                out.at[k],
            )
    if aligned:
        down_win, up_win = windows
        window, up_rows = down_win.shape[2], up_win.shape[1]
        share = replica * (features // packed.shape[0])
        lane = pl.multiple_of(first_lane(share, window, features), LANES)
        row = pl.multiple_of(replica * up_rows, up_rows)
        for i in range(3):
            add(state[i].at[:, pl.ds(lane, window)], down_win.at[i])
            add(state[3 + i].at[pl.ds(row, up_rows)], up_win.at[i])
    copies[0].wait()
    copies[1].wait()
    pack(down[...], up[...], packed)
    for copy in copies[2:]:
        copy.wait()


def split_kernel(in_ref, *outs):
    for k, out in enumerate(outs):
        out[...] = in_ref[k]


def prepare_kernel(own_ref, sibling_ref, own_gain, sibling_gain, *refs):
    before, (x_ref, sums_ref, squares) = refs[:-3], refs[-3:]
    block, features = own_ref.shape
    step = pl.program_id(0)
    first = 0 if x_ref.shape[0] == block else step * block
    tile = 16 if block % 16 == 0 else block

    @pl.loop(0, block // tile, unroll=2)
    def _(i):
        at = pl.ds(pl.multiple_of(i * tile, tile), tile)
        to = pl.ds(pl.multiple_of(first + i * tile, tile), tile)
        own = own_ref[at, :].astype(jnp.float32)
        x_ref[to, :features] = (own * own_gain[...]).astype(x_ref.dtype)
        total = own * own
        sibling = sibling_ref[at, :].astype(jnp.float32)
        x_ref[to, features:] = (sibling * sibling_gain[...]).astype(x_ref.dtype)
        total += sibling * sibling
        total = jnp.sum(total, axis=1, keepdims=True)
        to = pl.ds(pl.multiple_of(step * block + i * tile, tile), tile)
        squares[to, :] = jnp.broadcast_to(total, (tile, LANES))

    @pl.when(step == pl.num_programs(0) - 1)
    def _():
        done = 0
        for ref in before:
            sums_ref[: ref.shape[0]] = ref[...]
            done = ref.shape[0]
        for i in range(squares.shape[0] // LANES):
            row = squares[i * LANES : (i + 1) * LANES, :].T[:1]
            sums_ref[done + i : done + i + 1] = row


def message_kernel(factor_ref, sums_ref, out_ref, *refs):
    pieces, sem = refs[:-1], refs[-1]
    shares, up_rows = factor_ref.shape[0], out_ref.shape[1]
    copies = [
        pltpu.make_async_copy(
            factor_ref.at[:, pl.ds(factor_ref.shape[1] - up_rows, up_rows)],
            out_ref.at[pl.ds(0, shares)],
            sem.at[0],
        )
    ]
    for k, piece in enumerate(pieces):
        size = piece.shape[0]
        copies.append(
            pltpu.make_async_copy(factor_ref.at[pl.ds(k * size, size)], piece, sem.at[1 + k])
        )
    for copy in copies:
        copy.start()
    left = sums_ref[...]
    terms = []
    for _ in range(3):
        terms.append(left.astype(jnp.bfloat16).astype(jnp.float32))
        left = left - terms[-1]
    rest = (out_ref.shape[0] - shares) * up_rows - 3 * left.shape[0]
    if rest > 0:
        terms.append(jnp.zeros((rest, LANES), jnp.float32))
    rows = jnp.concatenate(terms, axis=0)
    for i in range(out_ref.shape[0] - shares):
        out_ref[shares + i] = rows[i * up_rows : (i + 1) * up_rows].astype(jnp.bfloat16)
    for copy in copies:
        copy.wait()


def inverse_kernel(width, shares, sums_ref, *refs):
    messages, out = refs[:-1], refs[-1]
    total = sums_ref[...]
    count = total.shape[0]
    for ref in messages:
        rows = [ref[i].astype(jnp.float32) for i in range(shares, ref.shape[0])]
        rows = jnp.concatenate(rows, axis=0)
        total += rows[:count] + rows[count : 2 * count] + rows[2 * count : 3 * count]
    inverse = lax.rsqrt(total / width + 1e-06)
    for i in range(count):
        out[i * LANES : (i + 1) * LANES, :] = jnp.broadcast_to(
            inverse[i : i + 1], (LANES, LANES)
        ).T


def update(total, down, up, a_ref, b_ref):
    down_rows = a_ref.shape[2]
    up_rows, columns = b_ref.shape[1:]
    strips = columns // LANES
    down_mean = total[:down_rows].T
    up_mean = jnp.concatenate(
        [total[down_rows + k * up_rows : down_rows + (k + 1) * up_rows] for k in range(strips)],
        axis=1,
    )
    p, m, v = adaptive_moment_update(*down(), down_mean)
    a_ref[0], a_ref[1], a_ref[2] = p, m, v
    pieces = [p.T]
    p, m, v = adaptive_moment_update(*up(), up_mean)
    b_ref[0], b_ref[1], b_ref[2] = p, m, v
    pieces += [p[:, k * LANES : (k + 1) * LANES] for k in range(strips)]
    return jnp.concatenate(pieces, axis=0).astype(jnp.bfloat16)


def adam_kernel(grad_in, down_in, up_in, a_ref, b_ref, factor_ref, grad_ref, down_win, up_win, sem):
    copies = [
        pltpu.make_async_copy(source, target, sem.at[i])
        for i, (source, target) in enumerate(
            ((grad_in, grad_ref), (down_in, down_win), (up_in, up_win))
        )
    ]
    for copy in copies:
        copy.start()
    for copy in copies:
        copy.wait()
    replicas = grad_ref.shape[0]
    down_rows, window = a_ref.shape[2], down_win.shape[2]
    total = jnp.sum(grad_ref[...].astype(jnp.float32), axis=0) / replicas

    def down():
        if window == down_rows:
            return [down_win[i] for i in range(3)]
        share = lax.axis_index("dp") * down_rows
        shift = window - (share - first_lane(share, window, down_rows * replicas))
        return [pltpu.roll(down_win[i], shift, 1)[:, :down_rows] for i in range(3)]

    rounded = update(total, down, lambda: [up_win[i] for i in range(3)], a_ref, b_ref)
    for i in range(replicas):
        factor_ref[i] = rounded


def factor_a(refs, down_rows):
    pieces = []
    for ref in refs:
        pieces += [ref[i].astype(jnp.float32)[:down_rows] for i in range(ref.shape[0])]
    return jnp.concatenate(pieces, axis=0).astype(jnp.bfloat16)


def factor_b(packed, part, parts, strip, up_rows):
    pieces = [
        packed[i].astype(jnp.float32)[strip * up_rows : (strip + 1) * up_rows]
        for i in range(packed.shape[0])
    ]
    value = jnp.concatenate(pieces, axis=0)
    rows = [jnp.where(part == j, value, jnp.zeros_like(value)) for j in range(parts)]
    return jnp.concatenate(rows, axis=0).astype(jnp.bfloat16)


def merge(scale, block, a, b):
    change = jnp.dot(a, b, preferred_element_type=jnp.float32)
    return (block.astype(jnp.float32) + scale * change).astype(jnp.bfloat16)


def multiply(x, weights, store):
    rows = x.shape[0]
    tile = rows // 2 if rows % 32 == 0 else rows

    @pl.loop(0, rows // tile)
    def _(i):
        at = pl.ds(pl.multiple_of(i * tile, tile), tile)
        store(i * tile, tile, jnp.dot(x[at, :], weights[...], preferred_element_type=jnp.float32))


def up_factor(static, packed, owner):
    _, parts, up_rows, strips, columns = static
    part = owner * columns // KEY_VALUE_WIDTH
    return jnp.concatenate(
        [factor_b(packed, part, parts, strip, up_rows) for strip in strips], axis=1
    )


def outside_kernel(static, chips, step, turn, b_ref, x, *refs):
    own_f, sibling_f = refs[:FACTOR_PIECES], refs[FACTOR_PIECES : 2 * FACTOR_PIECES]
    blocks, (weights, product) = refs[2 * FACTOR_PIECES :], refs[-2:]
    strips = static[3]
    features = blocks[0].shape[0]
    down_rows = own_f[0].shape[1] - b_ref.shape[1]
    shares = FACTOR_PIECES * own_f[0].shape[0]
    place, replica = lax.axis_index("tensor"), lax.axis_index("dp")
    owner = (place // CORES - step + chips) % chips * CORES + place % CORES
    b = up_factor(static, b_ref[:shares], owner)
    own_a, sibling_a = factor_a(own_f, down_rows), factor_a(sibling_f, down_rows)
    for k, strip in enumerate(strips):
        mine, other = blocks[2 * k : 2 * k + 2]
        even = replica // turn[strip] % 2 == 0
        lanes = slice(k * LANES, (k + 1) * LANES)
        block = jnp.where(even, mine[...], other[...])
        weights[:features, lanes] = merge(static[0], block, own_a, b[:, lanes])
        block = jnp.where(even, other[...], mine[...])
        weights[features:, lanes] = merge(static[0], block, sibling_a, b[:, lanes])
    more_kernel(x, weights, product)


def more_kernel(x, weights, product):
    def store(first, size, value):
        product[pl.ds(first, size), :] = value.astype(product.dtype)

    multiply(x, weights, store)


def own_kernel(static, own_block, sibling_block, *refs):
    own_f, sibling_f = refs[:FACTOR_PIECES], refs[FACTOR_PIECES : 2 * FACTOR_PIECES]
    refs = refs[2 * FACTOR_PIECES :]
    xs, weights = refs[: static[5]], refs[-1]
    outs = refs[len(refs) - 1 - static[6] : -1]
    features = own_block.shape[0]
    wide = outs[0].shape[1]
    down_rows = own_f[0].shape[1] - len(static[3]) * static[2]
    b = jnp.concatenate([piece[:, down_rows:] for piece in own_f], axis=0)
    b = up_factor(static[:5], b, lax.axis_index("tensor"))
    for at, factors, block in ((0, own_f, own_block), (features, sibling_f, sibling_block)):
        weights[at : at + features] = merge(static[0], block[...], factor_a(factors, down_rows), b)
    for h, x in enumerate(xs):

        def store(first, size, value):
            to = pl.ds(pl.multiple_of(h * x.shape[0] + first, 16), size)
            for k, out in enumerate(outs):
                out[to, :] = value[:, k * wide : (k + 1) * wide]

        multiply(x, weights, store)


def finish_kernel(sources, first, own, inv, *refs):
    rows = pl.ds(first, refs[-1].shape[0])
    total = own[rows, :]
    for value in refs[:sources]:
        total = total + value[...].astype(jnp.float32)
    refs[-1][...] = (total * inv[rows, :1]).astype(refs[-1].dtype)


def finish(own, inv_rms, received, at, shape, before):
    block = received[0].shape
    operands = [own, inv_rms] + received
    in_specs = in_vmem(len(operands))
    aliases = {}
    if before is not None:
        aliases = {len(operands): 0}
        in_specs += anywhere(1)
        operands.append(before)
    return pl.pallas_call(
        functools.partial(finish_kernel, len(received), at[0] * block[0]),
        grid=(1,),
        out_shape=jax.ShapeDtypeStruct(shape, jnp.bfloat16),
        in_specs=in_specs,
        out_specs=pl.BlockSpec(block, lambda i: at),
        input_output_aliases=aliases,
        compiler_params=params(),
    )(*operands)


def body(
    prompt_hidden_input,
    input_norm_gain,
    frozen_key_value,
    down_factor_matrix,
    down_moment_first,
    down_moment_second,
    up_factor_matrix,
    up_moment_first,
    up_moment_second,
    down_gradient,
    up_gradient,
):
    n_dp = lax.axis_size("dp")
    n_tensor = lax.axis_size("tensor")
    chips = n_tensor // CORES
    replica = lax.axis_index("dp")
    tokens, features = prompt_hidden_input.shape
    width, columns = frozen_key_value.shape
    rank = up_factor_matrix.shape[0]
    parts = down_factor_matrix.shape[1]
    factors = parts * rank
    strips = columns // LANES
    down_rows = features // n_dp
    up_rows = rank // n_dp
    packed_rows = down_rows + up_rows * strips
    steps = range(1, chips)
    f32, bf16 = jnp.float32, jnp.bfloat16

    def to_sibling(value):
        return lax.ppermute(value, "tensor", [(t, t ^ 1) for t in range(n_tensor)])

    def to_chip(value, step):
        pairs = [
            (CORES * q + k, CORES * ((q + step) % chips) + k)
            for q in range(chips)
            for k in range(CORES)
        ]
        return lax.ppermute(value, "tensor", pairs)

    def by_rank(value):
        return jnp.transpose(value, (1, 2, 0)).reshape(factors, features)

    down_sent = by_rank(down_gradient[0])
    down_state = [by_rank(v) for v in (down_factor_matrix, down_moment_first, down_moment_second)]
    up_state = [up_factor_matrix, up_moment_first, up_moment_second]
    shares = jax.ShapeDtypeStruct((n_dp, packed_rows, LANES), bf16)
    window = pl.cdiv(down_rows + LANES, LANES) * LANES
    aligned = features % LANES == 0 and window <= features
    aligned = aligned and up_rows % 8 == 0 and down_rows % 16 == 0
    window = window if aligned else down_rows
    windows = (
        jax.ShapeDtypeStruct((3, factors, window), f32),
        jax.ShapeDtypeStruct((3, up_rows, columns), f32),
    )

    turns = [1, 2] if n_dp % 4 == 0 else [1, 1]
    turn = [turns[strip % 2] for strip in range(strips)]
    halves = min(COLUMN_HALVES, strips)
    wide = columns // halves
    groups = [range(k * strips // halves, (k + 1) * strips // halves) for k in range(halves)]
    out_shape = (shares,) + windows * aligned
    out_shape += tuple(
        jax.ShapeDtypeStruct((len(group), features, LANES), bf16)
        for group in groups
        for _ in steps
    )
    state = (down_state + up_state) * aligned
    packed, *rest = pl.pallas_call(
        functools.partial(begin_kernel, chips, turn, aligned),
        out_shape=out_shape,
        in_specs=anywhere(3 + len(state)),
        out_specs=tuple(in_vmem(len(out_shape))),
        scratch_shapes=[
            pltpu.VMEM((factors, features), f32),
            pltpu.VMEM((rank, columns), f32),
            pltpu.SemaphoreType.DMA((2 + len(steps) * strips + len(state),)),
        ],
        compiler_params=pltpu.CompilerParams(vmem_limit_bytes=LARGE_VMEM_BYTES),
    )(down_sent, up_gradient[0], frozen_key_value, *state)
    exchanged = lax.all_to_all(packed, "dp", 0, 0, tiled=True)
    if aligned:
        down_win, up_win, *taken = rest
    else:
        taken = rest
        down_win = jnp.stack(
            [lax.dynamic_slice_in_dim(v, replica * down_rows, down_rows, 1) for v in down_state]
        )
        up_win = jnp.stack(
            [lax.dynamic_slice_in_dim(v, replica * up_rows, up_rows, 0) for v in up_state]
        )
    mine = []

    def send_half(half, after):
        blocks = taken[half * len(steps) : (half + 1) * len(steps)]
        if after is not None:
            blocks, _ = lax.optimization_barrier((blocks, after))
        mine.append([to_chip(value, step) for value, step in zip(blocks, steps)])

    send_half(0, None)

    gain = input_norm_gain[None, :]
    some = tokens // TOKEN_HALVES
    rows = LANES if some % LANES == 0 else some
    operands = [prompt_hidden_input, to_sibling(prompt_hidden_input), gain, to_sibling(gain)]

    def prepared(half, before, in_place, limit):
        token_block = pl.BlockSpec((rows, features), lambda i: (half * (some // rows) + i, 0))
        gain_block = pl.BlockSpec((1, features), lambda i: (0, 0))
        x_block = pl.BlockSpec((rows, CORES * features), lambda i: (i, 0))
        return pl.pallas_call(
            prepare_kernel,
            grid=(some // rows,),
            out_shape=(
                jax.ShapeDtypeStruct((some, CORES * features), bf16),
                jax.ShapeDtypeStruct(((half + 1) * some // LANES, LANES), f32),
            ),
            in_specs=[token_block, token_block, gain_block, gain_block] + in_vmem(len(before)),
            out_specs=(in_vmem(1)[0] if in_place else x_block, in_vmem(1)[0]),
            scratch_shapes=[pltpu.VMEM((some, LANES), f32)],
            compiler_params=pltpu.CompilerParams(vmem_limit_bytes=limit),
        )(*operands, *before)

    x0, squares = prepared(0, [], True, PREPARE_VMEM_BYTES)
    exchanged, squares = lax.optimization_barrier((exchanged, squares))
    x1, squares = prepared(1, [squares], False, LARGE_VMEM_BYTES)
    a_next, b_next, sent = pl.pallas_call(
        adam_kernel,
        out_shape=(
            jax.ShapeDtypeStruct((3, factors, down_rows), f32),
            jax.ShapeDtypeStruct((3, up_rows, columns), f32),
            shares,
        ),
        in_specs=anywhere(3),
        out_specs=tuple(in_vmem(3)),
        scratch_shapes=[
            pltpu.VMEM((n_dp, packed_rows, LANES), bf16),
            pltpu.VMEM((3, factors, window), f32),
            pltpu.VMEM((3, up_rows, columns), f32),
            pltpu.SemaphoreType.DMA((3,)),
        ],
        compiler_params=pltpu.CompilerParams(vmem_limit_bytes=LARGE_VMEM_BYTES),
    )(exchanged, down_win, up_win)
    own_f = lax.all_to_all(sent, "dp", 0, 0, tiled=True)
    for half in range(1, halves):
        send_half(half, (mine[-1], sent))
    a_next = jnp.transpose(a_next.reshape(3, parts, rank, down_rows), (0, 3, 1, 2))

    outside = [[] for _ in range(strips)]

    def swap_half(half, after):
        for value in mine[half]:
            value, _ = lax.optimization_barrier((value, after))
            split = pl.pallas_call(
                split_kernel,
                out_shape=(jax.ShapeDtypeStruct((features, LANES), bf16),) * len(groups[half]),
                in_specs=in_vmem(1),
                out_specs=tuple(in_vmem(len(groups[half]))),
                compiler_params=params(),
            )(value)
            for piece, strip in zip(split, groups[half]):
                pairs = [(i, i ^ turn[strip]) for i in range(n_dp)]
                outside[strip].append((piece, lax.ppermute(piece, "dp", pairs)))

    swap_half(0, sent)
    own_f, squares = lax.optimization_barrier((own_f, squares))
    up_packed = packed_rows - down_rows
    more = pl.cdiv(3 * (tokens // LANES), up_packed)
    piece = jax.ShapeDtypeStruct((n_dp // FACTOR_PIECES, packed_rows, LANES), bf16)
    message, *pieces = pl.pallas_call(
        message_kernel,
        out_shape=(jax.ShapeDtypeStruct((n_dp + more, up_packed, LANES), bf16),)
        + (piece,) * FACTOR_PIECES,
        in_specs=anywhere(1) + in_vmem(1),
        out_specs=tuple(in_vmem(1 + FACTOR_PIECES)),
        scratch_shapes=[pltpu.SemaphoreType.DMA((1 + FACTOR_PIECES,))],
        compiler_params=params(),
    )(own_f, squares)
    messages = [to_chip(message, step) for step in steps]
    sibling_f = [to_sibling(piece) for piece in pieces]

    inv_rms = pl.pallas_call(
        functools.partial(inverse_kernel, width, n_dp),
        out_shape=jax.ShapeDtypeStruct((tokens, LANES), f32),
        in_specs=in_vmem(chips),
        out_specs=in_vmem(1)[0],
        compiler_params=params(),
    )(squares, *messages)

    scale = 0.5 / math.sqrt(width * rank)

    received = {}
    after = []
    weights_shape = jax.ShapeDtypeStruct((CORES * features, wide), bf16)
    product_shape = jax.ShapeDtypeStruct((some, wide), bf16)
    for half, group in enumerate(groups):
        static = (scale, parts, up_rows, group, columns)
        if half > 0:
            swap_half(half, products[0])
        for step in steps:
            blocks = [value for strip in group for value in outside[strip][step - 1]]
            weights, product = pl.pallas_call(
                functools.partial(outside_kernel, static, chips, step, turn),
                out_shape=(weights_shape, product_shape),
                in_specs=in_vmem(2 + 2 * FACTOR_PIECES + len(blocks)) + anywhere(len(after)),
                out_specs=tuple(in_vmem(2)),
                compiler_params=params(),
            )(messages[step - 1], x0, *pieces, *sibling_f, *blocks, *after)
            received.setdefault((0, half), []).append(to_chip(product, chips - step))
            second = pl.pallas_call(
                more_kernel,
                out_shape=product_shape,
                in_specs=in_vmem(2),
                out_specs=in_vmem(1)[0],
                compiler_params=params(),
            )(x1, weights)
            products = [product, second]
            after = [second]
            received.setdefault((1, half), []).append(to_chip(second, chips - step))
        if half == 0:
            after = [received[0, 0][0]]

    after.append(received[1, 0][0])
    static = (scale, parts, up_rows, range(strips), columns, TOKEN_HALVES, halves)
    totals = pl.pallas_call(
        functools.partial(own_kernel, static),
        out_shape=(jax.ShapeDtypeStruct((tokens, wide), f32),) * halves,
        grid=(1,),
        in_specs=[
            pl.BlockSpec((features, columns), lambda i: (lax.axis_index("tensor"), 0)),
            pl.BlockSpec((features, columns), lambda i: (lax.axis_index("tensor") ^ 1, 0)),
        ]
        + in_vmem(2 * FACTOR_PIECES + TOKEN_HALVES)
        + anywhere(len(after)),
        out_specs=tuple(in_vmem(halves)),
        scratch_shapes=[pltpu.VMEM((CORES * features, columns), bf16)],
        compiler_params=params(),
        cost_estimate=pl.CostEstimate(
            flops=2 * tokens * CORES * features * columns,
            bytes_accessed=4 * tokens * features,
            transcendentals=0,
        ),
    )(frozen_key_value, frozen_key_value, *pieces, *sibling_f, x0, x1, *after)

    keys_values = None
    for at, values in received.items():
        keys_values = finish(
            totals[at[1]], inv_rms, values, at, (tokens, columns), keys_values
        )
    return (a_next, b_next, keys_values)


def solution(mesh):
    placed = (
        P("dp", "tensor"),
        P("tensor"),
        P(None, "tensor"),
        P("tensor", None, None),
        P("tensor", None, None),
        P("tensor", None, None),
        P(None, "tensor"),
        P(None, "tensor"),
        P(None, "tensor"),
        P("dp", "tensor", None, None),
        P("dp", None, "tensor"),
    )
    return jax.shard_map(
        body,
        mesh=mesh,
        in_specs=placed,
        out_specs=(
            P(None, ("tensor", "dp"), None, None),
            P(None, "dp", "tensor"),
            P("dp", "tensor"),
        ),
        check_vma=False,
    )
```

```python
import functools
import math

import jax
import jax.numpy as jnp
from jax import lax
from jax.experimental import pallas as pl
from jax.experimental.pallas import tpu as pltpu
from jax.sharding import PartitionSpec as P

KEY_VALUE_WIDTH = 1024
STEP = 100
CORES = 2
LANES = 128
COLUMN_HALVES = 2
TOKEN_HALVES = 2
FACTOR_PIECES = 2
VMEM_BYTES = 16 * 2**20
LARGE_VMEM_BYTES = 58 * 2**20
PREPARE_VMEM_BYTES = 40 * 2**20


def adaptive_moment_update(param, first, second, grad_mean):
    first_new = 0.9 * first + 0.1 * grad_mean
    second_new = 0.999 * second + 0.001 * grad_mean * grad_mean
    step_size = first_new / (1.0 - 0.9**STEP) / (jnp.sqrt(second_new / (1.0 - 0.999**STEP)) + 1e-08)
    return (param - 0.1 * step_size, first_new, second_new)


def in_vmem(count):
    return [pl.BlockSpec(memory_space=pltpu.VMEM)] * count


def anywhere(count):
    return [pl.BlockSpec(memory_space=pl.ANY)] * count


SCALARS = pl.BlockSpec(memory_space=pltpu.SMEM)


def params(**more):
    return pltpu.CompilerParams(vmem_limit_bytes=VMEM_BYTES, **more)


def pack(down, up, out_ref, ready):
    shares = out_ref.shape[0]
    down = down.T
    down_rows, up_rows = down.shape[0] // shares, up.shape[0] // shares
    for i in range(shares):
        pieces = [down[i * down_rows : (i + 1) * down_rows]]
        for k in range(up.shape[1] // LANES):
            pieces.append(up[i * up_rows : (i + 1) * up_rows, k * LANES : (k + 1) * LANES])
        out_ref[i] = jnp.concatenate(pieces, axis=0).astype(jnp.bfloat16)
        ready(i)


def first_lane(share, window, size):
    return jnp.minimum(share // LANES * LANES, size - window)


def begin_kernel(chips, turn, down_ref, up_ref, weights_ref, packed, *refs):
    outs, (down, up, blocks, strips, sem, sem_out) = refs[:-6], refs[-6:]
    features = strips.shape[1]
    place, replica = lax.axis_index("tensor"), lax.axis_index("dp")
    chip, core = place // CORES, place % CORES
    copies, back = [], []

    def add(source, target):
        copies.append(pltpu.make_async_copy(source, target, sem.at[len(copies)]))
        copies[-1].start()

    def add_back(source, target):
        back.append(pltpu.make_async_copy(source, target, sem_out.at[len(back)]))
        back[-1].start()

    add(down_ref, down)
    add(up_ref, up)
    targets = []
    for i, out in enumerate(outs):
        step, first = 1 + i % (chips - 1), i // (chips - 1) * out.shape[0]
        for k in range(out.shape[0]):
            half = (core + replica // turn[first + k]) % 2
            row = ((chip + step) % chips * CORES + half) * features
            add(
                weights_ref.at[
                    pl.ds(pl.multiple_of(row, features), features),
                    pl.ds((first + k) * LANES, LANES),
                ],
                strips.at[len(targets)],
            )
            targets.append(out.at[k])
    copies[0].wait()
    copies[1].wait()
    pack(down[...], up[...], blocks, lambda i: add_back(blocks.at[i], packed.at[i]))
    for i, target in enumerate(targets):
        copies[2 + i].wait()
        add_back(strips.at[i], target)
    for copy in back:
        copy.wait()


def split_kernel(in_ref, *outs):
    for k, out in enumerate(outs):
        out[...] = in_ref[k]


def prepare_kernel(own_ref, sibling_ref, own_gain, sibling_gain, *refs):
    block, features = own_ref.shape
    step = pl.program_id(0)
    sums_ref, squares = refs[-2:]
    sibling_x = refs[-3]
    if sibling_x.shape[1] == features:
        before, own_x, lane = refs[:-4], refs[-4], 0
    else:
        before, own_x, lane = refs[:-3], sibling_x, features
    first = 0 if refs[-3].shape[0] == block else step * block
    tile = 16 if block % 16 == 0 else block

    @pl.loop(0, block // tile, unroll=2)
    def _(i):
        at = pl.ds(pl.multiple_of(i * tile, tile), tile)
        to = pl.ds(pl.multiple_of(first + i * tile, tile), tile)
        own = own_ref[at, :].astype(jnp.float32)
        own_x[to, :features] = (own * own_gain[...]).astype(own_x.dtype)
        total = own * own
        sibling = sibling_ref[at, :].astype(jnp.float32)
        scaled = (sibling * sibling_gain[...]).astype(sibling_x.dtype)
        sibling_x[to, lane : lane + features] = scaled
        total += sibling * sibling
        total = jnp.sum(total, axis=1, keepdims=True)
        to = pl.ds(pl.multiple_of(step * block + i * tile, tile), tile)
        squares[to, :] = jnp.broadcast_to(total, (tile, LANES))

    @pl.when(step == pl.num_programs(0) - 1)
    def _():
        done = 0
        for ref in before:
            sums_ref[: ref.shape[0]] = ref[...]
            done = ref.shape[0]
        for i in range(squares.shape[0] // LANES):
            row = squares[i * LANES : (i + 1) * LANES, :].T[:1]
            sums_ref[done + i : done + i + 1] = row


def message_kernel(factor_ref, sums_ref, out_ref, *refs):
    pieces, (sums, sem) = refs[:-2], refs[-2:]
    shares, up_rows = factor_ref.shape[0], out_ref.shape[1]
    sums_copy = pltpu.make_async_copy(sums_ref, sums, sem.at[1 + len(pieces)])
    sums_copy.start()
    copies = [
        pltpu.make_async_copy(
            factor_ref.at[:, pl.ds(factor_ref.shape[1] - up_rows, up_rows)],
            out_ref.at[pl.ds(0, shares)],
            sem.at[0],
        )
    ]
    for k, piece in enumerate(pieces):
        size = piece.shape[0]
        copies.append(
            pltpu.make_async_copy(factor_ref.at[pl.ds(k * size, size)], piece, sem.at[1 + k])
        )
    for copy in copies:
        copy.start()
    sums_copy.wait()
    left = sums[...]
    terms = []
    for _ in range(3):
        terms.append(left.astype(jnp.bfloat16).astype(jnp.float32))
        left = left - terms[-1]
    rest = (out_ref.shape[0] - shares) * up_rows - 3 * left.shape[0]
    if rest > 0:
        terms.append(jnp.zeros((rest, LANES), jnp.float32))
    rows = jnp.concatenate(terms, axis=0)
    for i in range(out_ref.shape[0] - shares):
        out_ref[shares + i] = rows[i * up_rows : (i + 1) * up_rows].astype(jnp.bfloat16)
    for copy in copies:
        copy.wait()


def inverse_kernel(width, shares, sums_ref, *refs):
    messages, out = refs[:-1], refs[-1]
    total = sums_ref[...]
    count = total.shape[0]
    for ref in messages:
        rows = [ref[i].astype(jnp.float32) for i in range(shares, ref.shape[0])]
        rows = jnp.concatenate(rows, axis=0)
        total += rows[:count] + rows[count : 2 * count] + rows[2 * count : 3 * count]
    inverse = lax.rsqrt(total / width + 1e-06)
    for i in range(count):
        out[i * LANES : (i + 1) * LANES, :] = jnp.broadcast_to(
            inverse[i : i + 1], (LANES, LANES)
        ).T


def update(total, down, up, a_ref, b_ref):
    down_rows = a_ref.shape[2]
    up_rows, columns = b_ref.shape[1:]
    strips = columns // LANES
    down_mean = total[:down_rows].T
    up_mean = jnp.concatenate(
        [total[down_rows + k * up_rows : down_rows + (k + 1) * up_rows] for k in range(strips)],
        axis=1,
    )
    p, m, v = adaptive_moment_update(*down(), down_mean)
    a_ref[0], a_ref[1], a_ref[2] = p, m, v
    pieces = [p.T]
    p, m, v = adaptive_moment_update(*up(), up_mean)
    b_ref[0], b_ref[1], b_ref[2] = p, m, v
    pieces += [p[:, k * LANES : (k + 1) * LANES] for k in range(strips)]
    return jnp.concatenate(pieces, axis=0).astype(jnp.bfloat16)


def adam_kernel(grad_in, *refs):
    state, refs = refs[:6], refs[6:]
    a_ref, b_ref, factor_ref, grad_ref, down_win, up_win, sem = refs
    replicas = grad_ref.shape[0]
    down_rows, window = a_ref.shape[2], down_win.shape[2]
    up_rows = up_win.shape[1]
    replica = lax.axis_index("dp")
    share = replica * down_rows
    size = down_rows * replicas
    copies = [pltpu.make_async_copy(grad_in, grad_ref, sem.at[6])]
    for i in range(3):
        down, up = state[i], state[3 + i]
        if window != down_rows:
            lane = pl.multiple_of(first_lane(share, window, size), LANES)
            down = down.at[:, pl.ds(lane, window)]
            up = up.at[pl.ds(pl.multiple_of(replica * up_rows, up_rows), up_rows)]
        copies.append(pltpu.make_async_copy(down, down_win.at[i], sem.at[i]))
        copies.append(pltpu.make_async_copy(up, up_win.at[i], sem.at[3 + i]))
    for copy in copies:
        copy.start()
    copies[0].wait()
    total = jnp.sum(grad_ref[...].astype(jnp.float32), axis=0) / replicas
    for copy in copies[1:]:
        copy.wait()

    def down():
        if window == down_rows:
            return [down_win[i] for i in range(3)]
        shift = window - (share - first_lane(share, window, size))
        return [pltpu.roll(down_win[i], shift, 1)[:, :down_rows] for i in range(3)]

    rounded = update(total, down, lambda: [up_win[i] for i in range(3)], a_ref, b_ref)
    for i in range(replicas):
        factor_ref[i] = rounded


def factor_a(refs, down_rows):
    pieces = []
    for ref in refs:
        for i in range(ref.shape[0]):
            if down_rows % 16 == 0:
                pieces.append(ref[i, :down_rows, :])
            else:
                pieces.append(ref[i].astype(jnp.float32)[:down_rows])
    return jnp.concatenate(pieces, axis=0).astype(jnp.bfloat16)


def factor_b(packed, part, parts, strip, up_rows):
    pieces = [
        packed[i].astype(jnp.float32)[strip * up_rows : (strip + 1) * up_rows]
        for i in range(packed.shape[0])
    ]
    value = jnp.concatenate(pieces, axis=0)
    rows = [jnp.where(part == j, value, jnp.zeros_like(value)) for j in range(parts)]
    return jnp.concatenate(rows, axis=0).astype(jnp.bfloat16)


def merge(scale, block, a, b):
    change = jnp.dot(a, b, preferred_element_type=jnp.float32)
    return (block.astype(jnp.float32) + scale * change).astype(jnp.bfloat16)


def multiply(xs, weights, store):
    rows = xs[0].shape[0]
    tile = rows // 2 if rows % 32 == 0 else rows

    @pl.loop(0, rows // tile)
    def _(i):
        at = pl.ds(pl.multiple_of(i * tile, tile), tile)
        value, first = None, 0
        for x in xs:
            size = x.shape[1]
            part = jnp.dot(
                x[at, :], weights[first : first + size, :], preferred_element_type=jnp.float32
            )
            value, first = part if value is None else value + part, first + size
        store(i * tile, tile, value)


def up_factor(static, packed, owner):
    _, parts, up_rows, strips, columns = static
    part = owner * columns // KEY_VALUE_WIDTH
    return jnp.concatenate(
        [factor_b(packed, part, parts, strip, up_rows) for strip in strips], axis=1
    )


def outside_kernel(static, chips, step, turn, b_ref, x, *refs):
    own_f, sibling_f = refs[:FACTOR_PIECES], refs[FACTOR_PIECES : 2 * FACTOR_PIECES]
    blocks, (weights, product) = refs[2 * FACTOR_PIECES :], refs[-2:]
    strips = static[3]
    features = blocks[0].shape[0]
    down_rows = own_f[0].shape[1] - b_ref.shape[1]
    shares = FACTOR_PIECES * own_f[0].shape[0]
    place, replica = lax.axis_index("tensor"), lax.axis_index("dp")
    owner = (place // CORES - step + chips) % chips * CORES + place % CORES
    b = up_factor(static, b_ref[:shares], owner)
    own_a, sibling_a = factor_a(own_f, down_rows), factor_a(sibling_f, down_rows)
    for k, strip in enumerate(strips):
        mine, other = blocks[2 * k : 2 * k + 2]
        even = replica // turn[strip] % 2 == 0
        lanes = slice(k * LANES, (k + 1) * LANES)
        block = jnp.where(even, mine[...], other[...])
        weights[:features, lanes] = merge(static[0], block, own_a, b[:, lanes])
        block = jnp.where(even, other[...], mine[...])
        weights[features:, lanes] = merge(static[0], block, sibling_a, b[:, lanes])
    more_kernel(x, weights, product)


def more_kernel(*refs):
    xs, (weights, product) = refs[:-2], refs[-2:]

    def store(first, size, value):
        product[pl.ds(first, size), :] = value.astype(product.dtype)

    multiply(xs, weights, store)


def own_kernel(static, own_block, sibling_block, *refs):
    own_f, sibling_f = refs[:FACTOR_PIECES], refs[FACTOR_PIECES : 2 * FACTOR_PIECES]
    refs = refs[2 * FACTOR_PIECES :]
    xs, weights = [refs[:1], refs[1:3]], refs[-1]
    outs = refs[len(refs) - 1 - static[5] : -1]
    features = own_block.shape[0]
    wide = outs[0].shape[1]
    down_rows = own_f[0].shape[1] - len(static[3]) * static[2]
    b = jnp.concatenate([piece[:, down_rows:] for piece in own_f], axis=0)
    b = up_factor(static[:5], b, lax.axis_index("tensor"))
    for at, factors, block in ((0, own_f, own_block), (features, sibling_f, sibling_block)):
        weights[at : at + features] = merge(static[0], block[...], factor_a(factors, down_rows), b)
    for h, x in enumerate(xs):

        def store(first, size, value):
            to = pl.ds(pl.multiple_of(h * x[0].shape[0] + first, 16), size)
            for k, out in enumerate(outs):
                out[to, :] = value[:, k * wide : (k + 1) * wide]

        multiply(x, weights, store)


def finish_kernel(sources, first, own, inv, *refs):
    rows = pl.ds(first, refs[-1].shape[0])
    total = own[rows, :]
    for value in refs[:sources]:
        total = total + value[...].astype(jnp.float32)
    refs[-1][...] = (total * inv[rows, :1]).astype(refs[-1].dtype)


def finish(own, inv_rms, received, at, shape, before):
    block = received[0].shape
    operands = [own, inv_rms] + received
    in_specs = in_vmem(len(operands))
    aliases = {}
    if before is not None:
        aliases = {len(operands): 0}
        in_specs += anywhere(1)
        operands.append(before)
    return pl.pallas_call(
        functools.partial(finish_kernel, len(received), at[0] * block[0]),
        grid=(1,),
        out_shape=jax.ShapeDtypeStruct(shape, jnp.bfloat16),
        in_specs=in_specs,
        out_specs=pl.BlockSpec(block, lambda i: at),
        input_output_aliases=aliases,
        compiler_params=params(),
    )(*operands)


def body(
    prompt_hidden_input,
    input_norm_gain,
    frozen_key_value,
    down_factor_matrix,
    down_moment_first,
    down_moment_second,
    up_factor_matrix,
    up_moment_first,
    up_moment_second,
    down_gradient,
    up_gradient,
):
    n_dp = lax.axis_size("dp")
    n_tensor = lax.axis_size("tensor")
    chips = n_tensor // CORES
    replica = lax.axis_index("dp")
    tokens, features = prompt_hidden_input.shape
    width, columns = frozen_key_value.shape
    rank = up_factor_matrix.shape[0]
    parts = down_factor_matrix.shape[1]
    factors = parts * rank
    strips = columns // LANES
    down_rows = features // n_dp
    up_rows = rank // n_dp
    packed_rows = down_rows + up_rows * strips
    steps = range(1, chips)
    f32, bf16 = jnp.float32, jnp.bfloat16

    def to_sibling(value):
        return lax.ppermute(value, "tensor", [(t, t ^ 1) for t in range(n_tensor)])

    def to_chip(value, step):
        pairs = [
            (CORES * q + k, CORES * ((q + step) % chips) + k)
            for q in range(chips)
            for k in range(CORES)
        ]
        return lax.ppermute(value, "tensor", pairs)

    def by_rank(value):
        return jnp.transpose(value, (1, 2, 0)).reshape(factors, features)

    down_sent = by_rank(down_gradient[0])
    down_state = [by_rank(v) for v in (down_factor_matrix, down_moment_first, down_moment_second)]
    up_state = [up_factor_matrix, up_moment_first, up_moment_second]
    shares = jax.ShapeDtypeStruct((n_dp, packed_rows, LANES), bf16)
    window = pl.cdiv(down_rows + LANES, LANES) * LANES
    aligned = features % LANES == 0 and window <= features
    aligned = aligned and up_rows % 8 == 0 and down_rows % 16 == 0
    window = window if aligned else down_rows
    turns = [1, 2] if n_dp % 4 == 0 else [1, 1]
    turn = [turns[strip % 2] for strip in range(strips)]
    halves = min(COLUMN_HALVES, strips)
    wide = columns // halves
    groups = [range(k * strips // halves, (k + 1) * strips // halves) for k in range(halves)]
    out_shape = (shares,) + tuple(
        jax.ShapeDtypeStruct((len(group), features, LANES), bf16)
        for group in groups
        for _ in steps
    )
    packed, *taken = pl.pallas_call(
        functools.partial(begin_kernel, chips, turn),
        out_shape=out_shape,
        in_specs=anywhere(3),
        out_specs=tuple(anywhere(len(out_shape))),
        scratch_shapes=[
            pltpu.VMEM((factors, features), f32),
            pltpu.VMEM((rank, columns), f32),
            pltpu.VMEM(shares.shape, bf16),
            pltpu.VMEM((len(steps) * strips, features, LANES), bf16),
            pltpu.SemaphoreType.DMA((2 + len(steps) * strips,)),
            pltpu.SemaphoreType.DMA((n_dp + len(steps) * strips,)),
        ],
        compiler_params=pltpu.CompilerParams(vmem_limit_bytes=LARGE_VMEM_BYTES),
    )(down_sent, up_gradient[0], frozen_key_value)
    exchanged = lax.all_to_all(packed, "dp", 0, 0, tiled=True)
    if not aligned:
        down_state = [
            lax.dynamic_slice_in_dim(v, replica * down_rows, down_rows, 1) for v in down_state
        ]
        up_state = [lax.dynamic_slice_in_dim(v, replica * up_rows, up_rows, 0) for v in up_state]
    mine = []

    def send_half(half, after):
        blocks = taken[half * len(steps) : (half + 1) * len(steps)]
        if after is not None:
            blocks, _ = lax.optimization_barrier((blocks, after))
        mine.append([to_chip(value, step) for value, step in zip(blocks, steps)])

    send_half(0, None)

    gain = input_norm_gain[None, :]
    some = tokens // TOKEN_HALVES
    rows = LANES if some % LANES == 0 else some
    operands = [prompt_hidden_input, to_sibling(prompt_hidden_input), gain, to_sibling(gain)]

    def prepared(half, before, in_place, limit):
        token_block = pl.BlockSpec((rows, features), lambda i: (half * (some // rows) + i, 0))
        gain_block = pl.BlockSpec((1, features), lambda i: (0, 0))
        if in_place:
            x_shape = (jax.ShapeDtypeStruct((some, CORES * features), bf16),)
            x_specs = tuple(in_vmem(1))
        else:
            x_shape = (jax.ShapeDtypeStruct((some, features), bf16),) * 2
            x_specs = (pl.BlockSpec((rows, features), lambda i: (i, 0)),) * 2
        *x, squares = pl.pallas_call(
            prepare_kernel,
            grid=(some // rows,),
            out_shape=x_shape
            + (jax.ShapeDtypeStruct(((half + 1) * some // LANES, LANES), f32),),
            in_specs=[token_block, token_block, gain_block, gain_block] + in_vmem(len(before)),
            out_specs=x_specs + tuple(in_vmem(1)),
            scratch_shapes=[pltpu.VMEM((some, LANES), f32)],
            compiler_params=pltpu.CompilerParams(vmem_limit_bytes=limit),
        )(*operands, *before)
        return x, squares

    x0, squares = prepared(0, [], True, PREPARE_VMEM_BYTES)
    exchanged, squares = lax.optimization_barrier((exchanged, squares))
    x1, squares = prepared(1, [squares], False, LARGE_VMEM_BYTES)
    a_next, b_next, sent = pl.pallas_call(
        adam_kernel,
        out_shape=(
            jax.ShapeDtypeStruct((3, factors, down_rows), f32),
            jax.ShapeDtypeStruct((3, up_rows, columns), f32),
            shares,
        ),
        in_specs=anywhere(7),
        out_specs=tuple(in_vmem(3)),
        scratch_shapes=[
            pltpu.VMEM((n_dp, packed_rows, LANES), bf16),
            pltpu.VMEM((3, factors, window), f32),
            pltpu.VMEM((3, up_rows, columns), f32),
            pltpu.SemaphoreType.DMA((7,)),
        ],
        compiler_params=pltpu.CompilerParams(vmem_limit_bytes=LARGE_VMEM_BYTES),
    )(exchanged, *down_state, *up_state)
    own_f = lax.all_to_all(sent, "dp", 0, 0, tiled=True)
    for half in range(1, halves):
        send_half(half, (mine[-1], sent))
    a_next = jnp.transpose(a_next.reshape(3, parts, rank, down_rows), (0, 3, 1, 2))

    outside = [[] for _ in range(strips)]

    def swap_half(half, after):
        for value in mine[half]:
            value, _ = lax.optimization_barrier((value, after))
            split = pl.pallas_call(
                split_kernel,
                out_shape=(jax.ShapeDtypeStruct((features, LANES), bf16),) * len(groups[half]),
                in_specs=in_vmem(1),
                out_specs=tuple(in_vmem(len(groups[half]))),
                compiler_params=params(),
            )(value)
            for piece, strip in zip(split, groups[half]):
                pairs = [(i, i ^ turn[strip]) for i in range(n_dp)]
                outside[strip].append((piece, lax.ppermute(piece, "dp", pairs)))

    swap_half(0, sent)
    own_f, squares = lax.optimization_barrier((own_f, squares))
    up_packed = packed_rows - down_rows
    more = pl.cdiv(3 * (tokens // LANES), up_packed)
    piece = jax.ShapeDtypeStruct((n_dp // FACTOR_PIECES, packed_rows, LANES), bf16)
    message, *pieces = pl.pallas_call(
        message_kernel,
        out_shape=(jax.ShapeDtypeStruct((n_dp + more, up_packed, LANES), bf16),)
        + (piece,) * FACTOR_PIECES,
        in_specs=anywhere(2),
        out_specs=tuple(in_vmem(1 + FACTOR_PIECES)),
        scratch_shapes=[
            pltpu.VMEM(squares.shape, f32),
            pltpu.SemaphoreType.DMA((2 + FACTOR_PIECES,)),
        ],
        compiler_params=params(),
    )(own_f, squares)
    messages = [to_chip(message, step) for step in steps]
    sibling_f = [to_sibling(piece) for piece in pieces]

    inv_rms = pl.pallas_call(
        functools.partial(inverse_kernel, width, n_dp),
        out_shape=jax.ShapeDtypeStruct((tokens, LANES), f32),
        in_specs=in_vmem(chips),
        out_specs=in_vmem(1)[0],
        compiler_params=params(),
    )(squares, *messages)

    scale = 0.5 / math.sqrt(width * rank)

    received = {}
    after = []
    weights_shape = jax.ShapeDtypeStruct((CORES * features, wide), bf16)
    product_shape = jax.ShapeDtypeStruct((some, wide), bf16)
    for half, group in enumerate(groups):
        static = (scale, parts, up_rows, group, columns)
        if half > 0:
            swap_half(half, products[0])
        for step in steps:
            blocks = [value for strip in group for value in outside[strip][step - 1]]
            weights, product = pl.pallas_call(
                functools.partial(outside_kernel, static, chips, step, turn),
                out_shape=(weights_shape, product_shape),
                in_specs=in_vmem(2 + 2 * FACTOR_PIECES + len(blocks)) + anywhere(len(after)),
                out_specs=tuple(in_vmem(2)),
                compiler_params=params(),
            )(messages[step - 1], *x0, *pieces, *sibling_f, *blocks, *after)
            received.setdefault((0, half), []).append(to_chip(product, chips - step))
            second = pl.pallas_call(
                more_kernel,
                out_shape=product_shape,
                in_specs=in_vmem(3),
                out_specs=in_vmem(1)[0],
                compiler_params=params(),
            )(*x1, weights)
            products = [product, second]
            after = [second]
            received.setdefault((1, half), []).append(to_chip(second, chips - step))
        if half == 0:
            after = [received[0, 0][0]]

    after.append(received[1, 0][0])
    static = (scale, parts, up_rows, range(strips), columns, halves)
    totals = pl.pallas_call(
        functools.partial(own_kernel, static),
        out_shape=(jax.ShapeDtypeStruct((tokens, wide), f32),) * halves,
        grid=(1,),
        in_specs=[
            pl.BlockSpec((features, columns), lambda i: (lax.axis_index("tensor"), 0)),
            pl.BlockSpec((features, columns), lambda i: (lax.axis_index("tensor") ^ 1, 0)),
        ]
        + in_vmem(2 * FACTOR_PIECES + 3)
        + anywhere(len(after)),
        out_specs=tuple(in_vmem(halves)),
        scratch_shapes=[pltpu.VMEM((CORES * features, columns), bf16)],
        compiler_params=params(),
        cost_estimate=pl.CostEstimate(
            flops=2 * tokens * CORES * features * columns,
            bytes_accessed=4 * tokens * features,
            transcendentals=0,
        ),
    )(frozen_key_value, frozen_key_value, *pieces, *sibling_f, *x0, *x1, *after)

    keys_values = None
    for at, values in received.items():
        keys_values = finish(
            totals[at[1]], inv_rms, values, at, (tokens, columns), keys_values
        )
    return (a_next, b_next, keys_values)


def solution(mesh):
    placed = (
        P("dp", "tensor"),
        P("tensor"),
        P(None, "tensor"),
        P("tensor", None, None),
        P("tensor", None, None),
        P("tensor", None, None),
        P(None, "tensor"),
        P(None, "tensor"),
        P(None, "tensor"),
        P("dp", "tensor", None, None),
        P("dp", None, "tensor"),
    )
    return jax.shard_map(
        body,
        mesh=mesh,
        in_specs=placed,
        out_specs=(
            P(None, ("tensor", "dp"), None, None),
            P(None, "dp", "tensor"),
            P("dp", "tensor"),
        ),
        check_vma=False,
    )
```

```python
import functools
import math

import jax
import jax.numpy as jnp
from jax import lax
from jax.experimental import pallas as pl
from jax.experimental.pallas import tpu as pltpu
from jax.sharding import PartitionSpec as P

KEY_VALUE_WIDTH = 1024
STEP = 100
CORES = 2
LANES = 128
COLUMN_HALVES = 2
TOKEN_HALVES = 2
FACTOR_PIECES = 2
VMEM_BYTES = 16 * 2**20
LARGE_VMEM_BYTES = 58 * 2**20
PREPARE_VMEM_BYTES = 49 * 2**20


def adaptive_moment_update(param, first, second, grad_mean):
    first_new = 0.9 * first + 0.1 * grad_mean
    second_new = 0.999 * second + 0.001 * grad_mean * grad_mean
    step_size = first_new / (1.0 - 0.9**STEP) / (jnp.sqrt(second_new / (1.0 - 0.999**STEP)) + 1e-08)
    return (param - 0.1 * step_size, first_new, second_new)


def in_vmem(count):
    return [pl.BlockSpec(memory_space=pltpu.VMEM)] * count


def anywhere(count):
    return [pl.BlockSpec(memory_space=pl.ANY)] * count


SCALARS = pl.BlockSpec(memory_space=pltpu.SMEM)


def params(**more):
    return pltpu.CompilerParams(vmem_limit_bytes=VMEM_BYTES, **more)


def pack(down, up, out_ref, ready):
    shares = out_ref.shape[0]
    down = down.T
    down_rows, up_rows = down.shape[0] // shares, up.shape[0] // shares
    for i in range(shares):
        pieces = [down[i * down_rows : (i + 1) * down_rows]]
        for k in range(up.shape[1] // LANES):
            pieces.append(up[i * up_rows : (i + 1) * up_rows, k * LANES : (k + 1) * LANES])
        out_ref[i] = jnp.concatenate(pieces, axis=0).astype(jnp.bfloat16)
        ready(i)


def first_lane(share, window, size):
    return jnp.minimum(share // LANES * LANES, size - window)


def begin_kernel(chips, turn, down_ref, up_ref, weights_ref, packed, *refs):
    outs, (down, up, blocks, strips, sem, sem_out) = refs[:-6], refs[-6:]
    features = strips.shape[1]
    place, replica = lax.axis_index("tensor"), lax.axis_index("dp")
    chip, core = place // CORES, place % CORES
    copies, back = [], []

    def add(source, target):
        copies.append(pltpu.make_async_copy(source, target, sem.at[len(copies)]))
        copies[-1].start()

    def add_back(source, target):
        back.append(pltpu.make_async_copy(source, target, sem_out.at[len(back)]))
        back[-1].start()

    add(down_ref, down)
    add(up_ref, up)
    targets = []
    for i, out in enumerate(outs):
        step, first = 1 + i % (chips - 1), i // (chips - 1) * out.shape[0]
        for k in range(out.shape[0]):
            half = (core + replica // turn[first + k]) % 2
            row = ((chip + step) % chips * CORES + half) * features
            add(
                weights_ref.at[
                    pl.ds(pl.multiple_of(row, features), features),
                    pl.ds((first + k) * LANES, LANES),
                ],
                strips.at[len(targets)],
            )
            targets.append(out.at[k])
    copies[0].wait()
    copies[1].wait()
    pack(down[...], up[...], blocks, lambda i: add_back(blocks.at[i], packed.at[i]))
    for i, target in enumerate(targets):
        copies[2 + i].wait()
        add_back(strips.at[i], target)
    for copy in back:
        copy.wait()


def split_kernel(in_ref, *outs):
    for k, out in enumerate(outs):
        out[...] = in_ref[k]


def prepare_kernel(first, own_in, sibling_in, own_gain, sibling_gain, *refs):
    own, sibling, squares, sem = refs[-4:]
    rows, features = own.shape
    together = refs[-6].shape[1] > features
    outs, sums_ref = refs[-6 if together else -7 : -5], refs[-5]
    before = refs[: -6 if together else -7]
    block = LANES if rows % LANES == 0 else rows
    tile = 16 if block % 16 == 0 else block
    count = rows // block
    raw = ((own_in, own), (sibling_in, sibling))
    loads = [
        [
            pltpu.make_async_copy(
                source.at[pl.ds(first + k * block, block)],
                target.at[pl.ds(k * block, block)],
                sem.at[2 * k + side],
            )
            for side, (source, target) in enumerate(raw)
        ]
        for k in range(count)
    ]
    for pair in loads:
        for copy in pair:
            copy.start()
    stores = []
    for k in range(count):
        for copy in loads[k]:
            copy.wait()

        @pl.loop(0, block // tile, unroll=2)
        def _(i):
            at = pl.ds(pl.multiple_of(k * block + i * tile, tile), tile)
            total = None
            for side, (ref, gain) in enumerate(((own, own_gain), (sibling, sibling_gain))):
                value = ref[at, :].astype(jnp.float32)
                scaled = (value * gain[...]).astype(ref.dtype)
                if together:
                    outs[0][at, side * features : (side + 1) * features] = scaled
                else:
                    ref[at, :] = scaled
                total = value * value if total is None else total + value * value
            total = jnp.sum(total, axis=1, keepdims=True)
            squares[at, :] = jnp.broadcast_to(total, (tile, LANES))

        if not together:
            part = pl.ds(k * block, block)
            for side, (source, out) in enumerate(((own, outs[0]), (sibling, outs[1]))):
                place = sem.at[2 * (count + k) + side]
                stores.append(pltpu.make_async_copy(source.at[part], out.at[part], place))
                stores[-1].start()
    done = 0
    for ref in before:
        sums_ref[: ref.shape[0]] = ref[...]
        done = ref.shape[0]
    for i in range(rows // LANES):
        row = squares[i * LANES : (i + 1) * LANES, :].T[:1]
        sums_ref[done + i : done + i + 1] = row
    for copy in stores:
        copy.wait()


def message_kernel(factor_ref, sums_ref, out_ref, *refs):
    pieces, (sums, sem) = refs[:-2], refs[-2:]
    shares, up_rows = factor_ref.shape[0], out_ref.shape[1]
    sums_copy = pltpu.make_async_copy(sums_ref, sums, sem.at[1 + len(pieces)])
    sums_copy.start()
    copies = [
        pltpu.make_async_copy(
            factor_ref.at[:, pl.ds(factor_ref.shape[1] - up_rows, up_rows)],
            out_ref.at[pl.ds(0, shares)],
            sem.at[0],
        )
    ]
    for k, piece in enumerate(pieces):
        size = piece.shape[0]
        copies.append(
            pltpu.make_async_copy(factor_ref.at[pl.ds(k * size, size)], piece, sem.at[1 + k])
        )
    for copy in copies:
        copy.start()
    sums_copy.wait()
    left = sums[...]
    terms = []
    for _ in range(3):
        terms.append(left.astype(jnp.bfloat16).astype(jnp.float32))
        left = left - terms[-1]
    rest = (out_ref.shape[0] - shares) * up_rows - 3 * left.shape[0]
    if rest > 0:
        terms.append(jnp.zeros((rest, LANES), jnp.float32))
    rows = jnp.concatenate(terms, axis=0)
    for i in range(out_ref.shape[0] - shares):
        out_ref[shares + i] = rows[i * up_rows : (i + 1) * up_rows].astype(jnp.bfloat16)
    for copy in copies:
        copy.wait()


def inverse_kernel(width, shares, sums_ref, *refs):
    messages, out = refs[:-1], refs[-1]
    total = sums_ref[...]
    count = total.shape[0]
    for ref in messages:
        rows = [ref[i].astype(jnp.float32) for i in range(shares, ref.shape[0])]
        rows = jnp.concatenate(rows, axis=0)
        total += rows[:count] + rows[count : 2 * count] + rows[2 * count : 3 * count]
    inverse = lax.rsqrt(total / width + 1e-06)
    for i in range(count):
        out[i * LANES : (i + 1) * LANES, :] = jnp.broadcast_to(
            inverse[i : i + 1], (LANES, LANES)
        ).T


def update(total, down, up, a_ref, b_ref):
    down_rows = a_ref.shape[2]
    up_rows, columns = b_ref.shape[1:]
    strips = columns // LANES
    down_mean = total[:down_rows].T
    up_mean = jnp.concatenate(
        [total[down_rows + k * up_rows : down_rows + (k + 1) * up_rows] for k in range(strips)],
        axis=1,
    )
    p, m, v = adaptive_moment_update(*down(), down_mean)
    a_ref[0], a_ref[1], a_ref[2] = p, m, v
    pieces = [p.T]
    p, m, v = adaptive_moment_update(*up(), up_mean)
    b_ref[0], b_ref[1], b_ref[2] = p, m, v
    pieces += [p[:, k * LANES : (k + 1) * LANES] for k in range(strips)]
    return jnp.concatenate(pieces, axis=0).astype(jnp.bfloat16)


def adam_kernel(grad_in, *refs):
    state, refs = refs[:6], refs[6:]
    a_ref, b_ref, factor_ref, grad_ref, down_win, up_win, sem = refs
    replicas = grad_ref.shape[0]
    down_rows, window = a_ref.shape[2], down_win.shape[2]
    up_rows = up_win.shape[1]
    replica = lax.axis_index("dp")
    share = replica * down_rows
    size = down_rows * replicas
    copies = [pltpu.make_async_copy(grad_in, grad_ref, sem.at[6])]
    for i in range(3):
        down, up = state[i], state[3 + i]
        if window != down_rows:
            lane = pl.multiple_of(first_lane(share, window, size), LANES)
            down = down.at[:, pl.ds(lane, window)]
            up = up.at[pl.ds(pl.multiple_of(replica * up_rows, up_rows), up_rows)]
        copies.append(pltpu.make_async_copy(down, down_win.at[i], sem.at[i]))
        copies.append(pltpu.make_async_copy(up, up_win.at[i], sem.at[3 + i]))
    for copy in copies:
        copy.start()
    copies[0].wait()
    total = jnp.sum(grad_ref[...].astype(jnp.float32), axis=0) / replicas
    for copy in copies[1:]:
        copy.wait()

    def down():
        if window == down_rows:
            return [down_win[i] for i in range(3)]
        shift = window - (share - first_lane(share, window, size))
        return [pltpu.roll(down_win[i], shift, 1)[:, :down_rows] for i in range(3)]

    rounded = update(total, down, lambda: [up_win[i] for i in range(3)], a_ref, b_ref)
    for i in range(replicas):
        factor_ref[i] = rounded


def factor_a(refs, down_rows):
    pieces = []
    for ref in refs:
        for i in range(ref.shape[0]):
            if down_rows % 16 == 0:
                pieces.append(ref[i, :down_rows, :])
            else:
                pieces.append(ref[i].astype(jnp.float32)[:down_rows])
    return jnp.concatenate(pieces, axis=0).astype(jnp.bfloat16)


def factor_b(packed, part, parts, strip, up_rows):
    pieces = [
        packed[i].astype(jnp.float32)[strip * up_rows : (strip + 1) * up_rows]
        for i in range(packed.shape[0])
    ]
    value = jnp.concatenate(pieces, axis=0)
    rows = [jnp.where(part == j, value, jnp.zeros_like(value)) for j in range(parts)]
    return jnp.concatenate(rows, axis=0).astype(jnp.bfloat16)


def merge(scale, block, a, b):
    change = jnp.dot(a, b, preferred_element_type=jnp.float32)
    return (block.astype(jnp.float32) + scale * change).astype(jnp.bfloat16)


def multiply(xs, weights, store):
    rows = xs[0].shape[0]
    tile = rows // 2 if rows % 32 == 0 else rows

    @pl.loop(0, rows // tile)
    def _(i):
        at = pl.ds(pl.multiple_of(i * tile, tile), tile)
        value, first = None, 0
        for x in xs:
            size = x.shape[1]
            part = jnp.dot(
                x[at, :], weights[first : first + size, :], preferred_element_type=jnp.float32
            )
            value, first = part if value is None else value + part, first + size
        store(i * tile, tile, value)


def up_factor(static, packed, owner):
    _, parts, up_rows, strips, columns = static
    part = owner * columns // KEY_VALUE_WIDTH
    return jnp.concatenate(
        [factor_b(packed, part, parts, strip, up_rows) for strip in strips], axis=1
    )


def outside_kernel(static, chips, step, turn, b_ref, x, *refs):
    own_f, sibling_f = refs[:FACTOR_PIECES], refs[FACTOR_PIECES : 2 * FACTOR_PIECES]
    weights, product, blocks, sem = refs[-4:]
    strips = static[3]
    copies = [
        pltpu.make_async_copy(refs[2 * FACTOR_PIECES + k], blocks.at[k], sem.at[k])
        for k in range(2 * len(strips))
    ]
    for copy in copies:
        copy.start()
    features = blocks.shape[1]
    down_rows = own_f[0].shape[1] - b_ref.shape[1]
    shares = FACTOR_PIECES * own_f[0].shape[0]
    place, replica = lax.axis_index("tensor"), lax.axis_index("dp")
    owner = (place // CORES - step + chips) % chips * CORES + place % CORES
    b = up_factor(static, b_ref[:shares], owner)
    changes = [
        jnp.dot(factor_a(f, down_rows), b, preferred_element_type=jnp.float32)
        for f in (own_f, sibling_f)
    ]
    for copy in copies:
        copy.wait()
    for k, strip in enumerate(strips):
        mine, other = blocks.at[2 * k], blocks.at[2 * k + 1]
        even = replica // turn[strip] % 2 == 0
        lanes = slice(k * LANES, (k + 1) * LANES)
        for side, (near, far) in enumerate(((mine, other), (other, mine))):
            block = jnp.where(even, near[...], far[...]).astype(jnp.float32)
            block = (block + static[0] * changes[side][:, lanes]).astype(jnp.bfloat16)
            weights[side * features : (side + 1) * features, lanes] = block
    more_kernel(x, weights, product)


def more_kernel(*refs):
    xs, (weights, product) = refs[:-2], refs[-2:]

    def store(first, size, value):
        product[pl.ds(first, size), :] = value.astype(product.dtype)

    multiply(xs, weights, store)


def own_kernel(static, own_block, sibling_block, *refs):
    own_f, sibling_f = refs[:FACTOR_PIECES], refs[FACTOR_PIECES : 2 * FACTOR_PIECES]
    refs = refs[2 * FACTOR_PIECES :]
    xs, weights = [refs[:1], refs[1:3]], refs[-1]
    outs = refs[len(refs) - 1 - static[5] : -1]
    features = own_block.shape[0]
    wide = outs[0].shape[1]
    down_rows = own_f[0].shape[1] - len(static[3]) * static[2]
    b = jnp.concatenate([piece[:, down_rows:] for piece in own_f], axis=0)
    b = up_factor(static[:5], b, lax.axis_index("tensor"))
    for at, factors, block in ((0, own_f, own_block), (features, sibling_f, sibling_block)):
        weights[at : at + features] = merge(static[0], block[...], factor_a(factors, down_rows), b)
    for h, x in enumerate(xs):

        def store(first, size, value):
            to = pl.ds(pl.multiple_of(h * x[0].shape[0] + first, 16), size)
            for k, out in enumerate(outs):
                out[to, :] = value[:, k * wide : (k + 1) * wide]

        multiply(x, weights, store)


def finish_kernel(sources, first, own, inv, *refs):
    rows = pl.ds(first, refs[-1].shape[0])
    total = own[rows, :]
    for value in refs[:sources]:
        total = total + value[...].astype(jnp.float32)
    refs[-1][...] = (total * inv[rows, :1]).astype(refs[-1].dtype)


def finish(own, inv_rms, received, at, shape, before):
    block = received[0].shape
    operands = [own, inv_rms] + received
    in_specs = in_vmem(len(operands))
    aliases = {}
    if before is not None:
        aliases = {len(operands): 0}
        in_specs += anywhere(1)
        operands.append(before)
    return pl.pallas_call(
        functools.partial(finish_kernel, len(received), at[0] * block[0]),
        grid=(1,),
        out_shape=jax.ShapeDtypeStruct(shape, jnp.bfloat16),
        in_specs=in_specs,
        out_specs=pl.BlockSpec(block, lambda i: at),
        input_output_aliases=aliases,
        compiler_params=params(),
    )(*operands)


def body(
    prompt_hidden_input,
    input_norm_gain,
    frozen_key_value,
    down_factor_matrix,
    down_moment_first,
    down_moment_second,
    up_factor_matrix,
    up_moment_first,
    up_moment_second,
    down_gradient,
    up_gradient,
):
    n_dp = lax.axis_size("dp")
    n_tensor = lax.axis_size("tensor")
    chips = n_tensor // CORES
    replica = lax.axis_index("dp")
    tokens, features = prompt_hidden_input.shape
    width, columns = frozen_key_value.shape
    rank = up_factor_matrix.shape[0]
    parts = down_factor_matrix.shape[1]
    factors = parts * rank
    strips = columns // LANES
    down_rows = features // n_dp
    up_rows = rank // n_dp
    packed_rows = down_rows + up_rows * strips
    steps = range(1, chips)
    f32, bf16 = jnp.float32, jnp.bfloat16

    def to_sibling(value):
        return lax.ppermute(value, "tensor", [(t, t ^ 1) for t in range(n_tensor)])

    def to_chip(value, step):
        pairs = [
            (CORES * q + k, CORES * ((q + step) % chips) + k)
            for q in range(chips)
            for k in range(CORES)
        ]
        return lax.ppermute(value, "tensor", pairs)

    def by_rank(value):
        return jnp.transpose(value, (1, 2, 0)).reshape(factors, features)

    down_sent = by_rank(down_gradient[0])
    down_state = [by_rank(v) for v in (down_factor_matrix, down_moment_first, down_moment_second)]
    up_state = [up_factor_matrix, up_moment_first, up_moment_second]
    shares = jax.ShapeDtypeStruct((n_dp, packed_rows, LANES), bf16)
    window = pl.cdiv(down_rows + LANES, LANES) * LANES
    aligned = features % LANES == 0 and window <= features
    aligned = aligned and up_rows % 8 == 0 and down_rows % 16 == 0
    window = window if aligned else down_rows
    turns = [1, 2] if n_dp % 4 == 0 else [1, 1]
    turn = [turns[strip % 2] for strip in range(strips)]
    halves = min(COLUMN_HALVES, strips)
    wide = columns // halves
    groups = [range(k * strips // halves, (k + 1) * strips // halves) for k in range(halves)]
    out_shape = (shares,) + tuple(
        jax.ShapeDtypeStruct((len(group), features, LANES), bf16)
        for group in groups
        for _ in steps
    )
    packed, *taken = pl.pallas_call(
        functools.partial(begin_kernel, chips, turn),
        out_shape=out_shape,
        in_specs=anywhere(3),
        out_specs=tuple(anywhere(len(out_shape))),
        scratch_shapes=[
            pltpu.VMEM((factors, features), f32),
            pltpu.VMEM((rank, columns), f32),
            pltpu.VMEM(shares.shape, bf16),
            pltpu.VMEM((len(steps) * strips, features, LANES), bf16),
            pltpu.SemaphoreType.DMA((2 + len(steps) * strips,)),
            pltpu.SemaphoreType.DMA((n_dp + len(steps) * strips,)),
        ],
        compiler_params=pltpu.CompilerParams(vmem_limit_bytes=LARGE_VMEM_BYTES),
    )(down_sent, up_gradient[0], frozen_key_value)
    exchanged = lax.all_to_all(packed, "dp", 0, 0, tiled=True)
    if not aligned:
        down_state = [
            lax.dynamic_slice_in_dim(v, replica * down_rows, down_rows, 1) for v in down_state
        ]
        up_state = [lax.dynamic_slice_in_dim(v, replica * up_rows, up_rows, 0) for v in up_state]
    mine = []

    def send_half(half, after):
        blocks = taken[half * len(steps) : (half + 1) * len(steps)]
        if after is not None:
            blocks, _ = lax.optimization_barrier((blocks, after))
        mine.append([to_chip(value, step) for value, step in zip(blocks, steps)])

    send_half(0, None)

    gain = input_norm_gain[None, :]
    some = tokens // TOKEN_HALVES
    operands = [prompt_hidden_input, to_sibling(prompt_hidden_input), gain, to_sibling(gain)]

    def prepared(half, before, in_place, limit):
        if in_place:
            x_shape = (jax.ShapeDtypeStruct((some, CORES * features), bf16),)
            x_specs = tuple(in_vmem(1))
        else:
            x_shape = (jax.ShapeDtypeStruct((some, features), bf16),) * 2
            x_specs = tuple(anywhere(2))
        *x, squares = pl.pallas_call(
            functools.partial(prepare_kernel, half * some),
            out_shape=x_shape
            + (jax.ShapeDtypeStruct(((half + 1) * some // LANES, LANES), f32),),
            in_specs=anywhere(2) + in_vmem(2 + len(before)),
            out_specs=x_specs + tuple(in_vmem(1)),
            scratch_shapes=[
                pltpu.VMEM((some, features), bf16),
                pltpu.VMEM((some, features), bf16),
                pltpu.VMEM((some, LANES), f32),
                pltpu.SemaphoreType.DMA((4 * pl.cdiv(some, LANES),)),
            ],
            compiler_params=pltpu.CompilerParams(vmem_limit_bytes=limit),
        )(*operands, *before)
        return x, squares

    x0, squares = prepared(0, [], True, PREPARE_VMEM_BYTES)
    exchanged, squares = lax.optimization_barrier((exchanged, squares))
    x1, squares = prepared(1, [squares], False, LARGE_VMEM_BYTES)
    a_next, b_next, sent = pl.pallas_call(
        adam_kernel,
        out_shape=(
            jax.ShapeDtypeStruct((3, factors, down_rows), f32),
            jax.ShapeDtypeStruct((3, up_rows, columns), f32),
            shares,
        ),
        in_specs=anywhere(7),
        out_specs=tuple(in_vmem(3)),
        scratch_shapes=[
            pltpu.VMEM((n_dp, packed_rows, LANES), bf16),
            pltpu.VMEM((3, factors, window), f32),
            pltpu.VMEM((3, up_rows, columns), f32),
            pltpu.SemaphoreType.DMA((7,)),
        ],
        compiler_params=pltpu.CompilerParams(vmem_limit_bytes=LARGE_VMEM_BYTES),
    )(exchanged, *down_state, *up_state)
    own_f = lax.all_to_all(sent, "dp", 0, 0, tiled=True)
    for half in range(1, halves):
        send_half(half, (mine[-1], sent))
    a_next = jnp.transpose(a_next.reshape(3, parts, rank, down_rows), (0, 3, 1, 2))

    outside = [[] for _ in range(strips)]

    def swap_half(half, after):
        for value in mine[half]:
            value, _ = lax.optimization_barrier((value, after))
            split = pl.pallas_call(
                split_kernel,
                out_shape=(jax.ShapeDtypeStruct((features, LANES), bf16),) * len(groups[half]),
                in_specs=in_vmem(1),
                out_specs=tuple(in_vmem(len(groups[half]))),
                compiler_params=params(),
            )(value)
            for piece, strip in zip(split, groups[half]):
                pairs = [(i, i ^ turn[strip]) for i in range(n_dp)]
                outside[strip].append((piece, lax.ppermute(piece, "dp", pairs)))

    swap_half(0, sent)
    own_f, squares = lax.optimization_barrier((own_f, squares))
    up_packed = packed_rows - down_rows
    more = pl.cdiv(3 * (tokens // LANES), up_packed)
    piece = jax.ShapeDtypeStruct((n_dp // FACTOR_PIECES, packed_rows, LANES), bf16)
    message, *pieces = pl.pallas_call(
        message_kernel,
        out_shape=(jax.ShapeDtypeStruct((n_dp + more, up_packed, LANES), bf16),)
        + (piece,) * FACTOR_PIECES,
        in_specs=anywhere(2),
        out_specs=tuple(in_vmem(1 + FACTOR_PIECES)),
        scratch_shapes=[
            pltpu.VMEM(squares.shape, f32),
            pltpu.SemaphoreType.DMA((2 + FACTOR_PIECES,)),
        ],
        compiler_params=params(),
    )(own_f, squares)
    messages = [to_chip(message, step) for step in steps]
    sibling_f = [to_sibling(piece) for piece in pieces]

    inv_rms = pl.pallas_call(
        functools.partial(inverse_kernel, width, n_dp),
        out_shape=jax.ShapeDtypeStruct((tokens, LANES), f32),
        in_specs=in_vmem(chips),
        out_specs=in_vmem(1)[0],
        compiler_params=params(),
    )(squares, *messages)

    scale = 0.5 / math.sqrt(width * rank)

    received = {}
    after = []
    weights_shape = jax.ShapeDtypeStruct((CORES * features, wide), bf16)
    product_shape = jax.ShapeDtypeStruct((some, wide), bf16)
    for half, group in enumerate(groups):
        static = (scale, parts, up_rows, group, columns)
        if half > 0:
            swap_half(half, products[0])
        for step in steps:
            blocks = [value for strip in group for value in outside[strip][step - 1]]
            weights, product = pl.pallas_call(
                functools.partial(outside_kernel, static, chips, step, turn),
                out_shape=(weights_shape, product_shape),
                in_specs=in_vmem(2 + 2 * FACTOR_PIECES) + anywhere(len(blocks) + len(after)),
                out_specs=tuple(in_vmem(2)),
                scratch_shapes=[
                    pltpu.VMEM((len(blocks), features, LANES), bf16),
                    pltpu.SemaphoreType.DMA((len(blocks),)),
                ],
                compiler_params=params(),
            )(messages[step - 1], *x0, *pieces, *sibling_f, *blocks, *after)
            received.setdefault((0, half), []).append(to_chip(product, chips - step))
            second = pl.pallas_call(
                more_kernel,
                out_shape=product_shape,
                in_specs=in_vmem(3),
                out_specs=in_vmem(1)[0],
                compiler_params=params(),
            )(*x1, weights)
            products = [product, second]
            after = [second]
            received.setdefault((1, half), []).append(to_chip(second, chips - step))
        if half == 0:
            after = [received[0, 0][0]]

    after.append(received[1, 0][0])
    static = (scale, parts, up_rows, range(strips), columns, halves)
    totals = pl.pallas_call(
        functools.partial(own_kernel, static),
        out_shape=(jax.ShapeDtypeStruct((tokens, wide), f32),) * halves,
        grid=(1,),
        in_specs=[
            pl.BlockSpec((features, columns), lambda i: (lax.axis_index("tensor"), 0)),
            pl.BlockSpec((features, columns), lambda i: (lax.axis_index("tensor") ^ 1, 0)),
        ]
        + in_vmem(2 * FACTOR_PIECES + 3)
        + anywhere(len(after)),
        out_specs=tuple(in_vmem(halves)),
        scratch_shapes=[pltpu.VMEM((CORES * features, columns), bf16)],
        compiler_params=params(),
        cost_estimate=pl.CostEstimate(
            flops=2 * tokens * CORES * features * columns,
            bytes_accessed=4 * tokens * features,
            transcendentals=0,
        ),
    )(frozen_key_value, frozen_key_value, *pieces, *sibling_f, *x0, *x1, *after)

    keys_values = None
    for at, values in received.items():
        keys_values = finish(
            totals[at[1]], inv_rms, values, at, (tokens, columns), keys_values
        )
    return (a_next, b_next, keys_values)


def solution(mesh):
    placed = (
        P("dp", "tensor"),
        P("tensor"),
        P(None, "tensor"),
        P("tensor", None, None),
        P("tensor", None, None),
        P("tensor", None, None),
        P(None, "tensor"),
        P(None, "tensor"),
        P(None, "tensor"),
        P("dp", "tensor", None, None),
        P("dp", None, "tensor"),
    )
    return jax.shard_map(
        body,
        mesh=mesh,
        in_specs=placed,
        out_specs=(
            P(None, ("tensor", "dp"), None, None),
            P(None, "dp", "tensor"),
            P("dp", "tensor"),
        ),
        check_vma=False,
    )
```

```python
import functools
import math

import jax
import jax.numpy as jnp
from jax import lax
from jax.experimental import pallas as pl
from jax.experimental.pallas import tpu as pltpu
from jax.sharding import PartitionSpec as P

KEY_VALUE_WIDTH = 1024
STEP = 100
CORES = 2
LANES = 128
COLUMN_HALVES = 2
TOKEN_HALVES = 2
FACTOR_PIECES = 2
VMEM_BYTES = 16 * 2**20
LARGE_VMEM_BYTES = 58 * 2**20
PREPARE_VMEM_BYTES = 49 * 2**20


def adaptive_moment_update(param, first, second, grad_mean):
    first_new = 0.9 * first + 0.1 * grad_mean
    second_new = 0.999 * second + 0.001 * grad_mean * grad_mean
    step_size = first_new / (1.0 - 0.9**STEP) / (jnp.sqrt(second_new / (1.0 - 0.999**STEP)) + 1e-08)
    return (param - 0.1 * step_size, first_new, second_new)


def in_vmem(count):
    return [pl.BlockSpec(memory_space=pltpu.VMEM)] * count


def anywhere(count):
    return [pl.BlockSpec(memory_space=pl.ANY)] * count


SCALARS = pl.BlockSpec(memory_space=pltpu.SMEM)


def params(**more):
    return pltpu.CompilerParams(vmem_limit_bytes=VMEM_BYTES, **more)


def pack(down, up, out_ref, ready):
    shares = out_ref.shape[0]
    down = down.T
    down_rows, up_rows = down.shape[0] // shares, up.shape[0] // shares
    for i in range(shares):
        pieces = [down[i * down_rows : (i + 1) * down_rows]]
        for k in range(up.shape[1] // LANES):
            pieces.append(up[i * up_rows : (i + 1) * up_rows, k * LANES : (k + 1) * LANES])
        out_ref[i] = jnp.concatenate(pieces, axis=0).astype(jnp.bfloat16)
        ready(i)


def first_lane(share, window, size):
    return jnp.minimum(share // LANES * LANES, size - window)


def begin_kernel(chips, turn, down_ref, up_ref, weights_ref, packed, *refs):
    outs, (down, up, blocks, strips, sem, sem_out) = refs[:-6], refs[-6:]
    features = strips.shape[1]
    place, replica = lax.axis_index("tensor"), lax.axis_index("dp")
    chip, core = place // CORES, place % CORES
    copies, back = [], []

    def add(source, target):
        copies.append(pltpu.make_async_copy(source, target, sem.at[len(copies)]))
        copies[-1].start()

    def add_back(source, target):
        back.append(pltpu.make_async_copy(source, target, sem_out.at[len(back)]))
        back[-1].start()

    add(down_ref, down)
    add(up_ref, up)
    targets = []
    for i, out in enumerate(outs):
        step, first = 1 + i % (chips - 1), i // (chips - 1) * out.shape[0]
        for k in range(out.shape[0]):
            half = (core + replica // turn[first + k]) % 2
            row = ((chip + step) % chips * CORES + half) * features
            add(
                weights_ref.at[
                    pl.ds(pl.multiple_of(row, features), features),
                    pl.ds((first + k) * LANES, LANES),
                ],
                strips.at[len(targets)],
            )
            targets.append(out.at[k])
    copies[0].wait()
    copies[1].wait()
    pack(down[...], up[...], blocks, lambda i: add_back(blocks.at[i], packed.at[i]))
    for i, target in enumerate(targets):
        copies[2 + i].wait()
        add_back(strips.at[i], target)
    for copy in back:
        copy.wait()


def split_kernel(in_ref, *outs):
    for k, out in enumerate(outs):
        out[...] = in_ref[k]


def prepare_kernel(first, own_in, sibling_in, own_gain, sibling_gain, *refs):
    own, sibling, squares, sem = refs[-4:]
    rows, features = own.shape
    together = refs[-6].shape[1] > features
    outs, sums_ref = refs[-6 if together else -7 : -5], refs[-5]
    before = refs[: -6 if together else -7]
    block = LANES if rows % LANES == 0 else rows
    tile = 16 if block % 16 == 0 else block
    count = rows // block
    raw = ((own_in, own), (sibling_in, sibling))
    loads = [
        [
            pltpu.make_async_copy(
                source.at[pl.ds(first + k * block, block)],
                target.at[pl.ds(k * block, block)],
                sem.at[2 * k + side],
            )
            for side, (source, target) in enumerate(raw)
        ]
        for k in range(count)
    ]
    for pair in loads:
        for copy in pair:
            copy.start()
    stores = []
    for k in range(count):
        for copy in loads[k]:
            copy.wait()

        @pl.loop(0, block // tile, unroll=2)
        def _(i):
            at = pl.ds(pl.multiple_of(k * block + i * tile, tile), tile)
            total = None
            for side, (ref, gain) in enumerate(((own, own_gain), (sibling, sibling_gain))):
                value = ref[at, :].astype(jnp.float32)
                scaled = (value * gain[...]).astype(ref.dtype)
                if together:
                    outs[0][at, side * features : (side + 1) * features] = scaled
                else:
                    ref[at, :] = scaled
                total = value * value if total is None else total + value * value
            total = jnp.sum(total, axis=1, keepdims=True)
            squares[at, :] = jnp.broadcast_to(total, (tile, LANES))

        if not together:
            part = pl.ds(k * block, block)
            for side, (source, out) in enumerate(((own, outs[0]), (sibling, outs[1]))):
                place = sem.at[2 * (count + k) + side]
                stores.append(pltpu.make_async_copy(source.at[part], out.at[part], place))
                stores[-1].start()
    done = 0
    for ref in before:
        sums_ref[: ref.shape[0]] = ref[...]
        done = ref.shape[0]
    for i in range(rows // LANES):
        row = squares[i * LANES : (i + 1) * LANES, :].T[:1]
        sums_ref[done + i : done + i + 1] = row
    for copy in stores:
        copy.wait()


def message_kernel(factor_ref, sums_ref, out_ref, *refs):
    pieces, (sums, sem) = refs[:-2], refs[-2:]
    shares, up_rows = factor_ref.shape[0], out_ref.shape[1]
    sums_copy = pltpu.make_async_copy(sums_ref, sums, sem.at[1 + len(pieces)])
    sums_copy.start()
    copies = [
        pltpu.make_async_copy(
            factor_ref.at[:, pl.ds(factor_ref.shape[1] - up_rows, up_rows)],
            out_ref.at[pl.ds(0, shares)],
            sem.at[0],
        )
    ]
    for k, piece in enumerate(pieces):
        size = piece.shape[0]
        copies.append(
            pltpu.make_async_copy(factor_ref.at[pl.ds(k * size, size)], piece, sem.at[1 + k])
        )
    for copy in copies:
        copy.start()
    sums_copy.wait()
    left = sums[...]
    terms = []
    for _ in range(3):
        terms.append(left.astype(jnp.bfloat16).astype(jnp.float32))
        left = left - terms[-1]
    rest = (out_ref.shape[0] - shares) * up_rows - 3 * left.shape[0]
    if rest > 0:
        terms.append(jnp.zeros((rest, LANES), jnp.float32))
    rows = jnp.concatenate(terms, axis=0)
    for i in range(out_ref.shape[0] - shares):
        out_ref[shares + i] = rows[i * up_rows : (i + 1) * up_rows].astype(jnp.bfloat16)
    for copy in copies:
        copy.wait()


def inverse_kernel(width, shares, sums_ref, *refs):
    messages, out = refs[:-1], refs[-1]
    total = sums_ref[...]
    count = total.shape[0]
    for ref in messages:
        rows = [ref[i].astype(jnp.float32) for i in range(shares, ref.shape[0])]
        rows = jnp.concatenate(rows, axis=0)
        total += rows[:count] + rows[count : 2 * count] + rows[2 * count : 3 * count]
    inverse = lax.rsqrt(total / width + 1e-06)
    for i in range(count):
        out[i * LANES : (i + 1) * LANES, :] = jnp.broadcast_to(
            inverse[i : i + 1], (LANES, LANES)
        ).T


def update(total, down, up, a_ref, b_ref):
    down_rows = a_ref.shape[2]
    up_rows, columns = b_ref.shape[1:]
    strips = columns // LANES
    down_mean = total[:down_rows].T
    up_mean = jnp.concatenate(
        [total[down_rows + k * up_rows : down_rows + (k + 1) * up_rows] for k in range(strips)],
        axis=1,
    )
    p, m, v = adaptive_moment_update(*down(), down_mean)
    a_ref[0], a_ref[1], a_ref[2] = p, m, v
    pieces = [p.T]
    p, m, v = adaptive_moment_update(*up(), up_mean)
    b_ref[0], b_ref[1], b_ref[2] = p, m, v
    pieces += [p[:, k * LANES : (k + 1) * LANES] for k in range(strips)]
    return jnp.concatenate(pieces, axis=0).astype(jnp.bfloat16)


def adam_kernel(grad_in, *refs):
    state, refs = refs[:6], refs[6:]
    a_ref, b_ref, factor_ref, grad_ref, down_win, up_win, sem = refs
    replicas = grad_ref.shape[0]
    down_rows, window = a_ref.shape[2], down_win.shape[2]
    up_rows = up_win.shape[1]
    replica = lax.axis_index("dp")
    share = replica * down_rows
    size = down_rows * replicas
    copies = [pltpu.make_async_copy(grad_in, grad_ref, sem.at[6])]
    for i in range(3):
        down, up = state[i], state[3 + i]
        if window != down_rows:
            lane = pl.multiple_of(first_lane(share, window, size), LANES)
            down = down.at[:, pl.ds(lane, window)]
            up = up.at[pl.ds(pl.multiple_of(replica * up_rows, up_rows), up_rows)]
        copies.append(pltpu.make_async_copy(down, down_win.at[i], sem.at[i]))
        copies.append(pltpu.make_async_copy(up, up_win.at[i], sem.at[3 + i]))
    for copy in copies:
        copy.start()
    copies[0].wait()
    total = jnp.sum(grad_ref[...].astype(jnp.float32), axis=0) / replicas
    for copy in copies[1:]:
        copy.wait()

    def down():
        if window == down_rows:
            return [down_win[i] for i in range(3)]
        shift = window - (share - first_lane(share, window, size))
        return [pltpu.roll(down_win[i], shift, 1)[:, :down_rows] for i in range(3)]

    rounded = update(total, down, lambda: [up_win[i] for i in range(3)], a_ref, b_ref)
    for i in range(replicas):
        factor_ref[i] = rounded


def factor_a(refs, down_rows):
    pieces = []
    for ref in refs:
        for i in range(ref.shape[0]):
            if down_rows % 16 == 0:
                pieces.append(ref[i, :down_rows, :])
            else:
                pieces.append(ref[i].astype(jnp.float32)[:down_rows])
    return jnp.concatenate(pieces, axis=0).astype(jnp.bfloat16)


def factor_b(packed, part, parts, strip, up_rows):
    pieces = [
        packed[i].astype(jnp.float32)[strip * up_rows : (strip + 1) * up_rows]
        for i in range(packed.shape[0])
    ]
    value = jnp.concatenate(pieces, axis=0)
    rows = [jnp.where(part == j, value, jnp.zeros_like(value)) for j in range(parts)]
    return jnp.concatenate(rows, axis=0).astype(jnp.bfloat16)


def merge(scale, block, a, b):
    change = jnp.dot(a, b, preferred_element_type=jnp.float32)
    return (block.astype(jnp.float32) + scale * change).astype(jnp.bfloat16)


def multiply(xs, weights, store):
    rows = xs[0].shape[0]
    tile = rows // 2 if rows % 32 == 0 else rows

    @pl.loop(0, rows // tile)
    def _(i):
        at = pl.ds(pl.multiple_of(i * tile, tile), tile)
        value, first = None, 0
        for x in xs:
            size = x.shape[1]
            part = jnp.dot(
                x[at, :], weights[first : first + size, :], preferred_element_type=jnp.float32
            )
            value, first = part if value is None else value + part, first + size
        store(i * tile, tile, value)


def up_factor(static, packed, owner):
    _, parts, up_rows, strips, columns = static
    part = owner * columns // KEY_VALUE_WIDTH
    return jnp.concatenate(
        [factor_b(packed, part, parts, strip, up_rows) for strip in strips], axis=1
    )


def outside_kernel(static, chips, step, turn, b_ref, x, *refs):
    own_f, sibling_f = refs[:FACTOR_PIECES], refs[FACTOR_PIECES : 2 * FACTOR_PIECES]
    blocks, (weights, product) = refs[2 * FACTOR_PIECES :], refs[-2:]
    strips = static[3]
    features = blocks[0].shape[0]
    down_rows = own_f[0].shape[1] - b_ref.shape[1]
    shares = FACTOR_PIECES * own_f[0].shape[0]
    place, replica = lax.axis_index("tensor"), lax.axis_index("dp")
    owner = (place // CORES - step + chips) % chips * CORES + place % CORES
    b = up_factor(static, b_ref[:shares], owner)
    own_a, sibling_a = factor_a(own_f, down_rows), factor_a(sibling_f, down_rows)
    for k, strip in enumerate(strips):
        mine, other = blocks[2 * k : 2 * k + 2]
        even = replica // turn[strip] % 2 == 0
        lanes = slice(k * LANES, (k + 1) * LANES)
        block = jnp.where(even, mine[...], other[...])
        weights[:features, lanes] = merge(static[0], block, own_a, b[:, lanes])
        block = jnp.where(even, other[...], mine[...])
        weights[features:, lanes] = merge(static[0], block, sibling_a, b[:, lanes])
    more_kernel(x, weights, product)


def more_kernel(*refs):
    xs, (weights, product) = refs[:-2], refs[-2:]

    def store(first, size, value):
        product[pl.ds(first, size), :] = value.astype(product.dtype)

    multiply(xs, weights, store)


def own_kernel(static, own_block, sibling_block, *refs):
    own_f, sibling_f = refs[:FACTOR_PIECES], refs[FACTOR_PIECES : 2 * FACTOR_PIECES]
    refs = refs[2 * FACTOR_PIECES :]
    xs, weights = [refs[:1], refs[1:3]], refs[-1]
    outs = refs[len(refs) - 1 - static[5] : -1]
    features = own_block.shape[0]
    wide = outs[0].shape[1]
    down_rows = own_f[0].shape[1] - len(static[3]) * static[2]
    b = jnp.concatenate([piece[:, down_rows:] for piece in own_f], axis=0)
    b = up_factor(static[:5], b, lax.axis_index("tensor"))
    for at, factors, block in ((0, own_f, own_block), (features, sibling_f, sibling_block)):
        weights[at : at + features] = merge(static[0], block[...], factor_a(factors, down_rows), b)
    for h, x in enumerate(xs):

        def store(first, size, value):
            to = pl.ds(pl.multiple_of(h * x[0].shape[0] + first, 16), size)
            for k, out in enumerate(outs):
                out[to, :] = value[:, k * wide : (k + 1) * wide]

        multiply(x, weights, store)


def finish_kernel(sources, first, own, inv, *refs):
    rows = pl.ds(first, refs[-1].shape[0])
    total = own[rows, :]
    for value in refs[:sources]:
        total = total + value[...].astype(jnp.float32)
    refs[-1][...] = (total * inv[rows, :1]).astype(refs[-1].dtype)


def finish(own, inv_rms, received, at, shape, before):
    block = received[0].shape
    operands = [own, inv_rms] + received
    in_specs = in_vmem(len(operands))
    aliases = {}
    if before is not None:
        aliases = {len(operands): 0}
        in_specs += anywhere(1)
        operands.append(before)
    return pl.pallas_call(
        functools.partial(finish_kernel, len(received), at[0] * block[0]),
        grid=(1,),
        out_shape=jax.ShapeDtypeStruct(shape, jnp.bfloat16),
        in_specs=in_specs,
        out_specs=pl.BlockSpec(block, lambda i: at),
        input_output_aliases=aliases,
        compiler_params=params(),
    )(*operands)


def body(
    prompt_hidden_input,
    input_norm_gain,
    frozen_key_value,
    down_factor_matrix,
    down_moment_first,
    down_moment_second,
    up_factor_matrix,
    up_moment_first,
    up_moment_second,
    down_gradient,
    up_gradient,
):
    n_dp = lax.axis_size("dp")
    n_tensor = lax.axis_size("tensor")
    chips = n_tensor // CORES
    replica = lax.axis_index("dp")
    tokens, features = prompt_hidden_input.shape
    width, columns = frozen_key_value.shape
    rank = up_factor_matrix.shape[0]
    parts = down_factor_matrix.shape[1]
    factors = parts * rank
    strips = columns // LANES
    down_rows = features // n_dp
    up_rows = rank // n_dp
    packed_rows = down_rows + up_rows * strips
    steps = range(1, chips)
    f32, bf16 = jnp.float32, jnp.bfloat16

    def to_sibling(value):
        return lax.ppermute(value, "tensor", [(t, t ^ 1) for t in range(n_tensor)])

    def to_chip(value, step):
        pairs = [
            (CORES * q + k, CORES * ((q + step) % chips) + k)
            for q in range(chips)
            for k in range(CORES)
        ]
        return lax.ppermute(value, "tensor", pairs)

    def by_rank(value):
        return jnp.transpose(value, (1, 2, 0)).reshape(factors, features)

    down_sent = by_rank(down_gradient[0])
    down_state = [by_rank(v) for v in (down_factor_matrix, down_moment_first, down_moment_second)]
    up_state = [up_factor_matrix, up_moment_first, up_moment_second]
    shares = jax.ShapeDtypeStruct((n_dp, packed_rows, LANES), bf16)
    window = pl.cdiv(down_rows + LANES, LANES) * LANES
    aligned = features % LANES == 0 and window <= features
    aligned = aligned and up_rows % 8 == 0 and down_rows % 16 == 0
    window = window if aligned else down_rows
    turns = [1, 2] if n_dp % 4 == 0 else [1, 1]
    turn = [turns[strip % 2] for strip in range(strips)]
    halves = min(COLUMN_HALVES, strips)
    wide = columns // halves
    groups = [range(k * strips // halves, (k + 1) * strips // halves) for k in range(halves)]
    out_shape = (shares,) + tuple(
        jax.ShapeDtypeStruct((len(group), features, LANES), bf16)
        for group in groups
        for _ in steps
    )
    packed, *taken = pl.pallas_call(
        functools.partial(begin_kernel, chips, turn),
        out_shape=out_shape,
        in_specs=anywhere(3),
        out_specs=tuple(anywhere(len(out_shape))),
        scratch_shapes=[
            pltpu.VMEM((factors, features), f32),
            pltpu.VMEM((rank, columns), f32),
            pltpu.VMEM(shares.shape, bf16),
            pltpu.VMEM((len(steps) * strips, features, LANES), bf16),
            pltpu.SemaphoreType.DMA((2 + len(steps) * strips,)),
            pltpu.SemaphoreType.DMA((n_dp + len(steps) * strips,)),
        ],
        compiler_params=pltpu.CompilerParams(vmem_limit_bytes=LARGE_VMEM_BYTES),
    )(down_sent, up_gradient[0], frozen_key_value)
    exchanged = lax.all_to_all(packed, "dp", 0, 0, tiled=True)
    if not aligned:
        down_state = [
            lax.dynamic_slice_in_dim(v, replica * down_rows, down_rows, 1) for v in down_state
        ]
        up_state = [lax.dynamic_slice_in_dim(v, replica * up_rows, up_rows, 0) for v in up_state]
    mine = []

    def send_half(half, after):
        blocks = taken[half * len(steps) : (half + 1) * len(steps)]
        if after is not None:
            blocks, _ = lax.optimization_barrier((blocks, after))
        mine.append([to_chip(value, step) for value, step in zip(blocks, steps)])

    send_half(0, None)

    gain = input_norm_gain[None, :]
    some = tokens // TOKEN_HALVES
    operands = [prompt_hidden_input, to_sibling(prompt_hidden_input), gain, to_sibling(gain)]

    def prepared(half, before, in_place, limit):
        if in_place:
            x_shape = (jax.ShapeDtypeStruct((some, CORES * features), bf16),)
            x_specs = tuple(in_vmem(1))
        else:
            x_shape = (jax.ShapeDtypeStruct((some, features), bf16),) * 2
            x_specs = tuple(anywhere(2))
        *x, squares = pl.pallas_call(
            functools.partial(prepare_kernel, half * some),
            out_shape=x_shape
            + (jax.ShapeDtypeStruct(((half + 1) * some // LANES, LANES), f32),),
            in_specs=anywhere(2) + in_vmem(2 + len(before)),
            out_specs=x_specs + tuple(in_vmem(1)),
            scratch_shapes=[
                pltpu.VMEM((some, features), bf16),
                pltpu.VMEM((some, features), bf16),
                pltpu.VMEM((some, LANES), f32),
                pltpu.SemaphoreType.DMA((4 * pl.cdiv(some, LANES),)),
            ],
            compiler_params=pltpu.CompilerParams(vmem_limit_bytes=limit),
        )(*operands, *before)
        return x, squares

    x0, squares = prepared(0, [], True, PREPARE_VMEM_BYTES)
    x1, squares = prepared(1, [squares], False, LARGE_VMEM_BYTES)
    exchanged, squares = lax.optimization_barrier((exchanged, squares))
    a_next, b_next, sent = pl.pallas_call(
        adam_kernel,
        out_shape=(
            jax.ShapeDtypeStruct((3, factors, down_rows), f32),
            jax.ShapeDtypeStruct((3, up_rows, columns), f32),
            shares,
        ),
        in_specs=anywhere(7),
        out_specs=tuple(in_vmem(3)),
        scratch_shapes=[
            pltpu.VMEM((n_dp, packed_rows, LANES), bf16),
            pltpu.VMEM((3, factors, window), f32),
            pltpu.VMEM((3, up_rows, columns), f32),
            pltpu.SemaphoreType.DMA((7,)),
        ],
        compiler_params=pltpu.CompilerParams(vmem_limit_bytes=LARGE_VMEM_BYTES),
    )(exchanged, *down_state, *up_state)
    own_f = lax.all_to_all(sent, "dp", 0, 0, tiled=True)
    for half in range(1, halves):
        send_half(half, (mine[-1], sent))
    a_next = jnp.transpose(a_next.reshape(3, parts, rank, down_rows), (0, 3, 1, 2))

    outside = [[] for _ in range(strips)]

    def swap_half(half, after):
        for value in mine[half]:
            value, _ = lax.optimization_barrier((value, after))
            split = pl.pallas_call(
                split_kernel,
                out_shape=(jax.ShapeDtypeStruct((features, LANES), bf16),) * len(groups[half]),
                in_specs=in_vmem(1),
                out_specs=tuple(in_vmem(len(groups[half]))),
                compiler_params=params(),
            )(value)
            for piece, strip in zip(split, groups[half]):
                pairs = [(i, i ^ turn[strip]) for i in range(n_dp)]
                outside[strip].append((piece, lax.ppermute(piece, "dp", pairs)))

    swap_half(0, sent)
    up_packed = packed_rows - down_rows
    more = pl.cdiv(3 * (tokens // LANES), up_packed)
    piece = jax.ShapeDtypeStruct((n_dp // FACTOR_PIECES, packed_rows, LANES), bf16)
    message, *pieces = pl.pallas_call(
        message_kernel,
        out_shape=(jax.ShapeDtypeStruct((n_dp + more, up_packed, LANES), bf16),)
        + (piece,) * FACTOR_PIECES,
        in_specs=anywhere(2),
        out_specs=tuple(in_vmem(1 + FACTOR_PIECES)),
        scratch_shapes=[
            pltpu.VMEM(squares.shape, f32),
            pltpu.SemaphoreType.DMA((2 + FACTOR_PIECES,)),
        ],
        compiler_params=params(),
    )(own_f, squares)
    messages = [to_chip(message, step) for step in steps]
    sibling_f = [to_sibling(piece) for piece in pieces]

    inv_rms = pl.pallas_call(
        functools.partial(inverse_kernel, width, n_dp),
        out_shape=jax.ShapeDtypeStruct((tokens, LANES), f32),
        in_specs=in_vmem(chips),
        out_specs=in_vmem(1)[0],
        compiler_params=params(),
    )(squares, *messages)

    scale = 0.5 / math.sqrt(width * rank)

    received = {}
    after = []
    weights_shape = jax.ShapeDtypeStruct((CORES * features, wide), bf16)
    product_shape = jax.ShapeDtypeStruct((some, wide), bf16)
    for half, group in enumerate(groups):
        static = (scale, parts, up_rows, group, columns)
        if half > 0:
            swap_half(half, products[0])
        for step in steps:
            blocks = [value for strip in group for value in outside[strip][step - 1]]
            weights, product = pl.pallas_call(
                functools.partial(outside_kernel, static, chips, step, turn),
                out_shape=(weights_shape, product_shape),
                in_specs=in_vmem(2 + 2 * FACTOR_PIECES + len(blocks)) + anywhere(len(after)),
                out_specs=tuple(in_vmem(2)),
                compiler_params=params(),
            )(messages[step - 1], *x0, *pieces, *sibling_f, *blocks, *after)
            received.setdefault((0, half), []).append(to_chip(product, chips - step))
            second = pl.pallas_call(
                more_kernel,
                out_shape=product_shape,
                in_specs=in_vmem(3),
                out_specs=in_vmem(1)[0],
                compiler_params=params(),
            )(*x1, weights)
            products = [product, second]
            after = [second]
            received.setdefault((1, half), []).append(to_chip(second, chips - step))
        if half == 0:
            after = [received[0, 0][0]]

    after.append(received[1, 0][0])
    static = (scale, parts, up_rows, range(strips), columns, halves)
    totals = pl.pallas_call(
        functools.partial(own_kernel, static),
        out_shape=(jax.ShapeDtypeStruct((tokens, wide), f32),) * halves,
        grid=(1,),
        in_specs=[
            pl.BlockSpec((features, columns), lambda i: (lax.axis_index("tensor"), 0)),
            pl.BlockSpec((features, columns), lambda i: (lax.axis_index("tensor") ^ 1, 0)),
        ]
        + in_vmem(2 * FACTOR_PIECES + 3)
        + anywhere(len(after)),
        out_specs=tuple(in_vmem(halves)),
        scratch_shapes=[pltpu.VMEM((CORES * features, columns), bf16)],
        compiler_params=params(),
        cost_estimate=pl.CostEstimate(
            flops=2 * tokens * CORES * features * columns,
            bytes_accessed=4 * tokens * features,
            transcendentals=0,
        ),
    )(frozen_key_value, frozen_key_value, *pieces, *sibling_f, *x0, *x1, *after)

    keys_values = None
    for at, values in received.items():
        keys_values = finish(
            totals[at[1]], inv_rms, values, at, (tokens, columns), keys_values
        )
    return (a_next, b_next, keys_values)


def solution(mesh):
    placed = (
        P("dp", "tensor"),
        P("tensor"),
        P(None, "tensor"),
        P("tensor", None, None),
        P("tensor", None, None),
        P("tensor", None, None),
        P(None, "tensor"),
        P(None, "tensor"),
        P(None, "tensor"),
        P("dp", "tensor", None, None),
        P("dp", None, "tensor"),
    )
    return jax.shard_map(
        body,
        mesh=mesh,
        in_specs=placed,
        out_specs=(
            P(None, ("tensor", "dp"), None, None),
            P(None, "dp", "tensor"),
            P("dp", "tensor"),
        ),
        check_vma=False,
    )
```

```python
import functools
import math

import jax
import jax.numpy as jnp
from jax import lax
from jax.experimental import pallas as pl
from jax.experimental.pallas import tpu as pltpu
from jax.sharding import PartitionSpec as P

KEY_VALUE_WIDTH = 1024
STEP = 100
CORES = 2
LANES = 128
COLUMN_HALVES = 2
TOKEN_HALVES = 2
FACTOR_PIECES = 2
VMEM_BYTES = 16 * 2**20
LARGE_VMEM_BYTES = 58 * 2**20
PREPARE_VMEM_BYTES = 49 * 2**20


def adaptive_moment_update(param, first, second, grad_mean):
    first_new = 0.9 * first + 0.1 * grad_mean
    second_new = 0.999 * second + 0.001 * grad_mean * grad_mean
    step_size = first_new / (1.0 - 0.9**STEP) / (jnp.sqrt(second_new / (1.0 - 0.999**STEP)) + 1e-08)
    return (param - 0.1 * step_size, first_new, second_new)


def in_vmem(count):
    return [pl.BlockSpec(memory_space=pltpu.VMEM)] * count


def anywhere(count):
    return [pl.BlockSpec(memory_space=pl.ANY)] * count


SCALARS = pl.BlockSpec(memory_space=pltpu.SMEM)


def params(**more):
    return pltpu.CompilerParams(vmem_limit_bytes=VMEM_BYTES, **more)


def pack(down, up, out_ref, ready):
    shares = out_ref.shape[0]
    down = down.T
    down_rows, up_rows = down.shape[0] // shares, up.shape[0] // shares
    for i in range(shares):
        pieces = [down[i * down_rows : (i + 1) * down_rows]]
        for k in range(up.shape[1] // LANES):
            pieces.append(up[i * up_rows : (i + 1) * up_rows, k * LANES : (k + 1) * LANES])
        out_ref[i] = jnp.concatenate(pieces, axis=0).astype(jnp.bfloat16)
        ready(i)


def first_lane(share, window, size):
    return jnp.minimum(share // LANES * LANES, size - window)


def begin_kernel(chips, turn, down_ref, up_ref, weights_ref, packed, *refs):
    outs, (down, up, blocks, strips, sem, sem_out) = refs[:-6], refs[-6:]
    features = strips.shape[1]
    place, replica = lax.axis_index("tensor"), lax.axis_index("dp")
    chip, core = place // CORES, place % CORES
    copies, back = [], []

    def add(source, target):
        copies.append(pltpu.make_async_copy(source, target, sem.at[len(copies)]))
        copies[-1].start()

    def add_back(source, target):
        back.append(pltpu.make_async_copy(source, target, sem_out.at[len(back)]))
        back[-1].start()

    add(down_ref, down)
    add(up_ref, up)
    targets = []
    for i, out in enumerate(outs):
        step, first = 1 + i % (chips - 1), i // (chips - 1) * out.shape[0]
        for k in range(out.shape[0]):
            half = (core + replica // turn[first + k]) % 2
            row = ((chip + step) % chips * CORES + half) * features
            add(
                weights_ref.at[
                    pl.ds(pl.multiple_of(row, features), features),
                    pl.ds((first + k) * LANES, LANES),
                ],
                strips.at[len(targets)],
            )
            targets.append(out.at[k])
    copies[0].wait()
    copies[1].wait()
    pack(down[...], up[...], blocks, lambda i: add_back(blocks.at[i], packed.at[i]))
    for i, target in enumerate(targets):
        copies[2 + i].wait()
        add_back(strips.at[i], target)
    for copy in back:
        copy.wait()


def split_kernel(in_ref, *outs):
    for k, out in enumerate(outs):
        out[...] = in_ref[k]


def prepare_kernel(first, own_in, sibling_in, own_gain, sibling_gain, *refs):
    own, sibling, squares, sem = refs[-4:]
    rows, features = own.shape
    together = refs[-6].shape[1] > features
    outs, sums_ref = refs[-6 if together else -7 : -5], refs[-5]
    before = refs[: -6 if together else -7]
    block = LANES if rows % LANES == 0 else rows
    tile = 16 if block % 16 == 0 else block
    count = rows // block
    raw = ((own_in, own), (sibling_in, sibling))
    loads = [
        [
            pltpu.make_async_copy(
                source.at[pl.ds(first + k * block, block)],
                target.at[pl.ds(k * block, block)],
                sem.at[2 * k + side],
            )
            for side, (source, target) in enumerate(raw)
        ]
        for k in range(count)
    ]
    for pair in loads:
        for copy in pair:
            copy.start()
    stores = []
    for k in range(count):
        for copy in loads[k]:
            copy.wait()

        @pl.loop(0, block // tile, unroll=2)
        def _(i):
            at = pl.ds(pl.multiple_of(k * block + i * tile, tile), tile)
            total = None
            for side, (ref, gain) in enumerate(((own, own_gain), (sibling, sibling_gain))):
                value = ref[at, :].astype(jnp.float32)
                scaled = (value * gain[...]).astype(ref.dtype)
                if together:
                    outs[0][at, side * features : (side + 1) * features] = scaled
                else:
                    ref[at, :] = scaled
                total = value * value if total is None else total + value * value
            total = jnp.sum(total, axis=1, keepdims=True)
            squares[at, :] = jnp.broadcast_to(total, (tile, LANES))

        if not together:
            part = pl.ds(k * block, block)
            for side, (source, out) in enumerate(((own, outs[0]), (sibling, outs[1]))):
                place = sem.at[2 * (count + k) + side]
                stores.append(pltpu.make_async_copy(source.at[part], out.at[part], place))
                stores[-1].start()
    done = 0
    for ref in before:
        sums_ref[: ref.shape[0]] = ref[...]
        done = ref.shape[0]
    for i in range(rows // LANES):
        row = squares[i * LANES : (i + 1) * LANES, :].T[:1]
        sums_ref[done + i : done + i + 1] = row
    for copy in stores:
        copy.wait()


def message_kernel(factor_ref, sums_ref, out_ref, *refs):
    pieces, (sums, sem) = refs[:-2], refs[-2:]
    shares, up_rows = factor_ref.shape[0], out_ref.shape[1]
    sums_copy = pltpu.make_async_copy(sums_ref, sums, sem.at[1 + len(pieces)])
    sums_copy.start()
    copies = [
        pltpu.make_async_copy(
            factor_ref.at[:, pl.ds(factor_ref.shape[1] - up_rows, up_rows)],
            out_ref.at[pl.ds(0, shares)],
            sem.at[0],
        )
    ]
    for k, piece in enumerate(pieces):
        size = piece.shape[0]
        copies.append(
            pltpu.make_async_copy(factor_ref.at[pl.ds(k * size, size)], piece, sem.at[1 + k])
        )
    for copy in copies:
        copy.start()
    sums_copy.wait()
    left = sums[...]
    terms = []
    for _ in range(3):
        terms.append(left.astype(jnp.bfloat16).astype(jnp.float32))
        left = left - terms[-1]
    rest = (out_ref.shape[0] - shares) * up_rows - 3 * left.shape[0]
    if rest > 0:
        terms.append(jnp.zeros((rest, LANES), jnp.float32))
    rows = jnp.concatenate(terms, axis=0)
    for i in range(out_ref.shape[0] - shares):
        out_ref[shares + i] = rows[i * up_rows : (i + 1) * up_rows].astype(jnp.bfloat16)
    for copy in copies:
        copy.wait()


def inverse_kernel(width, shares, sums_ref, *refs):
    messages, out = refs[:-1], refs[-1]
    total = sums_ref[...]
    count = total.shape[0]
    for ref in messages:
        rows = [ref[i].astype(jnp.float32) for i in range(shares, ref.shape[0])]
        rows = jnp.concatenate(rows, axis=0)
        total += rows[:count] + rows[count : 2 * count] + rows[2 * count : 3 * count]
    inverse = lax.rsqrt(total / width + 1e-06)
    for i in range(count):
        out[i * LANES : (i + 1) * LANES, :] = jnp.broadcast_to(
            inverse[i : i + 1], (LANES, LANES)
        ).T


def update(total, down, up, a_ref, b_ref, folded):
    down_rows = a_ref.shape[2]
    up_rows, columns = b_ref.shape[1:]
    strips = columns // LANES
    down_mean = total[:down_rows].T
    up_mean = jnp.concatenate(
        [total[down_rows + k * up_rows : down_rows + (k + 1) * up_rows] for k in range(strips)],
        axis=1,
    )
    p, m, v = adaptive_moment_update(*down(), down_mean)
    a_ref[0], a_ref[1], a_ref[2] = p, m, v
    factors = fold(p.T, columns) if folded else [p.T]
    p, m, v = adaptive_moment_update(*up(), up_mean)
    b_ref[0], b_ref[1], b_ref[2] = p, m, v
    factors[0] = jnp.concatenate(
        [factors[0]] + [p[:, k * LANES : (k + 1) * LANES] for k in range(strips)], axis=0
    )
    return [value.astype(jnp.bfloat16) for value in factors]


def fold(value, columns):
    rows = value.shape[0] // 2
    turned = pltpu.roll(value, LANES // 2, 1)
    left = lax.broadcasted_iota(jnp.int32, (rows, LANES), 1) < LANES // 2
    low = jnp.where(left, value[:rows], turned[rows:])
    high = jnp.where(left, turned[:rows], value[rows:])
    own_low = lax.axis_index("tensor") * columns // KEY_VALUE_WIDTH == 0
    return [jnp.where(own_low, high, low), jnp.where(own_low, low, high)]


def adam_kernel(grad_in, *refs):
    state, refs = refs[:6], refs[6:]
    a_ref, b_ref, factor_refs = refs[0], refs[1], refs[2:-4]
    grad_ref, down_win, up_win, sem = refs[-4:]
    replicas = grad_ref.shape[0]
    down_rows, window = a_ref.shape[2], down_win.shape[2]
    up_rows = up_win.shape[1]
    replica = lax.axis_index("dp")
    share = replica * down_rows
    size = down_rows * replicas
    copies = [pltpu.make_async_copy(grad_in, grad_ref, sem.at[6])]
    for i in range(3):
        down, up = state[i], state[3 + i]
        if window != down_rows:
            lane = pl.multiple_of(first_lane(share, window, size), LANES)
            down = down.at[:, pl.ds(lane, window)]
            up = up.at[pl.ds(pl.multiple_of(replica * up_rows, up_rows), up_rows)]
        copies.append(pltpu.make_async_copy(down, down_win.at[i], sem.at[i]))
        copies.append(pltpu.make_async_copy(up, up_win.at[i], sem.at[3 + i]))
    for copy in copies:
        copy.start()
    copies[0].wait()
    total = jnp.sum(grad_ref[...].astype(jnp.float32), axis=0) / replicas
    for copy in copies[1:]:
        copy.wait()

    def down():
        if window == down_rows:
            return [down_win[i] for i in range(3)]
        shift = window - (share - first_lane(share, window, size))
        return [pltpu.roll(down_win[i], shift, 1)[:, :down_rows] for i in range(3)]

    folded = len(factor_refs) > 1
    rounded = update(total, down, lambda: [up_win[i] for i in range(3)], a_ref, b_ref, folded)
    for factor_ref, value in zip(factor_refs, rounded):
        for i in range(replicas):
            factor_ref[i] = value


def factor_a(refs, down_rows):
    pieces = []
    for ref in refs:
        for i in range(ref.shape[0]):
            if down_rows % 16 == 0:
                pieces.append(ref[i, :down_rows, :])
            else:
                pieces.append(ref[i].astype(jnp.float32)[:down_rows])
    return jnp.concatenate(pieces, axis=0).astype(jnp.bfloat16)


def factor_b(packed, part, parts, strip, up_rows):
    pieces = [
        packed[i].astype(jnp.float32)[strip * up_rows : (strip + 1) * up_rows]
        for i in range(packed.shape[0])
    ]
    value = jnp.concatenate(pieces, axis=0)
    rows = [jnp.where(part == j, value, jnp.zeros_like(value)) for j in range(parts)]
    return jnp.concatenate(rows, axis=0).astype(jnp.bfloat16)


def change_of(refs, a_rows, folded, b):
    a = factor_a(refs, a_rows)
    halves = [jnp.dot(a, value, preferred_element_type=jnp.float32) for value in b]
    if not folded:
        return halves[0]
    pieces = []
    for first in range(0, a.shape[0], a_rows):
        pieces += [value[first : first + a_rows] for value in halves]
    return jnp.concatenate(pieces, axis=0)


def merge(scale, block, change):
    return (block.astype(jnp.float32) + scale * change).astype(jnp.bfloat16)


def multiply(xs, weights, store):
    rows = xs[0].shape[0]
    tile = rows // 2 if rows % 32 == 0 else rows

    @pl.loop(0, rows // tile)
    def _(i):
        at = pl.ds(pl.multiple_of(i * tile, tile), tile)
        value, first = None, 0
        for x in xs:
            size = x.shape[1]
            part = jnp.dot(
                x[at, :], weights[first : first + size, :], preferred_element_type=jnp.float32
            )
            value, first = part if value is None else value + part, first + size
        store(i * tile, tile, value)


def up_factor(static, packed, owner, strip):
    _, parts, up_rows, _, columns, folded = static
    which = range(parts) if folded else [owner * columns // KEY_VALUE_WIDTH]
    return [factor_b(packed, part, parts, strip, up_rows) for part in which]


def outside_kernel(static, chips, step, turn, pieces, b_ref, x, *refs):
    own_f, sibling_f = refs[:pieces], refs[pieces : 2 * pieces]
    blocks, (weights, product) = refs[2 * pieces :], refs[-2:]
    strips, folded = static[3], static[5]
    features = blocks[0].shape[0]
    a_rows = own_f[0].shape[1] - b_ref.shape[1]
    shares = pieces * own_f[0].shape[0]
    place, replica = lax.axis_index("tensor"), lax.axis_index("dp")
    owner = (place // CORES - step + chips) % chips * CORES + place % CORES
    for k, strip in enumerate(strips):
        b = up_factor(static, b_ref[:shares], owner, strip)
        mine, other = blocks[2 * k : 2 * k + 2]
        even = replica // turn[strip] % 2 == 0
        lanes = slice(k * LANES, (k + 1) * LANES)
        block = jnp.where(even, mine[...], other[...])
        change = change_of(own_f, a_rows, folded, b)
        weights[:features, lanes] = merge(static[0], block, change)
        block = jnp.where(even, other[...], mine[...])
        change = change_of(sibling_f, a_rows, folded, b)
        weights[features:, lanes] = merge(static[0], block, change)
    more_kernel(x, weights, product)


def more_kernel(*refs):
    xs, (weights, product) = refs[:-2], refs[-2:]

    def store(first, size, value):
        product[pl.ds(first, size), :] = value.astype(product.dtype)

    multiply(xs, weights, store)


def own_kernel(static, pieces, halves, own_block, sibling_block, *refs):
    own_f, sibling_f = refs[:pieces], refs[pieces : 2 * pieces]
    b_refs, refs = refs[2 * pieces : 3 * pieces], refs[3 * pieces :]
    xs, weights = [refs[:1], refs[1:3]], refs[-1]
    outs = refs[len(refs) - 1 - halves : -1]
    features = own_block.shape[0]
    wide = outs[0].shape[1]
    strips, folded = static[3], static[5]
    up_packed = len(strips) * static[2]
    a_rows = own_f[0].shape[1] if folded else own_f[0].shape[1] - up_packed
    up_at = b_refs[0].shape[1] - up_packed
    packed = jnp.concatenate([ref[:, up_at:] for ref in b_refs], axis=0)
    b = [up_factor(static, packed, lax.axis_index("tensor"), strip) for strip in strips]
    b = [jnp.concatenate(values, axis=1) for values in zip(*b)]
    for at, factors, block in ((0, own_f, own_block), (features, sibling_f, sibling_block)):
        change = change_of(factors, a_rows, folded, b)
        weights[at : at + features] = merge(static[0], block[...], change)
    for h, x in enumerate(xs):

        def store(first, size, value):
            to = pl.ds(pl.multiple_of(h * x[0].shape[0] + first, 16), size)
            for k, out in enumerate(outs):
                out[to, :] = value[:, k * wide : (k + 1) * wide]

        multiply(x, weights, store)


def finish_kernel(sources, first, own, inv, *refs):
    rows = pl.ds(first, refs[-1].shape[0])
    total = own[rows, :]
    for value in refs[:sources]:
        total = total + value[...].astype(jnp.float32)
    refs[-1][...] = (total * inv[rows, :1]).astype(refs[-1].dtype)


def finish(own, inv_rms, received, at, shape, before):
    block = received[0].shape
    operands = [own, inv_rms] + received
    in_specs = in_vmem(len(operands))
    aliases = {}
    if before is not None:
        aliases = {len(operands): 0}
        in_specs += anywhere(1)
        operands.append(before)
    return pl.pallas_call(
        functools.partial(finish_kernel, len(received), at[0] * block[0]),
        grid=(1,),
        out_shape=jax.ShapeDtypeStruct(shape, jnp.bfloat16),
        in_specs=in_specs,
        out_specs=pl.BlockSpec(block, lambda i: at),
        input_output_aliases=aliases,
        compiler_params=params(),
    )(*operands)


def body(
    prompt_hidden_input,
    input_norm_gain,
    frozen_key_value,
    down_factor_matrix,
    down_moment_first,
    down_moment_second,
    up_factor_matrix,
    up_moment_first,
    up_moment_second,
    down_gradient,
    up_gradient,
):
    n_dp = lax.axis_size("dp")
    n_tensor = lax.axis_size("tensor")
    chips = n_tensor // CORES
    replica = lax.axis_index("dp")
    tokens, features = prompt_hidden_input.shape
    width, columns = frozen_key_value.shape
    rank = up_factor_matrix.shape[0]
    parts = down_factor_matrix.shape[1]
    factors = parts * rank
    strips = columns // LANES
    down_rows = features // n_dp
    up_rows = rank // n_dp
    up_packed = up_rows * strips
    packed_rows = down_rows + up_packed
    folded = chips == parts == 2 and factors == LANES and down_rows % 32 == 0
    a_rows = down_rows // 2 if folded else down_rows
    n_pieces = 1 if folded else FACTOR_PIECES
    steps = range(1, chips)
    f32, bf16 = jnp.float32, jnp.bfloat16

    def to_sibling(value):
        return lax.ppermute(value, "tensor", [(t, t ^ 1) for t in range(n_tensor)])

    def to_chip(value, step):
        pairs = [
            (CORES * q + k, CORES * ((q + step) % chips) + k)
            for q in range(chips)
            for k in range(CORES)
        ]
        return lax.ppermute(value, "tensor", pairs)

    def by_rank(value):
        return jnp.transpose(value, (1, 2, 0)).reshape(factors, features)

    down_sent = by_rank(down_gradient[0])
    down_state = [by_rank(v) for v in (down_factor_matrix, down_moment_first, down_moment_second)]
    up_state = [up_factor_matrix, up_moment_first, up_moment_second]
    shares = jax.ShapeDtypeStruct((n_dp, packed_rows, LANES), bf16)
    window = pl.cdiv(down_rows + LANES, LANES) * LANES
    aligned = features % LANES == 0 and window <= features
    aligned = aligned and up_rows % 8 == 0 and down_rows % 16 == 0
    window = window if aligned else down_rows
    turns = [1, 2] if n_dp % 4 == 0 else [1, 1]
    turn = [turns[strip % 2] for strip in range(strips)]
    halves = min(COLUMN_HALVES, strips)
    wide = columns // halves
    groups = [range(k * strips // halves, (k + 1) * strips // halves) for k in range(halves)]
    out_shape = (shares,) + tuple(
        jax.ShapeDtypeStruct((len(group), features, LANES), bf16)
        for group in groups
        for _ in steps
    )
    packed, *taken = pl.pallas_call(
        functools.partial(begin_kernel, chips, turn),
        out_shape=out_shape,
        in_specs=anywhere(3),
        out_specs=tuple(anywhere(len(out_shape))),
        scratch_shapes=[
            pltpu.VMEM((factors, features), f32),
            pltpu.VMEM((rank, columns), f32),
            pltpu.VMEM(shares.shape, bf16),
            pltpu.VMEM((len(steps) * strips, features, LANES), bf16),
            pltpu.SemaphoreType.DMA((2 + len(steps) * strips,)),
            pltpu.SemaphoreType.DMA((n_dp + len(steps) * strips,)),
        ],
        compiler_params=pltpu.CompilerParams(vmem_limit_bytes=LARGE_VMEM_BYTES),
    )(down_sent, up_gradient[0], frozen_key_value)
    exchanged = lax.all_to_all(packed, "dp", 0, 0, tiled=True)
    if not aligned:
        down_state = [
            lax.dynamic_slice_in_dim(v, replica * down_rows, down_rows, 1) for v in down_state
        ]
        up_state = [lax.dynamic_slice_in_dim(v, replica * up_rows, up_rows, 0) for v in up_state]
    mine = []

    def send_half(half, after):
        blocks = taken[half * len(steps) : (half + 1) * len(steps)]
        if after is not None:
            blocks, _ = lax.optimization_barrier((blocks, after))
        mine.append([to_chip(value, step) for value, step in zip(blocks, steps)])

    send_half(0, None)

    gain = input_norm_gain[None, :]
    some = tokens // TOKEN_HALVES
    operands = [prompt_hidden_input, to_sibling(prompt_hidden_input), gain, to_sibling(gain)]

    def prepared(half, before, in_place, limit):
        if in_place:
            x_shape = (jax.ShapeDtypeStruct((some, CORES * features), bf16),)
            x_specs = tuple(in_vmem(1))
        else:
            x_shape = (jax.ShapeDtypeStruct((some, features), bf16),) * 2
            x_specs = tuple(anywhere(2))
        *x, squares = pl.pallas_call(
            functools.partial(prepare_kernel, half * some),
            out_shape=x_shape
            + (jax.ShapeDtypeStruct(((half + 1) * some // LANES, LANES), f32),),
            in_specs=anywhere(2) + in_vmem(2 + len(before)),
            out_specs=x_specs + tuple(in_vmem(1)),
            scratch_shapes=[
                pltpu.VMEM((some, features), bf16),
                pltpu.VMEM((some, features), bf16),
                pltpu.VMEM((some, LANES), f32),
                pltpu.SemaphoreType.DMA((4 * pl.cdiv(some, LANES),)),
            ],
            compiler_params=pltpu.CompilerParams(vmem_limit_bytes=limit),
        )(*operands, *before)
        return x, squares

    x0, squares = prepared(0, [], True, PREPARE_VMEM_BYTES)
    exchanged, squares = lax.optimization_barrier((exchanged, squares))
    x1, squares = prepared(1, [squares], False, LARGE_VMEM_BYTES)
    sent_rows = [a_rows + up_packed] + [a_rows] * folded
    a_next, b_next, *sent = pl.pallas_call(
        adam_kernel,
        out_shape=(
            jax.ShapeDtypeStruct((3, factors, down_rows), f32),
            jax.ShapeDtypeStruct((3, up_rows, columns), f32),
        )
        + tuple(jax.ShapeDtypeStruct((n_dp, n, LANES), bf16) for n in sent_rows),
        in_specs=anywhere(7),
        out_specs=tuple(in_vmem(2 + len(sent_rows))),
        scratch_shapes=[
            pltpu.VMEM((n_dp, packed_rows, LANES), bf16),
            pltpu.VMEM((3, factors, window), f32),
            pltpu.VMEM((3, up_rows, columns), f32),
            pltpu.SemaphoreType.DMA((7,)),
        ],
        compiler_params=pltpu.CompilerParams(vmem_limit_bytes=LARGE_VMEM_BYTES),
    )(exchanged, *down_state, *up_state)
    own_f = lax.all_to_all(sent[0], "dp", 0, 0, tiled=True)
    for half in range(1, halves):
        send_half(half, (mine[-1], sent[0]))
    a_next = jnp.transpose(a_next.reshape(3, parts, rank, down_rows), (0, 3, 1, 2))

    outside = [[] for _ in range(strips)]

    def swap_half(half, after):
        for value in mine[half]:
            value, _ = lax.optimization_barrier((value, after))
            split = pl.pallas_call(
                split_kernel,
                out_shape=(jax.ShapeDtypeStruct((features, LANES), bf16),) * len(groups[half]),
                in_specs=in_vmem(1),
                out_specs=tuple(in_vmem(len(groups[half]))),
                compiler_params=params(),
            )(value)
            for piece, strip in zip(split, groups[half]):
                pairs = [(i, i ^ turn[strip]) for i in range(n_dp)]
                outside[strip].append((piece, lax.ppermute(piece, "dp", pairs)))

    swap_half(0, sent[0])
    own_f, squares = lax.optimization_barrier((own_f, squares))
    more = pl.cdiv(3 * (tokens // LANES), up_packed)
    piece = jax.ShapeDtypeStruct((n_dp // n_pieces, a_rows + up_packed, LANES), bf16)
    message, *pieces = pl.pallas_call(
        message_kernel,
        out_shape=(jax.ShapeDtypeStruct((n_dp + more, up_packed, LANES), bf16),)
        + (piece,) * n_pieces,
        in_specs=anywhere(2),
        out_specs=tuple(in_vmem(1 + n_pieces)),
        scratch_shapes=[
            pltpu.VMEM(squares.shape, f32),
            pltpu.SemaphoreType.DMA((2 + n_pieces,)),
        ],
        compiler_params=params(),
    )(own_f, squares)
    messages = [to_chip(message, step) for step in steps]
    sibling_f = [to_sibling(piece) for piece in pieces]

    inv_rms = pl.pallas_call(
        functools.partial(inverse_kernel, width, n_dp),
        out_shape=jax.ShapeDtypeStruct((tokens, LANES), f32),
        in_specs=in_vmem(chips),
        out_specs=in_vmem(1)[0],
        compiler_params=params(),
    )(squares, *messages)

    scale = 0.5 / math.sqrt(width * rank)

    received = {}
    after = []
    weights_shape = jax.ShapeDtypeStruct((CORES * features, wide), bf16)
    product_shape = jax.ShapeDtypeStruct((some, wide), bf16)
    for half, group in enumerate(groups):
        static = (scale, parts, up_rows, group, columns, folded)
        if half > 0:
            swap_half(half, products[0])
        for step in steps:
            blocks = [value for strip in group for value in outside[strip][step - 1]]
            weights, product = pl.pallas_call(
                functools.partial(outside_kernel, static, chips, step, turn, n_pieces),
                out_shape=(weights_shape, product_shape),
                in_specs=in_vmem(2 + 2 * n_pieces + len(blocks)) + anywhere(len(after)),
                out_specs=tuple(in_vmem(2)),
                compiler_params=params(),
            )(messages[step - 1], *x0, *pieces, *sibling_f, *blocks, *after)
            received.setdefault((0, half), []).append(to_chip(product, chips - step))
            second = pl.pallas_call(
                more_kernel,
                out_shape=product_shape,
                in_specs=in_vmem(3),
                out_specs=in_vmem(1)[0],
                compiler_params=params(),
            )(*x1, weights)
            products = [product, second]
            after = [second]
            received.setdefault((1, half), []).append(to_chip(second, chips - step))
        if half == 0:
            after = [received[0, 0][0]]
            first_products = products

    after.append(received[1, 0][0])
    own_a, sibling_a = pieces, sibling_f
    if folded:
        rest, _ = lax.optimization_barrier((sent[1], first_products))
        rest = lax.all_to_all(rest, "dp", 0, 0, tiled=True)
        rest, _ = lax.optimization_barrier((rest, products))
        own_a, sibling_a = [rest], [to_sibling(rest)]
    static = (scale, parts, up_rows, range(strips), columns, folded)
    totals = pl.pallas_call(
        functools.partial(own_kernel, static, n_pieces, halves),
        out_shape=(jax.ShapeDtypeStruct((tokens, wide), f32),) * halves,
        grid=(1,),
        in_specs=[
            pl.BlockSpec((features, columns), lambda i: (lax.axis_index("tensor"), 0)),
            pl.BlockSpec((features, columns), lambda i: (lax.axis_index("tensor") ^ 1, 0)),
        ]
        + in_vmem(3 * n_pieces + 3)
        + anywhere(len(after)),
        out_specs=tuple(in_vmem(halves)),
        scratch_shapes=[pltpu.VMEM((CORES * features, columns), bf16)],
        compiler_params=params(),
        cost_estimate=pl.CostEstimate(
            flops=2 * tokens * CORES * features * columns,
            bytes_accessed=4 * tokens * features,
            transcendentals=0,
        ),
    )(frozen_key_value, frozen_key_value, *own_a, *sibling_a, *pieces, *x0, *x1, *after)

    keys_values = None
    for at, values in received.items():
        keys_values = finish(
            totals[at[1]], inv_rms, values, at, (tokens, columns), keys_values
        )
    return (a_next, b_next, keys_values)


def solution(mesh):
    placed = (
        P("dp", "tensor"),
        P("tensor"),
        P(None, "tensor"),
        P("tensor", None, None),
        P("tensor", None, None),
        P("tensor", None, None),
        P(None, "tensor"),
        P(None, "tensor"),
        P(None, "tensor"),
        P("dp", "tensor", None, None),
        P("dp", None, "tensor"),
    )
    return jax.shard_map(
        body,
        mesh=mesh,
        in_specs=placed,
        out_specs=(
            P(None, ("tensor", "dp"), None, None),
            P(None, "dp", "tensor"),
            P("dp", "tensor"),
        ),
        check_vma=False,
    )
```

```python
import functools
import math

import jax
import jax.numpy as jnp
from jax import lax
from jax.experimental import pallas as pl
from jax.experimental.pallas import tpu as pltpu
from jax.sharding import PartitionSpec as P

KEY_VALUE_WIDTH = 1024
STEP = 100
CORES = 2
LANES = 128
COLUMN_HALVES = 2
TOKEN_HALVES = 2
FACTOR_PIECES = 2
VMEM_BYTES = 16 * 2**20
LARGE_VMEM_BYTES = 58 * 2**20
PREPARE_VMEM_BYTES = 49 * 2**20


def adaptive_moment_update(param, first, second, grad_mean):
    first_new = 0.9 * first + 0.1 * grad_mean
    second_new = 0.999 * second + 0.001 * grad_mean * grad_mean
    step_size = first_new / (1.0 - 0.9**STEP) / (jnp.sqrt(second_new / (1.0 - 0.999**STEP)) + 1e-08)
    return (param - 0.1 * step_size, first_new, second_new)


def in_vmem(count):
    return [pl.BlockSpec(memory_space=pltpu.VMEM)] * count


def anywhere(count):
    return [pl.BlockSpec(memory_space=pl.ANY)] * count


SCALARS = pl.BlockSpec(memory_space=pltpu.SMEM)


def params(**more):
    return pltpu.CompilerParams(vmem_limit_bytes=VMEM_BYTES, **more)


def pack(down, up, out_ref, ready):
    shares = out_ref.shape[0]
    down = down.T
    down_rows, up_rows = down.shape[0] // shares, up.shape[0] // shares
    for i in range(shares):
        pieces = [down[i * down_rows : (i + 1) * down_rows]]
        for k in range(up.shape[1] // LANES):
            pieces.append(up[i * up_rows : (i + 1) * up_rows, k * LANES : (k + 1) * LANES])
        out_ref[i] = jnp.concatenate(pieces, axis=0).astype(jnp.bfloat16)
        ready(i)


def first_lane(share, window, size):
    return jnp.minimum(share // LANES * LANES, size - window)


def begin_kernel(chips, turn, down_ref, up_ref, weights_ref, packed, *refs):
    outs, (down, up, blocks, strips, sem, sem_out) = refs[:-6], refs[-6:]
    features = strips.shape[1]
    place, replica = lax.axis_index("tensor"), lax.axis_index("dp")
    chip, core = place // CORES, place % CORES
    copies, back = [], []

    def add(source, target):
        copies.append(pltpu.make_async_copy(source, target, sem.at[len(copies)]))
        copies[-1].start()

    def add_back(source, target):
        back.append(pltpu.make_async_copy(source, target, sem_out.at[len(back)]))
        back[-1].start()

    add(down_ref, down)
    add(up_ref, up)
    targets = []
    for i, out in enumerate(outs):
        step, first = 1 + i % (chips - 1), i // (chips - 1) * out.shape[0]
        for k in range(out.shape[0]):
            half = (core + replica // turn[first + k]) % 2
            row = ((chip + step) % chips * CORES + half) * features
            add(
                weights_ref.at[
                    pl.ds(pl.multiple_of(row, features), features),
                    pl.ds((first + k) * LANES, LANES),
                ],
                strips.at[len(targets)],
            )
            targets.append(out.at[k])
    copies[0].wait()
    copies[1].wait()
    pack(down[...], up[...], blocks, lambda i: add_back(blocks.at[i], packed.at[i]))
    for i, target in enumerate(targets):
        copies[2 + i].wait()
        add_back(strips.at[i], target)
    for copy in back:
        copy.wait()


def split_kernel(in_ref, *outs):
    for k, out in enumerate(outs):
        out[...] = in_ref[k]


def prepare_kernel(first, own_in, sibling_in, own_gain, sibling_gain, *refs):
    own, sibling, squares, sem = refs[-4:]
    rows, features = own.shape
    together = refs[-6].shape[1] > features
    outs, sums_ref = refs[-6 if together else -7 : -5], refs[-5]
    before = refs[: -6 if together else -7]
    block = LANES if rows % LANES == 0 else rows
    tile = 16 if block % 16 == 0 else block
    count = rows // block
    raw = ((own_in, own), (sibling_in, sibling))
    loads = [
        [
            pltpu.make_async_copy(
                source.at[pl.ds(first + k * block, block)],
                target.at[pl.ds(k * block, block)],
                sem.at[2 * k + side],
            )
            for side, (source, target) in enumerate(raw)
        ]
        for k in range(count)
    ]
    for pair in loads:
        for copy in pair:
            copy.start()
    stores = []
    for k in range(count):
        for copy in loads[k]:
            copy.wait()

        @pl.loop(0, block // tile, unroll=2)
        def _(i):
            at = pl.ds(pl.multiple_of(k * block + i * tile, tile), tile)
            total = None
            for side, (ref, gain) in enumerate(((own, own_gain), (sibling, sibling_gain))):
                value = ref[at, :].astype(jnp.float32)
                scaled = (value * gain[...]).astype(ref.dtype)
                if together:
                    outs[0][at, side * features : (side + 1) * features] = scaled
                else:
                    ref[at, :] = scaled
                total = value * value if total is None else total + value * value
            total = jnp.sum(total, axis=1, keepdims=True)
            squares[at, :] = jnp.broadcast_to(total, (tile, LANES))

        if not together:
            part = pl.ds(k * block, block)
            for side, (source, out) in enumerate(((own, outs[0]), (sibling, outs[1]))):
                place = sem.at[2 * (count + k) + side]
                stores.append(pltpu.make_async_copy(source.at[part], out.at[part], place))
                stores[-1].start()
    done = 0
    for ref in before:
        sums_ref[: ref.shape[0]] = ref[...]
        done = ref.shape[0]
    for i in range(rows // LANES):
        row = squares[i * LANES : (i + 1) * LANES, :].T[:1]
        sums_ref[done + i : done + i + 1] = row
    for copy in stores:
        copy.wait()


def message_kernel(factor_ref, sums_ref, out_ref, *refs):
    pieces, (sums, sem) = refs[:-2], refs[-2:]
    shares, up_rows = factor_ref.shape[0], out_ref.shape[1]
    sums_copy = pltpu.make_async_copy(sums_ref, sums, sem.at[1 + len(pieces)])
    sums_copy.start()
    copies = [
        pltpu.make_async_copy(
            factor_ref.at[:, pl.ds(factor_ref.shape[1] - up_rows, up_rows)],
            out_ref.at[pl.ds(0, shares)],
            sem.at[0],
        )
    ]
    for k, piece in enumerate(pieces):
        size = piece.shape[0]
        copies.append(
            pltpu.make_async_copy(factor_ref.at[pl.ds(k * size, size)], piece, sem.at[1 + k])
        )
    for copy in copies:
        copy.start()
    sums_copy.wait()
    left = sums[...]
    terms = []
    for _ in range(3):
        terms.append(left.astype(jnp.bfloat16).astype(jnp.float32))
        left = left - terms[-1]
    rest = (out_ref.shape[0] - shares) * up_rows - 3 * left.shape[0]
    if rest > 0:
        terms.append(jnp.zeros((rest, LANES), jnp.float32))
    rows = jnp.concatenate(terms, axis=0)
    for i in range(out_ref.shape[0] - shares):
        out_ref[shares + i] = rows[i * up_rows : (i + 1) * up_rows].astype(jnp.bfloat16)
    for copy in copies:
        copy.wait()


def inverse_kernel(width, shares, sums_ref, *refs):
    messages, out = refs[:-1], refs[-1]
    total = sums_ref[...]
    count = total.shape[0]
    for ref in messages:
        rows = [ref[i].astype(jnp.float32) for i in range(shares, ref.shape[0])]
        rows = jnp.concatenate(rows, axis=0)
        total += rows[:count] + rows[count : 2 * count] + rows[2 * count : 3 * count]
    inverse = lax.rsqrt(total / width + 1e-06)
    for i in range(count):
        out[i * LANES : (i + 1) * LANES, :] = jnp.broadcast_to(
            inverse[i : i + 1], (LANES, LANES)
        ).T


def update(total, down, up, a_ref, b_ref):
    down_rows = a_ref.shape[2]
    up_rows, columns = b_ref.shape[1:]
    strips = columns // LANES
    down_mean = total[:down_rows].T
    up_mean = jnp.concatenate(
        [total[down_rows + k * up_rows : down_rows + (k + 1) * up_rows] for k in range(strips)],
        axis=1,
    )
    p, m, v = adaptive_moment_update(*down(), down_mean)
    a_ref[0], a_ref[1], a_ref[2] = p, m, v
    pieces = [p.T]
    p, m, v = adaptive_moment_update(*up(), up_mean)
    b_ref[0], b_ref[1], b_ref[2] = p, m, v
    pieces += [p[:, k * LANES : (k + 1) * LANES] for k in range(strips)]
    return jnp.concatenate(pieces, axis=0).astype(jnp.bfloat16)


def adam_kernel(grad_in, *refs):
    state, refs = refs[:6], refs[6:]
    a_ref, b_ref, factor_ref, grad_ref, down_win, up_win, sem = refs
    replicas = grad_ref.shape[0]
    down_rows, window = a_ref.shape[2], down_win.shape[2]
    up_rows = up_win.shape[1]
    replica = lax.axis_index("dp")
    share = replica * down_rows
    size = down_rows * replicas
    copies = [pltpu.make_async_copy(grad_in, grad_ref, sem.at[6])]
    for i in range(3):
        down, up = state[i], state[3 + i]
        if window != down_rows:
            lane = pl.multiple_of(first_lane(share, window, size), LANES)
            down = down.at[:, pl.ds(lane, window)]
            up = up.at[pl.ds(pl.multiple_of(replica * up_rows, up_rows), up_rows)]
        copies.append(pltpu.make_async_copy(down, down_win.at[i], sem.at[i]))
        copies.append(pltpu.make_async_copy(up, up_win.at[i], sem.at[3 + i]))
    for copy in copies:
        copy.start()
    copies[0].wait()
    total = jnp.sum(grad_ref[...].astype(jnp.float32), axis=0) / replicas
    for copy in copies[1:]:
        copy.wait()

    def down():
        if window == down_rows:
            return [down_win[i] for i in range(3)]
        shift = window - (share - first_lane(share, window, size))
        return [pltpu.roll(down_win[i], shift, 1)[:, :down_rows] for i in range(3)]

    rounded = update(total, down, lambda: [up_win[i] for i in range(3)], a_ref, b_ref)
    for i in range(replicas):
        factor_ref[i] = rounded


def factor_a(refs, down_rows):
    pieces = []
    for ref in refs:
        for i in range(ref.shape[0]):
            if down_rows % 16 == 0:
                pieces.append(ref[i, :down_rows, :])
            else:
                pieces.append(ref[i].astype(jnp.float32)[:down_rows])
    return jnp.concatenate(pieces, axis=0).astype(jnp.bfloat16)


def factor_b(packed, part, parts, strip, up_rows):
    pieces = [
        packed[i].astype(jnp.float32)[strip * up_rows : (strip + 1) * up_rows]
        for i in range(packed.shape[0])
    ]
    value = jnp.concatenate(pieces, axis=0)
    rows = [jnp.where(part == j, value, jnp.zeros_like(value)) for j in range(parts)]
    return jnp.concatenate(rows, axis=0).astype(jnp.bfloat16)


def merge(scale, block, a, b):
    change = jnp.dot(a, b, preferred_element_type=jnp.float32)
    return (block.astype(jnp.float32) + scale * change).astype(jnp.bfloat16)


def multiply(groups, weights, *outs):
    wide = outs[0].shape[1]
    done = 0
    for xs in groups:
        rows = xs[0].shape[0]
        tile = rows // 2 if rows % 32 == 0 else rows

        @pl.loop(0, rows // tile)
        def _(i):
            at = pl.ds(pl.multiple_of(i * tile, tile), tile)
            to = pl.ds(pl.multiple_of(done + i * tile, 16), tile)
            value, first = None, 0
            for x in xs:
                size = x.shape[1]
                part = jnp.dot(
                    x[at, :], weights[first : first + size, :], preferred_element_type=jnp.float32
                )
                value, first = part if value is None else value + part, first + size
            for k, out in enumerate(outs):
                out[to, :] = value[:, k * wide : (k + 1) * wide].astype(out.dtype)

        done += rows


def up_factor(static, packed, owner):
    _, parts, up_rows, strips, columns = static
    part = owner * columns // KEY_VALUE_WIDTH
    return jnp.concatenate(
        [factor_b(packed, part, parts, strip, up_rows) for strip in strips], axis=1
    )


def arrange_kernel(turn, *refs):
    out = refs[-1]
    replica = lax.axis_index("dp")
    features = out.shape[0] // CORES
    for k, alternate in enumerate(turn):
        mine, other = refs[2 * k : 2 * k + 2]
        even = replica // alternate % 2 == 0
        lanes = slice(k * LANES, (k + 1) * LANES)
        out[:features, lanes] = jnp.where(even, mine[...], other[...])
        out[features:, lanes] = jnp.where(even, other[...], mine[...])


def outside_kernel(static, chips, step, blocks, b_ref, x, *refs):
    own_f, sibling_f = refs[:FACTOR_PIECES], refs[FACTOR_PIECES : 2 * FACTOR_PIECES]
    weights, product = refs[-2:]
    features = blocks.shape[0] // CORES
    down_rows = own_f[0].shape[1] - b_ref.shape[1]
    shares = FACTOR_PIECES * own_f[0].shape[0]
    place = lax.axis_index("tensor")
    owner = (place // CORES - step + chips) % chips * CORES + place % CORES
    b = up_factor(static, b_ref[:shares], owner)
    tile = 256 if features % 256 == 0 else features
    for side, factors in enumerate((own_f, sibling_f)):
        a = factor_a(factors, down_rows)
        for first in range(0, features, tile):
            rows = slice(side * features + first, side * features + first + tile)
            weights[rows, :] = merge(static[0], blocks[rows, :], a[first : first + tile], b)
    multiply([[x]], weights, product)


def more_kernel(groups, *refs):
    xs, (weights, product) = refs[:-2], refs[-2:]
    size = len(xs) // groups
    multiply([xs[k * size : (k + 1) * size] for k in range(groups)], weights, product)


def own_kernel(static, own_block, sibling_block, *refs):
    own_f, sibling_f = refs[:FACTOR_PIECES], refs[FACTOR_PIECES : 2 * FACTOR_PIECES]
    refs = refs[2 * FACTOR_PIECES :]
    groups, weights = [refs[:1]], refs[-1]
    for k in range(static[6]):
        groups.append(refs[1 + 2 * k : 3 + 2 * k])
    outs = refs[len(refs) - 1 - static[5] : -1]
    features = own_block.shape[0]
    wide = outs[0].shape[1]
    down_rows = own_f[0].shape[1] - len(static[3]) * static[2]
    b = jnp.concatenate([piece[:, down_rows:] for piece in own_f], axis=0)
    b = up_factor(static[:5], b, lax.axis_index("tensor"))
    for at, factors, block in ((0, own_f, own_block), (features, sibling_f, sibling_block)):
        weights[at : at + features] = merge(static[0], block[...], factor_a(factors, down_rows), b)
    multiply(groups, weights, *outs)


def finish_kernel(sources, first, own, inv, *refs):
    rows = pl.ds(first, refs[-1].shape[0])
    total = own[rows, :]
    for value in refs[:sources]:
        total = total + value[...].astype(jnp.float32)
    refs[-1][...] = (total * inv[rows, :1]).astype(refs[-1].dtype)


def finish(own, inv_rms, received, at, shape, before):
    block = received[0].shape
    operands = [own, inv_rms] + received
    in_specs = in_vmem(len(operands))
    aliases = {}
    if before is not None:
        aliases = {len(operands): 0}
        in_specs += anywhere(1)
        operands.append(before)
    return pl.pallas_call(
        functools.partial(finish_kernel, len(received), at[0] * block[0]),
        grid=(1,),
        out_shape=jax.ShapeDtypeStruct(shape, jnp.bfloat16),
        in_specs=in_specs,
        out_specs=pl.BlockSpec(block, lambda i: at),
        input_output_aliases=aliases,
        compiler_params=params(),
    )(*operands)


def body(
    prompt_hidden_input,
    input_norm_gain,
    frozen_key_value,
    down_factor_matrix,
    down_moment_first,
    down_moment_second,
    up_factor_matrix,
    up_moment_first,
    up_moment_second,
    down_gradient,
    up_gradient,
):
    n_dp = lax.axis_size("dp")
    n_tensor = lax.axis_size("tensor")
    chips = n_tensor // CORES
    replica = lax.axis_index("dp")
    tokens, features = prompt_hidden_input.shape
    width, columns = frozen_key_value.shape
    rank = up_factor_matrix.shape[0]
    parts = down_factor_matrix.shape[1]
    factors = parts * rank
    strips = columns // LANES
    down_rows = features // n_dp
    up_rows = rank // n_dp
    packed_rows = down_rows + up_rows * strips
    steps = range(1, chips)
    f32, bf16 = jnp.float32, jnp.bfloat16

    def to_sibling(value):
        return lax.ppermute(value, "tensor", [(t, t ^ 1) for t in range(n_tensor)])

    def to_chip(value, step):
        pairs = [
            (CORES * q + k, CORES * ((q + step) % chips) + k)
            for q in range(chips)
            for k in range(CORES)
        ]
        return lax.ppermute(value, "tensor", pairs)

    def by_rank(value):
        return jnp.transpose(value, (1, 2, 0)).reshape(factors, features)

    down_sent = by_rank(down_gradient[0])
    down_state = [by_rank(v) for v in (down_factor_matrix, down_moment_first, down_moment_second)]
    up_state = [up_factor_matrix, up_moment_first, up_moment_second]
    shares = jax.ShapeDtypeStruct((n_dp, packed_rows, LANES), bf16)
    window = pl.cdiv(down_rows + LANES, LANES) * LANES
    aligned = features % LANES == 0 and window <= features
    aligned = aligned and up_rows % 8 == 0 and down_rows % 16 == 0
    window = window if aligned else down_rows
    turns = [1, 2] if n_dp % 4 == 0 else [1, 1]
    turn = [turns[strip % 2] for strip in range(strips)]
    halves = min(COLUMN_HALVES, strips)
    wide = columns // halves
    groups = [range(k * strips // halves, (k + 1) * strips // halves) for k in range(halves)]
    out_shape = (shares,) + tuple(
        jax.ShapeDtypeStruct((len(group), features, LANES), bf16)
        for group in groups
        for _ in steps
    )
    packed, *taken = pl.pallas_call(
        functools.partial(begin_kernel, chips, turn),
        out_shape=out_shape,
        in_specs=anywhere(3),
        out_specs=tuple(anywhere(len(out_shape))),
        scratch_shapes=[
            pltpu.VMEM((factors, features), f32),
            pltpu.VMEM((rank, columns), f32),
            pltpu.VMEM(shares.shape, bf16),
            pltpu.VMEM((len(steps) * strips, features, LANES), bf16),
            pltpu.SemaphoreType.DMA((2 + len(steps) * strips,)),
            pltpu.SemaphoreType.DMA((n_dp + len(steps) * strips,)),
        ],
        compiler_params=pltpu.CompilerParams(vmem_limit_bytes=LARGE_VMEM_BYTES),
    )(down_sent, up_gradient[0], frozen_key_value)
    exchanged = lax.all_to_all(packed, "dp", 0, 0, tiled=True)
    if not aligned:
        down_state = [
            lax.dynamic_slice_in_dim(v, replica * down_rows, down_rows, 1) for v in down_state
        ]
        up_state = [lax.dynamic_slice_in_dim(v, replica * up_rows, up_rows, 0) for v in up_state]
    mine = []

    def send_half(half, after):
        blocks = taken[half * len(steps) : (half + 1) * len(steps)]
        if after is not None:
            blocks, _ = lax.optimization_barrier((blocks, after))
        mine.append([to_chip(value, step) for value, step in zip(blocks, steps)])

    send_half(0, None)

    gain = input_norm_gain[None, :]
    some = tokens // TOKEN_HALVES
    operands = [prompt_hidden_input, to_sibling(prompt_hidden_input), gain, to_sibling(gain)]

    def prepared(first, size, before, in_place, limit):
        if in_place:
            x_shape = (jax.ShapeDtypeStruct((size, CORES * features), bf16),)
            x_specs = tuple(in_vmem(1))
        else:
            x_shape = (jax.ShapeDtypeStruct((size, features), bf16),) * 2
            x_specs = tuple(anywhere(2))
        *x, squares = pl.pallas_call(
            functools.partial(prepare_kernel, first),
            out_shape=x_shape
            + (jax.ShapeDtypeStruct(((first + size) // LANES, LANES), f32),),
            in_specs=anywhere(2) + in_vmem(2 + len(before)),
            out_specs=x_specs + tuple(in_vmem(1)),
            scratch_shapes=[
                pltpu.VMEM((size, features), bf16),
                pltpu.VMEM((size, features), bf16),
                pltpu.VMEM((size, LANES), f32),
                pltpu.SemaphoreType.DMA((4 * pl.cdiv(size, LANES),)),
            ],
            compiler_params=pltpu.CompilerParams(vmem_limit_bytes=limit),
        )(*operands, *before)
        return x, squares

    cut = some // 2 // LANES * LANES
    x0, squares = prepared(0, some, [], True, PREPARE_VMEM_BYTES)
    x1 = []
    if cut > 0:
        x1, squares = prepared(some, cut, [squares], False, LARGE_VMEM_BYTES)
    exchanged, squares = lax.optimization_barrier((exchanged, squares))
    last, squares = prepared(some + cut, some - cut, [squares], False, LARGE_VMEM_BYTES)
    x1 = x1 + last
    a_next, b_next, sent = pl.pallas_call(
        adam_kernel,
        out_shape=(
            jax.ShapeDtypeStruct((3, factors, down_rows), f32),
            jax.ShapeDtypeStruct((3, up_rows, columns), f32),
            shares,
        ),
        in_specs=anywhere(7),
        out_specs=tuple(in_vmem(3)),
        scratch_shapes=[
            pltpu.VMEM((n_dp, packed_rows, LANES), bf16),
            pltpu.VMEM((3, factors, window), f32),
            pltpu.VMEM((3, up_rows, columns), f32),
            pltpu.SemaphoreType.DMA((7,)),
        ],
        compiler_params=pltpu.CompilerParams(vmem_limit_bytes=LARGE_VMEM_BYTES),
    )(exchanged, *down_state, *up_state)
    own_f = lax.all_to_all(sent, "dp", 0, 0, tiled=True)
    for half in range(1, halves):
        send_half(half, (mine[-1], sent))
    a_next = jnp.transpose(a_next.reshape(3, parts, rank, down_rows), (0, 3, 1, 2))

    outside = [[] for _ in range(strips)]

    def swap_half(half, after):
        for value in mine[half]:
            value, _ = lax.optimization_barrier((value, after))
            split = pl.pallas_call(
                split_kernel,
                out_shape=(jax.ShapeDtypeStruct((features, LANES), bf16),) * len(groups[half]),
                in_specs=in_vmem(1),
                out_specs=tuple(in_vmem(len(groups[half]))),
                compiler_params=params(),
            )(value)
            for piece, strip in zip(split, groups[half]):
                pairs = [(i, i ^ turn[strip]) for i in range(n_dp)]
                outside[strip].append((piece, lax.ppermute(piece, "dp", pairs)))

    swap_half(0, sent)
    own_f, squares = lax.optimization_barrier((own_f, squares))
    up_packed = packed_rows - down_rows
    more = pl.cdiv(3 * (tokens // LANES), up_packed)
    piece = jax.ShapeDtypeStruct((n_dp // FACTOR_PIECES, packed_rows, LANES), bf16)
    message, *pieces = pl.pallas_call(
        message_kernel,
        out_shape=(jax.ShapeDtypeStruct((n_dp + more, up_packed, LANES), bf16),)
        + (piece,) * FACTOR_PIECES,
        in_specs=anywhere(2),
        out_specs=tuple(in_vmem(1 + FACTOR_PIECES)),
        scratch_shapes=[
            pltpu.VMEM(squares.shape, f32),
            pltpu.SemaphoreType.DMA((2 + FACTOR_PIECES,)),
        ],
        compiler_params=params(),
    )(own_f, squares)
    messages = [to_chip(message, step) for step in steps]
    sibling_f = [to_sibling(piece) for piece in pieces]

    inv_rms = pl.pallas_call(
        functools.partial(inverse_kernel, width, n_dp),
        out_shape=jax.ShapeDtypeStruct((tokens, LANES), f32),
        in_specs=in_vmem(chips),
        out_specs=in_vmem(1)[0],
        compiler_params=params(),
    )(squares, *messages)

    scale = 0.5 / math.sqrt(width * rank)

    received = {}
    after = []
    weights_shape = jax.ShapeDtypeStruct((CORES * features, wide), bf16)
    product_shape = jax.ShapeDtypeStruct((some, wide), bf16)
    for half, group in enumerate(groups):
        static = (scale, parts, up_rows, group, columns)
        if half > 0:
            swap_half(half, products[0])
        for step in steps:
            blocks = [value for strip in group for value in outside[strip][step - 1]]
            arranged = pl.pallas_call(
                functools.partial(arrange_kernel, [turn[strip] for strip in group]),
                out_shape=weights_shape,
                in_specs=in_vmem(len(blocks)) + anywhere(len(after)),
                out_specs=in_vmem(1)[0],
                compiler_params=params(),
            )(*blocks, *after)
            weights, product = pl.pallas_call(
                functools.partial(outside_kernel, static, chips, step),
                out_shape=(weights_shape, product_shape),
                in_specs=in_vmem(3 + 2 * FACTOR_PIECES),
                out_specs=tuple(in_vmem(2)),
                compiler_params=params(),
            )(arranged, messages[step - 1], *x0, *pieces, *sibling_f)
            received.setdefault((0, half), []).append(to_chip(product, chips - step))
            second = pl.pallas_call(
                functools.partial(more_kernel, len(x1) // 2),
                out_shape=product_shape,
                in_specs=in_vmem(1 + len(x1)),
                out_specs=in_vmem(1)[0],
                compiler_params=params(),
            )(*x1, weights)
            products = [product, second]
            after = [second]
            received.setdefault((1, half), []).append(to_chip(second, chips - step))
        if half == 0:
            after = [received[0, 0][0]]

    after.append(received[1, 0][0])
    static = (scale, parts, up_rows, range(strips), columns, halves, len(x1) // 2)
    totals = pl.pallas_call(
        functools.partial(own_kernel, static),
        out_shape=(jax.ShapeDtypeStruct((tokens, wide), f32),) * halves,
        grid=(1,),
        in_specs=[
            pl.BlockSpec((features, columns), lambda i: (lax.axis_index("tensor"), 0)),
            pl.BlockSpec((features, columns), lambda i: (lax.axis_index("tensor") ^ 1, 0)),
        ]
        + in_vmem(2 * FACTOR_PIECES + 1 + len(x1))
        + anywhere(len(after)),
        out_specs=tuple(in_vmem(halves)),
        scratch_shapes=[pltpu.VMEM((CORES * features, columns), bf16)],
        compiler_params=params(),
        cost_estimate=pl.CostEstimate(
            flops=2 * tokens * CORES * features * columns,
            bytes_accessed=4 * tokens * features,
            transcendentals=0,
        ),
    )(frozen_key_value, frozen_key_value, *pieces, *sibling_f, *x0, *x1, *after)

    keys_values = None
    for at, values in received.items():
        keys_values = finish(
            totals[at[1]], inv_rms, values, at, (tokens, columns), keys_values
        )
    return (a_next, b_next, keys_values)


def solution(mesh):
    placed = (
        P("dp", "tensor"),
        P("tensor"),
        P(None, "tensor"),
        P("tensor", None, None),
        P("tensor", None, None),
        P("tensor", None, None),
        P(None, "tensor"),
        P(None, "tensor"),
        P(None, "tensor"),
        P("dp", "tensor", None, None),
        P("dp", None, "tensor"),
    )
    return jax.shard_map(
        body,
        mesh=mesh,
        in_specs=placed,
        out_specs=(
            P(None, ("tensor", "dp"), None, None),
            P(None, "dp", "tensor"),
            P("dp", "tensor"),
        ),
        check_vma=False,
    )
```

```python
import functools
import math

import jax
import jax.numpy as jnp
from jax import lax
from jax.experimental import pallas as pl
from jax.experimental.pallas import tpu as pltpu
from jax.sharding import PartitionSpec as P

KEY_VALUE_WIDTH = 1024
STEP = 100
CORES = 2
LANES = 128
COLUMN_HALVES = 2
TOKEN_HALVES = 2
FACTOR_PIECES = 2
VMEM_BYTES = 16 * 2**20
LARGE_VMEM_BYTES = 58 * 2**20
PREPARE_VMEM_BYTES = 49 * 2**20
FINAL_VMEM_BYTES = 55 * 2**20


def adaptive_moment_update(param, first, second, grad_mean):
    first_new = 0.9 * first + 0.1 * grad_mean
    second_new = 0.999 * second + 0.001 * grad_mean * grad_mean
    step_size = first_new / (1.0 - 0.9**STEP) / (jnp.sqrt(second_new / (1.0 - 0.999**STEP)) + 1e-08)
    return (param - 0.1 * step_size, first_new, second_new)


def in_vmem(count):
    return [pl.BlockSpec(memory_space=pltpu.VMEM)] * count


def anywhere(count):
    return [pl.BlockSpec(memory_space=pl.ANY)] * count


SCALARS = pl.BlockSpec(memory_space=pltpu.SMEM)


def params(**more):
    return pltpu.CompilerParams(vmem_limit_bytes=VMEM_BYTES, **more)


def pack(down, up, out_ref, ready):
    shares = out_ref.shape[0]
    down = down.T
    down_rows, up_rows = down.shape[0] // shares, up.shape[0] // shares
    for i in range(shares):
        pieces = [down[i * down_rows : (i + 1) * down_rows]]
        for k in range(up.shape[1] // LANES):
            pieces.append(up[i * up_rows : (i + 1) * up_rows, k * LANES : (k + 1) * LANES])
        out_ref[i] = jnp.concatenate(pieces, axis=0).astype(jnp.bfloat16)
        ready(i)


def first_lane(share, window, size):
    return jnp.minimum(share // LANES * LANES, size - window)


def begin_kernel(chips, turn, down_ref, up_ref, weights_ref, packed, *refs):
    outs, (down, up, blocks, strips, sem, sem_out) = refs[:-6], refs[-6:]
    features = strips.shape[1]
    place, replica = lax.axis_index("tensor"), lax.axis_index("dp")
    chip, core = place // CORES, place % CORES
    copies, back = [], []

    def add(source, target):
        copies.append(pltpu.make_async_copy(source, target, sem.at[len(copies)]))
        copies[-1].start()

    def add_back(source, target):
        back.append(pltpu.make_async_copy(source, target, sem_out.at[len(back)]))
        back[-1].start()

    add(down_ref, down)
    add(up_ref, up)
    targets = []
    for i, out in enumerate(outs):
        step, first = 1 + i % (chips - 1), i // (chips - 1) * out.shape[0]
        for k in range(out.shape[0]):
            half = (core + replica // turn[first + k]) % 2
            row = ((chip + step) % chips * CORES + half) * features
            add(
                weights_ref.at[
                    pl.ds(pl.multiple_of(row, features), features),
                    pl.ds((first + k) * LANES, LANES),
                ],
                strips.at[len(targets)],
            )
            targets.append(out.at[k])
    copies[0].wait()
    copies[1].wait()
    pack(down[...], up[...], blocks, lambda i: add_back(blocks.at[i], packed.at[i]))
    for i, target in enumerate(targets):
        copies[2 + i].wait()
        add_back(strips.at[i], target)
    for copy in back:
        copy.wait()


def split_kernel(in_ref, *outs):
    for k, out in enumerate(outs):
        out[...] = in_ref[k]


def prepare_kernel(first, own_in, sibling_in, own_gain, sibling_gain, *refs):
    own, sibling, squares, sem = refs[-4:]
    rows, features = own.shape
    together = refs[-6].shape[1] > features
    outs, sums_ref = refs[-6 if together else -7 : -5], refs[-5]
    before = refs[: -6 if together else -7]
    block = LANES if rows % LANES == 0 else rows
    tile = 16 if block % 16 == 0 else block
    count = rows // block
    raw = ((own_in, own), (sibling_in, sibling))
    loads = [
        [
            pltpu.make_async_copy(
                source.at[pl.ds(first + k * block, block)],
                target.at[pl.ds(k * block, block)],
                sem.at[2 * k + side],
            )
            for side, (source, target) in enumerate(raw)
        ]
        for k in range(count)
    ]
    for pair in loads:
        for copy in pair:
            copy.start()
    stores = []
    for k in range(count):
        for copy in loads[k]:
            copy.wait()

        @pl.loop(0, block // tile, unroll=2)
        def _(i):
            at = pl.ds(pl.multiple_of(k * block + i * tile, tile), tile)
            total = None
            for side, (ref, gain) in enumerate(((own, own_gain), (sibling, sibling_gain))):
                value = ref[at, :].astype(jnp.float32)
                scaled = (value * gain[...]).astype(ref.dtype)
                if together:
                    outs[0][at, side * features : (side + 1) * features] = scaled
                else:
                    ref[at, :] = scaled
                total = value * value if total is None else total + value * value
            total = jnp.sum(total, axis=1, keepdims=True)
            squares[at, :] = jnp.broadcast_to(total, (tile, LANES))

        if not together:
            part = pl.ds(k * block, block)
            for side, (source, out) in enumerate(((own, outs[0]), (sibling, outs[1]))):
                place = sem.at[2 * (count + k) + side]
                stores.append(pltpu.make_async_copy(source.at[part], out.at[part], place))
                stores[-1].start()
    done = 0
    for ref in before:
        sums_ref[: ref.shape[0]] = ref[...]
        done = ref.shape[0]
    for i in range(rows // LANES):
        row = squares[i * LANES : (i + 1) * LANES, :].T[:1]
        sums_ref[done + i : done + i + 1] = row
    for copy in stores:
        copy.wait()


def message_kernel(factor_ref, sums_ref, out_ref, *refs):
    pieces, (sums, sem) = refs[:-2], refs[-2:]
    shares, up_rows = factor_ref.shape[0], out_ref.shape[1]
    sums_copy = pltpu.make_async_copy(sums_ref, sums, sem.at[1 + len(pieces)])
    sums_copy.start()
    copies = [
        pltpu.make_async_copy(
            factor_ref.at[:, pl.ds(factor_ref.shape[1] - up_rows, up_rows)],
            out_ref.at[pl.ds(0, shares)],
            sem.at[0],
        )
    ]
    for k, piece in enumerate(pieces):
        size = piece.shape[0]
        copies.append(
            pltpu.make_async_copy(factor_ref.at[pl.ds(k * size, size)], piece, sem.at[1 + k])
        )
    for copy in copies:
        copy.start()
    sums_copy.wait()
    left = sums[...]
    terms = []
    for _ in range(3):
        terms.append(left.astype(jnp.bfloat16).astype(jnp.float32))
        left = left - terms[-1]
    rest = (out_ref.shape[0] - shares) * up_rows - 3 * left.shape[0]
    if rest > 0:
        terms.append(jnp.zeros((rest, LANES), jnp.float32))
    rows = jnp.concatenate(terms, axis=0)
    for i in range(out_ref.shape[0] - shares):
        out_ref[shares + i] = rows[i * up_rows : (i + 1) * up_rows].astype(jnp.bfloat16)
    for copy in copies:
        copy.wait()


def inverse_kernel(width, shares, sums_ref, *refs):
    messages, out = refs[:-1], refs[-1]
    total = sums_ref[...]
    count = total.shape[0]
    for ref in messages:
        rows = [ref[i].astype(jnp.float32) for i in range(shares, ref.shape[0])]
        rows = jnp.concatenate(rows, axis=0)
        total += rows[:count] + rows[count : 2 * count] + rows[2 * count : 3 * count]
    inverse = lax.rsqrt(total / width + 1e-06)
    for i in range(count):
        out[i * LANES : (i + 1) * LANES, :] = jnp.broadcast_to(
            inverse[i : i + 1], (LANES, LANES)
        ).T


def update(total, down, up, down_rows, columns):
    up_rows = up[0].shape[0]
    down_mean = total[:down_rows].T
    up_mean = jnp.concatenate(
        [
            total[down_rows + k * up_rows : down_rows + (k + 1) * up_rows]
            for k in range(columns // LANES)
        ],
        axis=1,
    )
    return adaptive_moment_update(*down, down_mean), adaptive_moment_update(*up, up_mean)


def adam_kernel(down_rows, final, grad_in, *refs):
    state, refs = refs[:6], refs[6:]
    grad_ref, down_win, up_win, sem = refs[-4:]
    outs = refs[-6:-4]
    replicas = grad_ref.shape[0]
    window, up_rows, columns = down_win.shape[2], up_win.shape[1], up_win.shape[2]
    replica = lax.axis_index("dp")
    share = replica * down_rows
    size = down_rows * replicas
    copies = [pltpu.make_async_copy(grad_in, grad_ref, sem.at[6])]
    for i in range(3):
        down, up = state[i], state[3 + i]
        if window != down_rows:
            lane = pl.multiple_of(first_lane(share, window, size), LANES)
            down = down.at[:, pl.ds(lane, window)]
            up = up.at[pl.ds(pl.multiple_of(replica * up_rows, up_rows), up_rows)]
        copies.append(pltpu.make_async_copy(down, down_win.at[i], sem.at[i]))
        copies.append(pltpu.make_async_copy(up, up_win.at[i], sem.at[3 + i]))
    for copy in copies:
        copy.start()
    copies[0].wait()
    total = jnp.sum(grad_ref[...].astype(jnp.float32), axis=0) / replicas
    for copy in copies[1:]:
        copy.wait()
    down = [down_win[i] for i in range(3)]
    if window != down_rows:
        shift = window - (share - first_lane(share, window, size))
        down = [pltpu.roll(value, shift, 1)[:, :down_rows] for value in down]
    down, up = update(total, down, [up_win[i] for i in range(3)], down_rows, columns)
    if final:
        for i in range(3):
            outs[0][i], outs[1][i] = down[i], up[i]
        return
    target, rounded = outs
    pieces = [down[0].T]
    pieces += [up[0][:, k * LANES : (k + 1) * LANES] for k in range(columns // LANES)]
    rounded[...] = jnp.concatenate(pieces, axis=0).astype(jnp.bfloat16)
    copies = [pltpu.make_async_copy(rounded, target.at[i], sem.at[i]) for i in range(replicas)]
    for copy in copies:
        copy.start()
    for copy in copies:
        copy.wait()


def factor_a(refs, down_rows):
    pieces = []
    for ref in refs:
        for i in range(ref.shape[0]):
            if down_rows % 16 == 0:
                pieces.append(ref[i, :down_rows, :])
            else:
                pieces.append(ref[i].astype(jnp.float32)[:down_rows])
    return jnp.concatenate(pieces, axis=0).astype(jnp.bfloat16)


def factor_b(packed, part, parts, strip, up_rows):
    pieces = [
        packed[i].astype(jnp.float32)[strip * up_rows : (strip + 1) * up_rows]
        for i in range(packed.shape[0])
    ]
    value = jnp.concatenate(pieces, axis=0)
    rows = [jnp.where(part == j, value, jnp.zeros_like(value)) for j in range(parts)]
    return jnp.concatenate(rows, axis=0).astype(jnp.bfloat16)


def merge(scale, block, a, b):
    change = jnp.dot(a, b, preferred_element_type=jnp.float32)
    return (block.astype(jnp.float32) + scale * change).astype(jnp.bfloat16)


def multiply(groups, weights, *outs):
    wide = outs[0].shape[1]
    done = 0
    for xs in groups:
        rows = xs[0].shape[0]
        tile = rows // 2 if rows % 32 == 0 else rows

        @pl.loop(0, rows // tile)
        def _(i):
            at = pl.ds(pl.multiple_of(i * tile, tile), tile)
            to = pl.ds(pl.multiple_of(done + i * tile, 16), tile)
            value, first = None, 0
            for x in xs:
                size = x.shape[1]
                part = jnp.dot(
                    x[at, :], weights[first : first + size, :], preferred_element_type=jnp.float32
                )
                value, first = part if value is None else value + part, first + size
            for k, out in enumerate(outs):
                out[to, :] = value[:, k * wide : (k + 1) * wide].astype(out.dtype)

        done += rows


def up_factor(static, packed, owner):
    _, parts, up_rows, strips, columns = static
    part = owner * columns // KEY_VALUE_WIDTH
    return jnp.concatenate(
        [factor_b(packed, part, parts, strip, up_rows) for strip in strips], axis=1
    )


def arrange_kernel(turn, *refs):
    out = refs[-1]
    replica = lax.axis_index("dp")
    features = out.shape[0] // CORES
    for k, alternate in enumerate(turn):
        mine, other = refs[2 * k : 2 * k + 2]
        even = replica // alternate % 2 == 0
        lanes = slice(k * LANES, (k + 1) * LANES)
        out[:features, lanes] = jnp.where(even, mine[...], other[...])
        out[features:, lanes] = jnp.where(even, other[...], mine[...])


def outside_kernel(static, chips, step, blocks, b_ref, x, *refs):
    own_f, sibling_f = refs[:FACTOR_PIECES], refs[FACTOR_PIECES : 2 * FACTOR_PIECES]
    weights, product = refs[-2:]
    features = blocks.shape[0] // CORES
    down_rows = own_f[0].shape[1] - b_ref.shape[1]
    shares = FACTOR_PIECES * own_f[0].shape[0]
    place = lax.axis_index("tensor")
    owner = (place // CORES - step + chips) % chips * CORES + place % CORES
    b = up_factor(static, b_ref[:shares], owner)
    tile = 256 if features % 256 == 0 else features
    for side, factors in enumerate((own_f, sibling_f)):
        a = factor_a(factors, down_rows)
        for first in range(0, features, tile):
            rows = slice(side * features + first, side * features + first + tile)
            weights[rows, :] = merge(static[0], blocks[rows, :], a[first : first + tile], b)
    multiply([[x]], weights, product)


def more_kernel(groups, *refs):
    xs, (weights, product) = refs[:-2], refs[-2:]
    size = len(xs) // groups
    multiply([xs[k * size : (k + 1) * size] for k in range(groups)], weights, product)


def own_kernel(static, own_block, sibling_block, *refs):
    own_f, sibling_f = refs[:FACTOR_PIECES], refs[FACTOR_PIECES : 2 * FACTOR_PIECES]
    refs = refs[2 * FACTOR_PIECES :]
    groups, weights = [refs[:1]], refs[-1]
    for k in range(static[6]):
        groups.append(refs[1 + 2 * k : 3 + 2 * k])
    outs = refs[len(refs) - 1 - static[5] : -1]
    features = own_block.shape[0]
    wide = outs[0].shape[1]
    down_rows = own_f[0].shape[1] - len(static[3]) * static[2]
    b = jnp.concatenate([piece[:, down_rows:] for piece in own_f], axis=0)
    b = up_factor(static[:5], b, lax.axis_index("tensor"))
    for at, factors, block in ((0, own_f, own_block), (features, sibling_f, sibling_block)):
        weights[at : at + features] = merge(static[0], block[...], factor_a(factors, down_rows), b)
    multiply(groups, weights, *outs)


def finish_kernel(sources, first, own, inv, *refs):
    rows = pl.ds(first, refs[-1].shape[0])
    total = own[rows, :]
    for value in refs[:sources]:
        total = total + value[...].astype(jnp.float32)
    refs[-1][...] = (total * inv[rows, :1]).astype(refs[-1].dtype)


def finish(own, inv_rms, received, at, shape, before):
    block = received[0].shape
    operands = [own, inv_rms] + received
    in_specs = in_vmem(len(operands))
    aliases = {}
    if before is not None:
        aliases = {len(operands): 0}
        in_specs += anywhere(1)
        operands.append(before)
    return pl.pallas_call(
        functools.partial(finish_kernel, len(received), at[0] * block[0]),
        grid=(1,),
        out_shape=jax.ShapeDtypeStruct(shape, jnp.bfloat16),
        in_specs=in_specs,
        out_specs=pl.BlockSpec(block, lambda i: at),
        input_output_aliases=aliases,
        compiler_params=params(),
    )(*operands)


def body(
    prompt_hidden_input,
    input_norm_gain,
    frozen_key_value,
    down_factor_matrix,
    down_moment_first,
    down_moment_second,
    up_factor_matrix,
    up_moment_first,
    up_moment_second,
    down_gradient,
    up_gradient,
):
    n_dp = lax.axis_size("dp")
    n_tensor = lax.axis_size("tensor")
    chips = n_tensor // CORES
    replica = lax.axis_index("dp")
    tokens, features = prompt_hidden_input.shape
    width, columns = frozen_key_value.shape
    rank = up_factor_matrix.shape[0]
    parts = down_factor_matrix.shape[1]
    factors = parts * rank
    strips = columns // LANES
    down_rows = features // n_dp
    up_rows = rank // n_dp
    packed_rows = down_rows + up_rows * strips
    steps = range(1, chips)
    f32, bf16 = jnp.float32, jnp.bfloat16

    def to_sibling(value):
        return lax.ppermute(value, "tensor", [(t, t ^ 1) for t in range(n_tensor)])

    def to_chip(value, step):
        pairs = [
            (CORES * q + k, CORES * ((q + step) % chips) + k)
            for q in range(chips)
            for k in range(CORES)
        ]
        return lax.ppermute(value, "tensor", pairs)

    def by_rank(value):
        return jnp.transpose(value, (1, 2, 0)).reshape(factors, features)

    down_sent = by_rank(down_gradient[0])
    down_state = [by_rank(v) for v in (down_factor_matrix, down_moment_first, down_moment_second)]
    up_state = [up_factor_matrix, up_moment_first, up_moment_second]
    shares = jax.ShapeDtypeStruct((n_dp, packed_rows, LANES), bf16)
    window = pl.cdiv(down_rows + LANES, LANES) * LANES
    aligned = features % LANES == 0 and window <= features
    aligned = aligned and up_rows % 8 == 0 and down_rows % 16 == 0
    window = window if aligned else down_rows
    turns = [1, 2] if n_dp % 4 == 0 else [1, 1]
    turn = [turns[strip % 2] for strip in range(strips)]
    halves = min(COLUMN_HALVES, strips)
    wide = columns // halves
    groups = [range(k * strips // halves, (k + 1) * strips // halves) for k in range(halves)]
    out_shape = (shares,) + tuple(
        jax.ShapeDtypeStruct((len(group), features, LANES), bf16)
        for group in groups
        for _ in steps
    )
    packed, *taken = pl.pallas_call(
        functools.partial(begin_kernel, chips, turn),
        out_shape=out_shape,
        in_specs=anywhere(3),
        out_specs=tuple(anywhere(len(out_shape))),
        scratch_shapes=[
            pltpu.VMEM((factors, features), f32),
            pltpu.VMEM((rank, columns), f32),
            pltpu.VMEM(shares.shape, bf16),
            pltpu.VMEM((len(steps) * strips, features, LANES), bf16),
            pltpu.SemaphoreType.DMA((2 + len(steps) * strips,)),
            pltpu.SemaphoreType.DMA((n_dp + len(steps) * strips,)),
        ],
        compiler_params=pltpu.CompilerParams(vmem_limit_bytes=LARGE_VMEM_BYTES),
    )(down_sent, up_gradient[0], frozen_key_value)
    exchanged = lax.all_to_all(packed, "dp", 0, 0, tiled=True)
    if not aligned:
        down_state = [
            lax.dynamic_slice_in_dim(v, replica * down_rows, down_rows, 1) for v in down_state
        ]
        up_state = [lax.dynamic_slice_in_dim(v, replica * up_rows, up_rows, 0) for v in up_state]
    mine = []

    def send_half(half, after):
        blocks = taken[half * len(steps) : (half + 1) * len(steps)]
        if after is not None:
            blocks, _ = lax.optimization_barrier((blocks, after))
        mine.append([to_chip(value, step) for value, step in zip(blocks, steps)])

    send_half(0, None)

    gain = input_norm_gain[None, :]
    some = tokens // TOKEN_HALVES
    operands = [prompt_hidden_input, to_sibling(prompt_hidden_input), gain, to_sibling(gain)]

    def prepared(first, size, before, in_place, limit):
        if in_place:
            x_shape = (jax.ShapeDtypeStruct((size, CORES * features), bf16),)
            x_specs = tuple(in_vmem(1))
        else:
            x_shape = (jax.ShapeDtypeStruct((size, features), bf16),) * 2
            x_specs = tuple(anywhere(2))
        *x, squares = pl.pallas_call(
            functools.partial(prepare_kernel, first),
            out_shape=x_shape
            + (jax.ShapeDtypeStruct(((first + size) // LANES, LANES), f32),),
            in_specs=anywhere(2) + in_vmem(2 + len(before)),
            out_specs=x_specs + tuple(in_vmem(1)),
            scratch_shapes=[
                pltpu.VMEM((size, features), bf16),
                pltpu.VMEM((size, features), bf16),
                pltpu.VMEM((size, LANES), f32),
                pltpu.SemaphoreType.DMA((4 * pl.cdiv(size, LANES),)),
            ],
            compiler_params=pltpu.CompilerParams(vmem_limit_bytes=limit),
        )(*operands, *before)
        return x, squares

    cut = some // 2 // LANES * LANES
    x0, squares = prepared(0, some, [], True, PREPARE_VMEM_BYTES)
    x1 = []
    if cut > 0:
        x1, squares = prepared(some, cut, [squares], False, LARGE_VMEM_BYTES)
    exchanged, squares = lax.optimization_barrier((exchanged, squares))
    last, squares = prepared(some + cut, some - cut, [squares], False, LARGE_VMEM_BYTES)
    x1 = x1 + last
    def updated(final, after):
        scratch_shapes = [
            pltpu.VMEM((n_dp, packed_rows, LANES), bf16),
            pltpu.VMEM((3, factors, window), f32),
            pltpu.VMEM((3, up_rows, columns), f32),
            pltpu.SemaphoreType.DMA((max(7, n_dp),)),
        ]
        if final:
            out_shape = (
                jax.ShapeDtypeStruct((3, factors, down_rows), f32),
                jax.ShapeDtypeStruct((3, up_rows, columns), f32),
            )
        else:
            out_shape = (shares,)
            scratch_shapes.insert(0, pltpu.VMEM((packed_rows, LANES), bf16))
        return pl.pallas_call(
            functools.partial(adam_kernel, down_rows, final),
            out_shape=out_shape,
            in_specs=anywhere(7 + len(after)),
            out_specs=tuple(in_vmem(2) if final else anywhere(1)),
            scratch_shapes=scratch_shapes,
            compiler_params=pltpu.CompilerParams(
                vmem_limit_bytes=FINAL_VMEM_BYTES if final else LARGE_VMEM_BYTES
            ),
        )(exchanged, *down_state, *up_state, *after)

    (sent,) = updated(False, [])
    own_f = lax.all_to_all(sent, "dp", 0, 0, tiled=True)
    for half in range(1, halves):
        send_half(half, (mine[-1], sent))

    outside = [[] for _ in range(strips)]

    def swap_half(half, after):
        for value in mine[half]:
            value, _ = lax.optimization_barrier((value, after))
            split = pl.pallas_call(
                split_kernel,
                out_shape=(jax.ShapeDtypeStruct((features, LANES), bf16),) * len(groups[half]),
                in_specs=in_vmem(1),
                out_specs=tuple(in_vmem(len(groups[half]))),
                compiler_params=params(),
            )(value)
            for piece, strip in zip(split, groups[half]):
                pairs = [(i, i ^ turn[strip]) for i in range(n_dp)]
                outside[strip].append((piece, lax.ppermute(piece, "dp", pairs)))

    swap_half(0, sent)
    up_packed = packed_rows - down_rows
    more = pl.cdiv(3 * (tokens // LANES), up_packed)
    piece = jax.ShapeDtypeStruct((n_dp // FACTOR_PIECES, packed_rows, LANES), bf16)
    message, *pieces = pl.pallas_call(
        message_kernel,
        out_shape=(jax.ShapeDtypeStruct((n_dp + more, up_packed, LANES), bf16),)
        + (piece,) * FACTOR_PIECES,
        in_specs=anywhere(2),
        out_specs=tuple(in_vmem(1 + FACTOR_PIECES)),
        scratch_shapes=[
            pltpu.VMEM(squares.shape, f32),
            pltpu.SemaphoreType.DMA((2 + FACTOR_PIECES,)),
        ],
        compiler_params=params(),
    )(own_f, squares)
    messages = [to_chip(message, step) for step in steps]
    sibling_f = [to_sibling(piece) for piece in pieces]

    inv_rms = pl.pallas_call(
        functools.partial(inverse_kernel, width, n_dp),
        out_shape=jax.ShapeDtypeStruct((tokens, LANES), f32),
        in_specs=in_vmem(chips),
        out_specs=in_vmem(1)[0],
        compiler_params=params(),
    )(squares, *messages)

    scale = 0.5 / math.sqrt(width * rank)

    received = {}
    after = []
    weights_shape = jax.ShapeDtypeStruct((CORES * features, wide), bf16)
    product_shape = jax.ShapeDtypeStruct((some, wide), bf16)
    for half, group in enumerate(groups):
        static = (scale, parts, up_rows, group, columns)
        if half > 0:
            swap_half(half, products[0])
        for step in steps:
            blocks = [value for strip in group for value in outside[strip][step - 1]]
            arranged = pl.pallas_call(
                functools.partial(arrange_kernel, [turn[strip] for strip in group]),
                out_shape=weights_shape,
                in_specs=in_vmem(len(blocks)) + anywhere(len(after)),
                out_specs=in_vmem(1)[0],
                compiler_params=params(),
            )(*blocks, *after)
            weights, product = pl.pallas_call(
                functools.partial(outside_kernel, static, chips, step),
                out_shape=(weights_shape, product_shape),
                in_specs=in_vmem(3 + 2 * FACTOR_PIECES),
                out_specs=tuple(in_vmem(2)),
                compiler_params=params(),
            )(arranged, messages[step - 1], *x0, *pieces, *sibling_f)
            received.setdefault((0, half), []).append(to_chip(product, chips - step))
            second = pl.pallas_call(
                functools.partial(more_kernel, len(x1) // 2),
                out_shape=product_shape,
                in_specs=in_vmem(1 + len(x1)),
                out_specs=in_vmem(1)[0],
                compiler_params=params(),
            )(*x1, weights)
            products = [product, second]
            after = [second]
            received.setdefault((1, half), []).append(to_chip(second, chips - step))
        if half == 0:
            after = [received[0, 0][0]]

    after.append(received[1, 0][0])
    static = (scale, parts, up_rows, range(strips), columns, halves, len(x1) // 2)
    totals = pl.pallas_call(
        functools.partial(own_kernel, static),
        out_shape=(jax.ShapeDtypeStruct((tokens, wide), f32),) * halves,
        grid=(1,),
        in_specs=[
            pl.BlockSpec((features, columns), lambda i: (lax.axis_index("tensor"), 0)),
            pl.BlockSpec((features, columns), lambda i: (lax.axis_index("tensor") ^ 1, 0)),
        ]
        + in_vmem(2 * FACTOR_PIECES + 1 + len(x1))
        + anywhere(len(after)),
        out_specs=tuple(in_vmem(halves)),
        scratch_shapes=[pltpu.VMEM((CORES * features, columns), bf16)],
        compiler_params=params(),
        cost_estimate=pl.CostEstimate(
            flops=2 * tokens * CORES * features * columns,
            bytes_accessed=4 * tokens * features,
            transcendentals=0,
        ),
    )(frozen_key_value, frozen_key_value, *pieces, *sibling_f, *x0, *x1, *after)

    a_next, b_next = updated(True, totals[:1])
    a_next = jnp.transpose(a_next.reshape(3, parts, rank, down_rows), (0, 3, 1, 2))
    keys_values = None
    for at, values in received.items():
        keys_values = finish(
            totals[at[1]], inv_rms, values, at, (tokens, columns), keys_values
        )
    return (a_next, b_next, keys_values)


def solution(mesh):
    placed = (
        P("dp", "tensor"),
        P("tensor"),
        P(None, "tensor"),
        P("tensor", None, None),
        P("tensor", None, None),
        P("tensor", None, None),
        P(None, "tensor"),
        P(None, "tensor"),
        P(None, "tensor"),
        P("dp", "tensor", None, None),
        P("dp", None, "tensor"),
    )
    return jax.shard_map(
        body,
        mesh=mesh,
        in_specs=placed,
        out_specs=(
            P(None, ("tensor", "dp"), None, None),
            P(None, "dp", "tensor"),
            P("dp", "tensor"),
        ),
        check_vma=False,
    )
```

```python
import functools
import math

import jax
import jax.numpy as jnp
from jax import lax
from jax.experimental import pallas as pl
from jax.experimental.pallas import tpu as pltpu
from jax.sharding import PartitionSpec as P

KEY_VALUE_WIDTH = 1024
STEP = 100
CORES = 2
LANES = 128
COLUMN_HALVES = 2
TOKEN_HALVES = 2
FACTOR_PIECES = 2
VMEM_BYTES = 16 * 2**20
LARGE_VMEM_BYTES = 58 * 2**20
PREPARE_VMEM_BYTES = 49 * 2**20


def adaptive_moment_update(param, first, second, grad_mean):
    first_new = 0.9 * first + 0.1 * grad_mean
    second_new = 0.999 * second + 0.001 * grad_mean * grad_mean
    step_size = first_new / (1.0 - 0.9**STEP) / (jnp.sqrt(second_new / (1.0 - 0.999**STEP)) + 1e-08)
    return (param - 0.1 * step_size, first_new, second_new)


def in_vmem(count):
    return [pl.BlockSpec(memory_space=pltpu.VMEM)] * count


def anywhere(count):
    return [pl.BlockSpec(memory_space=pl.ANY)] * count


SCALARS = pl.BlockSpec(memory_space=pltpu.SMEM)


def params(**more):
    return pltpu.CompilerParams(vmem_limit_bytes=VMEM_BYTES, **more)


def pack(down, up, out_ref, ready):
    shares = out_ref.shape[0]
    down = down.T
    down_rows, up_rows = down.shape[0] // shares, up.shape[0] // shares
    for i in range(shares):
        pieces = [down[i * down_rows : (i + 1) * down_rows]]
        for k in range(up.shape[1] // LANES):
            pieces.append(up[i * up_rows : (i + 1) * up_rows, k * LANES : (k + 1) * LANES])
        out_ref[i] = jnp.concatenate(pieces, axis=0).astype(jnp.bfloat16)
        ready(i)


def first_lane(share, window, size):
    return jnp.minimum(share // LANES * LANES, size - window)


def begin_kernel(chips, turn, down_ref, up_ref, weights_ref, packed, *refs):
    outs, (down, up, blocks, strips, sem, sem_out) = refs[:-6], refs[-6:]
    features = strips.shape[1]
    place, replica = lax.axis_index("tensor"), lax.axis_index("dp")
    chip, core = place // CORES, place % CORES
    copies, back = [], []

    def add(source, target):
        copies.append(pltpu.make_async_copy(source, target, sem.at[len(copies)]))
        copies[-1].start()

    def add_back(source, target):
        back.append(pltpu.make_async_copy(source, target, sem_out.at[len(back)]))
        back[-1].start()

    add(down_ref, down)
    add(up_ref, up)
    targets = []
    for i, out in enumerate(outs):
        step, first = 1 + i % (chips - 1), i // (chips - 1) * out.shape[0]
        for k in range(out.shape[0]):
            half = (core + replica // turn[first + k]) % 2
            row = ((chip + step) % chips * CORES + half) * features
            add(
                weights_ref.at[
                    pl.ds(pl.multiple_of(row, features), features),
                    pl.ds((first + k) * LANES, LANES),
                ],
                strips.at[len(targets)],
            )
            targets.append(out.at[k])
    copies[0].wait()
    copies[1].wait()

    def ready(i):
        add_back(blocks.at[i], packed.at[i])
        if i == min(1, blocks.shape[0] - 1):
            for k, target in enumerate(targets):
                copies[2 + k].wait()
                add_back(strips.at[k], target)

    pack(down[...], up[...], blocks, ready)
    for copy in back:
        copy.wait()


def split_kernel(in_ref, *outs):
    for k, out in enumerate(outs):
        out[...] = in_ref[k]


def prepare_kernel(first, own_in, sibling_in, own_gain, sibling_gain, *refs):
    own, sibling, squares, sem = refs[-4:]
    rows, features = own.shape
    together = refs[-6].shape[1] > features
    outs, sums_ref = refs[-6 if together else -7 : -5], refs[-5]
    before = refs[: -6 if together else -7]
    block = LANES if rows % LANES == 0 else rows
    tile = 16 if block % 16 == 0 else block
    count = rows // block
    raw = ((own_in, own), (sibling_in, sibling))
    loads = [
        [
            pltpu.make_async_copy(
                source.at[pl.ds(first + k * block, block)],
                target.at[pl.ds(k * block, block)],
                sem.at[2 * k + side],
            )
            for side, (source, target) in enumerate(raw)
        ]
        for k in range(count)
    ]
    for pair in loads:
        for copy in pair:
            copy.start()
    stores = []
    for k in range(count):
        for copy in loads[k]:
            copy.wait()

        @pl.loop(0, block // tile, unroll=2)
        def _(i):
            at = pl.ds(pl.multiple_of(k * block + i * tile, tile), tile)
            total = None
            for side, (ref, gain) in enumerate(((own, own_gain), (sibling, sibling_gain))):
                value = ref[at, :].astype(jnp.float32)
                scaled = (value * gain[...]).astype(ref.dtype)
                if together:
                    outs[0][at, side * features : (side + 1) * features] = scaled
                else:
                    ref[at, :] = scaled
                total = value * value if total is None else total + value * value
            total = jnp.sum(total, axis=1, keepdims=True)
            squares[at, :] = jnp.broadcast_to(total, (tile, LANES))

        if not together:
            part = pl.ds(k * block, block)
            for side, (source, out) in enumerate(((own, outs[0]), (sibling, outs[1]))):
                place = sem.at[2 * (count + k) + side]
                stores.append(pltpu.make_async_copy(source.at[part], out.at[part], place))
                stores[-1].start()
    done = 0
    for ref in before:
        sums_ref[: ref.shape[0]] = ref[...]
        done = ref.shape[0]
    for i in range(rows // LANES):
        row = squares[i * LANES : (i + 1) * LANES, :].T[:1]
        sums_ref[done + i : done + i + 1] = row
    for copy in stores:
        copy.wait()


def message_kernel(factor_ref, sums_ref, out_ref, *refs):
    pieces, (sums, sem) = refs[:-2], refs[-2:]
    shares, up_rows = factor_ref.shape[0], out_ref.shape[1]
    sums_copy = pltpu.make_async_copy(sums_ref, sums, sem.at[1 + len(pieces)])
    sums_copy.start()
    copies = [
        pltpu.make_async_copy(
            factor_ref.at[:, pl.ds(factor_ref.shape[1] - up_rows, up_rows)],
            out_ref.at[pl.ds(0, shares)],
            sem.at[0],
        )
    ]
    for k, piece in enumerate(pieces):
        size = piece.shape[0]
        copies.append(
            pltpu.make_async_copy(factor_ref.at[pl.ds(k * size, size)], piece, sem.at[1 + k])
        )
    for copy in copies:
        copy.start()
    sums_copy.wait()
    left = sums[...]
    terms = []
    for _ in range(3):
        terms.append(left.astype(jnp.bfloat16).astype(jnp.float32))
        left = left - terms[-1]
    rest = (out_ref.shape[0] - shares) * up_rows - 3 * left.shape[0]
    if rest > 0:
        terms.append(jnp.zeros((rest, LANES), jnp.float32))
    rows = jnp.concatenate(terms, axis=0)
    for i in range(out_ref.shape[0] - shares):
        out_ref[shares + i] = rows[i * up_rows : (i + 1) * up_rows].astype(jnp.bfloat16)
    for copy in copies:
        copy.wait()


def inverse_kernel(width, shares, sums_ref, *refs):
    messages, out = refs[:-1], refs[-1]
    total = sums_ref[...]
    count = total.shape[0]
    for ref in messages:
        rows = [ref[i].astype(jnp.float32) for i in range(shares, ref.shape[0])]
        rows = jnp.concatenate(rows, axis=0)
        total += rows[:count] + rows[count : 2 * count] + rows[2 * count : 3 * count]
    inverse = lax.rsqrt(total / width + 1e-06)
    for i in range(count):
        out[i * LANES : (i + 1) * LANES, :] = jnp.broadcast_to(
            inverse[i : i + 1], (LANES, LANES)
        ).T


def update(total, down, up, a_ref, b_ref):
    down_rows = a_ref.shape[2]
    up_rows, columns = b_ref.shape[1:]
    strips = columns // LANES
    down_mean = total[:down_rows].T
    up_mean = jnp.concatenate(
        [total[down_rows + k * up_rows : down_rows + (k + 1) * up_rows] for k in range(strips)],
        axis=1,
    )
    p, m, v = adaptive_moment_update(*down(), down_mean)
    a_ref[0], a_ref[1], a_ref[2] = p, m, v
    pieces = [p.T]
    p, m, v = adaptive_moment_update(*up(), up_mean)
    b_ref[0], b_ref[1], b_ref[2] = p, m, v
    pieces += [p[:, k * LANES : (k + 1) * LANES] for k in range(strips)]
    return jnp.concatenate(pieces, axis=0).astype(jnp.bfloat16)


def adam_kernel(grad_in, *refs):
    state, refs = refs[:6], refs[6:]
    a_ref, b_ref, factor_ref, grad_ref, down_win, up_win, sem = refs
    replicas = grad_ref.shape[0]
    down_rows, window = a_ref.shape[2], down_win.shape[2]
    up_rows = up_win.shape[1]
    replica = lax.axis_index("dp")
    share = replica * down_rows
    size = down_rows * replicas
    copies = [pltpu.make_async_copy(grad_in, grad_ref, sem.at[6])]
    for i in range(3):
        down, up = state[i], state[3 + i]
        if window != down_rows:
            lane = pl.multiple_of(first_lane(share, window, size), LANES)
            down = down.at[:, pl.ds(lane, window)]
            up = up.at[pl.ds(pl.multiple_of(replica * up_rows, up_rows), up_rows)]
        copies.append(pltpu.make_async_copy(down, down_win.at[i], sem.at[i]))
        copies.append(pltpu.make_async_copy(up, up_win.at[i], sem.at[3 + i]))
    for copy in copies:
        copy.start()
    copies[0].wait()
    total = jnp.sum(grad_ref[...].astype(jnp.float32), axis=0) / replicas
    for copy in copies[1:]:
        copy.wait()

    def down():
        if window == down_rows:
            return [down_win[i] for i in range(3)]
        shift = window - (share - first_lane(share, window, size))
        return [pltpu.roll(down_win[i], shift, 1)[:, :down_rows] for i in range(3)]

    rounded = update(total, down, lambda: [up_win[i] for i in range(3)], a_ref, b_ref)
    for i in range(replicas):
        factor_ref[i] = rounded


def factor_a(refs, down_rows):
    pieces = []
    for ref in refs:
        for i in range(ref.shape[0]):
            if down_rows % 16 == 0:
                pieces.append(ref[i, :down_rows, :])
            else:
                pieces.append(ref[i].astype(jnp.float32)[:down_rows])
    return jnp.concatenate(pieces, axis=0).astype(jnp.bfloat16)


def factor_b(packed, part, parts, strip, up_rows):
    pieces = [
        packed[i].astype(jnp.float32)[strip * up_rows : (strip + 1) * up_rows]
        for i in range(packed.shape[0])
    ]
    value = jnp.concatenate(pieces, axis=0)
    rows = [jnp.where(part == j, value, jnp.zeros_like(value)) for j in range(parts)]
    return jnp.concatenate(rows, axis=0).astype(jnp.bfloat16)


def merge(scale, block, a, b):
    change = jnp.dot(a, b, preferred_element_type=jnp.float32)
    return (block.astype(jnp.float32) + scale * change).astype(jnp.bfloat16)


def multiply(groups, weights, *outs):
    wide = outs[0].shape[1]
    done = 0
    for xs in groups:
        rows = xs[0].shape[0]
        tile = rows // 2 if rows % 32 == 0 else rows

        @pl.loop(0, rows // tile)
        def _(i):
            at = pl.ds(pl.multiple_of(i * tile, tile), tile)
            to = pl.ds(pl.multiple_of(done + i * tile, 16), tile)
            value, first = None, 0
            for x in xs:
                size = x.shape[1]
                part = jnp.dot(
                    x[at, :], weights[first : first + size, :], preferred_element_type=jnp.float32
                )
                value, first = part if value is None else value + part, first + size
            for k, out in enumerate(outs):
                out[to, :] = value[:, k * wide : (k + 1) * wide].astype(out.dtype)

        done += rows


def up_factor(static, packed, owner):
    _, parts, up_rows, strips, columns = static
    part = owner * columns // KEY_VALUE_WIDTH
    return jnp.concatenate(
        [factor_b(packed, part, parts, strip, up_rows) for strip in strips], axis=1
    )


def arrange_kernel(turn, *refs):
    out = refs[-1]
    replica = lax.axis_index("dp")
    features = out.shape[0] // CORES
    for k, alternate in enumerate(turn):
        mine, other = refs[2 * k : 2 * k + 2]
        even = replica // alternate % 2 == 0
        lanes = slice(k * LANES, (k + 1) * LANES)
        out[:features, lanes] = jnp.where(even, mine[...], other[...])
        out[features:, lanes] = jnp.where(even, other[...], mine[...])


def outside_kernel(static, chips, step, blocks, b_ref, x, *refs):
    own_f, sibling_f = refs[:FACTOR_PIECES], refs[FACTOR_PIECES : 2 * FACTOR_PIECES]
    weights, product = refs[-2:]
    features = blocks.shape[0] // CORES
    down_rows = own_f[0].shape[1] - b_ref.shape[1]
    shares = FACTOR_PIECES * own_f[0].shape[0]
    place = lax.axis_index("tensor")
    owner = (place // CORES - step + chips) % chips * CORES + place % CORES
    b = up_factor(static, b_ref[:shares], owner)
    tile = 256 if features % 256 == 0 else features
    for side, factors in enumerate((own_f, sibling_f)):
        a = factor_a(factors, down_rows)
        for first in range(0, features, tile):
            rows = slice(side * features + first, side * features + first + tile)
            weights[rows, :] = merge(static[0], blocks[rows, :], a[first : first + tile], b)
    multiply([[x]], weights, product)


def more_kernel(groups, *refs):
    xs, (weights, product) = refs[:-2], refs[-2:]
    size = len(xs) // groups
    multiply([xs[k * size : (k + 1) * size] for k in range(groups)], weights, product)


def own_kernel(static, own_block, sibling_block, *refs):
    own_f, sibling_f = refs[:FACTOR_PIECES], refs[FACTOR_PIECES : 2 * FACTOR_PIECES]
    refs = refs[2 * FACTOR_PIECES :]
    groups, weights = [refs[:1]], refs[-1]
    for k in range(static[6]):
        groups.append(refs[1 + 2 * k : 3 + 2 * k])
    outs = refs[len(refs) - 1 - static[5] : -1]
    features = own_block.shape[0]
    wide = outs[0].shape[1]
    down_rows = own_f[0].shape[1] - len(static[3]) * static[2]
    b = jnp.concatenate([piece[:, down_rows:] for piece in own_f], axis=0)
    b = up_factor(static[:5], b, lax.axis_index("tensor"))
    for at, factors, block in ((0, own_f, own_block), (features, sibling_f, sibling_block)):
        weights[at : at + features] = merge(static[0], block[...], factor_a(factors, down_rows), b)
    multiply(groups, weights, *outs)


def finish_kernel(sources, first, own, inv, *refs):
    rows = pl.ds(first, refs[-1].shape[0])
    total = own[rows, :]
    for value in refs[:sources]:
        total = total + value[...].astype(jnp.float32)
    refs[-1][...] = (total * inv[rows, :1]).astype(refs[-1].dtype)


def finish(own, inv_rms, received, at, shape, before):
    block = received[0].shape
    operands = [own, inv_rms] + received
    in_specs = in_vmem(len(operands))
    aliases = {}
    if before is not None:
        aliases = {len(operands): 0}
        in_specs += anywhere(1)
        operands.append(before)
    return pl.pallas_call(
        functools.partial(finish_kernel, len(received), at[0] * block[0]),
        grid=(1,),
        out_shape=jax.ShapeDtypeStruct(shape, jnp.bfloat16),
        in_specs=in_specs,
        out_specs=pl.BlockSpec(block, lambda i: at),
        input_output_aliases=aliases,
        compiler_params=params(),
    )(*operands)


def body(
    prompt_hidden_input,
    input_norm_gain,
    frozen_key_value,
    down_factor_matrix,
    down_moment_first,
    down_moment_second,
    up_factor_matrix,
    up_moment_first,
    up_moment_second,
    down_gradient,
    up_gradient,
):
    n_dp = lax.axis_size("dp")
    n_tensor = lax.axis_size("tensor")
    chips = n_tensor // CORES
    replica = lax.axis_index("dp")
    tokens, features = prompt_hidden_input.shape
    width, columns = frozen_key_value.shape
    rank = up_factor_matrix.shape[0]
    parts = down_factor_matrix.shape[1]
    factors = parts * rank
    strips = columns // LANES
    down_rows = features // n_dp
    up_rows = rank // n_dp
    packed_rows = down_rows + up_rows * strips
    steps = range(1, chips)
    f32, bf16 = jnp.float32, jnp.bfloat16

    def to_sibling(value):
        return lax.ppermute(value, "tensor", [(t, t ^ 1) for t in range(n_tensor)])

    def to_chip(value, step):
        pairs = [
            (CORES * q + k, CORES * ((q + step) % chips) + k)
            for q in range(chips)
            for k in range(CORES)
        ]
        return lax.ppermute(value, "tensor", pairs)

    def by_rank(value):
        return jnp.transpose(value, (1, 2, 0)).reshape(factors, features)

    down_sent = by_rank(down_gradient[0])
    down_state = [by_rank(v) for v in (down_factor_matrix, down_moment_first, down_moment_second)]
    up_state = [up_factor_matrix, up_moment_first, up_moment_second]
    shares = jax.ShapeDtypeStruct((n_dp, packed_rows, LANES), bf16)
    window = pl.cdiv(down_rows + LANES, LANES) * LANES
    aligned = features % LANES == 0 and window <= features
    aligned = aligned and up_rows % 8 == 0 and down_rows % 16 == 0
    window = window if aligned else down_rows
    turns = [1, 2] if n_dp % 4 == 0 else [1, 1]
    turn = [turns[strip % 2] for strip in range(strips)]
    halves = min(COLUMN_HALVES, strips)
    wide = columns // halves
    groups = [range(k * strips // halves, (k + 1) * strips // halves) for k in range(halves)]
    out_shape = (shares,) + tuple(
        jax.ShapeDtypeStruct((len(group), features, LANES), bf16)
        for group in groups
        for _ in steps
    )
    packed, *taken = pl.pallas_call(
        functools.partial(begin_kernel, chips, turn),
        out_shape=out_shape,
        in_specs=anywhere(3),
        out_specs=tuple(anywhere(len(out_shape))),
        scratch_shapes=[
            pltpu.VMEM((factors, features), f32),
            pltpu.VMEM((rank, columns), f32),
            pltpu.VMEM(shares.shape, bf16),
            pltpu.VMEM((len(steps) * strips, features, LANES), bf16),
            pltpu.SemaphoreType.DMA((2 + len(steps) * strips,)),
            pltpu.SemaphoreType.DMA((n_dp + len(steps) * strips,)),
        ],
        compiler_params=pltpu.CompilerParams(vmem_limit_bytes=LARGE_VMEM_BYTES),
    )(down_sent, up_gradient[0], frozen_key_value)
    exchanged = lax.all_to_all(packed, "dp", 0, 0, tiled=True)
    if not aligned:
        down_state = [
            lax.dynamic_slice_in_dim(v, replica * down_rows, down_rows, 1) for v in down_state
        ]
        up_state = [lax.dynamic_slice_in_dim(v, replica * up_rows, up_rows, 0) for v in up_state]
    mine = []

    def send_half(half, after):
        blocks = taken[half * len(steps) : (half + 1) * len(steps)]
        if after is not None:
            blocks, _ = lax.optimization_barrier((blocks, after))
        mine.append([to_chip(value, step) for value, step in zip(blocks, steps)])

    send_half(0, None)

    gain = input_norm_gain[None, :]
    some = tokens // TOKEN_HALVES
    operands = [prompt_hidden_input, to_sibling(prompt_hidden_input), gain, to_sibling(gain)]

    def prepared(first, size, before, in_place, limit):
        if in_place:
            x_shape = (jax.ShapeDtypeStruct((size, CORES * features), bf16),)
            x_specs = tuple(in_vmem(1))
        else:
            x_shape = (jax.ShapeDtypeStruct((size, features), bf16),) * 2
            x_specs = tuple(anywhere(2))
        *x, squares = pl.pallas_call(
            functools.partial(prepare_kernel, first),
            out_shape=x_shape
            + (jax.ShapeDtypeStruct(((first + size) // LANES, LANES), f32),),
            in_specs=anywhere(2) + in_vmem(2 + len(before)),
            out_specs=x_specs + tuple(in_vmem(1)),
            scratch_shapes=[
                pltpu.VMEM((size, features), bf16),
                pltpu.VMEM((size, features), bf16),
                pltpu.VMEM((size, LANES), f32),
                pltpu.SemaphoreType.DMA((4 * pl.cdiv(size, LANES),)),
            ],
            compiler_params=pltpu.CompilerParams(vmem_limit_bytes=limit),
        )(*operands, *before)
        return x, squares

    cut = some // 2 // LANES * LANES
    x0, squares = prepared(0, some, [], True, PREPARE_VMEM_BYTES)
    x1 = []
    if cut > 0:
        x1, squares = prepared(some, cut, [squares], False, LARGE_VMEM_BYTES)
    exchanged, squares = lax.optimization_barrier((exchanged, squares))
    last, squares = prepared(some + cut, some - cut, [squares], False, LARGE_VMEM_BYTES)
    x1 = x1 + last
    a_next, b_next, sent = pl.pallas_call(
        adam_kernel,
        out_shape=(
            jax.ShapeDtypeStruct((3, factors, down_rows), f32),
            jax.ShapeDtypeStruct((3, up_rows, columns), f32),
            shares,
        ),
        in_specs=anywhere(7),
        out_specs=tuple(in_vmem(3)),
        scratch_shapes=[
            pltpu.VMEM((n_dp, packed_rows, LANES), bf16),
            pltpu.VMEM((3, factors, window), f32),
            pltpu.VMEM((3, up_rows, columns), f32),
            pltpu.SemaphoreType.DMA((7,)),
        ],
        compiler_params=pltpu.CompilerParams(vmem_limit_bytes=LARGE_VMEM_BYTES),
    )(exchanged, *down_state, *up_state)
    own_f = lax.all_to_all(sent, "dp", 0, 0, tiled=True)
    for half in range(1, halves):
        send_half(half, (mine[-1], sent))
    a_next = jnp.transpose(a_next.reshape(3, parts, rank, down_rows), (0, 3, 1, 2))

    outside = [[] for _ in range(strips)]

    def swap_half(half, after):
        for value in mine[half]:
            value, _ = lax.optimization_barrier((value, after))
            split = pl.pallas_call(
                split_kernel,
                out_shape=(jax.ShapeDtypeStruct((features, LANES), bf16),) * len(groups[half]),
                in_specs=in_vmem(1),
                out_specs=tuple(in_vmem(len(groups[half]))),
                compiler_params=params(),
            )(value)
            for piece, strip in zip(split, groups[half]):
                pairs = [(i, i ^ turn[strip]) for i in range(n_dp)]
                outside[strip].append((piece, lax.ppermute(piece, "dp", pairs)))

    swap_half(0, sent)
    up_packed = packed_rows - down_rows
    more = pl.cdiv(3 * (tokens // LANES), up_packed)
    piece = jax.ShapeDtypeStruct((n_dp // FACTOR_PIECES, packed_rows, LANES), bf16)
    message, *pieces = pl.pallas_call(
        message_kernel,
        out_shape=(jax.ShapeDtypeStruct((n_dp + more, up_packed, LANES), bf16),)
        + (piece,) * FACTOR_PIECES,
        in_specs=anywhere(2),
        out_specs=tuple(in_vmem(1 + FACTOR_PIECES)),
        scratch_shapes=[
            pltpu.VMEM(squares.shape, f32),
            pltpu.SemaphoreType.DMA((2 + FACTOR_PIECES,)),
        ],
        compiler_params=params(),
    )(own_f, squares)
    messages = [to_chip(message, step) for step in steps]
    sibling_f = [to_sibling(piece) for piece in pieces]

    inv_rms = pl.pallas_call(
        functools.partial(inverse_kernel, width, n_dp),
        out_shape=jax.ShapeDtypeStruct((tokens, LANES), f32),
        in_specs=in_vmem(chips),
        out_specs=in_vmem(1)[0],
        compiler_params=params(),
    )(squares, *messages)

    scale = 0.5 / math.sqrt(width * rank)

    received = {}
    after = []
    weights_shape = jax.ShapeDtypeStruct((CORES * features, wide), bf16)
    product_shape = jax.ShapeDtypeStruct((some, wide), bf16)
    for half, group in enumerate(groups):
        static = (scale, parts, up_rows, group, columns)
        if half > 0:
            swap_half(half, products[0])
        for step in steps:
            blocks = [value for strip in group for value in outside[strip][step - 1]]
            arranged = pl.pallas_call(
                functools.partial(arrange_kernel, [turn[strip] for strip in group]),
                out_shape=weights_shape,
                in_specs=in_vmem(len(blocks)) + anywhere(len(after)),
                out_specs=in_vmem(1)[0],
                compiler_params=params(),
            )(*blocks, *after)
            weights, product = pl.pallas_call(
                functools.partial(outside_kernel, static, chips, step),
                out_shape=(weights_shape, product_shape),
                in_specs=in_vmem(3 + 2 * FACTOR_PIECES),
                out_specs=tuple(in_vmem(2)),
                compiler_params=params(),
            )(arranged, messages[step - 1], *x0, *pieces, *sibling_f)
            received.setdefault((0, half), []).append(to_chip(product, chips - step))
            second = pl.pallas_call(
                functools.partial(more_kernel, len(x1) // 2),
                out_shape=product_shape,
                in_specs=in_vmem(1 + len(x1)),
                out_specs=in_vmem(1)[0],
                compiler_params=params(),
            )(*x1, weights)
            products = [product, second]
            after = [second]
            received.setdefault((1, half), []).append(to_chip(second, chips - step))
        if half == 0:
            after = [received[0, 0][0]]

    after.append(received[1, 0][0])
    static = (scale, parts, up_rows, range(strips), columns, halves, len(x1) // 2)
    totals = pl.pallas_call(
        functools.partial(own_kernel, static),
        out_shape=(jax.ShapeDtypeStruct((tokens, wide), f32),) * halves,
        grid=(1,),
        in_specs=[
            pl.BlockSpec((features, columns), lambda i: (lax.axis_index("tensor"), 0)),
            pl.BlockSpec((features, columns), lambda i: (lax.axis_index("tensor") ^ 1, 0)),
        ]
        + in_vmem(2 * FACTOR_PIECES + 1 + len(x1))
        + anywhere(len(after)),
        out_specs=tuple(in_vmem(halves)),
        scratch_shapes=[pltpu.VMEM((CORES * features, columns), bf16)],
        compiler_params=params(),
        cost_estimate=pl.CostEstimate(
            flops=2 * tokens * CORES * features * columns,
            bytes_accessed=4 * tokens * features,
            transcendentals=0,
        ),
    )(frozen_key_value, frozen_key_value, *pieces, *sibling_f, *x0, *x1, *after)

    keys_values = None
    for at, values in received.items():
        keys_values = finish(
            totals[at[1]], inv_rms, values, at, (tokens, columns), keys_values
        )
    return (a_next, b_next, keys_values)


def solution(mesh):
    placed = (
        P("dp", "tensor"),
        P("tensor"),
        P(None, "tensor"),
        P("tensor", None, None),
        P("tensor", None, None),
        P("tensor", None, None),
        P(None, "tensor"),
        P(None, "tensor"),
        P(None, "tensor"),
        P("dp", "tensor", None, None),
        P("dp", None, "tensor"),
    )
    return jax.shard_map(
        body,
        mesh=mesh,
        in_specs=placed,
        out_specs=(
            P(None, ("tensor", "dp"), None, None),
            P(None, "dp", "tensor"),
            P("dp", "tensor"),
        ),
        check_vma=False,
    )
```

```python
import functools
import math

import jax
import jax.numpy as jnp
from jax import lax
from jax.experimental import pallas as pl
from jax.experimental.pallas import tpu as pltpu
from jax.sharding import PartitionSpec as P

KEY_VALUE_WIDTH = 1024
STEP = 100
CORES = 2
LANES = 128
COLUMN_HALVES = 2
TOKEN_HALVES = 2
FACTOR_PIECES = 2
VMEM_BYTES = 16 * 2**20
LARGE_VMEM_BYTES = 58 * 2**20
PREPARE_VMEM_BYTES = 49 * 2**20


def adaptive_moment_update(param, first, second, grad_mean):
    first_new = 0.9 * first + 0.1 * grad_mean
    second_new = 0.999 * second + 0.001 * grad_mean * grad_mean
    step_size = first_new / (1.0 - 0.9**STEP) / (jnp.sqrt(second_new / (1.0 - 0.999**STEP)) + 1e-08)
    return (param - 0.1 * step_size, first_new, second_new)


def in_vmem(count):
    return [pl.BlockSpec(memory_space=pltpu.VMEM)] * count


def anywhere(count):
    return [pl.BlockSpec(memory_space=pl.ANY)] * count


SCALARS = pl.BlockSpec(memory_space=pltpu.SMEM)


def params(**more):
    return pltpu.CompilerParams(vmem_limit_bytes=VMEM_BYTES, **more)


def pack(down, up, out_ref, ready):
    shares = out_ref.shape[0]
    down = down.T
    down_rows, up_rows = down.shape[0] // shares, up.shape[0] // shares
    for i in range(shares):
        pieces = [down[i * down_rows : (i + 1) * down_rows]]
        for k in range(up.shape[1] // LANES):
            pieces.append(up[i * up_rows : (i + 1) * up_rows, k * LANES : (k + 1) * LANES])
        out_ref[i] = jnp.concatenate(pieces, axis=0).astype(jnp.bfloat16)
        ready(i)


def first_lane(share, window, size):
    return jnp.minimum(share // LANES * LANES, size - window)


def begin_kernel(chips, turn, down_ref, up_ref, weights_ref, packed, *refs):
    outs, (down, up, blocks, strips, sem, sem_out) = refs[:-6], refs[-6:]
    features = strips.shape[1]
    place, replica = lax.axis_index("tensor"), lax.axis_index("dp")
    chip, core = place // CORES, place % CORES
    copies, back = [], []

    def add(source, target):
        copies.append(pltpu.make_async_copy(source, target, sem.at[len(copies)]))
        copies[-1].start()

    def add_back(source, target):
        back.append(pltpu.make_async_copy(source, target, sem_out.at[len(back)]))
        back[-1].start()

    add(down_ref, down)
    add(up_ref, up)
    targets = []
    for i, out in enumerate(outs):
        step, first = 1 + i % (chips - 1), i // (chips - 1) * out.shape[0]
        for k in range(out.shape[0]):
            half = (core + replica // turn[first + k]) % 2
            row = ((chip + step) % chips * CORES + half) * features
            add(
                weights_ref.at[
                    pl.ds(pl.multiple_of(row, features), features),
                    pl.ds((first + k) * LANES, LANES),
                ],
                strips.at[len(targets)],
            )
            targets.append(out.at[k])
    copies[0].wait()
    copies[1].wait()

    def ready(i):
        add_back(blocks.at[i], packed.at[i])
        if i == min(1, blocks.shape[0] - 1):
            for k, target in enumerate(targets):
                copies[2 + k].wait()
                add_back(strips.at[k], target)

    pack(down[...], up[...], blocks, ready)
    for copy in back:
        copy.wait()


def split_kernel(in_ref, *outs):
    for k, out in enumerate(outs):
        out[...] = in_ref[k]


def prepare_kernel(first, summed, own_in, sibling_in, own_gain, sibling_gain, *refs):
    own, sibling, squares, sem = refs[-4:]
    copied, features = own.shape
    refs = refs[:-4]
    before, sums_ref = [], None
    if summed:
        refs, sums_ref = refs[:-1], refs[-1]
    together = refs[-1].shape[1] > features
    outs = refs[-1:] if together else refs[-2:]
    before = refs[: -len(outs)]
    rows = outs[0].shape[0]
    block = LANES if rows % LANES == 0 else rows
    tile = 16 if block % 16 == 0 else block
    raw = ((own_in, own), (sibling_in, sibling))
    loads = [
        [
            pltpu.make_async_copy(
                source.at[pl.ds(first + k * block, block)],
                target.at[pl.ds(k * block, block)],
                sem.at[2 * k + side],
            )
            for side, (source, target) in enumerate(raw)
        ]
        for k in range(copied // block)
    ]
    for pair in loads:
        for copy in pair:
            copy.start()
    stores = []
    for k, pair in enumerate(loads):
        for copy in pair:
            copy.wait()
        scale, add = k * block < rows, k * block < summed

        @pl.loop(0, block // tile, unroll=2)
        def _(i):
            at = pl.ds(pl.multiple_of(k * block + i * tile, tile), tile)
            total = None
            for side, (ref, gain) in enumerate(((own, own_gain), (sibling, sibling_gain))):
                value = ref[at, :].astype(jnp.float32)
                if scale:
                    scaled = (value * gain[...]).astype(ref.dtype)
                    if together:
                        outs[0][at, side * features : (side + 1) * features] = scaled
                    else:
                        ref[at, :] = scaled
                if add:
                    total = value * value if total is None else total + value * value
            if add:
                total = jnp.sum(total, axis=1, keepdims=True)
                squares[at, :] = jnp.broadcast_to(total, (tile, LANES))

        if scale and not together:
            part = pl.ds(k * block, block)
            for side, (source, out) in enumerate(((own, outs[0]), (sibling, outs[1]))):
                place = sem.at[2 * (len(loads) + k) + side]
                stores.append(pltpu.make_async_copy(source.at[part], out.at[part], place))
                stores[-1].start()
    if summed:
        done = 0
        for ref in before:
            sums_ref[: ref.shape[0]] = ref[...]
            done = ref.shape[0]
        for i in range(summed // LANES):
            row = squares[i * LANES : (i + 1) * LANES, :].T[:1]
            sums_ref[done + i : done + i + 1] = row
    for copy in stores:
        copy.wait()


def message_kernel(factor_ref, sums_ref, out_ref, *refs):
    pieces, (sums, sem) = refs[:-2], refs[-2:]
    shares, up_rows = factor_ref.shape[0], out_ref.shape[1]
    sums_copy = pltpu.make_async_copy(sums_ref, sums, sem.at[1 + len(pieces)])
    sums_copy.start()
    copies = [
        pltpu.make_async_copy(
            factor_ref.at[:, pl.ds(factor_ref.shape[1] - up_rows, up_rows)],
            out_ref.at[pl.ds(0, shares)],
            sem.at[0],
        )
    ]
    for k, piece in enumerate(pieces):
        size = piece.shape[0]
        copies.append(
            pltpu.make_async_copy(factor_ref.at[pl.ds(k * size, size)], piece, sem.at[1 + k])
        )
    for copy in copies:
        copy.start()
    sums_copy.wait()
    left = sums[...]
    terms = []
    for _ in range(3):
        terms.append(left.astype(jnp.bfloat16).astype(jnp.float32))
        left = left - terms[-1]
    rest = (out_ref.shape[0] - shares) * up_rows - 3 * left.shape[0]
    if rest > 0:
        terms.append(jnp.zeros((rest, LANES), jnp.float32))
    rows = jnp.concatenate(terms, axis=0)
    for i in range(out_ref.shape[0] - shares):
        out_ref[shares + i] = rows[i * up_rows : (i + 1) * up_rows].astype(jnp.bfloat16)
    for copy in copies:
        copy.wait()


def inverse_kernel(width, shares, sums_ref, *refs):
    messages, out = refs[:-1], refs[-1]
    total = sums_ref[...]
    count = total.shape[0]
    for ref in messages:
        rows = [ref[i].astype(jnp.float32) for i in range(shares, ref.shape[0])]
        rows = jnp.concatenate(rows, axis=0)
        total += rows[:count] + rows[count : 2 * count] + rows[2 * count : 3 * count]
    inverse = lax.rsqrt(total / width + 1e-06)
    for i in range(count):
        out[i * LANES : (i + 1) * LANES, :] = jnp.broadcast_to(
            inverse[i : i + 1], (LANES, LANES)
        ).T


def update(total, down, up, a_ref, b_ref):
    down_rows = a_ref.shape[2]
    up_rows, columns = b_ref.shape[1:]
    strips = columns // LANES
    down_mean = total[:down_rows].T
    up_mean = jnp.concatenate(
        [total[down_rows + k * up_rows : down_rows + (k + 1) * up_rows] for k in range(strips)],
        axis=1,
    )
    p, m, v = adaptive_moment_update(*down(), down_mean)
    a_ref[0], a_ref[1], a_ref[2] = p, m, v
    pieces = [p.T]
    p, m, v = adaptive_moment_update(*up(), up_mean)
    b_ref[0], b_ref[1], b_ref[2] = p, m, v
    pieces += [p[:, k * LANES : (k + 1) * LANES] for k in range(strips)]
    return jnp.concatenate(pieces, axis=0).astype(jnp.bfloat16)


def adam_kernel(grad_in, *refs):
    state, refs = refs[:6], refs[6:]
    a_ref, b_ref, factor_ref, grad_ref, down_win, up_win, sem = refs
    replicas = grad_ref.shape[0]
    down_rows, window = a_ref.shape[2], down_win.shape[2]
    up_rows = up_win.shape[1]
    replica = lax.axis_index("dp")
    share = replica * down_rows
    size = down_rows * replicas
    copies = [pltpu.make_async_copy(grad_in, grad_ref, sem.at[6])]
    for i in range(3):
        down, up = state[i], state[3 + i]
        if window != down_rows:
            lane = pl.multiple_of(first_lane(share, window, size), LANES)
            down = down.at[:, pl.ds(lane, window)]
            up = up.at[pl.ds(pl.multiple_of(replica * up_rows, up_rows), up_rows)]
        copies.append(pltpu.make_async_copy(down, down_win.at[i], sem.at[i]))
        copies.append(pltpu.make_async_copy(up, up_win.at[i], sem.at[3 + i]))
    for copy in copies:
        copy.start()
    copies[0].wait()
    total = jnp.sum(grad_ref[...].astype(jnp.float32), axis=0) / replicas
    for copy in copies[1:]:
        copy.wait()

    def down():
        if window == down_rows:
            return [down_win[i] for i in range(3)]
        shift = window - (share - first_lane(share, window, size))
        return [pltpu.roll(down_win[i], shift, 1)[:, :down_rows] for i in range(3)]

    rounded = update(total, down, lambda: [up_win[i] for i in range(3)], a_ref, b_ref)
    for i in range(replicas):
        factor_ref[i] = rounded


def factor_a(refs, down_rows):
    pieces = []
    for ref in refs:
        for i in range(ref.shape[0]):
            if down_rows % 16 == 0:
                pieces.append(ref[i, :down_rows, :])
            else:
                pieces.append(ref[i].astype(jnp.float32)[:down_rows])
    return jnp.concatenate(pieces, axis=0).astype(jnp.bfloat16)


def factor_b(packed, part, parts, strip, up_rows):
    pieces = [
        packed[i].astype(jnp.float32)[strip * up_rows : (strip + 1) * up_rows]
        for i in range(packed.shape[0])
    ]
    value = jnp.concatenate(pieces, axis=0)
    rows = [jnp.where(part == j, value, jnp.zeros_like(value)) for j in range(parts)]
    return jnp.concatenate(rows, axis=0).astype(jnp.bfloat16)


def merge(scale, block, a, b):
    change = jnp.dot(a, b, preferred_element_type=jnp.float32)
    return (block.astype(jnp.float32) + scale * change).astype(jnp.bfloat16)


def multiply(groups, weights, *outs):
    wide = outs[0].shape[1]
    done = 0
    for xs in groups:
        rows = xs[0].shape[0]
        tile = rows // 2 if rows % 32 == 0 else rows

        @pl.loop(0, rows // tile)
        def _(i):
            at = pl.ds(pl.multiple_of(i * tile, tile), tile)
            to = pl.ds(pl.multiple_of(done + i * tile, 16), tile)
            value, first = None, 0
            for x in xs:
                size = x.shape[1]
                part = jnp.dot(
                    x[at, :], weights[first : first + size, :], preferred_element_type=jnp.float32
                )
                value, first = part if value is None else value + part, first + size
            for k, out in enumerate(outs):
                out[to, :] = value[:, k * wide : (k + 1) * wide].astype(out.dtype)

        done += rows


def up_factor(static, packed, owner):
    _, parts, up_rows, strips, columns = static
    part = owner * columns // KEY_VALUE_WIDTH
    return jnp.concatenate(
        [factor_b(packed, part, parts, strip, up_rows) for strip in strips], axis=1
    )


def arrange_kernel(turn, *refs):
    out = refs[-1]
    replica = lax.axis_index("dp")
    features = out.shape[0] // CORES
    for k, alternate in enumerate(turn):
        mine, other = refs[2 * k : 2 * k + 2]
        even = replica // alternate % 2 == 0
        lanes = slice(k * LANES, (k + 1) * LANES)
        out[:features, lanes] = jnp.where(even, mine[...], other[...])
        out[features:, lanes] = jnp.where(even, other[...], mine[...])


def outside_kernel(static, chips, step, blocks, b_ref, x, *refs):
    own_f, sibling_f = refs[:FACTOR_PIECES], refs[FACTOR_PIECES : 2 * FACTOR_PIECES]
    weights, product = refs[-2:]
    features = blocks.shape[0] // CORES
    down_rows = own_f[0].shape[1] - b_ref.shape[1]
    shares = FACTOR_PIECES * own_f[0].shape[0]
    place = lax.axis_index("tensor")
    owner = (place // CORES - step + chips) % chips * CORES + place % CORES
    b = up_factor(static, b_ref[:shares], owner)
    tile = 256 if features % 256 == 0 else features
    for side, factors in enumerate((own_f, sibling_f)):
        a = factor_a(factors, down_rows)
        for first in range(0, features, tile):
            rows = slice(side * features + first, side * features + first + tile)
            weights[rows, :] = merge(static[0], blocks[rows, :], a[first : first + tile], b)
    multiply([[x]], weights, product)


def more_kernel(groups, *refs):
    xs, (weights, product) = refs[:-2], refs[-2:]
    size = len(xs) // groups
    multiply([xs[k * size : (k + 1) * size] for k in range(groups)], weights, product)


def own_kernel(static, own_block, sibling_block, *refs):
    own_f, sibling_f = refs[:FACTOR_PIECES], refs[FACTOR_PIECES : 2 * FACTOR_PIECES]
    refs = refs[2 * FACTOR_PIECES :]
    groups, weights = [refs[:1]], refs[-1]
    for k in range(static[6]):
        groups.append(refs[1 + 2 * k : 3 + 2 * k])
    outs = refs[len(refs) - 1 - static[5] : -1]
    features = own_block.shape[0]
    wide = outs[0].shape[1]
    down_rows = own_f[0].shape[1] - len(static[3]) * static[2]
    b = jnp.concatenate([piece[:, down_rows:] for piece in own_f], axis=0)
    b = up_factor(static[:5], b, lax.axis_index("tensor"))
    for at, factors, block in ((0, own_f, own_block), (features, sibling_f, sibling_block)):
        weights[at : at + features] = merge(static[0], block[...], factor_a(factors, down_rows), b)
    multiply(groups, weights, *outs)


def finish_kernel(sources, first, own, inv, *refs):
    rows = pl.ds(first, refs[-1].shape[0])
    total = own[rows, :]
    for value in refs[:sources]:
        total = total + value[...].astype(jnp.float32)
    refs[-1][...] = (total * inv[rows, :1]).astype(refs[-1].dtype)


def finish(own, inv_rms, received, at, shape, before):
    block = received[0].shape
    operands = [own, inv_rms] + received
    in_specs = in_vmem(len(operands))
    aliases = {}
    if before is not None:
        aliases = {len(operands): 0}
        in_specs += anywhere(1)
        operands.append(before)
    return pl.pallas_call(
        functools.partial(finish_kernel, len(received), at[0] * block[0]),
        grid=(1,),
        out_shape=jax.ShapeDtypeStruct(shape, jnp.bfloat16),
        in_specs=in_specs,
        out_specs=pl.BlockSpec(block, lambda i: at),
        input_output_aliases=aliases,
        compiler_params=params(),
    )(*operands)


def body(
    prompt_hidden_input,
    input_norm_gain,
    frozen_key_value,
    down_factor_matrix,
    down_moment_first,
    down_moment_second,
    up_factor_matrix,
    up_moment_first,
    up_moment_second,
    down_gradient,
    up_gradient,
):
    n_dp = lax.axis_size("dp")
    n_tensor = lax.axis_size("tensor")
    chips = n_tensor // CORES
    replica = lax.axis_index("dp")
    tokens, features = prompt_hidden_input.shape
    width, columns = frozen_key_value.shape
    rank = up_factor_matrix.shape[0]
    parts = down_factor_matrix.shape[1]
    factors = parts * rank
    strips = columns // LANES
    down_rows = features // n_dp
    up_rows = rank // n_dp
    packed_rows = down_rows + up_rows * strips
    steps = range(1, chips)
    f32, bf16 = jnp.float32, jnp.bfloat16

    def to_sibling(value):
        return lax.ppermute(value, "tensor", [(t, t ^ 1) for t in range(n_tensor)])

    def to_chip(value, step):
        pairs = [
            (CORES * q + k, CORES * ((q + step) % chips) + k)
            for q in range(chips)
            for k in range(CORES)
        ]
        return lax.ppermute(value, "tensor", pairs)

    def by_rank(value):
        return jnp.transpose(value, (1, 2, 0)).reshape(factors, features)

    down_sent = by_rank(down_gradient[0])
    down_state = [by_rank(v) for v in (down_factor_matrix, down_moment_first, down_moment_second)]
    up_state = [up_factor_matrix, up_moment_first, up_moment_second]
    shares = jax.ShapeDtypeStruct((n_dp, packed_rows, LANES), bf16)
    window = pl.cdiv(down_rows + LANES, LANES) * LANES
    aligned = features % LANES == 0 and window <= features
    aligned = aligned and up_rows % 8 == 0 and down_rows % 16 == 0
    window = window if aligned else down_rows
    turns = [1, 2] if n_dp % 4 == 0 else [1, 1]
    turn = [turns[strip % 2] for strip in range(strips)]
    halves = min(COLUMN_HALVES, strips)
    wide = columns // halves
    groups = [range(k * strips // halves, (k + 1) * strips // halves) for k in range(halves)]
    out_shape = (shares,) + tuple(
        jax.ShapeDtypeStruct((len(group), features, LANES), bf16)
        for group in groups
        for _ in steps
    )
    packed, *taken = pl.pallas_call(
        functools.partial(begin_kernel, chips, turn),
        out_shape=out_shape,
        in_specs=anywhere(3),
        out_specs=tuple(anywhere(len(out_shape))),
        scratch_shapes=[
            pltpu.VMEM((factors, features), f32),
            pltpu.VMEM((rank, columns), f32),
            pltpu.VMEM(shares.shape, bf16),
            pltpu.VMEM((len(steps) * strips, features, LANES), bf16),
            pltpu.SemaphoreType.DMA((2 + len(steps) * strips,)),
            pltpu.SemaphoreType.DMA((n_dp + len(steps) * strips,)),
        ],
        compiler_params=pltpu.CompilerParams(vmem_limit_bytes=LARGE_VMEM_BYTES),
    )(down_sent, up_gradient[0], frozen_key_value)
    exchanged = lax.all_to_all(packed, "dp", 0, 0, tiled=True)
    if not aligned:
        down_state = [
            lax.dynamic_slice_in_dim(v, replica * down_rows, down_rows, 1) for v in down_state
        ]
        up_state = [lax.dynamic_slice_in_dim(v, replica * up_rows, up_rows, 0) for v in up_state]
    mine = []

    def send_half(half, after):
        blocks = taken[half * len(steps) : (half + 1) * len(steps)]
        if after is not None:
            blocks, _ = lax.optimization_barrier((blocks, after))
        mine.append([to_chip(value, step) for value, step in zip(blocks, steps)])

    send_half(0, None)

    gain = input_norm_gain[None, :]
    some = tokens // TOKEN_HALVES
    operands = [prompt_hidden_input, to_sibling(prompt_hidden_input), gain, to_sibling(gain)]

    def prepared(first, size, summed, before, in_place, limit):
        if in_place:
            x_shape = (jax.ShapeDtypeStruct((size, CORES * features), bf16),)
            x_specs = tuple(in_vmem(1))
        else:
            x_shape = (jax.ShapeDtypeStruct((size, features), bf16),) * 2
            x_specs = tuple(anywhere(2))
        copied = max(size, summed)
        if summed:
            x_shape += (jax.ShapeDtypeStruct(((first + summed) // LANES, LANES), f32),)
            x_specs += tuple(in_vmem(1))
        outs = pl.pallas_call(
            functools.partial(prepare_kernel, first, summed),
            out_shape=x_shape,
            in_specs=anywhere(2) + in_vmem(2 + len(before)),
            out_specs=x_specs,
            scratch_shapes=[
                pltpu.VMEM((copied, features), bf16),
                pltpu.VMEM((copied, features), bf16),
                pltpu.VMEM((copied, LANES), f32),
                pltpu.SemaphoreType.DMA((4 * pl.cdiv(copied, LANES),)),
            ],
            compiler_params=pltpu.CompilerParams(vmem_limit_bytes=limit),
        )(*operands, *before)
        return (list(outs[:-1]), outs[-1]) if summed else (list(outs), None)

    cut = some // 2 // LANES * LANES
    x0, squares = prepared(0, some, some, [], True, PREPARE_VMEM_BYTES)
    x1, squares = prepared(some, cut, some, [squares], False, LARGE_VMEM_BYTES)
    exchanged, squares = lax.optimization_barrier((exchanged, squares))
    last, _ = prepared(some + cut, some - cut, 0, [], False, LARGE_VMEM_BYTES)
    a_next, b_next, sent = pl.pallas_call(
        adam_kernel,
        out_shape=(
            jax.ShapeDtypeStruct((3, factors, down_rows), f32),
            jax.ShapeDtypeStruct((3, up_rows, columns), f32),
            shares,
        ),
        in_specs=anywhere(7),
        out_specs=tuple(in_vmem(3)),
        scratch_shapes=[
            pltpu.VMEM((n_dp, packed_rows, LANES), bf16),
            pltpu.VMEM((3, factors, window), f32),
            pltpu.VMEM((3, up_rows, columns), f32),
            pltpu.SemaphoreType.DMA((7,)),
        ],
        compiler_params=pltpu.CompilerParams(vmem_limit_bytes=LARGE_VMEM_BYTES),
    )(exchanged, *down_state, *up_state)
    own_f = lax.all_to_all(sent, "dp", 0, 0, tiled=True)
    for half in range(1, halves):
        send_half(half, (mine[-1], sent))
    a_next = jnp.transpose(a_next.reshape(3, parts, rank, down_rows), (0, 3, 1, 2))

    outside = [[] for _ in range(strips)]

    def swap_half(half, after):
        for value in mine[half]:
            value, _ = lax.optimization_barrier((value, after))
            split = pl.pallas_call(
                split_kernel,
                out_shape=(jax.ShapeDtypeStruct((features, LANES), bf16),) * len(groups[half]),
                in_specs=in_vmem(1),
                out_specs=tuple(in_vmem(len(groups[half]))),
                compiler_params=params(),
            )(value)
            for piece, strip in zip(split, groups[half]):
                pairs = [(i, i ^ turn[strip]) for i in range(n_dp)]
                outside[strip].append((piece, lax.ppermute(piece, "dp", pairs)))

    swap_half(0, sent)
    own_f, last = lax.optimization_barrier((own_f, last))
    x1 = x1 + last
    up_packed = packed_rows - down_rows
    more = pl.cdiv(3 * (tokens // LANES), up_packed)
    piece = jax.ShapeDtypeStruct((n_dp // FACTOR_PIECES, packed_rows, LANES), bf16)
    message, *pieces = pl.pallas_call(
        message_kernel,
        out_shape=(jax.ShapeDtypeStruct((n_dp + more, up_packed, LANES), bf16),)
        + (piece,) * FACTOR_PIECES,
        in_specs=anywhere(2),
        out_specs=tuple(in_vmem(1 + FACTOR_PIECES)),
        scratch_shapes=[
            pltpu.VMEM(squares.shape, f32),
            pltpu.SemaphoreType.DMA((2 + FACTOR_PIECES,)),
        ],
        compiler_params=params(),
    )(own_f, squares)
    messages = [to_chip(message, step) for step in steps]
    sibling_f = [to_sibling(piece) for piece in pieces]

    inv_rms = pl.pallas_call(
        functools.partial(inverse_kernel, width, n_dp),
        out_shape=jax.ShapeDtypeStruct((tokens, LANES), f32),
        in_specs=in_vmem(chips),
        out_specs=in_vmem(1)[0],
        compiler_params=params(),
    )(squares, *messages)

    scale = 0.5 / math.sqrt(width * rank)

    received = {}
    after = []
    weights_shape = jax.ShapeDtypeStruct((CORES * features, wide), bf16)
    product_shape = jax.ShapeDtypeStruct((some, wide), bf16)
    for half, group in enumerate(groups):
        static = (scale, parts, up_rows, group, columns)
        if half > 0:
            swap_half(half, products[0])
        for step in steps:
            blocks = [value for strip in group for value in outside[strip][step - 1]]
            arranged = pl.pallas_call(
                functools.partial(arrange_kernel, [turn[strip] for strip in group]),
                out_shape=weights_shape,
                in_specs=in_vmem(len(blocks)) + anywhere(len(after)),
                out_specs=in_vmem(1)[0],
                compiler_params=params(),
            )(*blocks, *after)
            weights, product = pl.pallas_call(
                functools.partial(outside_kernel, static, chips, step),
                out_shape=(weights_shape, product_shape),
                in_specs=in_vmem(3 + 2 * FACTOR_PIECES),
                out_specs=tuple(in_vmem(2)),
                compiler_params=params(),
            )(arranged, messages[step - 1], *x0, *pieces, *sibling_f)
            received.setdefault((0, half), []).append(to_chip(product, chips - step))
            second = pl.pallas_call(
                functools.partial(more_kernel, len(x1) // 2),
                out_shape=product_shape,
                in_specs=in_vmem(1 + len(x1)),
                out_specs=in_vmem(1)[0],
                compiler_params=params(),
            )(*x1, weights)
            products = [product, second]
            after = [second]
            received.setdefault((1, half), []).append(to_chip(second, chips - step))
        if half == 0:
            after = [received[0, 0][0]]

    after.append(received[1, 0][0])
    static = (scale, parts, up_rows, range(strips), columns, halves, len(x1) // 2)
    totals = pl.pallas_call(
        functools.partial(own_kernel, static),
        out_shape=(jax.ShapeDtypeStruct((tokens, wide), f32),) * halves,
        grid=(1,),
        in_specs=[
            pl.BlockSpec((features, columns), lambda i: (lax.axis_index("tensor"), 0)),
            pl.BlockSpec((features, columns), lambda i: (lax.axis_index("tensor") ^ 1, 0)),
        ]
        + in_vmem(2 * FACTOR_PIECES + 1 + len(x1))
        + anywhere(len(after)),
        out_specs=tuple(in_vmem(halves)),
        scratch_shapes=[pltpu.VMEM((CORES * features, columns), bf16)],
        compiler_params=params(),
        cost_estimate=pl.CostEstimate(
            flops=2 * tokens * CORES * features * columns,
            bytes_accessed=4 * tokens * features,
            transcendentals=0,
        ),
    )(frozen_key_value, frozen_key_value, *pieces, *sibling_f, *x0, *x1, *after)

    keys_values = None
    for at, values in received.items():
        keys_values = finish(
            totals[at[1]], inv_rms, values, at, (tokens, columns), keys_values
        )
    return (a_next, b_next, keys_values)


def solution(mesh):
    placed = (
        P("dp", "tensor"),
        P("tensor"),
        P(None, "tensor"),
        P("tensor", None, None),
        P("tensor", None, None),
        P("tensor", None, None),
        P(None, "tensor"),
        P(None, "tensor"),
        P(None, "tensor"),
        P("dp", "tensor", None, None),
        P("dp", None, "tensor"),
    )
    return jax.shard_map(
        body,
        mesh=mesh,
        in_specs=placed,
        out_specs=(
            P(None, ("tensor", "dp"), None, None),
            P(None, "dp", "tensor"),
            P("dp", "tensor"),
        ),
        check_vma=False,
    )
```

```python
import functools
import math

import jax
import jax.numpy as jnp
from jax import lax
from jax.experimental import pallas as pl
from jax.experimental.pallas import tpu as pltpu
from jax.sharding import PartitionSpec as P

KEY_VALUE_WIDTH = 1024
STEP = 100
CORES = 2
LANES = 128
COLUMN_HALVES = 2
TOKEN_HALVES = 2
FACTOR_PIECES = 2
VMEM_BYTES = 16 * 2**20
LARGE_VMEM_BYTES = 58 * 2**20
PREPARE_VMEM_BYTES = 49 * 2**20


def adaptive_moment_update(param, first, second, grad_mean):
    first_new = 0.9 * first + 0.1 * grad_mean
    second_new = 0.999 * second + 0.001 * grad_mean * grad_mean
    step_size = first_new / (1.0 - 0.9**STEP) / (jnp.sqrt(second_new / (1.0 - 0.999**STEP)) + 1e-08)
    return (param - 0.1 * step_size, first_new, second_new)


def in_vmem(count):
    return [pl.BlockSpec(memory_space=pltpu.VMEM)] * count


def anywhere(count):
    return [pl.BlockSpec(memory_space=pl.ANY)] * count


SCALARS = pl.BlockSpec(memory_space=pltpu.SMEM)


def params(**more):
    return pltpu.CompilerParams(vmem_limit_bytes=VMEM_BYTES, **more)


def pack(down, up, out_ref, ready):
    shares = out_ref.shape[0]
    down = down.T
    down_rows, up_rows = down.shape[0] // shares, up.shape[0] // shares
    for i in range(shares):
        pieces = [down[i * down_rows : (i + 1) * down_rows]]
        for k in range(up.shape[1] // LANES):
            pieces.append(up[i * up_rows : (i + 1) * up_rows, k * LANES : (k + 1) * LANES])
        out_ref[i] = jnp.concatenate(pieces, axis=0).astype(jnp.bfloat16)
        ready(i)


def first_lane(share, window, size):
    return jnp.minimum(share // LANES * LANES, size - window)


def begin_kernel(chips, turn, down_ref, up_ref, weights_ref, packed, *refs):
    outs, (down, up, blocks, strips, sem, sem_out) = refs[:-6], refs[-6:]
    features = strips.shape[1]
    place, replica = lax.axis_index("tensor"), lax.axis_index("dp")
    chip, core = place // CORES, place % CORES
    copies, back = [], []

    def add(source, target):
        copies.append(pltpu.make_async_copy(source, target, sem.at[len(copies)]))
        copies[-1].start()

    def add_back(source, target):
        back.append(pltpu.make_async_copy(source, target, sem_out.at[len(back)]))
        back[-1].start()

    add(down_ref, down)
    add(up_ref, up)
    targets = []
    for i, out in enumerate(outs):
        step, first = 1 + i % (chips - 1), i // (chips - 1) * out.shape[0]
        for k in range(out.shape[0]):
            half = (core + replica // turn[first + k]) % 2
            row = ((chip + step) % chips * CORES + half) * features
            add(
                weights_ref.at[
                    pl.ds(pl.multiple_of(row, features), features),
                    pl.ds((first + k) * LANES, LANES),
                ],
                strips.at[len(targets)],
            )
            targets.append(out.at[k])
    copies[0].wait()
    copies[1].wait()

    def ready(i):
        add_back(blocks.at[i], packed.at[i])
        if i == min(1, blocks.shape[0] - 1):
            for k, target in enumerate(targets):
                copies[2 + k].wait()
                add_back(strips.at[k], target)

    pack(down[...], up[...], blocks, ready)
    for copy in back:
        copy.wait()


def split_kernel(in_ref, *outs):
    for k, out in enumerate(outs):
        out[...] = in_ref[k]


def prepare_kernel(first, summed, own_in, sibling_in, own_gain, sibling_gain, *refs):
    own, sibling, squares, sem = refs[-4:]
    copied, features = own.shape
    refs = refs[:-4]
    before, sums_ref = [], None
    if summed:
        refs, sums_ref = refs[:-1], refs[-1]
    together = refs[-1].shape[1] > features
    outs = refs[-1:] if together else refs[-2:]
    before = refs[: -len(outs)]
    rows = outs[0].shape[0]
    block = LANES if rows % LANES == 0 else rows
    tile = 16 if block % 16 == 0 else block
    raw = ((own_in, own), (sibling_in, sibling))
    loads = [
        [
            pltpu.make_async_copy(
                source.at[pl.ds(first + k * block, block)],
                target.at[pl.ds(k * block, block)],
                sem.at[2 * k + side],
            )
            for side, (source, target) in enumerate(raw)
        ]
        for k in range(copied // block)
    ]
    for pair in loads:
        for copy in pair:
            copy.start()
    stores = []
    for k, pair in enumerate(loads):
        for copy in pair:
            copy.wait()
        scale, add = k * block < rows, k * block < summed

        @pl.loop(0, block // tile, unroll=2)
        def _(i):
            at = pl.ds(pl.multiple_of(k * block + i * tile, tile), tile)
            total = None
            for side, (ref, gain) in enumerate(((own, own_gain), (sibling, sibling_gain))):
                value = ref[at, :].astype(jnp.float32)
                if scale:
                    scaled = (value * gain[...]).astype(ref.dtype)
                    if together:
                        outs[0][at, side * features : (side + 1) * features] = scaled
                    else:
                        ref[at, :] = scaled
                if add:
                    total = value * value if total is None else total + value * value
            if add:
                total = jnp.sum(total, axis=1, keepdims=True)
                squares[at, :] = jnp.broadcast_to(total, (tile, LANES))

        if scale and not together:
            part = pl.ds(k * block, block)
            for side, (source, out) in enumerate(((own, outs[0]), (sibling, outs[1]))):
                place = sem.at[2 * (len(loads) + k) + side]
                stores.append(pltpu.make_async_copy(source.at[part], out.at[part], place))
                stores[-1].start()
    if summed:
        done = 0
        for ref in before:
            sums_ref[: ref.shape[0]] = ref[...]
            done = ref.shape[0]
        for i in range(summed // LANES):
            row = squares[i * LANES : (i + 1) * LANES, :].T[:1]
            sums_ref[done + i : done + i + 1] = row
    for copy in stores:
        copy.wait()


def message_kernel(factor_ref, sums_ref, out_ref, *refs):
    pieces, (sums, sem) = refs[:-2], refs[-2:]
    shares, up_rows = factor_ref.shape[0], out_ref.shape[1]
    sums_copy = pltpu.make_async_copy(sums_ref, sums, sem.at[1 + len(pieces)])
    sums_copy.start()
    copies = [
        pltpu.make_async_copy(
            factor_ref.at[:, pl.ds(factor_ref.shape[1] - up_rows, up_rows)],
            out_ref.at[pl.ds(0, shares)],
            sem.at[0],
        )
    ]
    for k, piece in enumerate(pieces):
        size = piece.shape[0]
        copies.append(
            pltpu.make_async_copy(factor_ref.at[pl.ds(k * size, size)], piece, sem.at[1 + k])
        )
    for copy in copies:
        copy.start()
    sums_copy.wait()
    left = sums[...]
    terms = []
    for _ in range(3):
        terms.append(left.astype(jnp.bfloat16).astype(jnp.float32))
        left = left - terms[-1]
    rest = (out_ref.shape[0] - shares) * up_rows - 3 * left.shape[0]
    if rest > 0:
        terms.append(jnp.zeros((rest, LANES), jnp.float32))
    rows = jnp.concatenate(terms, axis=0)
    for i in range(out_ref.shape[0] - shares):
        out_ref[shares + i] = rows[i * up_rows : (i + 1) * up_rows].astype(jnp.bfloat16)
    for copy in copies:
        copy.wait()


def inverse_kernel(width, shares, sums_ref, *refs):
    messages, out = refs[:-1], refs[-1]
    total = sums_ref[...]
    count = total.shape[0]
    for ref in messages:
        rows = [ref[i].astype(jnp.float32) for i in range(shares, ref.shape[0])]
        rows = jnp.concatenate(rows, axis=0)
        total += rows[:count] + rows[count : 2 * count] + rows[2 * count : 3 * count]
    inverse = lax.rsqrt(total / width + 1e-06)
    for i in range(count):
        out[i * LANES : (i + 1) * LANES, :] = jnp.broadcast_to(
            inverse[i : i + 1], (LANES, LANES)
        ).T


def update(total, down, up, a_ref, b_ref):
    down_rows = a_ref.shape[2]
    up_rows, columns = b_ref.shape[1:]
    strips = columns // LANES
    down_mean = total[:down_rows].T
    up_mean = jnp.concatenate(
        [total[down_rows + k * up_rows : down_rows + (k + 1) * up_rows] for k in range(strips)],
        axis=1,
    )
    p, m, v = adaptive_moment_update(*down(), down_mean)
    a_ref[0], a_ref[1], a_ref[2] = p, m, v
    pieces = [p.T]
    p, m, v = adaptive_moment_update(*up(), up_mean)
    b_ref[0], b_ref[1], b_ref[2] = p, m, v
    pieces += [p[:, k * LANES : (k + 1) * LANES] for k in range(strips)]
    return jnp.concatenate(pieces, axis=0).astype(jnp.bfloat16)


def adam_kernel(grad_in, *refs):
    state, refs = refs[:6], refs[6:]
    a_ref, b_ref, factor_ref, grad_ref, down_win, up_win, sem = refs
    replicas = grad_ref.shape[0]
    down_rows, window = a_ref.shape[2], down_win.shape[2]
    up_rows = up_win.shape[1]
    replica = lax.axis_index("dp")
    share = replica * down_rows
    size = down_rows * replicas
    copies = [pltpu.make_async_copy(grad_in, grad_ref, sem.at[6])]
    for i in range(3):
        down, up = state[i], state[3 + i]
        if window != down_rows:
            lane = pl.multiple_of(first_lane(share, window, size), LANES)
            down = down.at[:, pl.ds(lane, window)]
            up = up.at[pl.ds(pl.multiple_of(replica * up_rows, up_rows), up_rows)]
        copies.append(pltpu.make_async_copy(down, down_win.at[i], sem.at[i]))
        copies.append(pltpu.make_async_copy(up, up_win.at[i], sem.at[3 + i]))
    for copy in copies:
        copy.start()
    copies[0].wait()
    total = jnp.sum(grad_ref[...].astype(jnp.float32), axis=0) / replicas
    for copy in copies[1:]:
        copy.wait()

    def down():
        if window == down_rows:
            return [down_win[i] for i in range(3)]
        shift = window - (share - first_lane(share, window, size))
        return [pltpu.roll(down_win[i], shift, 1)[:, :down_rows] for i in range(3)]

    rounded = update(total, down, lambda: [up_win[i] for i in range(3)], a_ref, b_ref)
    for i in range(replicas):
        factor_ref[i] = rounded


def factor_a(refs, down_rows):
    pieces = []
    for ref in refs:
        for i in range(ref.shape[0]):
            if down_rows % 16 == 0:
                pieces.append(ref[i, :down_rows, :])
            else:
                pieces.append(ref[i].astype(jnp.float32)[:down_rows])
    return jnp.concatenate(pieces, axis=0).astype(jnp.bfloat16)


def factor_b(packed, part, parts, strip, up_rows):
    pieces = [
        packed[i].astype(jnp.float32)[strip * up_rows : (strip + 1) * up_rows]
        for i in range(packed.shape[0])
    ]
    value = jnp.concatenate(pieces, axis=0)
    rows = [jnp.where(part == j, value, jnp.zeros_like(value)) for j in range(parts)]
    return jnp.concatenate(rows, axis=0).astype(jnp.bfloat16)


def merge(scale, block, a, b):
    change = jnp.dot(a, b, preferred_element_type=jnp.float32)
    return (block.astype(jnp.float32) + scale * change).astype(jnp.bfloat16)


def multiply(groups, weights, *outs):
    wide = outs[0].shape[1]
    done = 0
    for xs in groups:
        rows = xs[0].shape[0]
        tile = rows // 2 if rows % 32 == 0 else rows

        @pl.loop(0, rows // tile)
        def _(i):
            at = pl.ds(pl.multiple_of(i * tile, tile), tile)
            to = pl.ds(pl.multiple_of(done + i * tile, 16), tile)
            value, first = None, 0
            for x in xs:
                size = x.shape[1]
                part = jnp.dot(
                    x[at, :], weights[first : first + size, :], preferred_element_type=jnp.float32
                )
                value, first = part if value is None else value + part, first + size
            for k, out in enumerate(outs):
                out[to, :] = value[:, k * wide : (k + 1) * wide].astype(out.dtype)

        done += rows


def up_factor(static, packed, owner):
    _, parts, up_rows, strips, columns = static
    part = owner * columns // KEY_VALUE_WIDTH
    return jnp.concatenate(
        [factor_b(packed, part, parts, strip, up_rows) for strip in strips], axis=1
    )


def arrange_kernel(turn, *refs):
    out = refs[-1]
    replica = lax.axis_index("dp")
    features = out.shape[0] // CORES
    for k, alternate in enumerate(turn):
        mine, other = refs[2 * k : 2 * k + 2]
        even = replica // alternate % 2 == 0
        lanes = slice(k * LANES, (k + 1) * LANES)
        out[:features, lanes] = jnp.where(even, mine[...], other[...])
        out[features:, lanes] = jnp.where(even, other[...], mine[...])


def outside_kernel(static, chips, step, blocks, b_ref, x, *refs):
    own_f, sibling_f = refs[:FACTOR_PIECES], refs[FACTOR_PIECES : 2 * FACTOR_PIECES]
    weights, product = refs[-2:]
    features = blocks.shape[0] // CORES
    down_rows = own_f[0].shape[1] - b_ref.shape[1]
    shares = FACTOR_PIECES * own_f[0].shape[0]
    place = lax.axis_index("tensor")
    owner = (place // CORES - step + chips) % chips * CORES + place % CORES
    b = up_factor(static, b_ref[:shares], owner)
    tile = 256 if features % 256 == 0 else features
    for side, factors in enumerate((own_f, sibling_f)):
        a = factor_a(factors, down_rows)
        for first in range(0, features, tile):
            rows = slice(side * features + first, side * features + first + tile)
            weights[rows, :] = merge(static[0], blocks[rows, :], a[first : first + tile], b)
    multiply([[x]], weights, product)


def more_kernel(groups, *refs):
    xs, (weights, product) = refs[:-2], refs[-2:]
    size = len(xs) // groups
    multiply([xs[k * size : (k + 1) * size] for k in range(groups)], weights, product)


def own_kernel(static, own_block, sibling_block, *refs):
    own_f, sibling_f = refs[:FACTOR_PIECES], refs[FACTOR_PIECES : 2 * FACTOR_PIECES]
    refs = refs[2 * FACTOR_PIECES :]
    groups, weights = [refs[:1]], refs[-1]
    for k in range(static[6]):
        groups.append(refs[1 + 2 * k : 3 + 2 * k])
    outs = refs[len(refs) - 1 - static[5] : -1]
    features = own_block.shape[0]
    wide = outs[0].shape[1]
    down_rows = own_f[0].shape[1] - len(static[3]) * static[2]
    b = jnp.concatenate([piece[:, down_rows:] for piece in own_f], axis=0)
    b = up_factor(static[:5], b, lax.axis_index("tensor"))
    for at, factors, block in ((0, own_f, own_block), (features, sibling_f, sibling_block)):
        weights[at : at + features] = merge(static[0], block[...], factor_a(factors, down_rows), b)
    multiply(groups, weights, *outs)


def finish_kernel(sources, first, own, inv, *refs):
    rows = pl.ds(first, refs[-1].shape[0])
    total = own[rows, :]
    for value in refs[:sources]:
        total = total + value[...].astype(jnp.float32)
    refs[-1][...] = (total * inv[rows, :1]).astype(refs[-1].dtype)


def finish(own, inv_rms, received, at, shape, before):
    block = received[0].shape
    operands = [own, inv_rms] + received
    in_specs = in_vmem(len(operands))
    aliases = {}
    if before is not None:
        aliases = {len(operands): 0}
        in_specs += anywhere(1)
        operands.append(before)
    return pl.pallas_call(
        functools.partial(finish_kernel, len(received), at[0] * block[0]),
        grid=(1,),
        out_shape=jax.ShapeDtypeStruct(shape, jnp.bfloat16),
        in_specs=in_specs,
        out_specs=pl.BlockSpec(block, lambda i: at),
        input_output_aliases=aliases,
        compiler_params=params(),
    )(*operands)


def body(
    prompt_hidden_input,
    input_norm_gain,
    frozen_key_value,
    down_factor_matrix,
    down_moment_first,
    down_moment_second,
    up_factor_matrix,
    up_moment_first,
    up_moment_second,
    down_gradient,
    up_gradient,
):
    n_dp = lax.axis_size("dp")
    n_tensor = lax.axis_size("tensor")
    chips = n_tensor // CORES
    replica = lax.axis_index("dp")
    tokens, features = prompt_hidden_input.shape
    width, columns = frozen_key_value.shape
    rank = up_factor_matrix.shape[0]
    parts = down_factor_matrix.shape[1]
    factors = parts * rank
    strips = columns // LANES
    down_rows = features // n_dp
    up_rows = rank // n_dp
    packed_rows = down_rows + up_rows * strips
    steps = range(1, chips)
    f32, bf16 = jnp.float32, jnp.bfloat16

    def to_sibling(value):
        return lax.ppermute(value, "tensor", [(t, t ^ 1) for t in range(n_tensor)])

    def to_chip(value, step):
        pairs = [
            (CORES * q + k, CORES * ((q + step) % chips) + k)
            for q in range(chips)
            for k in range(CORES)
        ]
        return lax.ppermute(value, "tensor", pairs)

    def by_rank(value):
        return jnp.transpose(value, (1, 2, 0)).reshape(factors, features)

    down_sent = by_rank(down_gradient[0])
    down_state = [by_rank(v) for v in (down_factor_matrix, down_moment_first, down_moment_second)]
    up_state = [up_factor_matrix, up_moment_first, up_moment_second]
    shares = jax.ShapeDtypeStruct((n_dp, packed_rows, LANES), bf16)
    window = pl.cdiv(down_rows + LANES, LANES) * LANES
    aligned = features % LANES == 0 and window <= features
    aligned = aligned and up_rows % 8 == 0 and down_rows % 16 == 0
    window = window if aligned else down_rows
    turns = [1, 2] if n_dp % 4 == 0 else [1, 1]
    turn = [turns[strip % 2] for strip in range(strips)]
    halves = min(COLUMN_HALVES, strips)
    wide = columns // halves
    groups = [range(k * strips // halves, (k + 1) * strips // halves) for k in range(halves)]
    out_shape = (shares,) + tuple(
        jax.ShapeDtypeStruct((len(group), features, LANES), bf16)
        for group in groups
        for _ in steps
    )
    packed, *taken = pl.pallas_call(
        functools.partial(begin_kernel, chips, turn),
        out_shape=out_shape,
        in_specs=anywhere(3),
        out_specs=tuple(anywhere(len(out_shape))),
        scratch_shapes=[
            pltpu.VMEM((factors, features), f32),
            pltpu.VMEM((rank, columns), f32),
            pltpu.VMEM(shares.shape, bf16),
            pltpu.VMEM((len(steps) * strips, features, LANES), bf16),
            pltpu.SemaphoreType.DMA((2 + len(steps) * strips,)),
            pltpu.SemaphoreType.DMA((n_dp + len(steps) * strips,)),
        ],
        compiler_params=pltpu.CompilerParams(vmem_limit_bytes=LARGE_VMEM_BYTES),
    )(down_sent, up_gradient[0], frozen_key_value)
    exchanged = lax.all_to_all(packed, "dp", 0, 0, tiled=True)
    if not aligned:
        down_state = [
            lax.dynamic_slice_in_dim(v, replica * down_rows, down_rows, 1) for v in down_state
        ]
        up_state = [lax.dynamic_slice_in_dim(v, replica * up_rows, up_rows, 0) for v in up_state]
    mine = []

    def send_half(half, after):
        blocks = taken[half * len(steps) : (half + 1) * len(steps)]
        if after is not None:
            blocks, _ = lax.optimization_barrier((blocks, after))
        mine.append([to_chip(value, step) for value, step in zip(blocks, steps)])

    send_half(0, None)

    gain = input_norm_gain[None, :]
    some = tokens // TOKEN_HALVES
    operands = [prompt_hidden_input, to_sibling(prompt_hidden_input), gain, to_sibling(gain)]

    def prepared(first, size, summed, before, in_place, limit):
        if in_place:
            x_shape = (jax.ShapeDtypeStruct((size, CORES * features), bf16),)
            x_specs = tuple(in_vmem(1))
        else:
            x_shape = (jax.ShapeDtypeStruct((size, features), bf16),) * 2
            x_specs = tuple(anywhere(2))
        copied = max(size, summed)
        if summed:
            x_shape += (jax.ShapeDtypeStruct(((first + summed) // LANES, LANES), f32),)
            x_specs += tuple(in_vmem(1))
        outs = pl.pallas_call(
            functools.partial(prepare_kernel, first, summed),
            out_shape=x_shape,
            in_specs=anywhere(2) + in_vmem(2 + len(before)),
            out_specs=x_specs,
            scratch_shapes=[
                pltpu.VMEM((copied, features), bf16),
                pltpu.VMEM((copied, features), bf16),
                pltpu.VMEM((copied, LANES), f32),
                pltpu.SemaphoreType.DMA((4 * pl.cdiv(copied, LANES),)),
            ],
            compiler_params=pltpu.CompilerParams(vmem_limit_bytes=limit),
        )(*operands, *before)
        return (list(outs[:-1]), outs[-1]) if summed else (list(outs), None)

    cut = some // 2 // LANES * LANES
    x0, squares = prepared(0, some, tokens, [], True, PREPARE_VMEM_BYTES)
    x1, _ = prepared(some, cut, 0, [squares], False, LARGE_VMEM_BYTES)
    exchanged, squares, x1 = lax.optimization_barrier((exchanged, squares, x1))
    last, _ = prepared(some + cut, some - cut, 0, [], False, LARGE_VMEM_BYTES)
    a_next, b_next, sent = pl.pallas_call(
        adam_kernel,
        out_shape=(
            jax.ShapeDtypeStruct((3, factors, down_rows), f32),
            jax.ShapeDtypeStruct((3, up_rows, columns), f32),
            shares,
        ),
        in_specs=anywhere(7),
        out_specs=tuple(in_vmem(3)),
        scratch_shapes=[
            pltpu.VMEM((n_dp, packed_rows, LANES), bf16),
            pltpu.VMEM((3, factors, window), f32),
            pltpu.VMEM((3, up_rows, columns), f32),
            pltpu.SemaphoreType.DMA((7,)),
        ],
        compiler_params=pltpu.CompilerParams(vmem_limit_bytes=LARGE_VMEM_BYTES),
    )(exchanged, *down_state, *up_state)
    own_f = lax.all_to_all(sent, "dp", 0, 0, tiled=True)
    for half in range(1, halves):
        send_half(half, (mine[-1], sent))
    a_next = jnp.transpose(a_next.reshape(3, parts, rank, down_rows), (0, 3, 1, 2))

    outside = [[] for _ in range(strips)]

    def swap_half(half, after):
        for value in mine[half]:
            value, _ = lax.optimization_barrier((value, after))
            split = pl.pallas_call(
                split_kernel,
                out_shape=(jax.ShapeDtypeStruct((features, LANES), bf16),) * len(groups[half]),
                in_specs=in_vmem(1),
                out_specs=tuple(in_vmem(len(groups[half]))),
                compiler_params=params(),
            )(value)
            for piece, strip in zip(split, groups[half]):
                pairs = [(i, i ^ turn[strip]) for i in range(n_dp)]
                outside[strip].append((piece, lax.ppermute(piece, "dp", pairs)))

    swap_half(0, sent)
    own_f, last = lax.optimization_barrier((own_f, last))
    x1 = x1 + last
    up_packed = packed_rows - down_rows
    more = pl.cdiv(3 * (tokens // LANES), up_packed)
    piece = jax.ShapeDtypeStruct((n_dp // FACTOR_PIECES, packed_rows, LANES), bf16)
    message, *pieces = pl.pallas_call(
        message_kernel,
        out_shape=(jax.ShapeDtypeStruct((n_dp + more, up_packed, LANES), bf16),)
        + (piece,) * FACTOR_PIECES,
        in_specs=anywhere(2),
        out_specs=tuple(in_vmem(1 + FACTOR_PIECES)),
        scratch_shapes=[
            pltpu.VMEM(squares.shape, f32),
            pltpu.SemaphoreType.DMA((2 + FACTOR_PIECES,)),
        ],
        compiler_params=params(),
    )(own_f, squares)
    messages = [to_chip(message, step) for step in steps]
    sibling_f = [to_sibling(piece) for piece in pieces]

    inv_rms = pl.pallas_call(
        functools.partial(inverse_kernel, width, n_dp),
        out_shape=jax.ShapeDtypeStruct((tokens, LANES), f32),
        in_specs=in_vmem(chips),
        out_specs=in_vmem(1)[0],
        compiler_params=params(),
    )(squares, *messages)

    scale = 0.5 / math.sqrt(width * rank)

    received = {}
    after = []
    weights_shape = jax.ShapeDtypeStruct((CORES * features, wide), bf16)
    product_shape = jax.ShapeDtypeStruct((some, wide), bf16)
    for half, group in enumerate(groups):
        static = (scale, parts, up_rows, group, columns)
        if half > 0:
            swap_half(half, products[0])
        for step in steps:
            blocks = [value for strip in group for value in outside[strip][step - 1]]
            arranged = pl.pallas_call(
                functools.partial(arrange_kernel, [turn[strip] for strip in group]),
                out_shape=weights_shape,
                in_specs=in_vmem(len(blocks)) + anywhere(len(after)),
                out_specs=in_vmem(1)[0],
                compiler_params=params(),
            )(*blocks, *after)
            weights, product = pl.pallas_call(
                functools.partial(outside_kernel, static, chips, step),
                out_shape=(weights_shape, product_shape),
                in_specs=in_vmem(3 + 2 * FACTOR_PIECES),
                out_specs=tuple(in_vmem(2)),
                compiler_params=params(),
            )(arranged, messages[step - 1], *x0, *pieces, *sibling_f)
            received.setdefault((0, half), []).append(to_chip(product, chips - step))
            second = pl.pallas_call(
                functools.partial(more_kernel, len(x1) // 2),
                out_shape=product_shape,
                in_specs=in_vmem(1 + len(x1)),
                out_specs=in_vmem(1)[0],
                compiler_params=params(),
            )(*x1, weights)
            products = [product, second]
            after = [second]
            received.setdefault((1, half), []).append(to_chip(second, chips - step))
        if half == 0:
            after = [received[0, 0][0]]

    after.append(received[1, 0][0])
    static = (scale, parts, up_rows, range(strips), columns, halves, len(x1) // 2)
    totals = pl.pallas_call(
        functools.partial(own_kernel, static),
        out_shape=(jax.ShapeDtypeStruct((tokens, wide), f32),) * halves,
        grid=(1,),
        in_specs=[
            pl.BlockSpec((features, columns), lambda i: (lax.axis_index("tensor"), 0)),
            pl.BlockSpec((features, columns), lambda i: (lax.axis_index("tensor") ^ 1, 0)),
        ]
        + in_vmem(2 * FACTOR_PIECES + 1 + len(x1))
        + anywhere(len(after)),
        out_specs=tuple(in_vmem(halves)),
        scratch_shapes=[pltpu.VMEM((CORES * features, columns), bf16)],
        compiler_params=params(),
        cost_estimate=pl.CostEstimate(
            flops=2 * tokens * CORES * features * columns,
            bytes_accessed=4 * tokens * features,
            transcendentals=0,
        ),
    )(frozen_key_value, frozen_key_value, *pieces, *sibling_f, *x0, *x1, *after)

    keys_values = None
    for at, values in received.items():
        keys_values = finish(
            totals[at[1]], inv_rms, values, at, (tokens, columns), keys_values
        )
    return (a_next, b_next, keys_values)


def solution(mesh):
    placed = (
        P("dp", "tensor"),
        P("tensor"),
        P(None, "tensor"),
        P("tensor", None, None),
        P("tensor", None, None),
        P("tensor", None, None),
        P(None, "tensor"),
        P(None, "tensor"),
        P(None, "tensor"),
        P("dp", "tensor", None, None),
        P("dp", None, "tensor"),
    )
    return jax.shard_map(
        body,
        mesh=mesh,
        in_specs=placed,
        out_specs=(
            P(None, ("tensor", "dp"), None, None),
            P(None, "dp", "tensor"),
            P("dp", "tensor"),
        ),
        check_vma=False,
    )
```

```python
import functools
import math

import jax
import jax.numpy as jnp
from jax import lax
from jax.experimental import pallas as pl
from jax.experimental.pallas import tpu as pltpu
from jax.sharding import PartitionSpec as P

KEY_VALUE_WIDTH = 1024
STEP = 100
CORES = 2
LANES = 128
COLUMN_HALVES = 2
TOKEN_HALVES = 2
FACTOR_PIECES = 2
VMEM_BYTES = 16 * 2**20
LARGE_VMEM_BYTES = 58 * 2**20
PREPARE_VMEM_BYTES = 49 * 2**20


def adaptive_moment_update(param, first, second, grad_mean):
    first_new = 0.9 * first + 0.1 * grad_mean
    second_new = 0.999 * second + 0.001 * grad_mean * grad_mean
    step_size = first_new / (1.0 - 0.9**STEP) / (jnp.sqrt(second_new / (1.0 - 0.999**STEP)) + 1e-08)
    return (param - 0.1 * step_size, first_new, second_new)


def in_vmem(count):
    return [pl.BlockSpec(memory_space=pltpu.VMEM)] * count


def anywhere(count):
    return [pl.BlockSpec(memory_space=pl.ANY)] * count


SCALARS = pl.BlockSpec(memory_space=pltpu.SMEM)


def params(**more):
    return pltpu.CompilerParams(vmem_limit_bytes=VMEM_BYTES, **more)


def pack(down, up, out_ref, ready):
    shares = out_ref.shape[0]
    down = down.T
    down_rows, up_rows = down.shape[0] // shares, up.shape[0] // shares
    for i in range(shares):
        pieces = [down[i * down_rows : (i + 1) * down_rows]]
        for k in range(up.shape[1] // LANES):
            pieces.append(up[i * up_rows : (i + 1) * up_rows, k * LANES : (k + 1) * LANES])
        out_ref[i] = jnp.concatenate(pieces, axis=0).astype(jnp.bfloat16)
        ready(i)


def first_lane(share, window, size):
    return jnp.minimum(share // LANES * LANES, size - window)


def begin_kernel(chips, turn, down_ref, up_ref, weights_ref, packed, *refs):
    outs, (down, up, blocks, strips, sem, sem_out) = refs[:-6], refs[-6:]
    features = strips.shape[1]
    place, replica = lax.axis_index("tensor"), lax.axis_index("dp")
    chip, core = place // CORES, place % CORES
    copies, back = [], []

    def add(source, target):
        copies.append(pltpu.make_async_copy(source, target, sem.at[len(copies)]))
        copies[-1].start()

    def add_back(source, target):
        back.append(pltpu.make_async_copy(source, target, sem_out.at[len(back)]))
        back[-1].start()

    add(down_ref, down)
    add(up_ref, up)
    targets = []
    for i, out in enumerate(outs):
        step, first = 1 + i % (chips - 1), i // (chips - 1) * out.shape[0]
        for k in range(out.shape[0]):
            half = (core + replica // turn[first + k]) % 2
            row = ((chip + step) % chips * CORES + half) * features
            add(
                weights_ref.at[
                    pl.ds(pl.multiple_of(row, features), features),
                    pl.ds((first + k) * LANES, LANES),
                ],
                strips.at[len(targets)],
            )
            targets.append(out.at[k])
    copies[0].wait()
    copies[1].wait()

    def ready(i):
        add_back(blocks.at[i], packed.at[i])
        if i == min(1, blocks.shape[0] - 1):
            for k, target in enumerate(targets):
                copies[2 + k].wait()
                add_back(strips.at[k], target)

    pack(down[...], up[...], blocks, ready)
    for copy in back:
        copy.wait()


def split_kernel(in_ref, *outs):
    for k, out in enumerate(outs):
        out[...] = in_ref[k]


def prepare_kernel(first, summed, own_in, sibling_in, own_gain, sibling_gain, *refs):
    own, sibling, squares, sem = refs[-4:]
    copied, features = own.shape
    refs = refs[:-4]
    before, sums_ref = [], None
    if summed:
        refs, sums_ref = refs[:-1], refs[-1]
    together = refs[-1].shape[1] > features
    outs = refs[-1:] if together else refs[-2:]
    before = refs[: -len(outs)]
    rows = outs[0].shape[0]
    block = LANES if rows % LANES == 0 else rows
    tile = 16 if block % 16 == 0 else block
    raw = ((own_in, own), (sibling_in, sibling))
    loads = [
        [
            pltpu.make_async_copy(
                source.at[pl.ds(first + k * block, block)],
                target.at[pl.ds(k * block, block)],
                sem.at[2 * k + side],
            )
            for side, (source, target) in enumerate(raw)
        ]
        for k in range(copied // block)
    ]
    for pair in loads:
        for copy in pair:
            copy.start()
    stores = []
    for k, pair in enumerate(loads):
        for copy in pair:
            copy.wait()
        scale, add = k * block < rows, k * block < summed

        @pl.loop(0, block // tile, unroll=2)
        def _(i):
            at = pl.ds(pl.multiple_of(k * block + i * tile, tile), tile)
            total = None
            for side, (ref, gain) in enumerate(((own, own_gain), (sibling, sibling_gain))):
                value = ref[at, :].astype(jnp.float32)
                if scale:
                    scaled = (value * gain[...]).astype(ref.dtype)
                    if together:
                        outs[0][at, side * features : (side + 1) * features] = scaled
                    else:
                        ref[at, :] = scaled
                if add:
                    total = value * value if total is None else total + value * value
            if add:
                total = jnp.sum(total, axis=1, keepdims=True)
                squares[at, :] = jnp.broadcast_to(total, (tile, LANES))

        if scale and not together:
            part = pl.ds(k * block, block)
            for side, (source, out) in enumerate(((own, outs[0]), (sibling, outs[1]))):
                place = sem.at[2 * (len(loads) + k) + side]
                stores.append(pltpu.make_async_copy(source.at[part], out.at[part], place))
                stores[-1].start()
    if summed:
        done = 0
        for ref in before:
            sums_ref[: ref.shape[0]] = ref[...]
            done = ref.shape[0]
        for i in range(summed // LANES):
            row = squares[i * LANES : (i + 1) * LANES, :].T[:1]
            sums_ref[done + i : done + i + 1] = row
    for copy in stores:
        copy.wait()


def message_kernel(factor_ref, sums_ref, out_ref, *refs):
    pieces, (sums, sem) = refs[:-2], refs[-2:]
    shares, up_rows = factor_ref.shape[0], out_ref.shape[1]
    sums_copy = pltpu.make_async_copy(sums_ref, sums, sem.at[1 + len(pieces)])
    sums_copy.start()
    copies = [
        pltpu.make_async_copy(
            factor_ref.at[:, pl.ds(factor_ref.shape[1] - up_rows, up_rows)],
            out_ref.at[pl.ds(0, shares)],
            sem.at[0],
        )
    ]
    for k, piece in enumerate(pieces):
        size = piece.shape[0]
        copies.append(
            pltpu.make_async_copy(factor_ref.at[pl.ds(k * size, size)], piece, sem.at[1 + k])
        )
    for copy in copies:
        copy.start()
    sums_copy.wait()
    left = sums[...]
    terms = []
    for _ in range(3):
        terms.append(left.astype(jnp.bfloat16).astype(jnp.float32))
        left = left - terms[-1]
    rest = (out_ref.shape[0] - shares) * up_rows - 3 * left.shape[0]
    if rest > 0:
        terms.append(jnp.zeros((rest, LANES), jnp.float32))
    rows = jnp.concatenate(terms, axis=0)
    for i in range(out_ref.shape[0] - shares):
        out_ref[shares + i] = rows[i * up_rows : (i + 1) * up_rows].astype(jnp.bfloat16)
    for copy in copies:
        copy.wait()


def inverse_kernel(width, shares, sums_ref, *refs):
    messages, out = refs[:-1], refs[-1]
    total = sums_ref[...]
    count = total.shape[0]
    for ref in messages:
        rows = [ref[i].astype(jnp.float32) for i in range(shares, ref.shape[0])]
        rows = jnp.concatenate(rows, axis=0)
        total += rows[:count] + rows[count : 2 * count] + rows[2 * count : 3 * count]
    inverse = lax.rsqrt(total / width + 1e-06)
    for i in range(count):
        out[i * LANES : (i + 1) * LANES, :] = jnp.broadcast_to(
            inverse[i : i + 1], (LANES, LANES)
        ).T


def update(total, down, up, a_ref, b_ref):
    down_rows = a_ref.shape[2]
    up_rows, columns = b_ref.shape[1:]
    strips = columns // LANES
    down_mean = total[:down_rows].T
    up_mean = jnp.concatenate(
        [total[down_rows + k * up_rows : down_rows + (k + 1) * up_rows] for k in range(strips)],
        axis=1,
    )
    p, m, v = adaptive_moment_update(*down(), down_mean)
    a_ref[0], a_ref[1], a_ref[2] = p, m, v
    pieces = [p.T]
    p, m, v = adaptive_moment_update(*up(), up_mean)
    b_ref[0], b_ref[1], b_ref[2] = p, m, v
    pieces += [p[:, k * LANES : (k + 1) * LANES] for k in range(strips)]
    return jnp.concatenate(pieces, axis=0).astype(jnp.bfloat16)


def adam_kernel(grad_in, *refs):
    state, refs = refs[:6], refs[6:]
    a_ref, b_ref, factor_ref, grad_ref, down_win, up_win, sem = refs
    replicas = grad_ref.shape[0]
    down_rows, window = a_ref.shape[2], down_win.shape[2]
    up_rows = up_win.shape[1]
    replica = lax.axis_index("dp")
    share = replica * down_rows
    size = down_rows * replicas
    copies = [pltpu.make_async_copy(grad_in, grad_ref, sem.at[6])]
    for i in range(3):
        down, up = state[i], state[3 + i]
        if window != down_rows:
            lane = pl.multiple_of(first_lane(share, window, size), LANES)
            down = down.at[:, pl.ds(lane, window)]
            up = up.at[pl.ds(pl.multiple_of(replica * up_rows, up_rows), up_rows)]
        copies.append(pltpu.make_async_copy(down, down_win.at[i], sem.at[i]))
        copies.append(pltpu.make_async_copy(up, up_win.at[i], sem.at[3 + i]))
    for copy in copies:
        copy.start()
    copies[0].wait()
    total = jnp.sum(grad_ref[...].astype(jnp.float32), axis=0) / replicas
    for copy in copies[1:]:
        copy.wait()

    def down():
        if window == down_rows:
            return [down_win[i] for i in range(3)]
        shift = window - (share - first_lane(share, window, size))
        return [pltpu.roll(down_win[i], shift, 1)[:, :down_rows] for i in range(3)]

    rounded = update(total, down, lambda: [up_win[i] for i in range(3)], a_ref, b_ref)
    for i in range(replicas):
        factor_ref[i] = rounded


def factor_a(refs, down_rows):
    pieces = []
    for ref in refs:
        for i in range(ref.shape[0]):
            if down_rows % 16 == 0:
                pieces.append(ref[i, :down_rows, :])
            else:
                pieces.append(ref[i].astype(jnp.float32)[:down_rows])
    return jnp.concatenate(pieces, axis=0).astype(jnp.bfloat16)


def factor_b(packed, part, parts, strip, up_rows):
    pieces = [
        packed[i].astype(jnp.float32)[strip * up_rows : (strip + 1) * up_rows]
        for i in range(packed.shape[0])
    ]
    value = jnp.concatenate(pieces, axis=0)
    rows = [jnp.where(part == j, value, jnp.zeros_like(value)) for j in range(parts)]
    return jnp.concatenate(rows, axis=0).astype(jnp.bfloat16)


def merge(scale, block, a, b):
    change = jnp.dot(a, b, preferred_element_type=jnp.float32)
    return (block.astype(jnp.float32) + scale * change).astype(jnp.bfloat16)


def multiply(groups, weights, *outs):
    wide = outs[0].shape[1]
    done = 0
    for xs in groups:
        rows = xs[0].shape[0]
        tile = rows // 2 if rows % 32 == 0 else rows

        @pl.loop(0, rows // tile)
        def _(i):
            at = pl.ds(pl.multiple_of(i * tile, tile), tile)
            to = pl.ds(pl.multiple_of(done + i * tile, 16), tile)
            value, first = None, 0
            for x in xs:
                size = x.shape[1]
                part = jnp.dot(
                    x[at, :], weights[first : first + size, :], preferred_element_type=jnp.float32
                )
                value, first = part if value is None else value + part, first + size
            for k, out in enumerate(outs):
                out[to, :] = value[:, k * wide : (k + 1) * wide].astype(out.dtype)

        done += rows


def up_factor(static, packed, owner):
    _, parts, up_rows, strips, columns = static
    part = owner * columns // KEY_VALUE_WIDTH
    return jnp.concatenate(
        [factor_b(packed, part, parts, strip, up_rows) for strip in strips], axis=1
    )


def arrange_kernel(turn, *refs):
    out = refs[-1]
    replica = lax.axis_index("dp")
    features = out.shape[0] // CORES
    for k, alternate in enumerate(turn):
        mine, other = refs[2 * k : 2 * k + 2]
        even = replica // alternate % 2 == 0
        lanes = slice(k * LANES, (k + 1) * LANES)
        out[:features, lanes] = jnp.where(even, mine[...], other[...])
        out[features:, lanes] = jnp.where(even, other[...], mine[...])


def outside_kernel(static, chips, step, blocks, b_ref, x, *refs):
    own_f, sibling_f = refs[:FACTOR_PIECES], refs[FACTOR_PIECES : 2 * FACTOR_PIECES]
    weights, product = refs[-2:]
    features = blocks.shape[0] // CORES
    down_rows = own_f[0].shape[1] - b_ref.shape[1]
    shares = FACTOR_PIECES * own_f[0].shape[0]
    place = lax.axis_index("tensor")
    owner = (place // CORES - step + chips) % chips * CORES + place % CORES
    b = up_factor(static, b_ref[:shares], owner)
    tile = 256 if features % 256 == 0 else features
    for side, factors in enumerate((own_f, sibling_f)):
        a = factor_a(factors, down_rows)
        for first in range(0, features, tile):
            rows = slice(side * features + first, side * features + first + tile)
            weights[rows, :] = merge(static[0], blocks[rows, :], a[first : first + tile], b)
    multiply([[x]], weights, product)


def more_kernel(groups, *refs):
    xs, (weights, product) = refs[:-2], refs[-2:]
    size = len(xs) // groups
    multiply([xs[k * size : (k + 1) * size] for k in range(groups)], weights, product)


def own_kernel(static, own_block, sibling_block, *refs):
    own_f, sibling_f = refs[:FACTOR_PIECES], refs[FACTOR_PIECES : 2 * FACTOR_PIECES]
    refs = refs[2 * FACTOR_PIECES :]
    groups, weights = [refs[:1]], refs[-1]
    for k in range(static[6]):
        groups.append(refs[1 + 2 * k : 3 + 2 * k])
    outs = refs[len(refs) - 1 - static[5] : -1]
    features = own_block.shape[0]
    wide = outs[0].shape[1]
    down_rows = own_f[0].shape[1] - len(static[3]) * static[2]
    b = jnp.concatenate([piece[:, down_rows:] for piece in own_f], axis=0)
    b = up_factor(static[:5], b, lax.axis_index("tensor"))
    for at, factors, block in ((0, own_f, own_block), (features, sibling_f, sibling_block)):
        weights[at : at + features] = merge(static[0], block[...], factor_a(factors, down_rows), b)
    multiply(groups, weights, *outs)


def finish_kernel(sources, first, own, inv, *refs):
    rows = pl.ds(first, refs[-1].shape[0])
    total = own[rows, :]
    for value in refs[:sources]:
        total = total + value[...].astype(jnp.float32)
    refs[-1][...] = (total * inv[rows, :1]).astype(refs[-1].dtype)


def finish(own, inv_rms, received, at, shape, before):
    block = received[0].shape
    operands = [own, inv_rms] + received
    in_specs = in_vmem(len(operands))
    aliases = {}
    if before is not None:
        aliases = {len(operands): 0}
        in_specs += anywhere(1)
        operands.append(before)
    return pl.pallas_call(
        functools.partial(finish_kernel, len(received), at[0] * block[0]),
        grid=(1,),
        out_shape=jax.ShapeDtypeStruct(shape, jnp.bfloat16),
        in_specs=in_specs,
        out_specs=pl.BlockSpec(block, lambda i: at),
        input_output_aliases=aliases,
        compiler_params=params(),
    )(*operands)


def body(
    prompt_hidden_input,
    input_norm_gain,
    frozen_key_value,
    down_factor_matrix,
    down_moment_first,
    down_moment_second,
    up_factor_matrix,
    up_moment_first,
    up_moment_second,
    down_gradient,
    up_gradient,
):
    n_dp = lax.axis_size("dp")
    n_tensor = lax.axis_size("tensor")
    chips = n_tensor // CORES
    replica = lax.axis_index("dp")
    tokens, features = prompt_hidden_input.shape
    width, columns = frozen_key_value.shape
    rank = up_factor_matrix.shape[0]
    parts = down_factor_matrix.shape[1]
    factors = parts * rank
    strips = columns // LANES
    down_rows = features // n_dp
    up_rows = rank // n_dp
    packed_rows = down_rows + up_rows * strips
    steps = range(1, chips)
    f32, bf16 = jnp.float32, jnp.bfloat16

    def to_sibling(value):
        return lax.ppermute(value, "tensor", [(t, t ^ 1) for t in range(n_tensor)])

    def to_chip(value, step):
        pairs = [
            (CORES * q + k, CORES * ((q + step) % chips) + k)
            for q in range(chips)
            for k in range(CORES)
        ]
        return lax.ppermute(value, "tensor", pairs)

    def by_rank(value):
        return jnp.transpose(value, (1, 2, 0)).reshape(factors, features)

    down_sent = by_rank(down_gradient[0])
    down_state = [by_rank(v) for v in (down_factor_matrix, down_moment_first, down_moment_second)]
    up_state = [up_factor_matrix, up_moment_first, up_moment_second]
    shares = jax.ShapeDtypeStruct((n_dp, packed_rows, LANES), bf16)
    window = pl.cdiv(down_rows + LANES, LANES) * LANES
    aligned = features % LANES == 0 and window <= features
    aligned = aligned and up_rows % 8 == 0 and down_rows % 16 == 0
    window = window if aligned else down_rows
    turns = [1, 2] if n_dp % 4 == 0 else [1, 1]
    turn = [turns[strip % 2] for strip in range(strips)]
    halves = min(COLUMN_HALVES, strips)
    wide = columns // halves
    groups = [range(k * strips // halves, (k + 1) * strips // halves) for k in range(halves)]
    out_shape = (shares,) + tuple(
        jax.ShapeDtypeStruct((len(group), features, LANES), bf16)
        for group in groups
        for _ in steps
    )
    packed, *taken = pl.pallas_call(
        functools.partial(begin_kernel, chips, turn),
        out_shape=out_shape,
        in_specs=anywhere(3),
        out_specs=tuple(anywhere(len(out_shape))),
        scratch_shapes=[
            pltpu.VMEM((factors, features), f32),
            pltpu.VMEM((rank, columns), f32),
            pltpu.VMEM(shares.shape, bf16),
            pltpu.VMEM((len(steps) * strips, features, LANES), bf16),
            pltpu.SemaphoreType.DMA((2 + len(steps) * strips,)),
            pltpu.SemaphoreType.DMA((n_dp + len(steps) * strips,)),
        ],
        compiler_params=pltpu.CompilerParams(vmem_limit_bytes=LARGE_VMEM_BYTES),
    )(down_sent, up_gradient[0], frozen_key_value)
    exchanged = lax.all_to_all(packed, "dp", 0, 0, tiled=True)
    if not aligned:
        down_state = [
            lax.dynamic_slice_in_dim(v, replica * down_rows, down_rows, 1) for v in down_state
        ]
        up_state = [lax.dynamic_slice_in_dim(v, replica * up_rows, up_rows, 0) for v in up_state]
    mine = []

    def send_half(half, after):
        blocks = taken[half * len(steps) : (half + 1) * len(steps)]
        if after is not None:
            blocks, _ = lax.optimization_barrier((blocks, after))
        mine.append([to_chip(value, step) for value, step in zip(blocks, steps)])

    send_half(0, None)

    gain = input_norm_gain[None, :]
    some = tokens // TOKEN_HALVES
    operands = [prompt_hidden_input, to_sibling(prompt_hidden_input), gain, to_sibling(gain)]

    def prepared(first, size, summed, before, in_place, limit):
        if in_place:
            x_shape = (jax.ShapeDtypeStruct((size, CORES * features), bf16),)
            x_specs = tuple(in_vmem(1))
        else:
            x_shape = (jax.ShapeDtypeStruct((size, features), bf16),) * 2
            x_specs = tuple(anywhere(2))
        copied = max(size, summed)
        if summed:
            x_shape += (jax.ShapeDtypeStruct(((first + summed) // LANES, LANES), f32),)
            x_specs += tuple(in_vmem(1))
        outs = pl.pallas_call(
            functools.partial(prepare_kernel, first, summed),
            out_shape=x_shape,
            in_specs=anywhere(2) + in_vmem(2 + len(before)),
            out_specs=x_specs,
            scratch_shapes=[
                pltpu.VMEM((copied, features), bf16),
                pltpu.VMEM((copied, features), bf16),
                pltpu.VMEM((copied, LANES), f32),
                pltpu.SemaphoreType.DMA((4 * pl.cdiv(copied, LANES),)),
            ],
            compiler_params=pltpu.CompilerParams(vmem_limit_bytes=limit),
        )(*operands, *before)
        return (list(outs[:-1]), outs[-1]) if summed else (list(outs), None)

    x0, squares = prepared(0, some, tokens, [], True, PREPARE_VMEM_BYTES)
    exchanged, squares = lax.optimization_barrier((exchanged, squares))
    x1, _ = prepared(some, some, 0, [squares], False, LARGE_VMEM_BYTES)
    a_next, b_next, sent = pl.pallas_call(
        adam_kernel,
        out_shape=(
            jax.ShapeDtypeStruct((3, factors, down_rows), f32),
            jax.ShapeDtypeStruct((3, up_rows, columns), f32),
            shares,
        ),
        in_specs=anywhere(7),
        out_specs=tuple(in_vmem(3)),
        scratch_shapes=[
            pltpu.VMEM((n_dp, packed_rows, LANES), bf16),
            pltpu.VMEM((3, factors, window), f32),
            pltpu.VMEM((3, up_rows, columns), f32),
            pltpu.SemaphoreType.DMA((7,)),
        ],
        compiler_params=pltpu.CompilerParams(vmem_limit_bytes=LARGE_VMEM_BYTES),
    )(exchanged, *down_state, *up_state)
    own_f = lax.all_to_all(sent, "dp", 0, 0, tiled=True)
    for half in range(1, halves):
        send_half(half, (mine[-1], sent))
    a_next = jnp.transpose(a_next.reshape(3, parts, rank, down_rows), (0, 3, 1, 2))

    outside = [[] for _ in range(strips)]

    def swap_half(half, after):
        for value in mine[half]:
            value, _ = lax.optimization_barrier((value, after))
            split = pl.pallas_call(
                split_kernel,
                out_shape=(jax.ShapeDtypeStruct((features, LANES), bf16),) * len(groups[half]),
                in_specs=in_vmem(1),
                out_specs=tuple(in_vmem(len(groups[half]))),
                compiler_params=params(),
            )(value)
            for piece, strip in zip(split, groups[half]):
                pairs = [(i, i ^ turn[strip]) for i in range(n_dp)]
                outside[strip].append((piece, lax.ppermute(piece, "dp", pairs)))

    swap_half(0, sent)
    own_f, x1 = lax.optimization_barrier((own_f, x1))
    up_packed = packed_rows - down_rows
    more = pl.cdiv(3 * (tokens // LANES), up_packed)
    piece = jax.ShapeDtypeStruct((n_dp // FACTOR_PIECES, packed_rows, LANES), bf16)
    message, *pieces = pl.pallas_call(
        message_kernel,
        out_shape=(jax.ShapeDtypeStruct((n_dp + more, up_packed, LANES), bf16),)
        + (piece,) * FACTOR_PIECES,
        in_specs=anywhere(2),
        out_specs=tuple(in_vmem(1 + FACTOR_PIECES)),
        scratch_shapes=[
            pltpu.VMEM(squares.shape, f32),
            pltpu.SemaphoreType.DMA((2 + FACTOR_PIECES,)),
        ],
        compiler_params=params(),
    )(own_f, squares)
    messages = [to_chip(message, step) for step in steps]
    sibling_f = [to_sibling(piece) for piece in pieces]

    inv_rms = pl.pallas_call(
        functools.partial(inverse_kernel, width, n_dp),
        out_shape=jax.ShapeDtypeStruct((tokens, LANES), f32),
        in_specs=in_vmem(chips),
        out_specs=in_vmem(1)[0],
        compiler_params=params(),
    )(squares, *messages)

    scale = 0.5 / math.sqrt(width * rank)

    received = {}
    after = []
    weights_shape = jax.ShapeDtypeStruct((CORES * features, wide), bf16)
    product_shape = jax.ShapeDtypeStruct((some, wide), bf16)
    for half, group in enumerate(groups):
        static = (scale, parts, up_rows, group, columns)
        if half > 0:
            swap_half(half, products[0])
        for step in steps:
            blocks = [value for strip in group for value in outside[strip][step - 1]]
            arranged = pl.pallas_call(
                functools.partial(arrange_kernel, [turn[strip] for strip in group]),
                out_shape=weights_shape,
                in_specs=in_vmem(len(blocks)) + anywhere(len(after)),
                out_specs=in_vmem(1)[0],
                compiler_params=params(),
            )(*blocks, *after)
            weights, product = pl.pallas_call(
                functools.partial(outside_kernel, static, chips, step),
                out_shape=(weights_shape, product_shape),
                in_specs=in_vmem(3 + 2 * FACTOR_PIECES),
                out_specs=tuple(in_vmem(2)),
                compiler_params=params(),
            )(arranged, messages[step - 1], *x0, *pieces, *sibling_f)
            received.setdefault((0, half), []).append(to_chip(product, chips - step))
            second = pl.pallas_call(
                functools.partial(more_kernel, len(x1) // 2),
                out_shape=product_shape,
                in_specs=in_vmem(1 + len(x1)),
                out_specs=in_vmem(1)[0],
                compiler_params=params(),
            )(*x1, weights)
            products = [product, second]
            after = [second]
            received.setdefault((1, half), []).append(to_chip(second, chips - step))
        if half == 0:
            after = [received[0, 0][0]]

    after.append(received[1, 0][0])
    static = (scale, parts, up_rows, range(strips), columns, halves, len(x1) // 2)
    totals = pl.pallas_call(
        functools.partial(own_kernel, static),
        out_shape=(jax.ShapeDtypeStruct((tokens, wide), f32),) * halves,
        grid=(1,),
        in_specs=[
            pl.BlockSpec((features, columns), lambda i: (lax.axis_index("tensor"), 0)),
            pl.BlockSpec((features, columns), lambda i: (lax.axis_index("tensor") ^ 1, 0)),
        ]
        + in_vmem(2 * FACTOR_PIECES + 1 + len(x1))
        + anywhere(len(after)),
        out_specs=tuple(in_vmem(halves)),
        scratch_shapes=[pltpu.VMEM((CORES * features, columns), bf16)],
        compiler_params=params(),
        cost_estimate=pl.CostEstimate(
            flops=2 * tokens * CORES * features * columns,
            bytes_accessed=4 * tokens * features,
            transcendentals=0,
        ),
    )(frozen_key_value, frozen_key_value, *pieces, *sibling_f, *x0, *x1, *after)

    keys_values = None
    for at, values in received.items():
        keys_values = finish(
            totals[at[1]], inv_rms, values, at, (tokens, columns), keys_values
        )
    return (a_next, b_next, keys_values)


def solution(mesh):
    placed = (
        P("dp", "tensor"),
        P("tensor"),
        P(None, "tensor"),
        P("tensor", None, None),
        P("tensor", None, None),
        P("tensor", None, None),
        P(None, "tensor"),
        P(None, "tensor"),
        P(None, "tensor"),
        P("dp", "tensor", None, None),
        P("dp", None, "tensor"),
    )
    return jax.shard_map(
        body,
        mesh=mesh,
        in_specs=placed,
        out_specs=(
            P(None, ("tensor", "dp"), None, None),
            P(None, "dp", "tensor"),
            P("dp", "tensor"),
        ),
        check_vma=False,
    )
```

```python
import functools
import math

import jax
import jax.numpy as jnp
from jax import lax
from jax.experimental import pallas as pl
from jax.experimental.pallas import tpu as pltpu
from jax.sharding import PartitionSpec as P

KEY_VALUE_WIDTH = 1024
STEP = 100
CORES = 2
LANES = 128
COLUMN_HALVES = 2
TOKEN_HALVES = 2
FACTOR_PIECES = 2
VMEM_BYTES = 16 * 2**20
LARGE_VMEM_BYTES = 58 * 2**20
PREPARE_VMEM_BYTES = 49 * 2**20


def adaptive_moment_update(param, first, second, grad_mean):
    first_new = 0.9 * first + 0.1 * grad_mean
    second_new = 0.999 * second + 0.001 * grad_mean * grad_mean
    step_size = first_new / (1.0 - 0.9**STEP) / (jnp.sqrt(second_new / (1.0 - 0.999**STEP)) + 1e-08)
    return (param - 0.1 * step_size, first_new, second_new)


def in_vmem(count):
    return [pl.BlockSpec(memory_space=pltpu.VMEM)] * count


def anywhere(count):
    return [pl.BlockSpec(memory_space=pl.ANY)] * count


SCALARS = pl.BlockSpec(memory_space=pltpu.SMEM)


def params(**more):
    return pltpu.CompilerParams(vmem_limit_bytes=VMEM_BYTES, **more)


def pack(down, up, out_ref, ready):
    shares = out_ref.shape[0]
    down = down.T
    down_rows, up_rows = down.shape[0] // shares, up.shape[0] // shares
    for i in range(shares):
        pieces = [down[i * down_rows : (i + 1) * down_rows]]
        for k in range(up.shape[1] // LANES):
            pieces.append(up[i * up_rows : (i + 1) * up_rows, k * LANES : (k + 1) * LANES])
        out_ref[i] = jnp.concatenate(pieces, axis=0).astype(jnp.bfloat16)
        ready(i)


def first_lane(share, window, size):
    return jnp.minimum(share // LANES * LANES, size - window)


def begin_kernel(chips, turn, down_ref, up_ref, weights_ref, packed, *refs):
    outs, (down, up, blocks, strips, sem, sem_out) = refs[:-6], refs[-6:]
    features = strips.shape[1]
    place, replica = lax.axis_index("tensor"), lax.axis_index("dp")
    chip, core = place // CORES, place % CORES
    copies, back = [], []

    def add(source, target):
        copies.append(pltpu.make_async_copy(source, target, sem.at[len(copies)]))
        copies[-1].start()

    def add_back(source, target):
        back.append(pltpu.make_async_copy(source, target, sem_out.at[len(back)]))
        back[-1].start()

    add(down_ref, down)
    add(up_ref, up)
    targets = []
    for i, out in enumerate(outs):
        step, first = 1 + i % (chips - 1), i // (chips - 1) * out.shape[0]
        for k in range(out.shape[0]):
            half = (core + replica // turn[first + k]) % 2
            row = ((chip + step) % chips * CORES + half) * features
            add(
                weights_ref.at[
                    pl.ds(pl.multiple_of(row, features), features),
                    pl.ds((first + k) * LANES, LANES),
                ],
                strips.at[len(targets)],
            )
            targets.append(out.at[k])
    copies[0].wait()
    copies[1].wait()

    def ready(i):
        add_back(blocks.at[i], packed.at[i])
        if i == min(1, blocks.shape[0] - 1):
            for k, target in enumerate(targets):
                copies[2 + k].wait()
                add_back(strips.at[k], target)

    pack(down[...], up[...], blocks, ready)
    for copy in back:
        copy.wait()


def split_kernel(in_ref, *refs):
    outs, (buffer, sem_in, sem_out) = refs[:-3], refs[-3:]
    rows = buffer.shape[1] // 2
    pieces = [(k, pl.ds(half * rows, rows)) for k in range(len(outs)) for half in range(2)]
    loads = [
        pltpu.make_async_copy(in_ref.at[k, part], buffer.at[k, part], sem_in.at[i])
        for i, (k, part) in enumerate(pieces)
    ]
    stores = [
        pltpu.make_async_copy(buffer.at[k, part], outs[k].at[part], sem_out.at[i])
        for i, (k, part) in enumerate(pieces)
    ]
    for copy in loads:
        copy.start()
    for load, store in zip(loads, stores):
        load.wait()
        store.start()
    for copy in stores:
        copy.wait()


def prepare_kernel(first, summed, own_in, sibling_in, own_gain, sibling_gain, *refs):
    own, sibling, squares, sem = refs[-4:]
    copied, features = own.shape
    refs = refs[:-4]
    before, sums_ref = [], None
    if summed:
        refs, sums_ref = refs[:-1], refs[-1]
    together = refs[-1].shape[1] > features
    outs = refs[-1:] if together else refs[-2:]
    before = refs[: -len(outs)]
    rows = outs[0].shape[0]
    block = LANES if rows % LANES == 0 else rows
    tile = 16 if block % 16 == 0 else block
    raw = ((own_in, own), (sibling_in, sibling))
    loads = [
        [
            pltpu.make_async_copy(
                source.at[pl.ds(first + k * block, block)],
                target.at[pl.ds(k * block, block)],
                sem.at[2 * k + side],
            )
            for side, (source, target) in enumerate(raw)
        ]
        for k in range(copied // block)
    ]
    for pair in loads:
        for copy in pair:
            copy.start()
    stores = []
    for k, pair in enumerate(loads):
        for copy in pair:
            copy.wait()
        scale, add = k * block < rows, k * block < summed

        @pl.loop(0, block // tile, unroll=2)
        def _(i):
            at = pl.ds(pl.multiple_of(k * block + i * tile, tile), tile)
            total = None
            for side, (ref, gain) in enumerate(((own, own_gain), (sibling, sibling_gain))):
                value = ref[at, :].astype(jnp.float32)
                if scale:
                    scaled = (value * gain[...]).astype(ref.dtype)
                    if together:
                        outs[0][at, side * features : (side + 1) * features] = scaled
                    else:
                        ref[at, :] = scaled
                if add:
                    total = value * value if total is None else total + value * value
            if add:
                total = jnp.sum(total, axis=1, keepdims=True)
                squares[at, :] = jnp.broadcast_to(total, (tile, LANES))

        if scale and not together:
            part = pl.ds(k * block, block)
            for side, (source, out) in enumerate(((own, outs[0]), (sibling, outs[1]))):
                place = sem.at[2 * (len(loads) + k) + side]
                stores.append(pltpu.make_async_copy(source.at[part], out.at[part], place))
                stores[-1].start()
    if summed:
        done = 0
        for ref in before:
            sums_ref[: ref.shape[0]] = ref[...]
            done = ref.shape[0]
        for i in range(summed // LANES):
            row = squares[i * LANES : (i + 1) * LANES, :].T[:1]
            sums_ref[done + i : done + i + 1] = row
    for copy in stores:
        copy.wait()


def message_kernel(factor_ref, sums_ref, out_ref, *refs):
    pieces, (sums, sem) = refs[:-2], refs[-2:]
    shares, up_rows = factor_ref.shape[0], out_ref.shape[1]
    sums_copy = pltpu.make_async_copy(sums_ref, sums, sem.at[1 + len(pieces)])
    sums_copy.start()
    copies = [
        pltpu.make_async_copy(
            factor_ref.at[:, pl.ds(factor_ref.shape[1] - up_rows, up_rows)],
            out_ref.at[pl.ds(0, shares)],
            sem.at[0],
        )
    ]
    for k, piece in enumerate(pieces):
        size = piece.shape[0]
        copies.append(
            pltpu.make_async_copy(factor_ref.at[pl.ds(k * size, size)], piece, sem.at[1 + k])
        )
    for copy in copies:
        copy.start()
    sums_copy.wait()
    left = sums[...]
    terms = []
    for _ in range(3):
        terms.append(left.astype(jnp.bfloat16).astype(jnp.float32))
        left = left - terms[-1]
    rest = (out_ref.shape[0] - shares) * up_rows - 3 * left.shape[0]
    if rest > 0:
        terms.append(jnp.zeros((rest, LANES), jnp.float32))
    rows = jnp.concatenate(terms, axis=0)
    for i in range(out_ref.shape[0] - shares):
        out_ref[shares + i] = rows[i * up_rows : (i + 1) * up_rows].astype(jnp.bfloat16)
    for copy in copies:
        copy.wait()


def inverse_kernel(width, shares, sums_ref, *refs):
    messages, out = refs[:-1], refs[-1]
    total = sums_ref[...]
    count = total.shape[0]
    for ref in messages:
        rows = [ref[i].astype(jnp.float32) for i in range(shares, ref.shape[0])]
        rows = jnp.concatenate(rows, axis=0)
        total += rows[:count] + rows[count : 2 * count] + rows[2 * count : 3 * count]
    inverse = lax.rsqrt(total / width + 1e-06)
    for i in range(count):
        out[i * LANES : (i + 1) * LANES, :] = jnp.broadcast_to(
            inverse[i : i + 1], (LANES, LANES)
        ).T


def update(total, down, up, a_ref, b_ref):
    down_rows = a_ref.shape[2]
    up_rows, columns = b_ref.shape[1:]
    strips = columns // LANES
    down_mean = total[:down_rows].T
    up_mean = jnp.concatenate(
        [total[down_rows + k * up_rows : down_rows + (k + 1) * up_rows] for k in range(strips)],
        axis=1,
    )
    p, m, v = adaptive_moment_update(*down(), down_mean)
    a_ref[0], a_ref[1], a_ref[2] = p, m, v
    pieces = [p.T]
    p, m, v = adaptive_moment_update(*up(), up_mean)
    b_ref[0], b_ref[1], b_ref[2] = p, m, v
    pieces += [p[:, k * LANES : (k + 1) * LANES] for k in range(strips)]
    return jnp.concatenate(pieces, axis=0).astype(jnp.bfloat16)


def adam_kernel(grad_in, *refs):
    state, refs = refs[:6], refs[6:]
    a_ref, b_ref, factor_ref, grad_ref, down_win, up_win, sem = refs
    replicas = grad_ref.shape[0]
    down_rows, window = a_ref.shape[2], down_win.shape[2]
    up_rows = up_win.shape[1]
    replica = lax.axis_index("dp")
    share = replica * down_rows
    size = down_rows * replicas
    copies = [pltpu.make_async_copy(grad_in, grad_ref, sem.at[6])]
    for i in range(3):
        down, up = state[i], state[3 + i]
        if window != down_rows:
            lane = pl.multiple_of(first_lane(share, window, size), LANES)
            down = down.at[:, pl.ds(lane, window)]
            up = up.at[pl.ds(pl.multiple_of(replica * up_rows, up_rows), up_rows)]
        copies.append(pltpu.make_async_copy(down, down_win.at[i], sem.at[i]))
        copies.append(pltpu.make_async_copy(up, up_win.at[i], sem.at[3 + i]))
    for copy in copies:
        copy.start()
    copies[0].wait()
    total = jnp.sum(grad_ref[...].astype(jnp.float32), axis=0) / replicas
    for copy in copies[1:]:
        copy.wait()

    def down():
        if window == down_rows:
            return [down_win[i] for i in range(3)]
        shift = window - (share - first_lane(share, window, size))
        return [pltpu.roll(down_win[i], shift, 1)[:, :down_rows] for i in range(3)]

    rounded = update(total, down, lambda: [up_win[i] for i in range(3)], a_ref, b_ref)
    for i in range(replicas):
        factor_ref[i] = rounded


def factor_a(refs, down_rows):
    pieces = []
    for ref in refs:
        for i in range(ref.shape[0]):
            if down_rows % 16 == 0:
                pieces.append(ref[i, :down_rows, :])
            else:
                pieces.append(ref[i].astype(jnp.float32)[:down_rows])
    return jnp.concatenate(pieces, axis=0).astype(jnp.bfloat16)


def factor_b(packed, part, parts, strip, up_rows):
    pieces = [
        packed[i].astype(jnp.float32)[strip * up_rows : (strip + 1) * up_rows]
        for i in range(packed.shape[0])
    ]
    value = jnp.concatenate(pieces, axis=0)
    rows = [jnp.where(part == j, value, jnp.zeros_like(value)) for j in range(parts)]
    return jnp.concatenate(rows, axis=0).astype(jnp.bfloat16)


def merge(scale, block, a, b):
    change = jnp.dot(a, b, preferred_element_type=jnp.float32)
    return (block.astype(jnp.float32) + scale * change).astype(jnp.bfloat16)


def multiply(groups, weights, *outs):
    wide = outs[0].shape[1]
    done = 0
    for xs in groups:
        rows = xs[0].shape[0]
        tile = rows // 2 if rows % 32 == 0 else rows

        @pl.loop(0, rows // tile)
        def _(i):
            at = pl.ds(pl.multiple_of(i * tile, tile), tile)
            to = pl.ds(pl.multiple_of(done + i * tile, 16), tile)
            value, first = None, 0
            for x in xs:
                size = x.shape[1]
                part = jnp.dot(
                    x[at, :], weights[first : first + size, :], preferred_element_type=jnp.float32
                )
                value, first = part if value is None else value + part, first + size
            for k, out in enumerate(outs):
                out[to, :] = value[:, k * wide : (k + 1) * wide].astype(out.dtype)

        done += rows


def up_factor(static, packed, owner):
    _, parts, up_rows, strips, columns = static
    part = owner * columns // KEY_VALUE_WIDTH
    return jnp.concatenate(
        [factor_b(packed, part, parts, strip, up_rows) for strip in strips], axis=1
    )


def arrange_kernel(turn, *refs):
    out = refs[-1]
    replica = lax.axis_index("dp")
    features = out.shape[0] // CORES
    for k, alternate in enumerate(turn):
        mine, other = refs[2 * k : 2 * k + 2]
        even = replica // alternate % 2 == 0
        lanes = slice(k * LANES, (k + 1) * LANES)
        out[:features, lanes] = jnp.where(even, mine[...], other[...])
        out[features:, lanes] = jnp.where(even, other[...], mine[...])


def outside_kernel(static, chips, step, blocks, b_ref, x, *refs):
    own_f, sibling_f = refs[:FACTOR_PIECES], refs[FACTOR_PIECES : 2 * FACTOR_PIECES]
    weights, product = refs[-2:]
    features = blocks.shape[0] // CORES
    down_rows = own_f[0].shape[1] - b_ref.shape[1]
    shares = FACTOR_PIECES * own_f[0].shape[0]
    place = lax.axis_index("tensor")
    owner = (place // CORES - step + chips) % chips * CORES + place % CORES
    b = up_factor(static, b_ref[:shares], owner)
    tile = 256 if features % 256 == 0 else features
    for side, factors in enumerate((own_f, sibling_f)):
        a = factor_a(factors, down_rows)
        for first in range(0, features, tile):
            rows = slice(side * features + first, side * features + first + tile)
            weights[rows, :] = merge(static[0], blocks[rows, :], a[first : first + tile], b)
    multiply([[x]], weights, product)


def more_kernel(groups, *refs):
    xs, (weights, product) = refs[:-2], refs[-2:]
    size = len(xs) // groups
    multiply([xs[k * size : (k + 1) * size] for k in range(groups)], weights, product)


def own_kernel(static, own_block, sibling_block, *refs):
    own_f, sibling_f = refs[:FACTOR_PIECES], refs[FACTOR_PIECES : 2 * FACTOR_PIECES]
    refs = refs[2 * FACTOR_PIECES :]
    groups, weights = [refs[:1]], refs[-1]
    for k in range(static[6]):
        groups.append(refs[1 + 2 * k : 3 + 2 * k])
    outs = refs[len(refs) - 1 - static[5] : -1]
    features = own_block.shape[0]
    wide = outs[0].shape[1]
    down_rows = own_f[0].shape[1] - len(static[3]) * static[2]
    b = jnp.concatenate([piece[:, down_rows:] for piece in own_f], axis=0)
    b = up_factor(static[:5], b, lax.axis_index("tensor"))
    for at, factors, block in ((0, own_f, own_block), (features, sibling_f, sibling_block)):
        weights[at : at + features] = merge(static[0], block[...], factor_a(factors, down_rows), b)
    multiply(groups, weights, *outs)


def finish_kernel(sources, first, own, inv, *refs):
    rows = pl.ds(first, refs[-1].shape[0])
    total = own[rows, :]
    for value in refs[:sources]:
        total = total + value[...].astype(jnp.float32)
    refs[-1][...] = (total * inv[rows, :1]).astype(refs[-1].dtype)


def finish(own, inv_rms, received, at, shape, before):
    block = received[0].shape
    operands = [own, inv_rms] + received
    in_specs = in_vmem(len(operands))
    aliases = {}
    if before is not None:
        aliases = {len(operands): 0}
        in_specs += anywhere(1)
        operands.append(before)
    return pl.pallas_call(
        functools.partial(finish_kernel, len(received), at[0] * block[0]),
        grid=(1,),
        out_shape=jax.ShapeDtypeStruct(shape, jnp.bfloat16),
        in_specs=in_specs,
        out_specs=pl.BlockSpec(block, lambda i: at),
        input_output_aliases=aliases,
        compiler_params=params(),
    )(*operands)


def body(
    prompt_hidden_input,
    input_norm_gain,
    frozen_key_value,
    down_factor_matrix,
    down_moment_first,
    down_moment_second,
    up_factor_matrix,
    up_moment_first,
    up_moment_second,
    down_gradient,
    up_gradient,
):
    n_dp = lax.axis_size("dp")
    n_tensor = lax.axis_size("tensor")
    chips = n_tensor // CORES
    replica = lax.axis_index("dp")
    tokens, features = prompt_hidden_input.shape
    width, columns = frozen_key_value.shape
    rank = up_factor_matrix.shape[0]
    parts = down_factor_matrix.shape[1]
    factors = parts * rank
    strips = columns // LANES
    down_rows = features // n_dp
    up_rows = rank // n_dp
    packed_rows = down_rows + up_rows * strips
    steps = range(1, chips)
    f32, bf16 = jnp.float32, jnp.bfloat16

    def to_sibling(value):
        return lax.ppermute(value, "tensor", [(t, t ^ 1) for t in range(n_tensor)])

    def to_chip(value, step):
        pairs = [
            (CORES * q + k, CORES * ((q + step) % chips) + k)
            for q in range(chips)
            for k in range(CORES)
        ]
        return lax.ppermute(value, "tensor", pairs)

    def by_rank(value):
        return jnp.transpose(value, (1, 2, 0)).reshape(factors, features)

    down_sent = by_rank(down_gradient[0])
    down_state = [by_rank(v) for v in (down_factor_matrix, down_moment_first, down_moment_second)]
    up_state = [up_factor_matrix, up_moment_first, up_moment_second]
    shares = jax.ShapeDtypeStruct((n_dp, packed_rows, LANES), bf16)
    window = pl.cdiv(down_rows + LANES, LANES) * LANES
    aligned = features % LANES == 0 and window <= features
    aligned = aligned and up_rows % 8 == 0 and down_rows % 16 == 0
    window = window if aligned else down_rows
    turns = [1, 2] if n_dp % 4 == 0 else [1, 1]
    turn = [turns[strip % 2] for strip in range(strips)]
    halves = min(COLUMN_HALVES, strips)
    wide = columns // halves
    groups = [range(k * strips // halves, (k + 1) * strips // halves) for k in range(halves)]
    out_shape = (shares,) + tuple(
        jax.ShapeDtypeStruct((len(group), features, LANES), bf16)
        for group in groups
        for _ in steps
    )
    packed, *taken = pl.pallas_call(
        functools.partial(begin_kernel, chips, turn),
        out_shape=out_shape,
        in_specs=anywhere(3),
        out_specs=tuple(anywhere(len(out_shape))),
        scratch_shapes=[
            pltpu.VMEM((factors, features), f32),
            pltpu.VMEM((rank, columns), f32),
            pltpu.VMEM(shares.shape, bf16),
            pltpu.VMEM((len(steps) * strips, features, LANES), bf16),
            pltpu.SemaphoreType.DMA((2 + len(steps) * strips,)),
            pltpu.SemaphoreType.DMA((n_dp + len(steps) * strips,)),
        ],
        compiler_params=pltpu.CompilerParams(vmem_limit_bytes=LARGE_VMEM_BYTES),
    )(down_sent, up_gradient[0], frozen_key_value)
    exchanged = lax.all_to_all(packed, "dp", 0, 0, tiled=True)
    if not aligned:
        down_state = [
            lax.dynamic_slice_in_dim(v, replica * down_rows, down_rows, 1) for v in down_state
        ]
        up_state = [lax.dynamic_slice_in_dim(v, replica * up_rows, up_rows, 0) for v in up_state]
    mine = []

    def send_half(half, after):
        blocks = taken[half * len(steps) : (half + 1) * len(steps)]
        if after is not None:
            blocks, _ = lax.optimization_barrier((blocks, after))
        mine.append([to_chip(value, step) for value, step in zip(blocks, steps)])

    send_half(0, None)

    gain = input_norm_gain[None, :]
    some = tokens // TOKEN_HALVES
    operands = [prompt_hidden_input, to_sibling(prompt_hidden_input), gain, to_sibling(gain)]

    def prepared(first, size, summed, before, in_place, limit):
        if in_place:
            x_shape = (jax.ShapeDtypeStruct((size, CORES * features), bf16),)
            x_specs = tuple(in_vmem(1))
        else:
            x_shape = (jax.ShapeDtypeStruct((size, features), bf16),) * 2
            x_specs = tuple(anywhere(2))
        copied = max(size, summed)
        if summed:
            x_shape += (jax.ShapeDtypeStruct(((first + summed) // LANES, LANES), f32),)
            x_specs += tuple(in_vmem(1))
        outs = pl.pallas_call(
            functools.partial(prepare_kernel, first, summed),
            out_shape=x_shape,
            in_specs=anywhere(2) + in_vmem(2 + len(before)),
            out_specs=x_specs,
            scratch_shapes=[
                pltpu.VMEM((copied, features), bf16),
                pltpu.VMEM((copied, features), bf16),
                pltpu.VMEM((copied, LANES), f32),
                pltpu.SemaphoreType.DMA((4 * pl.cdiv(copied, LANES),)),
            ],
            compiler_params=pltpu.CompilerParams(vmem_limit_bytes=limit),
        )(*operands, *before)
        return (list(outs[:-1]), outs[-1]) if summed else (list(outs), None)

    x0, squares = prepared(0, some, tokens, [], True, PREPARE_VMEM_BYTES)
    exchanged, squares = lax.optimization_barrier((exchanged, squares))
    x1, _ = prepared(some, some, 0, [squares], False, LARGE_VMEM_BYTES)
    a_next, b_next, sent = pl.pallas_call(
        adam_kernel,
        out_shape=(
            jax.ShapeDtypeStruct((3, factors, down_rows), f32),
            jax.ShapeDtypeStruct((3, up_rows, columns), f32),
            shares,
        ),
        in_specs=anywhere(7),
        out_specs=tuple(in_vmem(3)),
        scratch_shapes=[
            pltpu.VMEM((n_dp, packed_rows, LANES), bf16),
            pltpu.VMEM((3, factors, window), f32),
            pltpu.VMEM((3, up_rows, columns), f32),
            pltpu.SemaphoreType.DMA((7,)),
        ],
        compiler_params=pltpu.CompilerParams(vmem_limit_bytes=LARGE_VMEM_BYTES),
    )(exchanged, *down_state, *up_state)
    own_f = lax.all_to_all(sent, "dp", 0, 0, tiled=True)
    for half in range(1, halves):
        send_half(half, (mine[-1], sent))
    a_next = jnp.transpose(a_next.reshape(3, parts, rank, down_rows), (0, 3, 1, 2))

    outside = [[] for _ in range(strips)]

    def swap_half(half, after):
        for value in mine[half]:
            value, _ = lax.optimization_barrier((value, after))
            split = pl.pallas_call(
                split_kernel,
                out_shape=(jax.ShapeDtypeStruct((features, LANES), bf16),) * len(groups[half]),
                in_specs=anywhere(1),
                out_specs=tuple(anywhere(len(groups[half]))),
                scratch_shapes=[
                    pltpu.VMEM(value.shape, bf16),
                    pltpu.SemaphoreType.DMA((2 * len(groups[half]),)),
                    pltpu.SemaphoreType.DMA((2 * len(groups[half]),)),
                ],
                compiler_params=params(),
            )(value)
            for piece, strip in zip(split, groups[half]):
                pairs = [(i, i ^ turn[strip]) for i in range(n_dp)]
                outside[strip].append((piece, lax.ppermute(piece, "dp", pairs)))

    swap_half(0, sent)
    own_f, x1 = lax.optimization_barrier((own_f, x1))
    up_packed = packed_rows - down_rows
    more = pl.cdiv(3 * (tokens // LANES), up_packed)
    piece = jax.ShapeDtypeStruct((n_dp // FACTOR_PIECES, packed_rows, LANES), bf16)
    message, *pieces = pl.pallas_call(
        message_kernel,
        out_shape=(jax.ShapeDtypeStruct((n_dp + more, up_packed, LANES), bf16),)
        + (piece,) * FACTOR_PIECES,
        in_specs=anywhere(2),
        out_specs=tuple(in_vmem(1 + FACTOR_PIECES)),
        scratch_shapes=[
            pltpu.VMEM(squares.shape, f32),
            pltpu.SemaphoreType.DMA((2 + FACTOR_PIECES,)),
        ],
        compiler_params=params(),
    )(own_f, squares)
    messages = [to_chip(message, step) for step in steps]
    sibling_f = [to_sibling(piece) for piece in pieces]

    inv_rms = pl.pallas_call(
        functools.partial(inverse_kernel, width, n_dp),
        out_shape=jax.ShapeDtypeStruct((tokens, LANES), f32),
        in_specs=in_vmem(chips),
        out_specs=in_vmem(1)[0],
        compiler_params=params(),
    )(squares, *messages)

    scale = 0.5 / math.sqrt(width * rank)

    received = {}
    after = []
    weights_shape = jax.ShapeDtypeStruct((CORES * features, wide), bf16)
    product_shape = jax.ShapeDtypeStruct((some, wide), bf16)
    for half, group in enumerate(groups):
        static = (scale, parts, up_rows, group, columns)
        if half > 0:
            swap_half(half, products[0])
        for step in steps:
            blocks = [value for strip in group for value in outside[strip][step - 1]]
            arranged = pl.pallas_call(
                functools.partial(arrange_kernel, [turn[strip] for strip in group]),
                out_shape=weights_shape,
                in_specs=in_vmem(len(blocks)) + anywhere(len(after)),
                out_specs=in_vmem(1)[0],
                compiler_params=params(),
            )(*blocks, *after)
            weights, product = pl.pallas_call(
                functools.partial(outside_kernel, static, chips, step),
                out_shape=(weights_shape, product_shape),
                in_specs=in_vmem(3 + 2 * FACTOR_PIECES),
                out_specs=tuple(in_vmem(2)),
                compiler_params=params(),
            )(arranged, messages[step - 1], *x0, *pieces, *sibling_f)
            received.setdefault((0, half), []).append(to_chip(product, chips - step))
            second = pl.pallas_call(
                functools.partial(more_kernel, len(x1) // 2),
                out_shape=product_shape,
                in_specs=in_vmem(1 + len(x1)),
                out_specs=in_vmem(1)[0],
                compiler_params=params(),
            )(*x1, weights)
            products = [product, second]
            after = [second]
            received.setdefault((1, half), []).append(to_chip(second, chips - step))
        if half == 0:
            after = [received[0, 0][0]]

    after.append(received[1, 0][0])
    static = (scale, parts, up_rows, range(strips), columns, halves, len(x1) // 2)
    totals = pl.pallas_call(
        functools.partial(own_kernel, static),
        out_shape=(jax.ShapeDtypeStruct((tokens, wide), f32),) * halves,
        grid=(1,),
        in_specs=[
            pl.BlockSpec((features, columns), lambda i: (lax.axis_index("tensor"), 0)),
            pl.BlockSpec((features, columns), lambda i: (lax.axis_index("tensor") ^ 1, 0)),
        ]
        + in_vmem(2 * FACTOR_PIECES + 1 + len(x1))
        + anywhere(len(after)),
        out_specs=tuple(in_vmem(halves)),
        scratch_shapes=[pltpu.VMEM((CORES * features, columns), bf16)],
        compiler_params=params(),
        cost_estimate=pl.CostEstimate(
            flops=2 * tokens * CORES * features * columns,
            bytes_accessed=4 * tokens * features,
            transcendentals=0,
        ),
    )(frozen_key_value, frozen_key_value, *pieces, *sibling_f, *x0, *x1, *after)

    keys_values = None
    for at, values in received.items():
        keys_values = finish(
            totals[at[1]], inv_rms, values, at, (tokens, columns), keys_values
        )
    return (a_next, b_next, keys_values)


def solution(mesh):
    placed = (
        P("dp", "tensor"),
        P("tensor"),
        P(None, "tensor"),
        P("tensor", None, None),
        P("tensor", None, None),
        P("tensor", None, None),
        P(None, "tensor"),
        P(None, "tensor"),
        P(None, "tensor"),
        P("dp", "tensor", None, None),
        P("dp", None, "tensor"),
    )
    return jax.shard_map(
        body,
        mesh=mesh,
        in_specs=placed,
        out_specs=(
            P(None, ("tensor", "dp"), None, None),
            P(None, "dp", "tensor"),
            P("dp", "tensor"),
        ),
        check_vma=False,
    )
```

```python
import functools
import math

import jax
import jax.numpy as jnp
from jax import lax
from jax.experimental import pallas as pl
from jax.experimental.pallas import tpu as pltpu
from jax.sharding import PartitionSpec as P

KEY_VALUE_WIDTH = 1024
STEP = 100
CORES = 2
LANES = 128
COLUMN_HALVES = 2
TOKEN_HALVES = 2
FACTOR_PIECES = 2
VMEM_BYTES = 16 * 2**20
LARGE_VMEM_BYTES = 58 * 2**20
PREPARE_VMEM_BYTES = 49 * 2**20


def adaptive_moment_update(param, first, second, grad_mean):
    first_new = 0.9 * first + 0.1 * grad_mean
    second_new = 0.999 * second + 0.001 * grad_mean * grad_mean
    step_size = first_new / (1.0 - 0.9**STEP) / (jnp.sqrt(second_new / (1.0 - 0.999**STEP)) + 1e-08)
    return (param - 0.1 * step_size, first_new, second_new)


def in_vmem(count):
    return [pl.BlockSpec(memory_space=pltpu.VMEM)] * count


def anywhere(count):
    return [pl.BlockSpec(memory_space=pl.ANY)] * count


SCALARS = pl.BlockSpec(memory_space=pltpu.SMEM)


def params(**more):
    return pltpu.CompilerParams(vmem_limit_bytes=VMEM_BYTES, **more)


def pack(down, up, out_ref, ready):
    shares = out_ref.shape[0]
    down = down.T
    down_rows, up_rows = down.shape[0] // shares, up.shape[0] // shares
    for i in range(shares):
        pieces = [down[i * down_rows : (i + 1) * down_rows]]
        for k in range(up.shape[1] // LANES):
            pieces.append(up[i * up_rows : (i + 1) * up_rows, k * LANES : (k + 1) * LANES])
        out_ref[i] = jnp.concatenate(pieces, axis=0).astype(jnp.bfloat16)
        ready(i)


def first_lane(share, window, size):
    return jnp.minimum(share // LANES * LANES, size - window)


def pack_kernel(down_ref, up_ref, packed, down, up, blocks, sem, sem_out):
    loads = [
        pltpu.make_async_copy(down_ref, down, sem.at[0]),
        pltpu.make_async_copy(up_ref, up, sem.at[1]),
    ]
    back = []
    for copy in loads:
        copy.start()
    for copy in loads:
        copy.wait()

    def ready(i):
        back.append(pltpu.make_async_copy(blocks.at[i], packed.at[i], sem_out.at[i]))
        back[-1].start()

    pack(down[...], up[...], blocks, ready)
    for copy in back:
        copy.wait()


def take_kernel(chips, turn, weights_ref, _, *refs):
    outs, (strips, sem, sem_out) = refs[:-3], refs[-3:]
    features = strips.shape[1]
    place, replica = lax.axis_index("tensor"), lax.axis_index("dp")
    chip, core = place // CORES, place % CORES
    loads, stores = [], []
    for i, out in enumerate(outs):
        step, first = 1 + i % (chips - 1), i // (chips - 1) * out.shape[0]
        for k in range(out.shape[0]):
            half = (core + replica // turn[first + k]) % 2
            row = ((chip + step) % chips * CORES + half) * features
            source = weights_ref.at[
                pl.ds(pl.multiple_of(row, features), features),
                pl.ds((first + k) * LANES, LANES),
            ]
            at = len(loads)
            loads.append(pltpu.make_async_copy(source, strips.at[at], sem.at[at]))
            stores.append(pltpu.make_async_copy(strips.at[at], out.at[k], sem_out.at[at]))
    for copy in loads:
        copy.start()
    for load, store in zip(loads, stores):
        load.wait()
        store.start()
    for copy in stores:
        copy.wait()


def split_kernel(in_ref, *refs):
    outs, (buffer, sem_in, sem_out) = refs[:-3], refs[-3:]
    rows = buffer.shape[1] // 2
    pieces = [(k, pl.ds(half * rows, rows)) for k in range(len(outs)) for half in range(2)]
    loads = [
        pltpu.make_async_copy(in_ref.at[k, part], buffer.at[k, part], sem_in.at[i])
        for i, (k, part) in enumerate(pieces)
    ]
    stores = [
        pltpu.make_async_copy(buffer.at[k, part], outs[k].at[part], sem_out.at[i])
        for i, (k, part) in enumerate(pieces)
    ]
    for copy in loads:
        copy.start()
    for load, store in zip(loads, stores):
        load.wait()
        store.start()
    for copy in stores:
        copy.wait()


def prepare_kernel(first, summed, own_in, sibling_in, own_gain, sibling_gain, *refs):
    own, sibling, squares, sem = refs[-4:]
    copied, features = own.shape
    refs = refs[:-4]
    before, sums_ref = [], None
    if summed:
        refs, sums_ref = refs[:-1], refs[-1]
    together = refs[-1].shape[1] > features
    outs = refs[-1:] if together else refs[-2:]
    before = refs[: -len(outs)]
    rows = outs[0].shape[0]
    block = LANES if rows % LANES == 0 else rows
    tile = 16 if block % 16 == 0 else block
    raw = ((own_in, own), (sibling_in, sibling))
    loads = [
        [
            pltpu.make_async_copy(
                source.at[pl.ds(first + k * block, block)],
                target.at[pl.ds(k * block, block)],
                sem.at[2 * k + side],
            )
            for side, (source, target) in enumerate(raw)
        ]
        for k in range(copied // block)
    ]
    for pair in loads:
        for copy in pair:
            copy.start()
    stores = []
    for k, pair in enumerate(loads):
        for copy in pair:
            copy.wait()
        scale, add = k * block < rows, k * block < summed

        @pl.loop(0, block // tile, unroll=2)
        def _(i):
            at = pl.ds(pl.multiple_of(k * block + i * tile, tile), tile)
            total = None
            for side, (ref, gain) in enumerate(((own, own_gain), (sibling, sibling_gain))):
                value = ref[at, :].astype(jnp.float32)
                if scale:
                    scaled = (value * gain[...]).astype(ref.dtype)
                    if together:
                        outs[0][at, side * features : (side + 1) * features] = scaled
                    else:
                        ref[at, :] = scaled
                if add:
                    total = value * value if total is None else total + value * value
            if add:
                total = jnp.sum(total, axis=1, keepdims=True)
                squares[at, :] = jnp.broadcast_to(total, (tile, LANES))

        if scale and not together:
            part = pl.ds(k * block, block)
            for side, (source, out) in enumerate(((own, outs[0]), (sibling, outs[1]))):
                place = sem.at[2 * (len(loads) + k) + side]
                stores.append(pltpu.make_async_copy(source.at[part], out.at[part], place))
                stores[-1].start()
    if summed:
        done = 0
        for ref in before:
            sums_ref[: ref.shape[0]] = ref[...]
            done = ref.shape[0]
        for i in range(summed // LANES):
            row = squares[i * LANES : (i + 1) * LANES, :].T[:1]
            sums_ref[done + i : done + i + 1] = row
    for copy in stores:
        copy.wait()


def message_kernel(factor_ref, sums_ref, out_ref, *refs):
    pieces, (sums, sem) = refs[:-2], refs[-2:]
    shares, up_rows = factor_ref.shape[0], out_ref.shape[1]
    sums_copy = pltpu.make_async_copy(sums_ref, sums, sem.at[1 + len(pieces)])
    sums_copy.start()
    copies = [
        pltpu.make_async_copy(
            factor_ref.at[:, pl.ds(factor_ref.shape[1] - up_rows, up_rows)],
            out_ref.at[pl.ds(0, shares)],
            sem.at[0],
        )
    ]
    for k, piece in enumerate(pieces):
        size = piece.shape[0]
        copies.append(
            pltpu.make_async_copy(factor_ref.at[pl.ds(k * size, size)], piece, sem.at[1 + k])
        )
    for copy in copies:
        copy.start()
    sums_copy.wait()
    left = sums[...]
    terms = []
    for _ in range(3):
        terms.append(left.astype(jnp.bfloat16).astype(jnp.float32))
        left = left - terms[-1]
    rest = (out_ref.shape[0] - shares) * up_rows - 3 * left.shape[0]
    if rest > 0:
        terms.append(jnp.zeros((rest, LANES), jnp.float32))
    rows = jnp.concatenate(terms, axis=0)
    for i in range(out_ref.shape[0] - shares):
        out_ref[shares + i] = rows[i * up_rows : (i + 1) * up_rows].astype(jnp.bfloat16)
    for copy in copies:
        copy.wait()


def inverse_kernel(width, shares, sums_ref, *refs):
    messages, out = refs[:-1], refs[-1]
    total = sums_ref[...]
    count = total.shape[0]
    for ref in messages:
        rows = [ref[i].astype(jnp.float32) for i in range(shares, ref.shape[0])]
        rows = jnp.concatenate(rows, axis=0)
        total += rows[:count] + rows[count : 2 * count] + rows[2 * count : 3 * count]
    inverse = lax.rsqrt(total / width + 1e-06)
    for i in range(count):
        out[i * LANES : (i + 1) * LANES, :] = jnp.broadcast_to(
            inverse[i : i + 1], (LANES, LANES)
        ).T


def update(total, down, up, a_ref, b_ref):
    down_rows = a_ref.shape[2]
    up_rows, columns = b_ref.shape[1:]
    strips = columns // LANES
    down_mean = total[:down_rows].T
    up_mean = jnp.concatenate(
        [total[down_rows + k * up_rows : down_rows + (k + 1) * up_rows] for k in range(strips)],
        axis=1,
    )
    p, m, v = adaptive_moment_update(*down(), down_mean)
    a_ref[0], a_ref[1], a_ref[2] = p, m, v
    pieces = [p.T]
    p, m, v = adaptive_moment_update(*up(), up_mean)
    b_ref[0], b_ref[1], b_ref[2] = p, m, v
    pieces += [p[:, k * LANES : (k + 1) * LANES] for k in range(strips)]
    return jnp.concatenate(pieces, axis=0).astype(jnp.bfloat16)


def adam_kernel(grad_in, *refs):
    state, refs = refs[:6], refs[6:]
    a_ref, b_ref, factor_ref, grad_ref, down_win, up_win, sem = refs
    replicas = grad_ref.shape[0]
    down_rows, window = a_ref.shape[2], down_win.shape[2]
    up_rows = up_win.shape[1]
    replica = lax.axis_index("dp")
    share = replica * down_rows
    size = down_rows * replicas
    copies = [pltpu.make_async_copy(grad_in, grad_ref, sem.at[6])]
    for i in range(3):
        down, up = state[i], state[3 + i]
        if window != down_rows:
            lane = pl.multiple_of(first_lane(share, window, size), LANES)
            down = down.at[:, pl.ds(lane, window)]
            up = up.at[pl.ds(pl.multiple_of(replica * up_rows, up_rows), up_rows)]
        copies.append(pltpu.make_async_copy(down, down_win.at[i], sem.at[i]))
        copies.append(pltpu.make_async_copy(up, up_win.at[i], sem.at[3 + i]))
    for copy in copies:
        copy.start()
    copies[0].wait()
    total = jnp.sum(grad_ref[...].astype(jnp.float32), axis=0) / replicas
    for copy in copies[1:]:
        copy.wait()

    def down():
        if window == down_rows:
            return [down_win[i] for i in range(3)]
        shift = window - (share - first_lane(share, window, size))
        return [pltpu.roll(down_win[i], shift, 1)[:, :down_rows] for i in range(3)]

    rounded = update(total, down, lambda: [up_win[i] for i in range(3)], a_ref, b_ref)
    for i in range(replicas):
        factor_ref[i] = rounded


def factor_a(refs, down_rows):
    pieces = []
    for ref in refs:
        for i in range(ref.shape[0]):
            if down_rows % 16 == 0:
                pieces.append(ref[i, :down_rows, :])
            else:
                pieces.append(ref[i].astype(jnp.float32)[:down_rows])
    return jnp.concatenate(pieces, axis=0).astype(jnp.bfloat16)


def factor_b(packed, part, parts, strip, up_rows):
    pieces = [
        packed[i].astype(jnp.float32)[strip * up_rows : (strip + 1) * up_rows]
        for i in range(packed.shape[0])
    ]
    value = jnp.concatenate(pieces, axis=0)
    rows = [jnp.where(part == j, value, jnp.zeros_like(value)) for j in range(parts)]
    return jnp.concatenate(rows, axis=0).astype(jnp.bfloat16)


def merge(scale, block, a, b):
    change = jnp.dot(a, b, preferred_element_type=jnp.float32)
    return (block.astype(jnp.float32) + scale * change).astype(jnp.bfloat16)


def multiply(groups, weights, *outs):
    wide = outs[0].shape[1]
    done = 0
    for xs in groups:
        rows = xs[0].shape[0]
        tile = rows // 2 if rows % 32 == 0 else rows

        @pl.loop(0, rows // tile)
        def _(i):
            at = pl.ds(pl.multiple_of(i * tile, tile), tile)
            to = pl.ds(pl.multiple_of(done + i * tile, 16), tile)
            value, first = None, 0
            for x in xs:
                size = x.shape[1]
                part = jnp.dot(
                    x[at, :], weights[first : first + size, :], preferred_element_type=jnp.float32
                )
                value, first = part if value is None else value + part, first + size
            for k, out in enumerate(outs):
                out[to, :] = value[:, k * wide : (k + 1) * wide].astype(out.dtype)

        done += rows


def up_factor(static, packed, owner):
    _, parts, up_rows, strips, columns = static
    part = owner * columns // KEY_VALUE_WIDTH
    return jnp.concatenate(
        [factor_b(packed, part, parts, strip, up_rows) for strip in strips], axis=1
    )


def arrange_kernel(turn, *refs):
    out = refs[-1]
    replica = lax.axis_index("dp")
    features = out.shape[0] // CORES
    for k, alternate in enumerate(turn):
        mine, other = refs[2 * k : 2 * k + 2]
        even = replica // alternate % 2 == 0
        lanes = slice(k * LANES, (k + 1) * LANES)
        out[:features, lanes] = jnp.where(even, mine[...], other[...])
        out[features:, lanes] = jnp.where(even, other[...], mine[...])


def outside_kernel(static, chips, step, blocks, b_ref, x, *refs):
    own_f, sibling_f = refs[:FACTOR_PIECES], refs[FACTOR_PIECES : 2 * FACTOR_PIECES]
    weights, product = refs[-2:]
    features = blocks.shape[0] // CORES
    down_rows = own_f[0].shape[1] - b_ref.shape[1]
    shares = FACTOR_PIECES * own_f[0].shape[0]
    place = lax.axis_index("tensor")
    owner = (place // CORES - step + chips) % chips * CORES + place % CORES
    b = up_factor(static, b_ref[:shares], owner)
    tile = 256 if features % 256 == 0 else features
    for side, factors in enumerate((own_f, sibling_f)):
        a = factor_a(factors, down_rows)
        for first in range(0, features, tile):
            rows = slice(side * features + first, side * features + first + tile)
            weights[rows, :] = merge(static[0], blocks[rows, :], a[first : first + tile], b)
    multiply([[x]], weights, product)


def more_kernel(groups, *refs):
    xs, (weights, product) = refs[:-2], refs[-2:]
    size = len(xs) // groups
    multiply([xs[k * size : (k + 1) * size] for k in range(groups)], weights, product)


def own_kernel(static, own_block, sibling_block, *refs):
    own_f, sibling_f = refs[:FACTOR_PIECES], refs[FACTOR_PIECES : 2 * FACTOR_PIECES]
    refs = refs[2 * FACTOR_PIECES :]
    groups, weights = [refs[:1]], refs[-1]
    for k in range(static[6]):
        groups.append(refs[1 + 2 * k : 3 + 2 * k])
    outs = refs[len(refs) - 1 - static[5] : -1]
    features = own_block.shape[0]
    wide = outs[0].shape[1]
    down_rows = own_f[0].shape[1] - len(static[3]) * static[2]
    b = jnp.concatenate([piece[:, down_rows:] for piece in own_f], axis=0)
    b = up_factor(static[:5], b, lax.axis_index("tensor"))
    for at, factors, block in ((0, own_f, own_block), (features, sibling_f, sibling_block)):
        weights[at : at + features] = merge(static[0], block[...], factor_a(factors, down_rows), b)
    multiply(groups, weights, *outs)


def finish_kernel(sources, first, own, inv, *refs):
    rows = pl.ds(first, refs[-1].shape[0])
    total = own[rows, :]
    for value in refs[:sources]:
        total = total + value[...].astype(jnp.float32)
    refs[-1][...] = (total * inv[rows, :1]).astype(refs[-1].dtype)


def finish(own, inv_rms, received, at, shape, before):
    block = received[0].shape
    operands = [own, inv_rms] + received
    in_specs = in_vmem(len(operands))
    aliases = {}
    if before is not None:
        aliases = {len(operands): 0}
        in_specs += anywhere(1)
        operands.append(before)
    return pl.pallas_call(
        functools.partial(finish_kernel, len(received), at[0] * block[0]),
        grid=(1,),
        out_shape=jax.ShapeDtypeStruct(shape, jnp.bfloat16),
        in_specs=in_specs,
        out_specs=pl.BlockSpec(block, lambda i: at),
        input_output_aliases=aliases,
        compiler_params=params(),
    )(*operands)


def body(
    prompt_hidden_input,
    input_norm_gain,
    frozen_key_value,
    down_factor_matrix,
    down_moment_first,
    down_moment_second,
    up_factor_matrix,
    up_moment_first,
    up_moment_second,
    down_gradient,
    up_gradient,
):
    n_dp = lax.axis_size("dp")
    n_tensor = lax.axis_size("tensor")
    chips = n_tensor // CORES
    replica = lax.axis_index("dp")
    tokens, features = prompt_hidden_input.shape
    width, columns = frozen_key_value.shape
    rank = up_factor_matrix.shape[0]
    parts = down_factor_matrix.shape[1]
    factors = parts * rank
    strips = columns // LANES
    down_rows = features // n_dp
    up_rows = rank // n_dp
    packed_rows = down_rows + up_rows * strips
    steps = range(1, chips)
    f32, bf16 = jnp.float32, jnp.bfloat16

    def to_sibling(value):
        return lax.ppermute(value, "tensor", [(t, t ^ 1) for t in range(n_tensor)])

    def to_chip(value, step):
        pairs = [
            (CORES * q + k, CORES * ((q + step) % chips) + k)
            for q in range(chips)
            for k in range(CORES)
        ]
        return lax.ppermute(value, "tensor", pairs)

    def by_rank(value):
        return jnp.transpose(value, (1, 2, 0)).reshape(factors, features)

    down_sent = by_rank(down_gradient[0])
    down_state = [by_rank(v) for v in (down_factor_matrix, down_moment_first, down_moment_second)]
    up_state = [up_factor_matrix, up_moment_first, up_moment_second]
    shares = jax.ShapeDtypeStruct((n_dp, packed_rows, LANES), bf16)
    window = pl.cdiv(down_rows + LANES, LANES) * LANES
    aligned = features % LANES == 0 and window <= features
    aligned = aligned and up_rows % 8 == 0 and down_rows % 16 == 0
    window = window if aligned else down_rows
    turns = [1, 2] if n_dp % 4 == 0 else [1, 1]
    turn = [turns[strip % 2] for strip in range(strips)]
    halves = min(COLUMN_HALVES, strips)
    wide = columns // halves
    groups = [range(k * strips // halves, (k + 1) * strips // halves) for k in range(halves)]
    packed = pl.pallas_call(
        pack_kernel,
        out_shape=shares,
        in_specs=anywhere(2),
        out_specs=anywhere(1)[0],
        scratch_shapes=[
            pltpu.VMEM((factors, features), f32),
            pltpu.VMEM((rank, columns), f32),
            pltpu.VMEM(shares.shape, bf16),
            pltpu.SemaphoreType.DMA((2,)),
            pltpu.SemaphoreType.DMA((n_dp,)),
        ],
        compiler_params=pltpu.CompilerParams(vmem_limit_bytes=LARGE_VMEM_BYTES),
    )(down_sent, up_gradient[0])
    out_shape = tuple(
        jax.ShapeDtypeStruct((len(group), features, LANES), bf16)
        for group in groups
        for _ in steps
    )
    taken = pl.pallas_call(
        functools.partial(take_kernel, chips, turn),
        out_shape=out_shape,
        in_specs=anywhere(2),
        out_specs=tuple(anywhere(len(out_shape))),
        scratch_shapes=[
            pltpu.VMEM((len(steps) * strips, features, LANES), bf16),
            pltpu.SemaphoreType.DMA((len(steps) * strips,)),
            pltpu.SemaphoreType.DMA((len(steps) * strips,)),
        ],
        compiler_params=pltpu.CompilerParams(vmem_limit_bytes=LARGE_VMEM_BYTES),
    )(frozen_key_value, packed)
    exchanged = lax.all_to_all(packed, "dp", 0, 0, tiled=True)
    if not aligned:
        down_state = [
            lax.dynamic_slice_in_dim(v, replica * down_rows, down_rows, 1) for v in down_state
        ]
        up_state = [lax.dynamic_slice_in_dim(v, replica * up_rows, up_rows, 0) for v in up_state]
    mine = []

    def send_half(half, after):
        blocks = taken[half * len(steps) : (half + 1) * len(steps)]
        if after is not None:
            blocks, _ = lax.optimization_barrier((blocks, after))
        mine.append([to_chip(value, step) for value, step in zip(blocks, steps)])

    send_half(0, None)

    gain = input_norm_gain[None, :]
    some = tokens // TOKEN_HALVES
    operands = [prompt_hidden_input, to_sibling(prompt_hidden_input), gain, to_sibling(gain)]

    def prepared(first, size, summed, before, in_place, limit):
        if in_place:
            x_shape = (jax.ShapeDtypeStruct((size, CORES * features), bf16),)
            x_specs = tuple(in_vmem(1))
        else:
            x_shape = (jax.ShapeDtypeStruct((size, features), bf16),) * 2
            x_specs = tuple(anywhere(2))
        copied = max(size, summed)
        if summed:
            x_shape += (jax.ShapeDtypeStruct(((first + summed) // LANES, LANES), f32),)
            x_specs += tuple(in_vmem(1))
        outs = pl.pallas_call(
            functools.partial(prepare_kernel, first, summed),
            out_shape=x_shape,
            in_specs=anywhere(2) + in_vmem(2 + len(before)),
            out_specs=x_specs,
            scratch_shapes=[
                pltpu.VMEM((copied, features), bf16),
                pltpu.VMEM((copied, features), bf16),
                pltpu.VMEM((copied, LANES), f32),
                pltpu.SemaphoreType.DMA((4 * pl.cdiv(copied, LANES),)),
            ],
            compiler_params=pltpu.CompilerParams(vmem_limit_bytes=limit),
        )(*operands, *before)
        return (list(outs[:-1]), outs[-1]) if summed else (list(outs), None)

    x0, squares = prepared(0, some, tokens, [], True, PREPARE_VMEM_BYTES)
    exchanged, squares = lax.optimization_barrier((exchanged, squares))
    x1, _ = prepared(some, some, 0, [squares], False, LARGE_VMEM_BYTES)
    a_next, b_next, sent = pl.pallas_call(
        adam_kernel,
        out_shape=(
            jax.ShapeDtypeStruct((3, factors, down_rows), f32),
            jax.ShapeDtypeStruct((3, up_rows, columns), f32),
            shares,
        ),
        in_specs=anywhere(7),
        out_specs=tuple(in_vmem(3)),
        scratch_shapes=[
            pltpu.VMEM((n_dp, packed_rows, LANES), bf16),
            pltpu.VMEM((3, factors, window), f32),
            pltpu.VMEM((3, up_rows, columns), f32),
            pltpu.SemaphoreType.DMA((7,)),
        ],
        compiler_params=pltpu.CompilerParams(vmem_limit_bytes=LARGE_VMEM_BYTES),
    )(exchanged, *down_state, *up_state)
    own_f = lax.all_to_all(sent, "dp", 0, 0, tiled=True)
    for half in range(1, halves):
        send_half(half, (mine[-1], sent))
    a_next = jnp.transpose(a_next.reshape(3, parts, rank, down_rows), (0, 3, 1, 2))

    outside = [[] for _ in range(strips)]

    def swap_half(half, after):
        for value in mine[half]:
            value, _ = lax.optimization_barrier((value, after))
            split = pl.pallas_call(
                split_kernel,
                out_shape=(jax.ShapeDtypeStruct((features, LANES), bf16),) * len(groups[half]),
                in_specs=anywhere(1),
                out_specs=tuple(anywhere(len(groups[half]))),
                scratch_shapes=[
                    pltpu.VMEM(value.shape, bf16),
                    pltpu.SemaphoreType.DMA((2 * len(groups[half]),)),
                    pltpu.SemaphoreType.DMA((2 * len(groups[half]),)),
                ],
                compiler_params=params(),
            )(value)
            for piece, strip in zip(split, groups[half]):
                pairs = [(i, i ^ turn[strip]) for i in range(n_dp)]
                outside[strip].append((piece, lax.ppermute(piece, "dp", pairs)))

    swap_half(0, sent)
    own_f, x1 = lax.optimization_barrier((own_f, x1))
    up_packed = packed_rows - down_rows
    more = pl.cdiv(3 * (tokens // LANES), up_packed)
    piece = jax.ShapeDtypeStruct((n_dp // FACTOR_PIECES, packed_rows, LANES), bf16)
    message, *pieces = pl.pallas_call(
        message_kernel,
        out_shape=(jax.ShapeDtypeStruct((n_dp + more, up_packed, LANES), bf16),)
        + (piece,) * FACTOR_PIECES,
        in_specs=anywhere(2),
        out_specs=tuple(in_vmem(1 + FACTOR_PIECES)),
        scratch_shapes=[
            pltpu.VMEM(squares.shape, f32),
            pltpu.SemaphoreType.DMA((2 + FACTOR_PIECES,)),
        ],
        compiler_params=params(),
    )(own_f, squares)
    messages = [to_chip(message, step) for step in steps]
    sibling_f = [to_sibling(piece) for piece in pieces]

    inv_rms = pl.pallas_call(
        functools.partial(inverse_kernel, width, n_dp),
        out_shape=jax.ShapeDtypeStruct((tokens, LANES), f32),
        in_specs=in_vmem(chips),
        out_specs=in_vmem(1)[0],
        compiler_params=params(),
    )(squares, *messages)

    scale = 0.5 / math.sqrt(width * rank)

    received = {}
    after = []
    weights_shape = jax.ShapeDtypeStruct((CORES * features, wide), bf16)
    product_shape = jax.ShapeDtypeStruct((some, wide), bf16)
    for half, group in enumerate(groups):
        static = (scale, parts, up_rows, group, columns)
        if half > 0:
            swap_half(half, products[0])
        for step in steps:
            blocks = [value for strip in group for value in outside[strip][step - 1]]
            arranged = pl.pallas_call(
                functools.partial(arrange_kernel, [turn[strip] for strip in group]),
                out_shape=weights_shape,
                in_specs=in_vmem(len(blocks)) + anywhere(len(after)),
                out_specs=in_vmem(1)[0],
                compiler_params=params(),
            )(*blocks, *after)
            weights, product = pl.pallas_call(
                functools.partial(outside_kernel, static, chips, step),
                out_shape=(weights_shape, product_shape),
                in_specs=in_vmem(3 + 2 * FACTOR_PIECES),
                out_specs=tuple(in_vmem(2)),
                compiler_params=params(),
            )(arranged, messages[step - 1], *x0, *pieces, *sibling_f)
            received.setdefault((0, half), []).append(to_chip(product, chips - step))
            second = pl.pallas_call(
                functools.partial(more_kernel, len(x1) // 2),
                out_shape=product_shape,
                in_specs=in_vmem(1 + len(x1)),
                out_specs=in_vmem(1)[0],
                compiler_params=params(),
            )(*x1, weights)
            products = [product, second]
            after = [second]
            received.setdefault((1, half), []).append(to_chip(second, chips - step))
        if half == 0:
            after = [received[0, 0][0]]

    after.append(received[1, 0][0])
    static = (scale, parts, up_rows, range(strips), columns, halves, len(x1) // 2)
    totals = pl.pallas_call(
        functools.partial(own_kernel, static),
        out_shape=(jax.ShapeDtypeStruct((tokens, wide), f32),) * halves,
        grid=(1,),
        in_specs=[
            pl.BlockSpec((features, columns), lambda i: (lax.axis_index("tensor"), 0)),
            pl.BlockSpec((features, columns), lambda i: (lax.axis_index("tensor") ^ 1, 0)),
        ]
        + in_vmem(2 * FACTOR_PIECES + 1 + len(x1))
        + anywhere(len(after)),
        out_specs=tuple(in_vmem(halves)),
        scratch_shapes=[pltpu.VMEM((CORES * features, columns), bf16)],
        compiler_params=params(),
        cost_estimate=pl.CostEstimate(
            flops=2 * tokens * CORES * features * columns,
            bytes_accessed=4 * tokens * features,
            transcendentals=0,
        ),
    )(frozen_key_value, frozen_key_value, *pieces, *sibling_f, *x0, *x1, *after)

    keys_values = None
    for at, values in received.items():
        keys_values = finish(
            totals[at[1]], inv_rms, values, at, (tokens, columns), keys_values
        )
    return (a_next, b_next, keys_values)


def solution(mesh):
    placed = (
        P("dp", "tensor"),
        P("tensor"),
        P(None, "tensor"),
        P("tensor", None, None),
        P("tensor", None, None),
        P("tensor", None, None),
        P(None, "tensor"),
        P(None, "tensor"),
        P(None, "tensor"),
        P("dp", "tensor", None, None),
        P("dp", None, "tensor"),
    )
    return jax.shard_map(
        body,
        mesh=mesh,
        in_specs=placed,
        out_specs=(
            P(None, ("tensor", "dp"), None, None),
            P(None, "dp", "tensor"),
            P("dp", "tensor"),
        ),
        check_vma=False,
    )
```

```python
import functools
import math

import jax
import jax.numpy as jnp
from jax import lax
from jax.experimental import pallas as pl
from jax.experimental.pallas import tpu as pltpu
from jax.sharding import PartitionSpec as P

KEY_VALUE_WIDTH = 1024
STEP = 100
CORES = 2
LANES = 128
COLUMN_HALVES = 2
TOKEN_HALVES = 2
FACTOR_PIECES = 2
VMEM_BYTES = 16 * 2**20
LARGE_VMEM_BYTES = 58 * 2**20
PREPARE_VMEM_BYTES = 49 * 2**20


def adaptive_moment_update(param, first, second, grad_mean):
    first_new = 0.9 * first + 0.1 * grad_mean
    second_new = 0.999 * second + 0.001 * grad_mean * grad_mean
    step_size = first_new / (1.0 - 0.9**STEP) / (jnp.sqrt(second_new / (1.0 - 0.999**STEP)) + 1e-08)
    return (param - 0.1 * step_size, first_new, second_new)


def in_vmem(count):
    return [pl.BlockSpec(memory_space=pltpu.VMEM)] * count


def anywhere(count):
    return [pl.BlockSpec(memory_space=pl.ANY)] * count


SCALARS = pl.BlockSpec(memory_space=pltpu.SMEM)


def params(**more):
    return pltpu.CompilerParams(vmem_limit_bytes=VMEM_BYTES, **more)


def pack(down, up, out_ref, ready):
    shares = out_ref.shape[0]
    down = down.T
    down_rows, up_rows = down.shape[0] // shares, up.shape[0] // shares
    for i in range(shares):
        pieces = [down[i * down_rows : (i + 1) * down_rows]]
        for k in range(up.shape[1] // LANES):
            pieces.append(up[i * up_rows : (i + 1) * up_rows, k * LANES : (k + 1) * LANES])
        out_ref[i] = jnp.concatenate(pieces, axis=0).astype(jnp.bfloat16)
        ready(i)


def first_lane(share, window, size):
    return jnp.minimum(share // LANES * LANES, size - window)


def begin_kernel(chips, turn, down_ref, up_ref, weights_ref, packed, *refs):
    outs, (down, up, blocks, strips, sem, sem_out) = refs[:-6], refs[-6:]
    features = strips.shape[1]
    place, replica = lax.axis_index("tensor"), lax.axis_index("dp")
    chip, core = place // CORES, place % CORES
    copies, back = [], []

    def add(source, target):
        copies.append(pltpu.make_async_copy(source, target, sem.at[len(copies)]))
        copies[-1].start()

    def add_back(source, target):
        back.append(pltpu.make_async_copy(source, target, sem_out.at[len(back)]))
        back[-1].start()

    add(down_ref, down)
    add(up_ref, up)
    targets = []
    for i, out in enumerate(outs):
        step, first = 1 + i % (chips - 1), i // (chips - 1) * out.shape[0]
        for k in range(out.shape[0]):
            half = (core + replica // turn[first + k]) % 2
            row = ((chip + step) % chips * CORES + half) * features
            add(
                weights_ref.at[
                    pl.ds(pl.multiple_of(row, features), features),
                    pl.ds((first + k) * LANES, LANES),
                ],
                strips.at[len(targets)],
            )
            targets.append(out.at[k])
    copies[0].wait()
    copies[1].wait()

    def ready(i):
        add_back(blocks.at[i], packed.at[i])
        if i == min(1, blocks.shape[0] - 1):
            for k, target in enumerate(targets):
                copies[2 + k].wait()
                add_back(strips.at[k], target)

    pack(down[...], up[...], blocks, ready)
    for copy in back:
        copy.wait()


def split_kernel(in_ref, *refs):
    outs, (buffer, sem_in, sem_out) = refs[:-3], refs[-3:]
    rows = buffer.shape[1] // 2
    pieces = [(k, pl.ds(half * rows, rows)) for k in range(len(outs)) for half in range(2)]
    loads = [
        pltpu.make_async_copy(in_ref.at[k, part], buffer.at[k, part], sem_in.at[i])
        for i, (k, part) in enumerate(pieces)
    ]
    stores = [
        pltpu.make_async_copy(buffer.at[k, part], outs[k].at[part], sem_out.at[i])
        for i, (k, part) in enumerate(pieces)
    ]
    for copy in loads:
        copy.start()
    for load, store in zip(loads, stores):
        load.wait()
        store.start()
    for copy in stores:
        copy.wait()


def prepare_kernel(first, summed, own_in, sibling_in, own_gain, sibling_gain, *refs):
    own, sibling, squares, sem = refs[-4:]
    copied, features = own.shape
    refs = refs[:-4]
    before, sums_ref = [], None
    if summed:
        refs, sums_ref = refs[:-1], refs[-1]
    together = refs[-1].shape[1] > features
    outs = refs[-1:] if together else refs[-2:]
    before = refs[: -len(outs)]
    rows = outs[0].shape[0]
    block = LANES if rows % LANES == 0 else rows
    tile = 16 if block % 16 == 0 else block
    raw = ((own_in, own), (sibling_in, sibling))
    loads = [
        [
            pltpu.make_async_copy(
                source.at[pl.ds(first + k * block, block)],
                target.at[pl.ds(k * block, block)],
                sem.at[2 * k + side],
            )
            for side, (source, target) in enumerate(raw)
        ]
        for k in range(copied // block)
    ]
    for pair in loads:
        for copy in pair:
            copy.start()
    stores = []
    for k, pair in enumerate(loads):
        for copy in pair:
            copy.wait()
        scale, add = k * block < rows, k * block < summed

        @pl.loop(0, block // tile, unroll=2)
        def _(i):
            at = pl.ds(pl.multiple_of(k * block + i * tile, tile), tile)
            total = None
            for side, (ref, gain) in enumerate(((own, own_gain), (sibling, sibling_gain))):
                value = ref[at, :].astype(jnp.float32)
                if scale:
                    scaled = (value * gain[...]).astype(ref.dtype)
                    if together:
                        outs[0][at, side * features : (side + 1) * features] = scaled
                    else:
                        ref[at, :] = scaled
                if add:
                    total = value * value if total is None else total + value * value
            if add:
                total = jnp.sum(total, axis=1, keepdims=True)
                squares[at, :] = jnp.broadcast_to(total, (tile, LANES))

        if scale and not together:
            part = pl.ds(k * block, block)
            for side, (source, out) in enumerate(((own, outs[0]), (sibling, outs[1]))):
                place = sem.at[2 * (len(loads) + k) + side]
                stores.append(pltpu.make_async_copy(source.at[part], out.at[part], place))
                stores[-1].start()
    if summed:
        done = 0
        for ref in before:
            sums_ref[: ref.shape[0]] = ref[...]
            done = ref.shape[0]
        for i in range(summed // LANES):
            row = squares[i * LANES : (i + 1) * LANES, :].T[:1]
            sums_ref[done + i : done + i + 1] = row
    for copy in stores:
        copy.wait()


def message_kernel(factor_ref, sums_ref, out_ref, *refs):
    pieces, (sums, sem) = refs[:-2], refs[-2:]
    shares, up_rows = factor_ref.shape[0], out_ref.shape[1]
    sums_copy = pltpu.make_async_copy(sums_ref, sums, sem.at[1 + len(pieces)])
    sums_copy.start()
    copies = [
        pltpu.make_async_copy(
            factor_ref.at[:, pl.ds(factor_ref.shape[1] - up_rows, up_rows)],
            out_ref.at[pl.ds(0, shares)],
            sem.at[0],
        )
    ]
    for k, piece in enumerate(pieces):
        size = piece.shape[0]
        copies.append(
            pltpu.make_async_copy(factor_ref.at[pl.ds(k * size, size)], piece, sem.at[1 + k])
        )
    for copy in copies:
        copy.start()
    sums_copy.wait()
    left = sums[...]
    terms = []
    for _ in range(3):
        terms.append(left.astype(jnp.bfloat16).astype(jnp.float32))
        left = left - terms[-1]
    rest = (out_ref.shape[0] - shares) * up_rows - 3 * left.shape[0]
    if rest > 0:
        terms.append(jnp.zeros((rest, LANES), jnp.float32))
    rows = jnp.concatenate(terms, axis=0)
    for i in range(out_ref.shape[0] - shares):
        out_ref[shares + i] = rows[i * up_rows : (i + 1) * up_rows].astype(jnp.bfloat16)
    for copy in copies:
        copy.wait()


def inverse_kernel(width, shares, sums_ref, *refs):
    messages, out = refs[:-1], refs[-1]
    total = sums_ref[...]
    count = total.shape[0]
    for ref in messages:
        rows = [ref[i].astype(jnp.float32) for i in range(shares, ref.shape[0])]
        rows = jnp.concatenate(rows, axis=0)
        total += rows[:count] + rows[count : 2 * count] + rows[2 * count : 3 * count]
    inverse = lax.rsqrt(total / width + 1e-06)
    for i in range(count):
        out[i * LANES : (i + 1) * LANES, :] = jnp.broadcast_to(
            inverse[i : i + 1], (LANES, LANES)
        ).T


def update(total, down, up, a_ref, b_ref):
    down_rows = a_ref.shape[2]
    up_rows, columns = b_ref.shape[1:]
    strips = columns // LANES
    down_mean = total[:down_rows].T
    up_mean = jnp.concatenate(
        [total[down_rows + k * up_rows : down_rows + (k + 1) * up_rows] for k in range(strips)],
        axis=1,
    )
    p, m, v = adaptive_moment_update(*down(), down_mean)
    a_ref[0], a_ref[1], a_ref[2] = p, m, v
    pieces = [p.T]
    p, m, v = adaptive_moment_update(*up(), up_mean)
    b_ref[0], b_ref[1], b_ref[2] = p, m, v
    pieces += [p[:, k * LANES : (k + 1) * LANES] for k in range(strips)]
    return jnp.concatenate(pieces, axis=0).astype(jnp.bfloat16)


def adam_kernel(grad_in, *refs):
    state, refs = refs[:6], refs[6:]
    a_ref, b_ref, factor_ref, grad_ref, down_win, up_win, sem = refs
    replicas = grad_ref.shape[0]
    down_rows, window = a_ref.shape[2], down_win.shape[2]
    up_rows = up_win.shape[1]
    replica = lax.axis_index("dp")
    share = replica * down_rows
    size = down_rows * replicas
    copies = [pltpu.make_async_copy(grad_in, grad_ref, sem.at[6])]
    for i in range(3):
        down, up = state[i], state[3 + i]
        if window != down_rows:
            lane = pl.multiple_of(first_lane(share, window, size), LANES)
            down = down.at[:, pl.ds(lane, window)]
            up = up.at[pl.ds(pl.multiple_of(replica * up_rows, up_rows), up_rows)]
        copies.append(pltpu.make_async_copy(down, down_win.at[i], sem.at[i]))
        copies.append(pltpu.make_async_copy(up, up_win.at[i], sem.at[3 + i]))
    for copy in copies:
        copy.start()
    copies[0].wait()
    total = jnp.sum(grad_ref[...].astype(jnp.float32), axis=0) / replicas
    for copy in copies[1:]:
        copy.wait()

    def down():
        if window == down_rows:
            return [down_win[i] for i in range(3)]
        shift = window - (share - first_lane(share, window, size))
        return [pltpu.roll(down_win[i], shift, 1)[:, :down_rows] for i in range(3)]

    rounded = update(total, down, lambda: [up_win[i] for i in range(3)], a_ref, b_ref)
    for i in range(replicas):
        factor_ref[i] = rounded


def factor_a(refs, down_rows):
    pieces = []
    for ref in refs:
        for i in range(ref.shape[0]):
            if down_rows % 16 == 0:
                pieces.append(ref[i, :down_rows, :])
            else:
                pieces.append(ref[i].astype(jnp.float32)[:down_rows])
    return jnp.concatenate(pieces, axis=0).astype(jnp.bfloat16)


def factor_b(packed, part, parts, strip, up_rows):
    pieces = [
        packed[i].astype(jnp.float32)[strip * up_rows : (strip + 1) * up_rows]
        for i in range(packed.shape[0])
    ]
    value = jnp.concatenate(pieces, axis=0)
    rows = [jnp.where(part == j, value, jnp.zeros_like(value)) for j in range(parts)]
    return jnp.concatenate(rows, axis=0).astype(jnp.bfloat16)


def merge(scale, block, a, b):
    change = jnp.dot(a, b, preferred_element_type=jnp.float32)
    return (block.astype(jnp.float32) + scale * change).astype(jnp.bfloat16)


def multiply(groups, weights, *outs):
    wide = outs[0].shape[1]
    done = 0
    for xs in groups:
        rows = xs[0].shape[0]
        tile = rows // 2 if rows % 32 == 0 else rows

        @pl.loop(0, rows // tile)
        def _(i):
            at = pl.ds(pl.multiple_of(i * tile, tile), tile)
            to = pl.ds(pl.multiple_of(done + i * tile, 16), tile)
            value, first = None, 0
            for x in xs:
                size = x.shape[1]
                part = jnp.dot(
                    x[at, :], weights[first : first + size, :], preferred_element_type=jnp.float32
                )
                value, first = part if value is None else value + part, first + size
            for k, out in enumerate(outs):
                out[to, :] = value[:, k * wide : (k + 1) * wide].astype(out.dtype)

        done += rows


def up_factor(static, packed, owner):
    _, parts, up_rows, strips, columns = static
    part = owner * columns // KEY_VALUE_WIDTH
    return jnp.concatenate(
        [factor_b(packed, part, parts, strip, up_rows) for strip in strips], axis=1
    )


def arrange_kernel(turn, *refs):
    out = refs[-1]
    replica = lax.axis_index("dp")
    features = out.shape[0] // CORES
    for k, alternate in enumerate(turn):
        mine, other = refs[2 * k : 2 * k + 2]
        even = replica // alternate % 2 == 0
        lanes = slice(k * LANES, (k + 1) * LANES)
        out[:features, lanes] = jnp.where(even, mine[...], other[...])
        out[features:, lanes] = jnp.where(even, other[...], mine[...])


def outside_kernel(static, chips, step, blocks, b_ref, x, *refs):
    own_f, sibling_f = refs[:FACTOR_PIECES], refs[FACTOR_PIECES : 2 * FACTOR_PIECES]
    weights, product = refs[-2:]
    features = blocks.shape[0] // CORES
    down_rows = own_f[0].shape[1] - b_ref.shape[1]
    shares = FACTOR_PIECES * own_f[0].shape[0]
    place = lax.axis_index("tensor")
    owner = (place // CORES - step + chips) % chips * CORES + place % CORES
    b = up_factor(static, b_ref[:shares], owner)
    tile = 256 if features % 256 == 0 else features
    for side, factors in enumerate((own_f, sibling_f)):
        a = factor_a(factors, down_rows)
        for first in range(0, features, tile):
            rows = slice(side * features + first, side * features + first + tile)
            weights[rows, :] = merge(static[0], blocks[rows, :], a[first : first + tile], b)
    multiply([[x]], weights, product)


def more_kernel(groups, *refs):
    xs, (weights, product) = refs[:-2], refs[-2:]
    size = len(xs) // groups
    multiply([xs[k * size : (k + 1) * size] for k in range(groups)], weights, product)


def own_kernel(static, own_block, sibling_block, *refs):
    own_f, sibling_f = refs[:FACTOR_PIECES], refs[FACTOR_PIECES : 2 * FACTOR_PIECES]
    refs = refs[2 * FACTOR_PIECES :]
    groups, weights = [refs[:1]], refs[-1]
    for k in range(static[6]):
        groups.append(refs[1 + 2 * k : 3 + 2 * k])
    outs = refs[len(refs) - 1 - static[5] : -1]
    features = own_block.shape[0]
    wide = outs[0].shape[1]
    down_rows = own_f[0].shape[1] - len(static[3]) * static[2]
    b = jnp.concatenate([piece[:, down_rows:] for piece in own_f], axis=0)
    b = up_factor(static[:5], b, lax.axis_index("tensor"))
    for at, factors, block in ((0, own_f, own_block), (features, sibling_f, sibling_block)):
        weights[at : at + features] = merge(static[0], block[...], factor_a(factors, down_rows), b)
    multiply(groups, weights, *outs)


def finish_kernel(sources, first, own, inv, *refs):
    rows = pl.ds(first, refs[-1].shape[0])
    total = own[rows, :]
    for value in refs[:sources]:
        total = total + value[...].astype(jnp.float32)
    refs[-1][...] = (total * inv[rows, :1]).astype(refs[-1].dtype)


def finish(own, inv_rms, received, at, shape, before):
    block = received[0].shape
    operands = [own, inv_rms] + received
    in_specs = in_vmem(len(operands))
    aliases = {}
    if before is not None:
        aliases = {len(operands): 0}
        in_specs += anywhere(1)
        operands.append(before)
    return pl.pallas_call(
        functools.partial(finish_kernel, len(received), at[0] * block[0]),
        grid=(1,),
        out_shape=jax.ShapeDtypeStruct(shape, jnp.bfloat16),
        in_specs=in_specs,
        out_specs=pl.BlockSpec(block, lambda i: at),
        input_output_aliases=aliases,
        compiler_params=params(),
    )(*operands)


def body(
    prompt_hidden_input,
    input_norm_gain,
    frozen_key_value,
    down_factor_matrix,
    down_moment_first,
    down_moment_second,
    up_factor_matrix,
    up_moment_first,
    up_moment_second,
    down_gradient,
    up_gradient,
):
    n_dp = lax.axis_size("dp")
    n_tensor = lax.axis_size("tensor")
    chips = n_tensor // CORES
    replica = lax.axis_index("dp")
    tokens, features = prompt_hidden_input.shape
    width, columns = frozen_key_value.shape
    rank = up_factor_matrix.shape[0]
    parts = down_factor_matrix.shape[1]
    factors = parts * rank
    strips = columns // LANES
    down_rows = features // n_dp
    up_rows = rank // n_dp
    packed_rows = down_rows + up_rows * strips
    steps = range(1, chips)
    f32, bf16 = jnp.float32, jnp.bfloat16

    def to_sibling(value):
        return lax.ppermute(value, "tensor", [(t, t ^ 1) for t in range(n_tensor)])

    def to_chip(value, step):
        pairs = [
            (CORES * q + k, CORES * ((q + step) % chips) + k)
            for q in range(chips)
            for k in range(CORES)
        ]
        return lax.ppermute(value, "tensor", pairs)

    def by_rank(value):
        return jnp.transpose(value, (1, 2, 0)).reshape(factors, features)

    down_sent = by_rank(down_gradient[0])
    down_state = [by_rank(v) for v in (down_factor_matrix, down_moment_first, down_moment_second)]
    up_state = [up_factor_matrix, up_moment_first, up_moment_second]
    shares = jax.ShapeDtypeStruct((n_dp, packed_rows, LANES), bf16)
    window = pl.cdiv(down_rows + LANES, LANES) * LANES
    aligned = features % LANES == 0 and window <= features
    aligned = aligned and up_rows % 8 == 0 and down_rows % 16 == 0
    window = window if aligned else down_rows
    turns = [2, 1] if n_dp % 4 == 0 else [1, 1]
    turn = [turns[strip % 2] for strip in range(strips)]
    halves = min(COLUMN_HALVES, strips)
    wide = columns // halves
    groups = [range(k * strips // halves, (k + 1) * strips // halves) for k in range(halves)]
    out_shape = (shares,) + tuple(
        jax.ShapeDtypeStruct((len(group), features, LANES), bf16)
        for group in groups
        for _ in steps
    )
    packed, *taken = pl.pallas_call(
        functools.partial(begin_kernel, chips, turn),
        out_shape=out_shape,
        in_specs=anywhere(3),
        out_specs=tuple(anywhere(len(out_shape))),
        scratch_shapes=[
            pltpu.VMEM((factors, features), f32),
            pltpu.VMEM((rank, columns), f32),
            pltpu.VMEM(shares.shape, bf16),
            pltpu.VMEM((len(steps) * strips, features, LANES), bf16),
            pltpu.SemaphoreType.DMA((2 + len(steps) * strips,)),
            pltpu.SemaphoreType.DMA((n_dp + len(steps) * strips,)),
        ],
        compiler_params=pltpu.CompilerParams(vmem_limit_bytes=LARGE_VMEM_BYTES),
    )(down_sent, up_gradient[0], frozen_key_value)
    exchanged = lax.all_to_all(packed, "dp", 0, 0, tiled=True)
    if not aligned:
        down_state = [
            lax.dynamic_slice_in_dim(v, replica * down_rows, down_rows, 1) for v in down_state
        ]
        up_state = [lax.dynamic_slice_in_dim(v, replica * up_rows, up_rows, 0) for v in up_state]
    mine = []

    def send_half(half, after):
        blocks = taken[half * len(steps) : (half + 1) * len(steps)]
        if after is not None:
            blocks, _ = lax.optimization_barrier((blocks, after))
        mine.append([to_chip(value, step) for value, step in zip(blocks, steps)])

    send_half(0, None)

    gain = input_norm_gain[None, :]
    some = tokens // TOKEN_HALVES
    operands = [prompt_hidden_input, to_sibling(prompt_hidden_input), gain, to_sibling(gain)]

    def prepared(first, size, summed, before, in_place, limit):
        if in_place:
            x_shape = (jax.ShapeDtypeStruct((size, CORES * features), bf16),)
            x_specs = tuple(in_vmem(1))
        else:
            x_shape = (jax.ShapeDtypeStruct((size, features), bf16),) * 2
            x_specs = tuple(anywhere(2))
        copied = max(size, summed)
        if summed:
            x_shape += (jax.ShapeDtypeStruct(((first + summed) // LANES, LANES), f32),)
            x_specs += tuple(in_vmem(1))
        outs = pl.pallas_call(
            functools.partial(prepare_kernel, first, summed),
            out_shape=x_shape,
            in_specs=anywhere(2) + in_vmem(2 + len(before)),
            out_specs=x_specs,
            scratch_shapes=[
                pltpu.VMEM((copied, features), bf16),
                pltpu.VMEM((copied, features), bf16),
                pltpu.VMEM((copied, LANES), f32),
                pltpu.SemaphoreType.DMA((4 * pl.cdiv(copied, LANES),)),
            ],
            compiler_params=pltpu.CompilerParams(vmem_limit_bytes=limit),
        )(*operands, *before)
        return (list(outs[:-1]), outs[-1]) if summed else (list(outs), None)

    x0, squares = prepared(0, some, tokens, [], True, PREPARE_VMEM_BYTES)
    exchanged, squares = lax.optimization_barrier((exchanged, squares))
    x1, _ = prepared(some, some, 0, [squares], False, LARGE_VMEM_BYTES)
    a_next, b_next, sent = pl.pallas_call(
        adam_kernel,
        out_shape=(
            jax.ShapeDtypeStruct((3, factors, down_rows), f32),
            jax.ShapeDtypeStruct((3, up_rows, columns), f32),
            shares,
        ),
        in_specs=anywhere(7),
        out_specs=tuple(in_vmem(3)),
        scratch_shapes=[
            pltpu.VMEM((n_dp, packed_rows, LANES), bf16),
            pltpu.VMEM((3, factors, window), f32),
            pltpu.VMEM((3, up_rows, columns), f32),
            pltpu.SemaphoreType.DMA((7,)),
        ],
        compiler_params=pltpu.CompilerParams(vmem_limit_bytes=LARGE_VMEM_BYTES),
    )(exchanged, *down_state, *up_state)
    own_f = lax.all_to_all(sent, "dp", 0, 0, tiled=True)
    for half in range(1, halves):
        send_half(half, (mine[-1], sent))
    a_next = jnp.transpose(a_next.reshape(3, parts, rank, down_rows), (0, 3, 1, 2))

    outside = [[] for _ in range(strips)]

    def swap_half(half, after):
        for value in mine[half]:
            value, _ = lax.optimization_barrier((value, after))
            split = pl.pallas_call(
                split_kernel,
                out_shape=(jax.ShapeDtypeStruct((features, LANES), bf16),) * len(groups[half]),
                in_specs=anywhere(1),
                out_specs=tuple(anywhere(len(groups[half]))),
                scratch_shapes=[
                    pltpu.VMEM(value.shape, bf16),
                    pltpu.SemaphoreType.DMA((2 * len(groups[half]),)),
                    pltpu.SemaphoreType.DMA((2 * len(groups[half]),)),
                ],
                compiler_params=params(),
            )(value)
            for piece, strip in zip(split, groups[half]):
                pairs = [(i, i ^ turn[strip]) for i in range(n_dp)]
                outside[strip].append((piece, lax.ppermute(piece, "dp", pairs)))

    swap_half(0, sent)
    own_f, x1 = lax.optimization_barrier((own_f, x1))
    up_packed = packed_rows - down_rows
    more = pl.cdiv(3 * (tokens // LANES), up_packed)
    piece = jax.ShapeDtypeStruct((n_dp // FACTOR_PIECES, packed_rows, LANES), bf16)
    message, *pieces = pl.pallas_call(
        message_kernel,
        out_shape=(jax.ShapeDtypeStruct((n_dp + more, up_packed, LANES), bf16),)
        + (piece,) * FACTOR_PIECES,
        in_specs=anywhere(2),
        out_specs=tuple(in_vmem(1 + FACTOR_PIECES)),
        scratch_shapes=[
            pltpu.VMEM(squares.shape, f32),
            pltpu.SemaphoreType.DMA((2 + FACTOR_PIECES,)),
        ],
        compiler_params=params(),
    )(own_f, squares)
    messages = [to_chip(message, step) for step in steps]
    sibling_f = [to_sibling(piece) for piece in pieces]

    inv_rms = pl.pallas_call(
        functools.partial(inverse_kernel, width, n_dp),
        out_shape=jax.ShapeDtypeStruct((tokens, LANES), f32),
        in_specs=in_vmem(chips),
        out_specs=in_vmem(1)[0],
        compiler_params=params(),
    )(squares, *messages)

    scale = 0.5 / math.sqrt(width * rank)

    received = {}
    after = []
    weights_shape = jax.ShapeDtypeStruct((CORES * features, wide), bf16)
    product_shape = jax.ShapeDtypeStruct((some, wide), bf16)
    for half, group in enumerate(groups):
        static = (scale, parts, up_rows, group, columns)
        if half > 0:
            swap_half(half, products[0])
        for step in steps:
            blocks = [value for strip in group for value in outside[strip][step - 1]]
            arranged = pl.pallas_call(
                functools.partial(arrange_kernel, [turn[strip] for strip in group]),
                out_shape=weights_shape,
                in_specs=in_vmem(len(blocks)) + anywhere(len(after)),
                out_specs=in_vmem(1)[0],
                compiler_params=params(),
            )(*blocks, *after)
            weights, product = pl.pallas_call(
                functools.partial(outside_kernel, static, chips, step),
                out_shape=(weights_shape, product_shape),
                in_specs=in_vmem(3 + 2 * FACTOR_PIECES),
                out_specs=tuple(in_vmem(2)),
                compiler_params=params(),
            )(arranged, messages[step - 1], *x0, *pieces, *sibling_f)
            received.setdefault((0, half), []).append(to_chip(product, chips - step))
            second = pl.pallas_call(
                functools.partial(more_kernel, len(x1) // 2),
                out_shape=product_shape,
                in_specs=in_vmem(1 + len(x1)),
                out_specs=in_vmem(1)[0],
                compiler_params=params(),
            )(*x1, weights)
            products = [product, second]
            after = [second]
            received.setdefault((1, half), []).append(to_chip(second, chips - step))
        if half == 0:
            after = [received[0, 0][0]]

    after.append(received[1, 0][0])
    static = (scale, parts, up_rows, range(strips), columns, halves, len(x1) // 2)
    totals = pl.pallas_call(
        functools.partial(own_kernel, static),
        out_shape=(jax.ShapeDtypeStruct((tokens, wide), f32),) * halves,
        grid=(1,),
        in_specs=[
            pl.BlockSpec((features, columns), lambda i: (lax.axis_index("tensor"), 0)),
            pl.BlockSpec((features, columns), lambda i: (lax.axis_index("tensor") ^ 1, 0)),
        ]
        + in_vmem(2 * FACTOR_PIECES + 1 + len(x1))
        + anywhere(len(after)),
        out_specs=tuple(in_vmem(halves)),
        scratch_shapes=[pltpu.VMEM((CORES * features, columns), bf16)],
        compiler_params=params(),
        cost_estimate=pl.CostEstimate(
            flops=2 * tokens * CORES * features * columns,
            bytes_accessed=4 * tokens * features,
            transcendentals=0,
        ),
    )(frozen_key_value, frozen_key_value, *pieces, *sibling_f, *x0, *x1, *after)

    keys_values = None
    for at, values in received.items():
        keys_values = finish(
            totals[at[1]], inv_rms, values, at, (tokens, columns), keys_values
        )
    return (a_next, b_next, keys_values)


def solution(mesh):
    placed = (
        P("dp", "tensor"),
        P("tensor"),
        P(None, "tensor"),
        P("tensor", None, None),
        P("tensor", None, None),
        P("tensor", None, None),
        P(None, "tensor"),
        P(None, "tensor"),
        P(None, "tensor"),
        P("dp", "tensor", None, None),
        P("dp", None, "tensor"),
    )
    return jax.shard_map(
        body,
        mesh=mesh,
        in_specs=placed,
        out_specs=(
            P(None, ("tensor", "dp"), None, None),
            P(None, "dp", "tensor"),
            P("dp", "tensor"),
        ),
        check_vma=False,
    )
```
